32 devices in a mesh: dp: 16 (over z, y, x), narrow: 2 (over core).
Axes of the slice: x: 2, y: 2, z: 4, core: 2. Of those that a mesh axis runs over, the one named last changes fastest.
Arguments:
- tokens: bfloat16 [16384, 768], P(('dp', 'narrow')), may hold values from -6 to 6
- cotangent: bfloat16 [16384, 768], P(('dp', 'narrow')), may hold values from -6 to 6
- gains: float32 [2, 768], replicated, may hold values from 0.5 to 1.5
- gain_moments: float32 [2, 768], replicated, may hold values from 10485 to 41943
- qkv_master: float32 [3, 2, 128, 48, 48], P(None, 'narrow', 'dp'), may hold values from -0.21875 to 0.21875
- out_master: float32 [2, 128, 48, 48], P('narrow', 'dp'), may hold values from -1.25 to 1.25
- ffn_master: float32 [2, 2, 128, 48, 128], P(None, 'narrow', 'dp'), may hold values from -0.21875 to 0.21875
- down_master: float32 [2, 128, 128, 48], P('narrow', 'dp'), may hold values from -0.125 to 0.125
- attn_left: float32 [4, 2, 128, 48, 48], P(None, 'narrow', 'dp'), as said below
- attn_right: float32 [4, 2, 128, 48, 48], P(None, 'narrow', 'dp'), as said below
- attn_left_root: float32 [4, 2, 128, 48, 48], P(None, 'narrow', 'dp'), as said below
- attn_right_root: float32 [4, 2, 128, 48, 48], P(None, 'narrow', 'dp'), as said below
- ffn_left: float32 [2, 2, 128, 48, 48], P(None, 'narrow', 'dp'), as said below
- ffn_right: float32 [2, 2, 128, 128, 128], P(None, 'narrow', 'dp'), as said below
- ffn_left_root: float32 [2, 2, 128, 48, 48], P(None, 'narrow', 'dp'), as said below
- ffn_right_root: float32 [2, 2, 128, 128, 128], P(None, 'narrow', 'dp'), as said below
- down_left: float32 [2, 128, 128, 128], P('narrow', 'dp'), as said below
- down_right: float32 [2, 128, 48, 48], P('narrow', 'dp'), as said below
- down_left_root: float32 [2, 128, 128, 128], P('narrow', 'dp'), as said below
- down_right_root: float32 [2, 128, 48, 48], P('narrow', 'dp'), as said below
Outputs:
- layer_out: bfloat16 [16384, 768], P(('dp', 'narrow'))
- input_grad: float32 [16384, 768], P(('dp', 'narrow'))
- gain_grad: float32 [2, 768], replicated
- gain_moment_new: float32 [2, 768], replicated
- gain_new: float32 [2, 768], replicated
- attn_grad: float32 [4, 2, 128, 48, 48], P(None, 'narrow', 'dp')
- attn_left_new: float32 [4, 2, 128, 48, 48], P(None, 'narrow', 'dp')
- attn_right_new: float32 [4, 2, 128, 48, 48], P(None, 'narrow', 'dp')
- qkv_new: float32 [3, 2, 128, 48, 48], P(None, 'narrow', 'dp')
- out_new: float32 [2, 128, 48, 48], P('narrow', 'dp')
- ffn_grad: float32 [2, 2, 128, 48, 128], P(None, 'narrow', 'dp')
- ffn_left_new: float32 [2, 2, 128, 48, 48], P(None, 'narrow', 'dp')
- ffn_right_new: float32 [2, 2, 128, 128, 128], P(None, 'narrow', 'dp')
- ffn_new: float32 [2, 2, 128, 48, 128], P(None, 'narrow', 'dp')
- down_grad: float32 [2, 128, 128, 48], P('narrow', 'dp')
- down_left_new: float32 [2, 128, 128, 128], P('narrow', 'dp')
- down_right_new: float32 [2, 128, 48, 48], P('narrow', 'dp')
- down_new: float32 [2, 128, 128, 48], P('narrow', 'dp')
The draws below stay inside these ranges and needn't reach their ends.
Inputs may be any that keep to these rules, and one draw needn't show every extreme that they name: `attn_left`: symmetric positive definite blocks. `attn_right`: symmetric positive definite blocks. `attn_left_root`: symmetric blocks. `attn_right_root`: symmetric blocks. `ffn_left`: symmetric positive definite blocks. `ffn_right`: symmetric positive definite blocks. `ffn_left_root`: symmetric blocks. `ffn_right_root`: symmetric blocks. `down_left`: symmetric positive definite blocks. `down_right`: symmetric positive definite blocks. `down_left_root`: symmetric blocks. `down_right_root`: symmetric blocks.
All inputs are finite; a program needn't handle non-finite values.
Results may differ from the reference program's by a relative error of at most 0.014.
Values may be sent and summed in bfloat16 or wider, within the bound.
No kernel may reach another device: no remote copies, remote signals or barrier semaphores. Data moves between devices by JAX's collectives and lax.ppermute only.
A program may use at most 192 MiB of HBM per device.

```python
import math
from functools import partial
import jax
import jax.numpy as jnp
from jax import lax

D = 768
HEADS = 12
HEAD_DIM = 64
FF = 2048
LEN = 1024
GRID = 16
DBLK = 48
FBLK = 128
HALF_BLOCKS = 128
TOKENS = 16384


def stat_blocks(key, lead_shape, magnitude):
    block_size = lead_shape[-1]
    uniform_draw = jax.random.uniform(key, lead_shape, jnp.float32)
    factors = jnp.exp(uniform_draw * math.log(4.0))
    return factors[..., None] * jnp.eye(block_size, dtype=jnp.float32) * magnitude


def root_blocks(key, lead_shape, magnitude):
    block_size = lead_shape[-1]
    key_diagonal, key_noise = jax.random.split(key)
    uniform_draw = jax.random.uniform(key_diagonal, lead_shape, jnp.float32)
    diagonal = jnp.exp((2.0 * uniform_draw - 1.0) * math.log(2.0))
    full_shape = lead_shape + (block_size,)
    normal_noise = jnp.clip(jax.random.normal(key_noise, full_shape, jnp.float32), -4.0, 4.0)
    noise_draw = normal_noise
    identity = jnp.eye(block_size, dtype=jnp.float32)
    crossing = (noise_draw + jnp.swapaxes(noise_draw, -1, -2)) * (0.3 / math.sqrt(block_size))
    return (diagonal[..., None] * identity + crossing * (1.0 - identity)) * magnitude ** (-0.25)


def draw_attn_left(key, part):
    key = jax.random.fold_in(key, 11)
    return stat_blocks(key, (4, 2, HALF_BLOCKS, DBLK), DBLK * TOKENS * 0.1)


def draw_attn_right(key, part):
    key = jax.random.fold_in(key, 12)
    return stat_blocks(key, (4, 2, HALF_BLOCKS, DBLK), DBLK * TOKENS * 0.1)


def draw_attn_left_root(key, part):
    key = jax.random.fold_in(key, 13)
    return root_blocks(key, (4, 2, HALF_BLOCKS, DBLK), DBLK * TOKENS * 0.1)


def draw_attn_right_root(key, part):
    key = jax.random.fold_in(key, 14)
    return root_blocks(key, (4, 2, HALF_BLOCKS, DBLK), DBLK * TOKENS * 0.1)


def draw_ffn_left(key, part):
    key = jax.random.fold_in(key, 15)
    return stat_blocks(key, (2, 2, HALF_BLOCKS, DBLK), FBLK * TOKENS * 0.16)


def draw_ffn_right(key, part):
    key = jax.random.fold_in(key, 16)
    return stat_blocks(key, (2, 2, HALF_BLOCKS, FBLK), DBLK * TOKENS * 0.16)


def draw_ffn_left_root(key, part):
    key = jax.random.fold_in(key, 17)
    return root_blocks(key, (2, 2, HALF_BLOCKS, DBLK), FBLK * TOKENS * 0.16)


def draw_ffn_right_root(key, part):
    key = jax.random.fold_in(key, 18)
    return root_blocks(key, (2, 2, HALF_BLOCKS, FBLK), DBLK * TOKENS * 0.16)


def draw_down_left(key, part):
    key = jax.random.fold_in(key, 19)
    return stat_blocks(key, (2, HALF_BLOCKS, FBLK), DBLK * TOKENS * 0.36)


def draw_down_right(key, part):
    key = jax.random.fold_in(key, 20)
    return stat_blocks(key, (2, HALF_BLOCKS, DBLK), FBLK * TOKENS * 0.36)


def draw_down_left_root(key, part):
    key = jax.random.fold_in(key, 21)
    return root_blocks(key, (2, HALF_BLOCKS, FBLK), DBLK * TOKENS * 0.36)


def draw_down_right_root(key, part):
    key = jax.random.fold_in(key, 22)
    return root_blocks(key, (2, HALF_BLOCKS, DBLK), FBLK * TOKENS * 0.36)


def levels(rng, shape, cuts, smallest, high):
    def one(dim, blocks):
        heights = jax.random.uniform(jax.random.fold_in(jax.random.fold_in(rng, 6), dim), (blocks,), jnp.float32, smallest / len(cuts), high / len(cuts))
        return jnp.repeat(jnp.exp(heights), shape[dim] // blocks).reshape((-1,) + (1,) * (len(shape) - dim - 1))

    loudness = one(*cuts[0])
    for cut in cuts[1:]:
        loudness = loudness * one(*cut)
    return loudness


def normal_values(key, extent, deviation, bound, shards=(), kind=jnp.bfloat16):
    result = jax.random.normal(key, extent, jnp.float32) * deviation
    if len(shards) > 0:
        result = levels(key, extent, shards, -0.22, 0.18) * result
    return jnp.clip(result, min=-bound, max=bound).astype(kind)


def setup_inputs(seed: int = 0) -> dict:
    arg_keys = jax.random.split(jax.random.key(seed), 21)
    return {
        "tokens": normal_values(arg_keys[0], (TOKENS, D), 1.0, 6.0, ((0, 32),)),
        "cotangent": normal_values(arg_keys[1], (TOKENS, D), 1.0, 6.0, ((0, 32),)),
        "gains": jnp.clip(1.0 + 0.1 * jax.random.normal(arg_keys[2], (2, D), jnp.float32), 0.5, 1.5),
        "gain_moments": jnp.clip(jnp.exp(jax.random.uniform(arg_keys[3], (2, D), jnp.float32, math.log(10485.0), math.log(41943.0))), 10485.0, 41943.0),
        "qkv_master": normal_values(arg_keys[4], (3, 2, HALF_BLOCKS, DBLK, DBLK), D ** -0.5, 0.21875, ((1, 2), (2, 16)), jnp.float32),
        "out_master": normal_values(arg_keys[5], (2, HALF_BLOCKS, DBLK, DBLK), (max(D // 32, D * 16 // LEN)) ** -0.5, 1.25, ((0, 2), (1, 16)), jnp.float32),
        "ffn_master": normal_values(arg_keys[6], (2, 2, HALF_BLOCKS, DBLK, FBLK), D ** -0.5, 0.21875, ((1, 2), (2, 16)), jnp.float32),
        "down_master": normal_values(arg_keys[7], (2, HALF_BLOCKS, FBLK, DBLK), FF ** -0.5, 0.125, ((0, 2), (1, 16)), jnp.float32),
        "attn_left": draw_attn_left(jax.random.fold_in(arg_keys[20], 71), 0),
        "attn_right": draw_attn_right(jax.random.fold_in(arg_keys[20], 71), 0),
        "attn_left_root": draw_attn_left_root(jax.random.fold_in(arg_keys[20], 71), 0),
        "attn_right_root": draw_attn_right_root(jax.random.fold_in(arg_keys[20], 71), 0),
        "ffn_left": draw_ffn_left(jax.random.fold_in(arg_keys[20], 71), 0),
        "ffn_right": draw_ffn_right(jax.random.fold_in(arg_keys[20], 71), 0),
        "ffn_left_root": draw_ffn_left_root(jax.random.fold_in(arg_keys[20], 71), 0),
        "ffn_right_root": draw_ffn_right_root(jax.random.fold_in(arg_keys[20], 71), 0),
        "down_left": draw_down_left(jax.random.fold_in(arg_keys[20], 71), 0),
        "down_right": draw_down_right(jax.random.fold_in(arg_keys[20], 71), 0),
        "down_left_root": draw_down_left_root(jax.random.fold_in(arg_keys[20], 71), 0),
        "down_right_root": draw_down_right_root(jax.random.fold_in(arg_keys[20], 71), 0),
    }


EPSILON = 1e-05
DECAY = 0.5
STEP_RATE = 0.25
GAIN_RATE = 0.1
NEG_FILL = -1e+30
HIGHEST_PRECISION = lax.Precision.HIGHEST

@jax.custom_vjp
def low(v):
    return lax.optimization_barrier(v.astype(jnp.bfloat16)).astype(jnp.float32)

@jax.custom_vjp
def low_back(v):
    return v

def low_keep(v):
    return (low(v), None)

def low_pass(kept, grad):
    return (grad,)

def back_keep(v):
    return (v, None)

def back_low(kept, grad):
    return (low(grad),)
low.defvjp(low_keep, low_pass)
low_back.defvjp(back_keep, back_low)

def rotate(features, cosine, sine_part):
    half_dim = features.shape[-1] // 2
    lower_half = features[..., :half_dim]
    upper_half = features[..., half_dim:]
    return jnp.concatenate([lower_half * cosine - upper_half * sine_part, upper_half * cosine + lower_half * sine_part], -1)

def columns_matrix(blocks, block_rows, block_cols):
    tiled = blocks.reshape(2, GRID, GRID // 2, block_rows, block_cols)
    return tiled.transpose(1, 3, 0, 2, 4).reshape(GRID * block_rows, GRID * block_cols)

def rows_matrix(blocks, block_rows, block_cols):
    tiled = blocks.reshape(2, GRID // 2, GRID, block_rows, block_cols)
    return tiled.transpose(0, 1, 3, 2, 4).reshape(GRID * block_rows, GRID * block_cols)

def columns_blocks(matrix, block_rows, block_cols):
    tiled = matrix.reshape(GRID, block_rows, 2, GRID // 2, block_cols)
    return tiled.transpose(2, 0, 3, 1, 4).reshape(2, GRID * GRID // 2, block_rows, block_cols)

def rows_blocks(matrix, block_rows, block_cols):
    tiled = matrix.reshape(2, GRID // 2, block_rows, GRID, block_cols)
    return tiled.transpose(0, 1, 3, 2, 4).reshape(2, GRID * GRID // 2, block_rows, block_cols)

def precondition(block_grad, left_stat, right_stat, left_root, right_root, master):
    new_left = DECAY * left_stat + (1.0 - DECAY) * jnp.einsum('...ij,...kj->...ik', block_grad, block_grad, precision=HIGHEST_PRECISION)
    new_right = DECAY * right_stat + (1.0 - DECAY) * jnp.einsum('...ji,...jk->...ik', block_grad, block_grad, precision=HIGHEST_PRECISION)
    turned = jnp.einsum('...ij,...jk->...ik', left_root, block_grad, precision=HIGHEST_PRECISION)
    turned = jnp.einsum('...ij,...jk->...ik', turned, right_root, precision=HIGHEST_PRECISION)
    return (new_left, new_right, master - STEP_RATE * turned)

def layer(inputs, gain_one, gain_two, w_query, w_key, w_value, w_out, w_gate, w_up, w_down, cosine, sine_part):
    group_rows = inputs.shape[0]
    score_scale = 1.0 / math.sqrt(HEAD_DIM)
    scale_one = lax.rsqrt(lax.optimization_barrier(jnp.mean(inputs * inputs, -1, keepdims=True)) + EPSILON)
    normed_one = low(inputs * scale_one * gain_one)

    def heads_of(weight):
        return jnp.dot(normed_one, weight, precision=HIGHEST_PRECISION).reshape(group_rows, HEADS, HEAD_DIM)
    queries = low(rotate(low_back(heads_of(w_query)), cosine, sine_part))
    key_rows = low(rotate(low_back(heads_of(w_key)), cosine, sine_part))
    value_rows = low(low_back(heads_of(w_value)))
    scores = low_back(jnp.einsum('qhd,khd->hqk', queries, key_rows, precision=HIGHEST_PRECISION)) * score_scale
    causal = jnp.arange(group_rows)[:, None] >= jnp.arange(group_rows)[None, :]
    scores = jnp.where(causal[None], scores, NEG_FILL)
    probs = low(jax.nn.softmax(scores, axis=-1))
    attended = jnp.einsum('hqk,khd->qhd', probs, value_rows, precision=HIGHEST_PRECISION).reshape(group_rows, D)
    attended = low(low_back(attended))
    middle = inputs + low_back(jnp.dot(attended, w_out, precision=HIGHEST_PRECISION))
    scale_two = lax.rsqrt(lax.optimization_barrier(jnp.mean(middle * middle, -1, keepdims=True)) + EPSILON)
    normed_two = low(middle * scale_two * gain_two)
    gate_pre = low_back(jnp.dot(normed_two, w_gate, precision=HIGHEST_PRECISION))
    up_pre = low_back(jnp.dot(normed_two, w_up, precision=HIGHEST_PRECISION))
    hidden = low(jax.nn.silu(gate_pre) * up_pre)
    return middle + low_back(jnp.dot(hidden, w_down, precision=HIGHEST_PRECISION))

def reference(tokens, cotangent, gains, gain_moments, qkv_master, out_master, ffn_master, down_master, attn_left, attn_right, attn_left_root, attn_right_root, ffn_left, ffn_right, ffn_left_root, ffn_right_root, down_left, down_right, down_left_root, down_right_root):
    width_block = D // GRID
    hidden_block = FF // GRID
    qkv_low = low(qkv_master)
    out_low = low(out_master)
    ffn_low = low(ffn_master)
    down_low = low(down_master)
    weights = (gains[0], gains[1], columns_matrix(qkv_low[0], width_block, width_block), columns_matrix(qkv_low[1], width_block, width_block), columns_matrix(qkv_low[2], width_block, width_block), rows_matrix(out_low, width_block, width_block), columns_matrix(ffn_low[0], width_block, hidden_block), columns_matrix(ffn_low[1], width_block, hidden_block), rows_matrix(down_low, hidden_block, width_block))
    frequency = jnp.power(10000.0, -2.0 * jnp.arange(HEAD_DIM // 2, dtype=jnp.float32) / HEAD_DIM)
    angles = jnp.arange(LEN, dtype=jnp.float32)[:, None] * frequency[None, :]
    forward = partial(layer, cosine=jnp.cos(angles)[:, None, :], sine_part=jnp.sin(angles)[:, None, :])

    def one_sequence(totals, seq_pair):
        seq_input, seq_back = seq_pair
        outputs, pullback = jax.vjp(forward, seq_input.astype(jnp.float32), *weights)
        seq_grads = pullback(seq_back.astype(jnp.float32))
        summed = tuple((total + grad_part for total, grad_part in zip(totals, seq_grads[1:])))
        return (summed, (outputs.astype(jnp.bfloat16), seq_grads[0]))
    initial = tuple((jnp.zeros_like(weight) for weight in weights))
    totals, (layer_out, input_grad) = lax.scan(one_sequence, initial, (tokens.reshape(-1, LEN, D), cotangent.reshape(-1, LEN, D)))
    layer_out = layer_out.reshape(-1, D)
    input_grad = input_grad.reshape(-1, D)
    gain_grad = jnp.stack([totals[0], totals[1]])
    gain_moment_new = DECAY * gain_moments + (1.0 - DECAY) * gain_grad * gain_grad
    gain_new = gains - GAIN_RATE * gain_grad / (jnp.sqrt(gain_moment_new) + 1e-08)
    attn_grad = jnp.stack([columns_blocks(totals[2], width_block, width_block), columns_blocks(totals[3], width_block, width_block), columns_blocks(totals[4], width_block, width_block), rows_blocks(totals[5], width_block, width_block)])
    ffn_grad = jnp.stack([columns_blocks(totals[6], width_block, hidden_block), columns_blocks(totals[7], width_block, hidden_block)])
    down_grad = rows_blocks(totals[8], hidden_block, width_block)
    attn_master = jnp.concatenate([qkv_master, out_master[None]], 0)
    attn_left_new, attn_right_new, attn_new = precondition(attn_grad, attn_left, attn_right, attn_left_root, attn_right_root, attn_master)
    ffn_left_new, ffn_right_new, ffn_new = precondition(ffn_grad, ffn_left, ffn_right, ffn_left_root, ffn_right_root, ffn_master)
    down_left_new, down_right_new, down_new = precondition(down_grad, down_left, down_right, down_left_root, down_right_root, down_master)
    return (layer_out, input_grad, gain_grad, gain_moment_new, gain_new, attn_grad, attn_left_new, attn_right_new, attn_new[:3], attn_new[3], ffn_grad, ffn_left_new, ffn_right_new, ffn_new, down_grad, down_left_new, down_right_new, down_new)
```

```python
import math

import jax
import jax.numpy as jnp
from jax import lax
from jax.experimental import pallas as pl
from jax.experimental.pallas import tpu as pltpu
from jax.sharding import PartitionSpec as P

D = 768
HEAD_DIM = 64
FF = 2048
LEN = 1024
GRID = 16
DBLK = D // GRID
FBLK = FF // GRID
HALF_GRID = GRID // 2
HALF_D = D // 2
HALF_FF = FF // 2
PAIR = 2 * HEAD_DIM
ROWS = 256

EPSILON = 1e-05
DECAY = 0.5
STEP_RATE = 0.25
GAIN_RATE = 0.1
NEG_FILL = -1e30
HIGHEST_PRECISION = lax.Precision.HIGHEST
BF16 = jnp.bfloat16
F32 = jnp.float32
VMEM_BYTES = 56 * 1024 * 1024


def dot_nn(left, right):
    return lax.dot_general(left, right, (((1,), (0,)), ((), ())), preferred_element_type=F32)


def dot_nt(left, right):
    return lax.dot_general(left, right, (((1,), (1,)), ((), ())), preferred_element_type=F32)


def dot_tn(left, right):
    return lax.dot_general(left, right, (((0,), (0,)), ((), ())), preferred_element_type=F32)


def kernel_params():
    return pltpu.CompilerParams(vmem_limit_bytes=VMEM_BYTES)


def cost(flops, bytes_accessed, transcendentals=0):
    return pl.CostEstimate(
        flops=flops, bytes_accessed=bytes_accessed, transcendentals=transcendentals
    )


def rows_spec(columns):
    return pl.BlockSpec((ROWS, columns), lambda i: (i, 0))


def whole_spec(*shape):
    return pl.BlockSpec(shape, lambda i: (0,) * len(shape))


def lower_lanes(shape):
    return lax.broadcasted_iota(jnp.int32, shape, 1) % HEAD_DIM < HEAD_DIM // 2


def turn(features, cosine, sine_part, lower):
    half = HEAD_DIM // 2
    partner = jnp.where(
        lower, pltpu.roll(features, PAIR - half, 1), pltpu.roll(features, half, 1)
    )
    return features * cosine + partner * sine_part


def project_kernel(x_ref, gain_ref, w_ref, cos_ref, sin_ref, n1_ref, q_ref, k_ref, v_ref):
    x = x_ref[...].astype(F32)
    scale = lax.rsqrt(jnp.mean(x * x, -1, keepdims=True) + EPSILON)
    normed = (x * scale * gain_ref[0:1, :]).astype(BF16)
    n1_ref[...] = normed
    lower = lower_lanes((ROWS, PAIR))
    cosine, sine_part = cos_ref[...], sin_ref[...]
    both = dot_nn(normed, w_ref[...])
    for tile in range(HALF_D // PAIR):
        lanes = slice(tile * PAIR, (tile + 1) * PAIR)
        query = both[:, tile * PAIR : (tile + 1) * PAIR]
        key = both[:, HALF_D + tile * PAIR : HALF_D + (tile + 1) * PAIR]
        turned = turn(query, cosine, sine_part, lower).astype(BF16)
        q_ref[:, lanes] = turned * BF16(1.0 / math.sqrt(HEAD_DIM))
        k_ref[:, lanes] = turn(key, cosine, sine_part, lower).astype(BF16)
    v_ref[...] = both[:, 2 * HALF_D :].astype(BF16)


def project(x, gains, weight, cosine, sine_part):
    length = x.shape[0]
    half = jax.ShapeDtypeStruct((length, HALF_D), BF16)
    return pl.pallas_call(
        project_kernel,
        grid=(length // ROWS,),
        in_specs=[
            rows_spec(D),
            whole_spec(2, D),
            whole_spec(D, 3 * HALF_D),
            rows_spec(PAIR),
            rows_spec(PAIR),
        ],
        out_specs=[rows_spec(D), rows_spec(HALF_D), rows_spec(HALF_D), rows_spec(HALF_D)],
        out_shape=[jax.ShapeDtypeStruct((length, D), BF16), half, half, half],
        compiler_params=kernel_params(),
        cost_estimate=cost(2 * length * D * 3 * HALF_D, 8 * length * D),
        name="project",
    )(x, gains, weight, cosine, sine_part)


def attend_kernel(q_ref, k_ref, v_ref, o_ref, lse_ref):
    length = q_ref.shape[0]
    first_head = lax.broadcasted_iota(jnp.int32, (ROWS, PAIR), 1) < HEAD_DIM
    keys = k_ref[...]
    values = jnp.concatenate([v_ref[...], jnp.ones((length, PAIR), BF16)], 1)
    causal = lax.broadcasted_iota(jnp.int32, (ROWS, ROWS), 0) >= lax.broadcasted_iota(
        jnp.int32, (ROWS, ROWS), 1
    )
    for block in range(length // ROWS):
        rows = slice(block * ROWS, (block + 1) * ROWS)
        width = (block + 1) * ROWS
        query_block = q_ref[rows, :]
        parts, sums = [], []
        for head in range(2):
            mine = first_head if head == 0 else jnp.logical_not(first_head)
            query = jnp.where(mine, query_block, jnp.zeros_like(query_block))
            scores = jnp.where(causal, dot_nt(query, keys[block * ROWS : width]), NEG_FILL)
            if block:
                scores = jnp.concatenate([dot_nt(query, keys[: block * ROWS]), scores], 1)
            top = jnp.max(scores, 1, keepdims=True)
            exponent = jnp.exp(scores - top).astype(BF16)
            product = dot_nn(exponent, values[:width])
            total = product[:, PAIR:]
            parts.append(product[:, :PAIR] / total)
            sums.append(top + jnp.log(total))
        o_ref[rows, :] = jnp.where(first_head, parts[0], parts[1]).astype(BF16)
        lane = lax.broadcasted_iota(jnp.int32, (ROWS, PAIR), 1)
        lse_ref[:, rows] = jnp.transpose(jnp.where(lane == 0, sums[0], sums[1]))[:8, :]


def attend(q, k, v):
    length = q.shape[0]
    pairs = q.shape[1] // PAIR
    block = pl.BlockSpec((length, PAIR), lambda h: (0, h))
    return pl.pallas_call(
        attend_kernel,
        grid=(pairs,),
        in_specs=[block] * 3,
        out_specs=[block, pl.BlockSpec((8, length), lambda h: (h, 0))],
        out_shape=[
            jax.ShapeDtypeStruct(q.shape, BF16),
            jax.ShapeDtypeStruct((8 * pairs, length), F32),
        ],
        compiler_params=kernel_params(),
        cost_estimate=cost(8 * length * length * PAIR * pairs, 8 * length * PAIR * pairs),
        name="attend",
    )(q, k, v)


def attend_back_kernel(
    q_ref, k_ref, v_ref, do_ref, o_ref, lse_ref, cos_ref, sin_ref, dq_ref, dk_ref, dv_ref, dqt_ref
):
    length = q_ref.shape[0]
    first_head = lax.broadcasted_iota(jnp.int32, (length, PAIR), 1) < HEAD_DIM
    zero = BF16(0)
    queries = [
        jnp.where(first_head, q_ref[...], zero),
        jnp.where(first_head, zero, q_ref[...]),
    ]
    grads = [
        jnp.where(first_head, do_ref[...], zero),
        jnp.where(first_head, zero, do_ref[...]),
    ]
    product = do_ref[...].astype(F32) * o_ref[...].astype(F32)
    head_row = lax.broadcasted_iota(jnp.int32, (8, PAIR), 0)
    head_lane = lax.broadcasted_iota(jnp.int32, (8, PAIR), 1) // HEAD_DIM
    inner = lax.dot_general(
        (head_row == head_lane).astype(F32),
        product,
        (((1,), (1,)), ((), ())),
        preferred_element_type=F32,
        precision=HIGHEST_PRECISION,
    )
    turned_keys = jnp.transpose(k_ref[...].astype(F32)).astype(BF16)
    first_rows = lax.broadcasted_iota(jnp.int32, turned_keys.shape, 0) < HEAD_DIM
    key_heads = [
        jnp.where(first_rows, turned_keys, zero),
        jnp.where(first_rows, zero, turned_keys),
    ]
    causal = lax.broadcasted_iota(jnp.int32, (ROWS, ROWS), 0) <= lax.broadcasted_iota(
        jnp.int32, (ROWS, ROWS), 1
    )
    dqt_ref[...] = jnp.zeros_like(dqt_ref)
    lower = lower_lanes((ROWS, PAIR))
    for block in range(length // ROWS):
        rows = slice(block * ROWS, (block + 1) * ROWS)
        start = block * ROWS
        key_block, value_block = k_ref[rows, :], v_ref[rows, :]
        dk = jnp.zeros((ROWS, PAIR), F32)
        dv = jnp.zeros((ROWS, PAIR), F32)
        for head in range(2):
            scores = dot_nt(key_block, queries[head][start:])
            probs = jnp.exp(scores - lse_ref[head : head + 1, start:])
            diagonal = jnp.where(causal, probs[:, :ROWS], 0.0)
            if start + ROWS == length:
                probs = diagonal
            else:
                probs = jnp.concatenate([diagonal, probs[:, ROWS:]], 1)
            prob_grad = dot_nt(value_block, grads[head][start:])
            score_grad = (probs * (prob_grad - inner[head : head + 1, start:])).astype(BF16)
            dv = dv + dot_nn(probs.astype(BF16), grads[head][start:])
            dk = dk + dot_nn(score_grad, queries[head][start:])
            dqt_ref[:, start:] += dot_nn(key_heads[head][:, rows], score_grad)
        dk_ref[rows, :] = turn(dk, cos_ref[rows, :], -sin_ref[rows, :], lower).astype(BF16)
        dv_ref[rows, :] = dv.astype(BF16)
    for block in range(length // ROWS):
        rows = slice(block * ROWS, (block + 1) * ROWS)
        dq = jnp.transpose(dqt_ref[:, rows]) * (1.0 / math.sqrt(HEAD_DIM))
        dq_ref[rows, :] = turn(dq, cos_ref[rows, :], -sin_ref[rows, :], lower).astype(BF16)


def attend_back(q, k, v, grad, o, lse, cosine, sine_part):
    length = q.shape[0]
    pairs = q.shape[1] // PAIR
    block = pl.BlockSpec((length, PAIR), lambda h: (0, h))
    table = pl.BlockSpec((length, PAIR), lambda h: (0, 0))
    return pl.pallas_call(
        attend_back_kernel,
        grid=(pairs,),
        in_specs=[block] * 5 + [pl.BlockSpec((8, length), lambda h: (h, 0)), table, table],
        out_specs=[block] * 3,
        out_shape=[jax.ShapeDtypeStruct(q.shape, BF16)] * 3,
        scratch_shapes=[pltpu.VMEM((PAIR, length), F32)],
        compiler_params=kernel_params(),
        cost_estimate=cost(14 * length * length * PAIR * pairs, 20 * length * PAIR * pairs),
        name="attend_back",
    )(q, k, v, grad, o, lse, cosine, sine_part)


def ffn_kernel(
    x_ref, o_ref, o_far_ref, wo_ref, wo_far_ref, gain_ref, wg_ref, wu_ref,
    x1_ref, n2_ref, gate_ref, up_ref, hidden_ref,
):
    middle = (
        x_ref[...].astype(F32)
        + dot_nn(o_ref[...], wo_ref[...])
        + dot_nn(o_far_ref[...], wo_far_ref[...])
    )
    x1_ref[...] = middle
    scale = lax.rsqrt(jnp.mean(middle * middle, -1, keepdims=True) + EPSILON)
    normed = (middle * scale * gain_ref[1:2, :]).astype(BF16)
    n2_ref[...] = normed
    gate = dot_nn(normed, wg_ref[...])
    up = dot_nn(normed, wu_ref[...])
    gate_ref[...] = gate
    up_ref[...] = up
    hidden_ref[...] = (gate * jax.nn.sigmoid(gate) * up).astype(BF16)


def ffn(x, o, o_far, wo, wo_far, gains, wg, wu):
    length = x.shape[0]
    wide = jax.ShapeDtypeStruct((length, HALF_FF), F32)
    return pl.pallas_call(
        ffn_kernel,
        grid=(length // ROWS,),
        in_specs=[
            rows_spec(D),
            rows_spec(HALF_D),
            rows_spec(HALF_D),
            whole_spec(HALF_D, D),
            whole_spec(HALF_D, D),
            whole_spec(2, D),
            whole_spec(D, HALF_FF),
            whole_spec(D, HALF_FF),
        ],
        out_specs=[rows_spec(D), rows_spec(D)] + [rows_spec(HALF_FF)] * 3,
        out_shape=[
            jax.ShapeDtypeStruct((length, D), F32),
            jax.ShapeDtypeStruct((length, D), BF16),
            wide,
            wide,
            jax.ShapeDtypeStruct((length, HALF_FF), BF16),
        ],
        compiler_params=kernel_params(),
        cost_estimate=cost(2 * length * D * (D + FF), length * (10 * D + 10 * HALF_FF)),
        name="ffn",
    )(x, o, o_far, wo, wo_far, gains, wg, wu)


def ffn_back_kernel(
    cot_ref, gate_ref, up_ref, hidden_ref, wdt_ref, wg_ref, wu_ref,
    part_ref, dgate_ref, dup_ref, dn2_ref,
):
    part_ref[...] = dot_nt(hidden_ref[...], wdt_ref[...]).astype(BF16)
    hidden_grad = dot_nn(cot_ref[...], wdt_ref[...])
    gate, up = gate_ref[...], up_ref[...]
    sigma = jax.nn.sigmoid(gate)
    gate_grad = (hidden_grad * up * sigma * (1.0 + gate * (1.0 - sigma))).astype(BF16)
    up_grad = (hidden_grad * gate * sigma).astype(BF16)
    dgate_ref[...] = gate_grad
    dup_ref[...] = up_grad
    dn2_ref[...] = (dot_nt(gate_grad, wg_ref[...]) + dot_nt(up_grad, wu_ref[...])).astype(BF16)


def ffn_back(cot, gate, up, hidden, wdt, wg, wu):
    length = cot.shape[0]
    wide = jax.ShapeDtypeStruct((length, HALF_FF), BF16)
    narrow = jax.ShapeDtypeStruct((length, D), BF16)
    return pl.pallas_call(
        ffn_back_kernel,
        grid=(length // ROWS,),
        in_specs=[rows_spec(D)] + [rows_spec(HALF_FF)] * 3 + [whole_spec(D, HALF_FF)] * 3,
        out_specs=[rows_spec(D), rows_spec(HALF_FF), rows_spec(HALF_FF), rows_spec(D)],
        out_shape=[narrow, wide, wide, narrow],
        compiler_params=kernel_params(),
        cost_estimate=cost(4 * length * D * FF, length * (6 * D + 14 * HALF_FF)),
        name="ffn_back",
    )(cot, gate, up, hidden, wdt, wg, wu)


def middle_back_kernel(
    cot_ref, x1_ref, near_ref, far_ref, gain_ref, wo_ref, dx1_ref, da_ref, do_ref, g2_ref
):
    middle = x1_ref[...]
    scale = lax.rsqrt(jnp.mean(middle * middle, -1, keepdims=True) + EPSILON)
    grad = near_ref[...].astype(F32) + far_ref[...].astype(F32)
    weighted = grad * gain_ref[1:2, :]
    inner = jnp.mean(weighted * middle, -1, keepdims=True)
    middle_grad = (
        cot_ref[...].astype(F32) + scale * weighted - middle * (scale * scale * scale * inner)
    )
    dx1_ref[...] = middle_grad
    branch = middle_grad.astype(BF16)
    da_ref[...] = branch
    do_ref[...] = dot_nt(branch, wo_ref[...]).astype(BF16)

    @pl.when(pl.program_id(0) == 0)
    def _():
        g2_ref[...] = jnp.zeros_like(g2_ref)

    g2_ref[...] += jnp.sum(grad * middle * scale, 0, keepdims=True)


def middle_back(cot, x1, near, far, gains, wo):
    length = cot.shape[0]
    return pl.pallas_call(
        middle_back_kernel,
        grid=(length // ROWS,),
        in_specs=[rows_spec(D)] * 4 + [whole_spec(2, D), whole_spec(HALF_D, D)],
        out_specs=[rows_spec(D), rows_spec(D), rows_spec(HALF_D), whole_spec(1, D)],
        out_shape=[
            jax.ShapeDtypeStruct((length, D), F32),
            jax.ShapeDtypeStruct((length, D), BF16),
            jax.ShapeDtypeStruct((length, HALF_D), BF16),
            jax.ShapeDtypeStruct((1, D), F32),
        ],
        compiler_params=kernel_params(),
        cost_estimate=cost(2 * length * D * HALF_D, length * D * 17),
        name="middle_back",
    )(cot, x1, near, far, gains, wo)


def input_back_kernel(x_ref, dq_ref, dk_ref, dv_ref, w_ref, part_ref, g1_ref):
    w = w_ref[...]
    grad = (
        dot_nt(dq_ref[...], w[:, :HALF_D])
        + dot_nt(dk_ref[...], w[:, HALF_D : 2 * HALF_D])
        + dot_nt(dv_ref[...], w[:, 2 * HALF_D :])
    )
    part_ref[...] = grad.astype(BF16)
    x = x_ref[...].astype(F32)
    scale = lax.rsqrt(jnp.mean(x * x, -1, keepdims=True) + EPSILON)

    @pl.when(pl.program_id(0) == 0)
    def _():
        g1_ref[...] = jnp.zeros_like(g1_ref)

    g1_ref[...] += jnp.sum(grad * x * scale, 0, keepdims=True)


def input_back(x, dq, dk, dv, w):
    length = x.shape[0]
    return pl.pallas_call(
        input_back_kernel,
        grid=(length // ROWS,),
        in_specs=[rows_spec(D)] + [rows_spec(HALF_D)] * 3 + [whole_spec(D, 3 * HALF_D)],
        out_specs=[rows_spec(D), whole_spec(1, D)],
        out_shape=[
            jax.ShapeDtypeStruct((length, D), BF16),
            jax.ShapeDtypeStruct((1, D), F32),
        ],
        compiler_params=kernel_params(),
        cost_estimate=cost(2 * length * D * 3 * HALF_D, length * D * 8),
        name="input_back",
    )(x, dq, dk, dv, w)


def pair_up(bit, count):
    return [(i, i ^ bit) for i in range(count)]


def gather_pieces(shard, count):
    high = count // 4
    pieces = [shard]
    for shift in range(1, high):
        hop = [(i, (i + 4 * shift) % count) for i in range(count)]
        pieces.append(lax.ppermute(shard, "dp", hop))
    near = jnp.stack(pieces)
    along_x = lax.ppermute(near, "dp", pair_up(1, count))
    along_y = lax.ppermute(near, "dp", pair_up(2, count))
    first = lax.ppermute(along_x[: high // 2], "dp", pair_up(2, count))
    second = lax.ppermute(along_y[high // 2 :], "dp", pair_up(1, count))
    return near, along_x, along_y, first, second


def place_kernel(place, high, me_ref, near_ref, x_ref, y_ref, first_ref, second_ref, *out_refs):
    me = me_ref[0]
    x, y, z = me % 2, me // 2 % 2, me // 4
    for shift in range(high):
        from_z = (z - shift + high) % high
        far_ref, far = (
            (first_ref, shift) if shift < high // 2 else (second_ref, shift - high // 2)
        )
        for ref, index, from_y, from_x in (
            (near_ref, shift, y, x),
            (x_ref, shift, y, 1 - x),
            (y_ref, shift, 1 - y, x),
            (far_ref, far, 1 - y, 1 - x),
        ):
            place(from_z * 4 + from_y * 2 + from_x, ref[index], *out_refs)


def assemble(pieces, me, place, shapes, name):
    high = pieces[0].shape[0]

    def kernel(*refs):
        place_kernel(place, high, *refs)

    total = sum(math.prod(shape) for shape in shapes)
    vmem = pl.BlockSpec(memory_space=pltpu.VMEM)
    return pl.pallas_call(
        kernel,
        in_specs=[pl.BlockSpec(memory_space=pltpu.SMEM)] + [vmem] * 5,
        out_specs=[vmem] * len(shapes),
        out_shape=[jax.ShapeDtypeStruct(shape, BF16) for shape in shapes],
        compiler_params=kernel_params(),
        cost_estimate=cost(0, 4 * total),
        name=name,
    )(me, *pieces)


def block_rows(owner):
    return pl.ds(pl.multiple_of(owner * DBLK, 16), DBLK)


def place_rows(owner, piece, out_ref):
    out_ref[block_rows(owner), :] = piece


def place_out_gate(owner, piece, out_ref, gate_ref):
    lanes = pl.ds(pl.multiple_of(owner % 2 * HALF_D, 128), HALF_D)
    out_ref[block_rows(owner // 2), lanes] = piece[:, :HALF_D]
    gate_ref[block_rows(owner), :] = piece[:, HALF_D:]


def place_down(owner, piece, out_ref):
    lanes = pl.ds(pl.multiple_of(owner // 2 * FBLK, 128), FBLK)
    for block in range(HALF_GRID):
        rows = block_rows(owner % 2 * HALF_GRID + block)
        out_ref[rows, lanes] = piece[:, block * FBLK : (block + 1) * FBLK]


def side_by_side(blocks):
    matrices, many, height, width = blocks.shape
    return blocks.transpose(2, 0, 1, 3).reshape(height, matrices * many * width)


def gather_weights(qkv_master, out_master, ffn_master, down_master, me, count):
    qkv, out, ffn_part = (t.astype(BF16) for t in (qkv_master[:, 0], out_master, ffn_master[:, 0]))
    down = down_master[0].astype(BF16)
    if qkv.shape[1] == HALF_GRID:
        first = gather_pieces(side_by_side(qkv), count)
        second = gather_pieces(
            jnp.concatenate([side_by_side(out), side_by_side(ffn_part[:1])], 1), count
        )
        third = gather_pieces(side_by_side(ffn_part[1:]), count)
        fourth = gather_pieces(side_by_side(jnp.swapaxes(down, 1, 2)[None]), count)
        (w_qkv,) = assemble(first, me, place_rows, [(D, 3 * HALF_D)], "place_qkv")
        w_out, w_gate = assemble(
            second, me, place_out_gate, [(HALF_D, D), (D, HALF_FF)], "place_out_gate"
        )
        (w_up,) = assemble(third, me, place_rows, [(D, HALF_FF)], "place_up")
        (w_down,) = assemble(fourth, me, place_down, [(D, HALF_FF)], "place_down")
        return w_qkv, w_out, w_gate, w_up, w_down
    qkv_all = lax.all_gather(qkv, "dp", axis=1, tiled=True)
    out_all = lax.all_gather(out[0], "dp", axis=0, tiled=True)
    ffn_all = lax.all_gather(ffn_part, "dp", axis=1, tiled=True)
    down_all = lax.all_gather(down, "dp", axis=0, tiled=True)
    w_qkv = qkv_all.reshape(3, GRID, HALF_GRID, DBLK, DBLK).transpose(1, 3, 0, 2, 4)
    w_out = out_all.reshape(HALF_GRID, GRID, DBLK, DBLK).transpose(0, 2, 1, 3)
    w_ffn = ffn_all.reshape(2, GRID, HALF_GRID, DBLK, FBLK).transpose(0, 1, 3, 2, 4)
    w_down = down_all.reshape(HALF_GRID, GRID, FBLK, DBLK).transpose(1, 3, 0, 2)
    w_ffn = w_ffn.reshape(2, D, HALF_FF)
    return (
        w_qkv.reshape(D, 3 * HALF_D),
        w_out.reshape(HALF_D, D),
        w_ffn[0],
        w_ffn[1],
        w_down.reshape(D, HALF_FF),
    )


def reduce_blocks(partial, count, me):
    high = count // 4
    x, y, z = me % 2, me // 2 % 2, me // 4
    grid = partial.reshape((high, 2, 2) + partial.shape[1:])

    def pick(at_y, at_x):
        column = lax.dynamic_index_in_dim(grid, at_y, 1, keepdims=False)
        return lax.dynamic_index_in_dim(column, at_x, 1, keepdims=False)

    cut = high // 2
    far = pick(1 - y, 1 - x).astype(BF16)
    by_y = lax.ppermute(far[:cut], "dp", pair_up(2, count)).astype(F32)
    by_x = lax.ppermute(far[cut:], "dp", pair_up(1, count)).astype(F32)
    to_x, to_y = pick(y, 1 - x), pick(1 - y, x)
    to_x = jnp.concatenate([to_x[:cut] + by_y, to_x[cut:]]).astype(BF16)
    to_y = jnp.concatenate([to_y[:cut], to_y[cut:] + by_x]).astype(BF16)
    from_x = lax.ppermute(to_x, "dp", pair_up(1, count)).astype(F32)
    from_y = lax.ppermute(to_y, "dp", pair_up(2, count)).astype(F32)
    mine = pick(y, x) + from_x + from_y
    total = lax.dynamic_index_in_dim(mine, z, 0, keepdims=False)
    for shift in range(1, high):
        hop = [(i, (i + 4 * shift) % count) for i in range(count)]
        block = lax.dynamic_index_in_dim(mine, (z + shift) % high, 0, keepdims=False)
        total = total + lax.ppermute(block.astype(BF16), "dp", hop).astype(F32)
    return total


def apart(rows, matrices, width):
    height = rows.shape[0]
    return rows.reshape(height, matrices, -1, width).transpose(1, 2, 0, 3)


def reduce_columns(grad, matrices, width, count, me):
    if count == GRID:
        return apart(
            reduce_blocks(grad.reshape(GRID, DBLK, -1), count, me), matrices, width
        )
    blocks = grad.reshape(GRID, DBLK, matrices, HALF_GRID, width).transpose(2, 0, 3, 1, 4)
    blocks = blocks.reshape(matrices, GRID * HALF_GRID, DBLK, width)
    return lax.psum_scatter(blocks, "dp", scatter_dimension=1, tiled=True)


def reduce_out(grad, count, me):
    if count == GRID:
        halves = grad.reshape(HALF_GRID, DBLK, 2, HALF_D).transpose(0, 2, 1, 3)
        return apart(reduce_blocks(halves.reshape(GRID, DBLK, HALF_D), count, me), 1, DBLK)[0]
    blocks = grad.reshape(HALF_GRID, DBLK, GRID, DBLK).transpose(0, 2, 1, 3)
    blocks = blocks.reshape(HALF_GRID * GRID, DBLK, DBLK)
    return lax.psum_scatter(blocks, "dp", scatter_dimension=0, tiled=True)


def reduce_down(grad, count, me):
    if count == GRID:
        tiles = grad.reshape(2, HALF_GRID, DBLK, HALF_GRID, FBLK).transpose(3, 0, 2, 1, 4)
        tiles = tiles.reshape(GRID, DBLK, HALF_GRID * FBLK)
        return jnp.swapaxes(apart(reduce_blocks(tiles, count, me), 1, FBLK)[0], 1, 2)
    blocks = grad.reshape(GRID, DBLK, HALF_GRID, FBLK).transpose(2, 0, 3, 1)
    blocks = blocks.reshape(HALF_GRID * GRID, FBLK, DBLK)
    return lax.psum_scatter(blocks, "dp", scatter_dimension=0, tiled=True)


def sum_everywhere(values, count):
    if count & (count - 1):
        return lax.psum(values, ("dp", "narrow"))
    values = values + lax.ppermute(values, "narrow", [(0, 1), (1, 0)])
    bit = 1
    while bit < count:
        values = values + lax.ppermute(values, "dp", pair_up(bit, count))
        bit *= 2
    return values


def precondition(block_grad, left_stat, right_stat, left_root, right_root, master):
    new_left = DECAY * left_stat + (1.0 - DECAY) * jnp.einsum(
        "...ij,...kj->...ik", block_grad, block_grad, precision=HIGHEST_PRECISION
    )
    new_right = DECAY * right_stat + (1.0 - DECAY) * jnp.einsum(
        "...ji,...jk->...ik", block_grad, block_grad, precision=HIGHEST_PRECISION
    )
    turned = jnp.einsum("...ij,...jk->...ik", left_root, block_grad, precision=HIGHEST_PRECISION)
    turned = jnp.einsum("...ij,...jk->...ik", turned, right_root, precision=HIGHEST_PRECISION)
    return (new_left, new_right, master - STEP_RATE * turned)


def other_core(values):
    return lax.ppermute(values, "narrow", [(0, 1), (1, 0)])


def in_order(mine, core):
    other = other_core(mine)
    return jnp.where(
        core == 0, jnp.concatenate([mine, other], 0), jnp.concatenate([other, mine], 0)
    )


def body(
    tokens,
    cotangent,
    gains,
    gain_moments,
    qkv_master,
    out_master,
    ffn_master,
    down_master,
    attn_left,
    attn_right,
    attn_left_root,
    attn_right_root,
    ffn_left,
    ffn_right,
    ffn_left_root,
    ffn_right_root,
    down_left,
    down_right,
    down_left_root,
    down_right_root,
):
    count = lax.axis_size("dp")
    index = lax.axis_index("dp").astype(jnp.int32)
    core = lax.axis_index("narrow")
    own_rows = tokens.shape[0]
    length = 2 * own_rows

    w_qkv, w_out, w_gate, w_up, w_down = gather_weights(
        qkv_master, out_master, ffn_master, down_master, index[None], count
    )
    x = in_order(tokens, core)
    cot = in_order(cotangent, core)

    frequency = jnp.power(10000.0, -2.0 * jnp.arange(HEAD_DIM // 2, dtype=F32) / HEAD_DIM)
    angles = (jnp.arange(length) % LEN).astype(F32)[:, None] * frequency[None, :]
    sine = jnp.sin(angles)
    cosine = jnp.tile(jnp.cos(angles), (1, 4))
    sine_part = jnp.tile(jnp.concatenate([-sine, sine], 1), (1, 2))

    normed_one, q, k, v = project(x, gains, w_qkv, cosine, sine_part)
    attended, lse = attend(q, k, v)
    attended_far = other_core(attended)
    w_out_far = other_core(w_out)
    middle, normed_two, gate, up, hidden = ffn(
        x, attended, attended_far, w_out, w_out_far, gains, w_gate, w_up
    )
    down_weight_grad = dot_tn(cot, hidden)
    down_owned = reduce_down(down_weight_grad, count, index)
    out_part, gate_grad, up_grad, normed_part = ffn_back(
        cot, gate, up, hidden, w_down, w_gate, w_up
    )
    normed_far = other_core(normed_part)
    ffn_weight_grad = dot_tn(normed_two, jnp.concatenate([gate_grad, up_grad], 1))
    ffn_owned = reduce_columns(ffn_weight_grad, 2, FBLK, count, index)

    mine, theirs = core * own_rows, (1 - core) * own_rows
    out_far = other_core(lax.dynamic_slice_in_dim(out_part, theirs, own_rows))
    layer_out = (
        lax.dynamic_slice_in_dim(middle, mine, own_rows)
        + lax.dynamic_slice_in_dim(out_part, mine, own_rows).astype(F32)
        + out_far.astype(F32)
    ).astype(BF16)

    middle_grad, branch, attended_grad, gain_two = middle_back(
        cot, middle, normed_part, normed_far, gains, w_out
    )
    out_weight_grad = dot_tn(attended, branch)
    out_owned = reduce_out(out_weight_grad, count, index)
    dq, dk, dv = attend_back(q, k, v, attended_grad, attended, lse, cosine, sine_part)
    input_part, gain_one = input_back(x, dq, dk, dv, w_qkv)
    qkv_weight_grad = dot_tn(normed_one, jnp.concatenate([dq, dk, dv], 1))
    qkv_owned = reduce_columns(qkv_weight_grad, 3, DBLK, count, index)

    input_far = other_core(lax.dynamic_slice_in_dim(input_part, theirs, own_rows))
    grad = lax.dynamic_slice_in_dim(input_part, mine, own_rows).astype(F32) + input_far.astype(F32)
    inputs = tokens.astype(F32)
    scale = lax.rsqrt(jnp.mean(inputs * inputs, -1, keepdims=True) + EPSILON)
    weighted = grad * gains[0]
    input_grad = (
        lax.dynamic_slice_in_dim(middle_grad, mine, own_rows)
        + scale * weighted
        - inputs * scale**3 * jnp.mean(weighted * inputs, -1, keepdims=True)
    )
    gain_grad = sum_everywhere(jnp.concatenate([gain_one, 0.5 * gain_two]), count)
    gain_moment_new = DECAY * gain_moments + (1.0 - DECAY) * gain_grad * gain_grad
    gain_new = gains - GAIN_RATE * gain_grad / (jnp.sqrt(gain_moment_new) + 1e-08)

    attn_grad = jnp.concatenate([qkv_owned, out_owned[None]], 0)[:, None]
    ffn_grad = ffn_owned[:, None]
    down_grad = down_owned[None]
    attn_master = jnp.concatenate([qkv_master, out_master[None]], 0)
    attn_left_new, attn_right_new, attn_new = precondition(
        attn_grad, attn_left, attn_right, attn_left_root, attn_right_root, attn_master
    )
    ffn_left_new, ffn_right_new, ffn_new = precondition(
        ffn_grad, ffn_left, ffn_right, ffn_left_root, ffn_right_root, ffn_master
    )
    down_left_new, down_right_new, down_new = precondition(
        down_grad, down_left, down_right, down_left_root, down_right_root, down_master
    )
    return (
        layer_out,
        input_grad,
        gain_grad,
        gain_moment_new,
        gain_new,
        attn_grad,
        attn_left_new,
        attn_right_new,
        attn_new[:3],
        attn_new[3],
        ffn_grad,
        ffn_left_new,
        ffn_right_new,
        ffn_new,
        down_grad,
        down_left_new,
        down_right_new,
        down_new,
    )


def solution(mesh):
    tokens = P(("dp", "narrow"), None)
    stacked = P(None, "narrow", "dp", None, None)
    single = P("narrow", "dp", None, None)
    return jax.shard_map(
        body,
        mesh=mesh,
        in_specs=(tokens, tokens, P(), P(), stacked, single, stacked, single)
        + (stacked,) * 8
        + (single,) * 4,
        out_specs=(tokens, tokens, P(), P(), P())
        + (stacked,) * 4
        + (single,)
        + (stacked,) * 4
        + (single,) * 4,
        check_vma=False,
    )
```

```python
import math

import jax
import jax.numpy as jnp
from jax import lax
from jax.experimental import pallas as pl
from jax.experimental.pallas import tpu as pltpu
from jax.sharding import PartitionSpec as P

D = 768
HEAD_DIM = 64
FF = 2048
LEN = 1024
GRID = 16
DBLK = D // GRID
FBLK = FF // GRID
HALF_GRID = GRID // 2
HALF_D = D // 2
HALF_FF = FF // 2
PAIR = 2 * HEAD_DIM
ROWS = 256

EPSILON = 1e-05
DECAY = 0.5
STEP_RATE = 0.25
GAIN_RATE = 0.1
NEG_FILL = -1e30
HIGHEST_PRECISION = lax.Precision.HIGHEST
BF16 = jnp.bfloat16
F32 = jnp.float32
VMEM_BYTES = 24 * 1024 * 1024


def dot_nn(left, right):
    return lax.dot_general(left, right, (((1,), (0,)), ((), ())), preferred_element_type=F32)


def dot_nt(left, right):
    return lax.dot_general(left, right, (((1,), (1,)), ((), ())), preferred_element_type=F32)


def dot_tn(left, right):
    return lax.dot_general(left, right, (((0,), (0,)), ((), ())), preferred_element_type=F32)


def kernel_params():
    return pltpu.CompilerParams(vmem_limit_bytes=VMEM_BYTES)


def cost():
    return pl.CostEstimate(flops=0, bytes_accessed=0, transcendentals=0)


def rows_spec(columns):
    return pl.BlockSpec((ROWS, columns), lambda i: (i, 0))


def whole_spec(*shape):
    return pl.BlockSpec(shape, lambda i: (0,) * len(shape))


def lower_lanes(shape):
    return lax.broadcasted_iota(jnp.int32, shape, 1) % HEAD_DIM < HEAD_DIM // 2


def turn(features, cosine, sine_part, lower):
    half = HEAD_DIM // 2
    partner = jnp.where(
        lower, pltpu.roll(features, PAIR - half, 1), pltpu.roll(features, half, 1)
    )
    return features * cosine + partner * sine_part


def project_kernel(x_ref, gain_ref, w_ref, cos_ref, sin_ref, n1_ref, q_ref, k_ref, v_ref):
    x = x_ref[...].astype(F32)
    scale = lax.rsqrt(jnp.mean(x * x, -1, keepdims=True) + EPSILON)
    normed = (x * scale * gain_ref[0:1, :]).astype(BF16)
    n1_ref[...] = normed
    lower = lower_lanes((ROWS, PAIR))
    cosine, sine_part = cos_ref[...], sin_ref[...]
    both = dot_nn(normed, w_ref[...])
    for tile in range(HALF_D // PAIR):
        lanes = slice(tile * PAIR, (tile + 1) * PAIR)
        query = both[:, tile * PAIR : (tile + 1) * PAIR]
        key = both[:, HALF_D + tile * PAIR : HALF_D + (tile + 1) * PAIR]
        turned = turn(query, cosine, sine_part, lower).astype(BF16)
        q_ref[:, lanes] = turned * BF16(1.0 / math.sqrt(HEAD_DIM))
        k_ref[:, lanes] = turn(key, cosine, sine_part, lower).astype(BF16)
    v_ref[...] = both[:, 2 * HALF_D :].astype(BF16)


def project(x, gains, weight, cosine, sine_part):
    length = x.shape[0]
    half = jax.ShapeDtypeStruct((length, HALF_D), BF16)
    return pl.pallas_call(
        project_kernel,
        grid=(length // ROWS,),
        in_specs=[
            rows_spec(D),
            whole_spec(2, D),
            whole_spec(D, 3 * HALF_D),
            rows_spec(PAIR),
            rows_spec(PAIR),
        ],
        out_specs=[rows_spec(D), rows_spec(HALF_D), rows_spec(HALF_D), rows_spec(HALF_D)],
        out_shape=[jax.ShapeDtypeStruct((length, D), BF16), half, half, half],
        compiler_params=kernel_params(),
        cost_estimate=cost(),
        name="project",
    )(x, gains, weight, cosine, sine_part)


def attend_kernel(q_ref, k_ref, v_ref, o_ref, lse_ref):
    length = q_ref.shape[0]
    first_head = lax.broadcasted_iota(jnp.int32, (ROWS, PAIR), 1) < HEAD_DIM
    keys = k_ref[...]
    values = jnp.concatenate([v_ref[...], jnp.ones((length, PAIR), BF16)], 1)
    causal = lax.broadcasted_iota(jnp.int32, (ROWS, ROWS), 0) >= lax.broadcasted_iota(
        jnp.int32, (ROWS, ROWS), 1
    )
    for block in range(length // ROWS):
        rows = slice(block * ROWS, (block + 1) * ROWS)
        width = (block + 1) * ROWS
        query_block = q_ref[rows, :]
        parts, sums = [], []
        for head in range(2):
            mine = first_head if head == 0 else jnp.logical_not(first_head)
            query = jnp.where(mine, query_block, jnp.zeros_like(query_block))
            scores = jnp.where(causal, dot_nt(query, keys[block * ROWS : width]), NEG_FILL)
            if block:
                scores = jnp.concatenate([dot_nt(query, keys[: block * ROWS]), scores], 1)
            top = jnp.max(scores, 1, keepdims=True)
            exponent = jnp.exp(scores - top).astype(BF16)
            product = dot_nn(exponent, values[:width])
            total = product[:, PAIR:]
            parts.append(product[:, :PAIR] / total)
            sums.append(top + jnp.log(total))
        o_ref[rows, :] = jnp.where(first_head, parts[0], parts[1]).astype(BF16)
        lane = lax.broadcasted_iota(jnp.int32, (ROWS, PAIR), 1)
        lse_ref[:, rows] = jnp.transpose(jnp.where(lane == 0, sums[0], sums[1]))[:8, :]


def attend(q, k, v):
    length = q.shape[0]
    pairs = q.shape[1] // PAIR
    block = pl.BlockSpec((length, PAIR), lambda h: (0, h))
    return pl.pallas_call(
        attend_kernel,
        grid=(pairs,),
        in_specs=[block] * 3,
        out_specs=[block, pl.BlockSpec((8, length), lambda h: (h, 0))],
        out_shape=[
            jax.ShapeDtypeStruct(q.shape, BF16),
            jax.ShapeDtypeStruct((8 * pairs, length), F32),
        ],
        compiler_params=kernel_params(),
        cost_estimate=cost(),
        name="attend",
    )(q, k, v)


def attend_back_kernel(
    q_ref, k_ref, v_ref, do_ref, o_ref, lse_ref, cos_ref, sin_ref, dq_ref, dk_ref, dv_ref, dqt_ref
):
    length = q_ref.shape[0]
    first_head = lax.broadcasted_iota(jnp.int32, (length, PAIR), 1) < HEAD_DIM
    zero = BF16(0)
    queries = [
        jnp.where(first_head, q_ref[...], zero),
        jnp.where(first_head, zero, q_ref[...]),
    ]
    grads = [
        jnp.where(first_head, do_ref[...], zero),
        jnp.where(first_head, zero, do_ref[...]),
    ]
    product = do_ref[...].astype(F32) * o_ref[...].astype(F32)
    head_row = lax.broadcasted_iota(jnp.int32, (8, PAIR), 0)
    head_lane = lax.broadcasted_iota(jnp.int32, (8, PAIR), 1) // HEAD_DIM
    inner = lax.dot_general(
        (head_row == head_lane).astype(F32),
        product,
        (((1,), (1,)), ((), ())),
        preferred_element_type=F32,
        precision=HIGHEST_PRECISION,
    )
    turned_keys = jnp.transpose(k_ref[...].astype(F32)).astype(BF16)
    first_rows = lax.broadcasted_iota(jnp.int32, turned_keys.shape, 0) < HEAD_DIM
    key_heads = [
        jnp.where(first_rows, turned_keys, zero),
        jnp.where(first_rows, zero, turned_keys),
    ]
    causal = lax.broadcasted_iota(jnp.int32, (ROWS, ROWS), 0) <= lax.broadcasted_iota(
        jnp.int32, (ROWS, ROWS), 1
    )
    dqt_ref[...] = jnp.zeros_like(dqt_ref)
    lower = lower_lanes((ROWS, PAIR))
    for block in range(length // ROWS):
        rows = slice(block * ROWS, (block + 1) * ROWS)
        start = block * ROWS
        key_block, value_block = k_ref[rows, :], v_ref[rows, :]
        dk = jnp.zeros((ROWS, PAIR), F32)
        dv = jnp.zeros((ROWS, PAIR), F32)
        for head in range(2):
            scores = dot_nt(key_block, queries[head][start:])
            probs = jnp.exp(scores - lse_ref[head : head + 1, start:])
            diagonal = jnp.where(causal, probs[:, :ROWS], 0.0)
            if start + ROWS == length:
                probs = diagonal
            else:
                probs = jnp.concatenate([diagonal, probs[:, ROWS:]], 1)
            prob_grad = dot_nt(value_block, grads[head][start:])
            score_grad = (probs * (prob_grad - inner[head : head + 1, start:])).astype(BF16)
            dv = dv + dot_nn(probs.astype(BF16), grads[head][start:])
            dk = dk + dot_nn(score_grad, queries[head][start:])
            dqt_ref[:, start:] += dot_nn(key_heads[head][:, rows], score_grad)
        dk_ref[rows, :] = turn(dk, cos_ref[rows, :], -sin_ref[rows, :], lower).astype(BF16)
        dv_ref[rows, :] = dv.astype(BF16)
    for block in range(length // ROWS):
        rows = slice(block * ROWS, (block + 1) * ROWS)
        dq = jnp.transpose(dqt_ref[:, rows]) * (1.0 / math.sqrt(HEAD_DIM))
        dq_ref[rows, :] = turn(dq, cos_ref[rows, :], -sin_ref[rows, :], lower).astype(BF16)


def attend_back(q, k, v, grad, o, lse, cosine, sine_part):
    length = q.shape[0]
    pairs = q.shape[1] // PAIR
    block = pl.BlockSpec((length, PAIR), lambda h: (0, h))
    table = pl.BlockSpec((length, PAIR), lambda h: (0, 0))
    return pl.pallas_call(
        attend_back_kernel,
        grid=(pairs,),
        in_specs=[block] * 5 + [pl.BlockSpec((8, length), lambda h: (h, 0)), table, table],
        out_specs=[block] * 3,
        out_shape=[jax.ShapeDtypeStruct(q.shape, BF16)] * 3,
        scratch_shapes=[pltpu.VMEM((PAIR, length), F32)],
        compiler_params=kernel_params(),
        cost_estimate=cost(),
        name="attend_back",
    )(q, k, v, grad, o, lse, cosine, sine_part)


def ffn_kernel(
    x_ref, o_ref, o_far_ref, wo_ref, wo_far_ref, gain_ref, wg_ref, wu_ref,
    x1_ref, n2_ref, gate_ref, up_ref, hidden_ref,
):
    middle = (
        x_ref[...].astype(F32)
        + dot_nn(o_ref[...], wo_ref[...])
        + dot_nn(o_far_ref[...], wo_far_ref[...])
    )
    x1_ref[...] = middle
    scale = lax.rsqrt(jnp.mean(middle * middle, -1, keepdims=True) + EPSILON)
    normed = (middle * scale * gain_ref[1:2, :]).astype(BF16)
    n2_ref[...] = normed
    gate = dot_nn(normed, wg_ref[...])
    up = dot_nn(normed, wu_ref[...])
    gate_ref[...] = gate
    up_ref[...] = up
    hidden_ref[...] = (gate * jax.nn.sigmoid(gate) * up).astype(BF16)


def ffn(x, o, o_far, wo, wo_far, gains, wg, wu):
    length = x.shape[0]
    wide = jax.ShapeDtypeStruct((length, HALF_FF), F32)
    return pl.pallas_call(
        ffn_kernel,
        grid=(length // ROWS,),
        in_specs=[
            rows_spec(D),
            rows_spec(HALF_D),
            rows_spec(HALF_D),
            whole_spec(HALF_D, D),
            whole_spec(HALF_D, D),
            whole_spec(2, D),
            whole_spec(D, HALF_FF),
            whole_spec(D, HALF_FF),
        ],
        out_specs=[rows_spec(D), rows_spec(D)] + [rows_spec(HALF_FF)] * 3,
        out_shape=[
            jax.ShapeDtypeStruct((length, D), F32),
            jax.ShapeDtypeStruct((length, D), BF16),
            wide,
            wide,
            jax.ShapeDtypeStruct((length, HALF_FF), BF16),
        ],
        compiler_params=kernel_params(),
        cost_estimate=cost(),
        name="ffn",
    )(x, o, o_far, wo, wo_far, gains, wg, wu)


def ffn_back_kernel(
    cot_ref, gate_ref, up_ref, hidden_ref, wdt_ref, wg_ref, wu_ref,
    part_ref, dgu_ref, dn2_ref,
):
    part_ref[...] = dot_nt(hidden_ref[...], wdt_ref[...]).astype(BF16)
    hidden_grad = dot_nn(cot_ref[...], wdt_ref[...])
    gate, up = gate_ref[...], up_ref[...]
    sigma = jax.nn.sigmoid(gate)
    gate_grad = (hidden_grad * up * sigma * (1.0 + gate * (1.0 - sigma))).astype(BF16)
    up_grad = (hidden_grad * gate * sigma).astype(BF16)
    dgu_ref[:, :HALF_FF] = gate_grad
    dgu_ref[:, HALF_FF:] = up_grad
    dn2_ref[...] = (dot_nt(gate_grad, wg_ref[...]) + dot_nt(up_grad, wu_ref[...])).astype(BF16)


def ffn_back(cot, gate, up, hidden, wdt, wg, wu):
    length = cot.shape[0]
    wide = jax.ShapeDtypeStruct((length, FF), BF16)
    narrow = jax.ShapeDtypeStruct((length, D), BF16)
    return pl.pallas_call(
        ffn_back_kernel,
        grid=(length // ROWS,),
        in_specs=[rows_spec(D)] + [rows_spec(HALF_FF)] * 3 + [whole_spec(D, HALF_FF)] * 3,
        out_specs=[rows_spec(D), rows_spec(FF), rows_spec(D)],
        out_shape=[narrow, wide, narrow],
        compiler_params=kernel_params(),
        cost_estimate=cost(),
        name="ffn_back",
    )(cot, gate, up, hidden, wdt, wg, wu)


def middle_back_kernel(
    cot_ref, x1_ref, near_ref, far_ref, gain_ref, wo_ref, dx1_ref, da_ref, do_ref, g2_ref
):
    middle = x1_ref[...]
    scale = lax.rsqrt(jnp.mean(middle * middle, -1, keepdims=True) + EPSILON)
    grad = near_ref[...].astype(F32) + far_ref[...].astype(F32)
    weighted = grad * gain_ref[1:2, :]
    inner = jnp.mean(weighted * middle, -1, keepdims=True)
    middle_grad = (
        cot_ref[...].astype(F32) + scale * weighted - middle * (scale * scale * scale * inner)
    )
    dx1_ref[...] = middle_grad
    branch = middle_grad.astype(BF16)
    da_ref[...] = branch
    do_ref[...] = dot_nt(branch, wo_ref[...]).astype(BF16)

    @pl.when(pl.program_id(0) == 0)
    def _():
        g2_ref[...] = jnp.zeros_like(g2_ref)

    g2_ref[...] += jnp.sum(grad * middle * scale, 0, keepdims=True)


def middle_back(cot, x1, near, far, gains, wo):
    length = cot.shape[0]
    return pl.pallas_call(
        middle_back_kernel,
        grid=(length // ROWS,),
        in_specs=[rows_spec(D)] * 4 + [whole_spec(2, D), whole_spec(HALF_D, D)],
        out_specs=[rows_spec(D), rows_spec(D), rows_spec(HALF_D), whole_spec(1, D)],
        out_shape=[
            jax.ShapeDtypeStruct((length, D), F32),
            jax.ShapeDtypeStruct((length, D), BF16),
            jax.ShapeDtypeStruct((length, HALF_D), BF16),
            jax.ShapeDtypeStruct((1, D), F32),
        ],
        compiler_params=kernel_params(),
        cost_estimate=cost(),
        name="middle_back",
    )(cot, x1, near, far, gains, wo)


def input_back_kernel(x_ref, dq_ref, dk_ref, dv_ref, w_ref, part_ref, g1_ref):
    w = w_ref[...]
    grad = (
        dot_nt(dq_ref[...], w[:, :HALF_D])
        + dot_nt(dk_ref[...], w[:, HALF_D : 2 * HALF_D])
        + dot_nt(dv_ref[...], w[:, 2 * HALF_D :])
    )
    part_ref[...] = grad.astype(BF16)
    x = x_ref[...].astype(F32)
    scale = lax.rsqrt(jnp.mean(x * x, -1, keepdims=True) + EPSILON)

    @pl.when(pl.program_id(0) == 0)
    def _():
        g1_ref[...] = jnp.zeros_like(g1_ref)

    g1_ref[...] += jnp.sum(grad * x * scale, 0, keepdims=True)


def input_back(x, dq, dk, dv, w):
    length = x.shape[0]
    return pl.pallas_call(
        input_back_kernel,
        grid=(length // ROWS,),
        in_specs=[rows_spec(D)] + [rows_spec(HALF_D)] * 3 + [whole_spec(D, 3 * HALF_D)],
        out_specs=[rows_spec(D), whole_spec(1, D)],
        out_shape=[
            jax.ShapeDtypeStruct((length, D), BF16),
            jax.ShapeDtypeStruct((1, D), F32),
        ],
        compiler_params=kernel_params(),
        cost_estimate=cost(),
        name="input_back",
    )(x, dq, dk, dv, w)


def whole_call(kernel, inputs, shapes, name, scalars=0):
    vmem = pl.BlockSpec(memory_space=pltpu.VMEM)
    smem = pl.BlockSpec(memory_space=pltpu.SMEM)
    return pl.pallas_call(
        kernel,
        in_specs=[smem] * scalars + [vmem] * (len(inputs) - scalars),
        out_specs=[vmem] * len(shapes),
        out_shape=shapes,
        compiler_params=kernel_params(),
        cost_estimate=cost(),
        name=name,
    )(*inputs)


def pair_up(bit, count):
    return [(i, i ^ bit) for i in range(count)]


def after(value, *others):
    return lax.optimization_barrier((value,) + others)[0]


def along(values, bit, count):
    return lax.ppermute(values, "dp", pair_up(bit, count))


def shifted(values, steps, count):
    return lax.ppermute(values, "dp", [(i, (i + 4 * steps) % count) for i in range(count)])


def other_core(values):
    return lax.ppermute(values, "narrow", [(0, 1), (1, 0)])


def all_shifted(values, count):
    return [shifted(values, step, count) for step in range(1, count // 4)]


def stack(pieces, parts, name):
    each = [piece.shape[0] if piece.ndim == 3 else 1 for piece in pieces]
    size = sum(each) // parts
    shape = jax.ShapeDtypeStruct((size,) + pieces[0].shape[-2:], pieces[0].dtype)

    def kernel(*refs):
        at = 0
        for ref, many in zip(refs, each):
            for index in range(many):
                out_ref = refs[len(pieces) + at // size]
                out_ref[at % size] = ref[...] if len(ref.shape) == 2 else ref[index]
                at += 1

    return whole_call(kernel, pieces, [shape] * parts, name)


def spread(first, second, count):
    first_x, second_y = along(first, 1, count), along(second, 2, count)
    first_y, second_x = along(first, 2, count), along(second, 1, count)
    return (
        (first, first_x, first_y, along(first_x, 2, count)),
        (second, second_x, second_y, along(second_y, 1, count)),
    )


def block_rows(owner):
    return pl.ds(pl.multiple_of(owner * DBLK, 16), DBLK)


def place_qkv_out(owner, piece, qkv_ref, out_ref):
    lanes = pl.ds(pl.multiple_of(owner % 2 * HALF_D, 128), HALF_D)
    qkv_ref[block_rows(owner), :] = piece[:, : 3 * HALF_D]
    out_ref[block_rows(owner // 2), lanes] = piece[:, 3 * HALF_D :]


def place_gate_up(owner, piece, gate_ref, up_ref):
    gate_ref[block_rows(owner), :] = piece[:, :HALF_FF]
    up_ref[block_rows(owner), :] = piece[:, HALF_FF:]


def place_down(owner, piece, out_ref):
    lanes = pl.ds(pl.multiple_of(owner // 2 * FBLK, 128), FBLK)
    for block in range(HALF_GRID):
        rows = block_rows(owner % 2 * HALF_GRID + block)
        out_ref[rows, lanes] = piece[:, block * FBLK : (block + 1) * FBLK]


def assemble(me, groups, place, shapes, name):
    flat = [array for group in groups for array in group]

    def kernel(me_ref, *refs):
        me = me_ref[0]
        x, y, z = me % 2, me // 2 % 2, me // 4
        high = sum(group[0].shape[0] for group in groups)
        step = at = 0
        for group in groups:
            for index in range(group[0].shape[0]):
                slow = (z - step + high) % high
                for part in range(4):
                    from_x = 1 - x if part % 2 else x
                    from_y = 1 - y if part // 2 else y
                    piece = refs[at + part][index]
                    place(slow * 4 + from_y * 2 + from_x, piece, *refs[len(flat) :])
                step += 1
            at += 4

    return whole_call(
        kernel, [me] + flat, [jax.ShapeDtypeStruct(shape, BF16) for shape in shapes], name, 1
    )


def assemble_down(me, squares):
    high = len(squares)

    def kernel(me_ref, *refs):
        me = me_ref[0]
        x, y, z = me % 2, me // 2 % 2, me // 4
        for step in range(high):
            slow = (z - step + high) % high
            for part in range(4):
                from_x = 1 - x if part % 2 else x
                from_y = 1 - y if part // 2 else y
                place_down(slow * 4 + from_y * 2 + from_x, refs[step][part], refs[high])

    shape = jax.ShapeDtypeStruct((D, HALF_FF), BF16)
    return whole_call(kernel, [me] + list(squares), [shape], "place_down", 1)[0]


def side_by_side(blocks):
    matrices, many, height, width = blocks.shape
    return blocks.transpose(2, 0, 1, 3).reshape(height, matrices * many * width)


def gather_by_name(qkv, out, ffn_part, down):
    qkv_all = lax.all_gather(qkv, "dp", axis=1, tiled=True)
    out_all = lax.all_gather(out[0], "dp", axis=0, tiled=True)
    ffn_all = lax.all_gather(ffn_part, "dp", axis=1, tiled=True)
    down_all = lax.all_gather(down, "dp", axis=0, tiled=True)
    w_qkv = qkv_all.reshape(3, GRID, HALF_GRID, DBLK, DBLK).transpose(1, 3, 0, 2, 4)
    w_out = out_all.reshape(HALF_GRID, GRID, DBLK, DBLK).transpose(0, 2, 1, 3)
    w_ffn = ffn_all.reshape(2, GRID, HALF_GRID, DBLK, FBLK).transpose(0, 1, 3, 2, 4)
    w_down = down_all.reshape(HALF_GRID, GRID, FBLK, DBLK).transpose(1, 3, 0, 2)
    w_ffn = w_ffn.reshape(2, D, HALF_FF)
    return (
        w_qkv.reshape(D, 3 * HALF_D),
        w_out.reshape(HALF_D, D),
        w_ffn[0],
        w_ffn[1],
        w_down.reshape(D, HALF_FF),
    )


def take_rows(owner, ref):
    return ref[block_rows(owner), :]


def take_out(owner, ref):
    return ref[block_rows(owner // 2), pl.ds(pl.multiple_of(owner % 2 * HALF_D, 128), HALF_D)]


def take_down(owner, ref):
    lanes = pl.ds(pl.multiple_of(owner // 2 * FBLK, 128), FBLK)
    return jnp.concatenate(
        [ref[block_rows(owner % 2 * HALF_GRID + block), lanes] for block in range(HALF_GRID)], 1
    )


def reduction(takes, columns, count, me, grads):
    high = count // 4
    half = high // 2
    many = len(grads)

    def step(kernel, inputs, shapes, name):
        return whole_call(kernel, [me] + grads + inputs, shapes, name, 1)

    def find(refs, slow, y, x):
        owner = slow * 4 + y * 2 + x
        found = [take(owner, ref).astype(F32) for take, ref in zip(takes, refs)]
        return found[0] if len(found) == 1 else jnp.concatenate(found, 1)

    def place(me_ref):
        return me_ref[0] % 2, me_ref[0] // 2 % 2, me_ref[0] // 4

    def diagonal_kernel(me_ref, *refs):
        x, y, _ = place(me_ref)
        to_y_ref, to_x_ref = refs[many:]
        for slow in range(high):
            block = find(refs, slow, 1 - y, 1 - x).astype(BF16)
            if slow < half:
                to_y_ref[slow] = block
            else:
                to_x_ref[slow - half] = block

    def side_kernel(me_ref, *refs):
        x, y, _ = place(me_ref)
        by_y_ref, by_x_ref, to_x_ref, to_y_ref = refs[many:]
        for slow in range(high):
            to_x = find(refs, slow, y, 1 - x)
            to_y = find(refs, slow, 1 - y, x)
            if slow < half:
                to_x = to_x + by_y_ref[slow].astype(F32)
            else:
                to_y = to_y + by_x_ref[slow - half].astype(F32)
            to_x_ref[slow] = to_x.astype(BF16)
            to_y_ref[slow] = to_y.astype(BF16)

    def slow_kernel(me_ref, *refs):
        x, y, z = place(me_ref)
        from_x_ref, from_y_ref, own_ref = refs[many : many + 3]
        for shift in range(high):
            slow = (z + shift) % high
            total = (
                find(refs, slow, y, x)
                + from_x_ref[slow].astype(F32)
                + from_y_ref[slow].astype(F32)
            )
            if shift:
                refs[many + 2 + shift][...] = total.astype(BF16)
            else:
                own_ref[...] = total

    block = jax.ShapeDtypeStruct((DBLK, columns), BF16)
    two = [jax.ShapeDtypeStruct((half, DBLK, columns), BF16)] * 2
    four = [jax.ShapeDtypeStruct((high, DBLK, columns), BF16)] * 2

    def first():
        return step(diagonal_kernel, [], two, "send_diagonal")

    def second(by_y, by_x):
        return step(side_kernel, [by_y, by_x], four, "send_sides")

    def third(from_x, from_y):
        shapes = [jax.ShapeDtypeStruct((DBLK, columns), F32)] + [block] * (high - 1)
        return step(slow_kernel, [from_x, from_y], shapes, "send_slow")

    return first, second, third


def send_first(to_y, to_x, count):
    return along(to_y, 2, count), along(to_x, 1, count)


def send_second(to_x, to_y, count):
    return along(to_x, 1, count), along(to_y, 2, count)


def send_third(own, *others, count):
    return [own] + [shifted(block, step + 1, count) for step, block in enumerate(others)]


def scatter_all(qkv, out, ffn_grad, down, count):
    qkv = qkv.reshape(GRID, DBLK, 3, HALF_GRID, DBLK).transpose(2, 0, 3, 1, 4)
    out = out.reshape(HALF_GRID, DBLK, GRID, DBLK).transpose(0, 2, 1, 3)
    ffn_grad = ffn_grad.reshape(GRID, DBLK, 2, HALF_GRID, FBLK).transpose(2, 0, 3, 1, 4)
    down = down.reshape(GRID, DBLK, HALF_GRID, FBLK).transpose(2, 0, 3, 1)
    return (
        lax.psum_scatter(
            qkv.reshape(3, -1, DBLK, DBLK), "dp", scatter_dimension=1, tiled=True
        ),
        lax.psum_scatter(out.reshape(-1, DBLK, DBLK), "dp", scatter_dimension=0, tiled=True),
        lax.psum_scatter(
            ffn_grad.reshape(2, -1, DBLK, FBLK), "dp", scatter_dimension=1, tiled=True
        ),
        lax.psum_scatter(down.reshape(-1, FBLK, DBLK), "dp", scatter_dimension=0, tiled=True),
    )


def sum_everywhere(values, count):
    if count & (count - 1):
        return lax.psum(values, ("dp", "narrow"))
    values = values + lax.ppermute(values, "narrow", [(0, 1), (1, 0)])
    bit = 1
    while bit < count:
        values = values + lax.ppermute(values, "dp", pair_up(bit, count))
        bit *= 2
    return values


def full_dot(left, right, left_dim, right_dim):
    return lax.dot_general(
        left,
        right,
        (((left_dim,), (right_dim,)), ((), ())),
        preferred_element_type=F32,
        precision=lax.Precision.HIGH,
    )


def precondition(parts, width, left, right, left_root, right_root, masters, turned=False):
    counts = [master.shape[0] for master in masters]
    many = len(parts)

    def kernel(*refs):
        part_refs, refs = refs[:many], refs[many:]
        left_ref, right_ref, left_root_ref, right_root_ref = refs[:4]
        master_refs, refs = refs[4 : 4 + len(counts)], refs[4 + len(counts) :]
        grad_ref, left_new_ref, right_new_ref = refs[:3]
        new_refs = refs[3:]
        total = part_refs[0][...]
        for ref in part_refs[1:]:
            total = total + ref[...].astype(F32)
        matrix = 0
        for master_ref, new_ref, many_here in zip(master_refs, new_refs, counts):
            for here in range(many_here):
                for block in range(HALF_GRID):
                    at = (matrix * HALF_GRID + block) * width
                    grad = total[:, at : at + width]
                    grad_ref[matrix, block] = grad
                    outer, inner = full_dot(grad, grad, 1, 1), full_dot(grad, grad, 0, 0)
                    if turned:
                        outer, inner = inner, outer
                        step = full_dot(grad, left_root_ref[matrix, block], 1, 1)
                        step = full_dot(right_root_ref[matrix, block], step, 0, 0)
                    else:
                        step = full_dot(left_root_ref[matrix, block], grad, 1, 0)
                        step = full_dot(step, right_root_ref[matrix, block], 1, 0)
                    left_new_ref[matrix, block] = (
                        DECAY * left_ref[matrix, block] + (1.0 - DECAY) * outer
                    )
                    right_new_ref[matrix, block] = (
                        DECAY * right_ref[matrix, block] + (1.0 - DECAY) * inner
                    )
                    new_ref[here, block] = master_ref[here, block] - STEP_RATE * step
                matrix += 1

    grads = jax.ShapeDtypeStruct((sum(counts),) + masters[0].shape[1:], F32)
    like = [jax.ShapeDtypeStruct(array.shape, F32) for array in (left, right)]
    news = [jax.ShapeDtypeStruct(master.shape, F32) for master in masters]
    return whole_call(
        kernel,
        list(parts) + [left, right, left_root, right_root] + list(masters),
        [grads] + like + news,
        "precondition",
    )


def plain_precondition(block_grad, left_stat, right_stat, left_root, right_root, master):
    new_left = DECAY * left_stat + (1.0 - DECAY) * jnp.einsum(
        "...ij,...kj->...ik", block_grad, block_grad, precision=HIGHEST_PRECISION
    )
    new_right = DECAY * right_stat + (1.0 - DECAY) * jnp.einsum(
        "...ji,...jk->...ik", block_grad, block_grad, precision=HIGHEST_PRECISION
    )
    turned = jnp.einsum("...ij,...jk->...ik", left_root, block_grad, precision=HIGHEST_PRECISION)
    turned = jnp.einsum("...ij,...jk->...ik", turned, right_root, precision=HIGHEST_PRECISION)
    return (new_left, new_right, master - STEP_RATE * turned)


def in_order_kernel(core_ref, mine_ref, other_ref, out_ref):
    rows = mine_ref.shape[0]
    core = core_ref[0]
    out_ref[pl.ds(pl.multiple_of(core * rows, 16), rows), :] = mine_ref[...]
    out_ref[pl.ds(pl.multiple_of((1 - core) * rows, 16), rows), :] = other_ref[...]


def in_order(mine, core):
    shape = jax.ShapeDtypeStruct((2 * mine.shape[0], mine.shape[1]), mine.dtype)
    return whole_call(in_order_kernel, [core, mine, other_core(mine)], [shape], "in_order", 1)[0]


def layer_out_kernel(core_ref, x1_ref, near_ref, far_ref, out_ref):
    total = x1_ref[...] + near_ref[...].astype(F32) + far_ref[...].astype(F32)
    out_ref[...] = total.astype(BF16)


def input_grad_kernel(core_ref, x_ref, dx1_ref, near_ref, far_ref, gain_ref, out_ref):
    x = x_ref[...].astype(F32)
    scale = lax.rsqrt(jnp.mean(x * x, -1, keepdims=True) + EPSILON)
    weighted = (near_ref[...].astype(F32) + far_ref[...].astype(F32)) * gain_ref[0:1, :]
    inner = jnp.mean(weighted * x, -1, keepdims=True)
    out_ref[...] = dx1_ref[...] + scale * weighted - x * (scale * scale * scale * inner)


def own_rows_call(kernel, core, blocked, whole, own_rows, dtype, name):
    steps = own_rows // ROWS
    return pl.pallas_call(
        kernel,
        grid_spec=pltpu.PrefetchScalarGridSpec(
            num_scalar_prefetch=1,
            grid=(steps,),
            in_specs=[pl.BlockSpec((ROWS, D), lambda i, core: (core[0] * steps + i, 0))]
            * len(blocked)
            + [pl.BlockSpec(array.shape, lambda i, core: (0, 0)) for array in whole],
            out_specs=pl.BlockSpec((ROWS, D), lambda i, core: (i, 0)),
        ),
        out_shape=jax.ShapeDtypeStruct((own_rows, D), dtype),
        compiler_params=kernel_params(),
        cost_estimate=cost(),
        name=name,
    )(core, *blocked, *whole)


def rotary_tables(length):
    frequency = jnp.power(10000.0, -2.0 * jnp.arange(HEAD_DIM // 2, dtype=F32) / HEAD_DIM)
    angles = (jnp.arange(length) % LEN).astype(F32)[:, None] * frequency[None, :]
    sine = jnp.sin(angles)
    return (
        jnp.tile(jnp.cos(angles), (1, 4)),
        jnp.tile(jnp.concatenate([-sine, sine], 1), (1, 2)),
    )


def body(
    tokens,
    cotangent,
    gains,
    gain_moments,
    qkv_master,
    out_master,
    ffn_master,
    down_master,
    attn_left,
    attn_right,
    attn_left_root,
    attn_right_root,
    ffn_left,
    ffn_right,
    ffn_left_root,
    ffn_right_root,
    down_left,
    down_right,
    down_left_root,
    down_right_root,
):
    count = lax.axis_size("dp")
    me = lax.axis_index("dp").astype(jnp.int32)[None]
    core = lax.axis_index("narrow").astype(jnp.int32)[None]
    own_rows = tokens.shape[0]
    by_hand = count == GRID

    qkv, out, ffn_part = (t.astype(BF16) for t in (qkv_master[:, 0], out_master, ffn_master[:, 0]))
    down = down_master[0].astype(BF16)
    if by_hand:
        first = jnp.concatenate([side_by_side(qkv), side_by_side(out)], 1)
        second = side_by_side(ffn_part)
        last = side_by_side(jnp.swapaxes(down, 1, 2)[None])
        first_far = all_shifted(first, count)
        last_x = along(last, 1, count)
        (pair,) = stack([last, last_x], 1, "stack_pair")
        pair_y = along(pair, 2, count)

    x = in_order(tokens, core)
    cot = in_order(cotangent, core)
    cosine, sine_part = rotary_tables(x.shape[0])

    if by_hand:
        early = after(first, x, cosine, sine_part, pair)
        first_a, first_b = stack([early] + first_far, 2, "stack_first")
        first_groups = spread(first_a, first_b, count)
        second_far = all_shifted(after(second, first_a), count)
        second_a, second_b = stack([second] + second_far, 2, "stack_second")
        second_groups = spread(second_a, second_b, count)
        (square,) = stack([pair, after(pair_y, second_a)], 1, "stack_square")
        squares = [square] + all_shifted(square, count)
        w_qkv, w_out = assemble(
            me, first_groups, place_qkv_out, [(D, 3 * HALF_D), (HALF_D, D)], "place_qkv_out"
        )
        x_late = after(x, second_a)
    else:
        w_qkv, w_out, w_gate, w_up, w_down = gather_by_name(qkv, out, ffn_part, down)
        x_late = x
    normed_one, q, k, v = project(x_late, gains, w_qkv, cosine, sine_part)
    w_out_far = other_core(w_out)
    attended, lse = attend(q, k, v)
    attended_far = other_core(attended)
    if by_hand:
        w_gate, w_up = assemble(
            me, second_groups, place_gate_up, [(D, HALF_FF)] * 2, "place_gate_up"
        )
        w_down = assemble_down(me, squares)
    middle, normed_two, gate, up, hidden = ffn(
        x, attended, attended_far, w_out, w_out_far, gains, w_gate, w_up
    )

    down_weight_grad = dot_tn(cot, hidden)
    cot_late = cot
    if by_hand:
        down_sum = reduction([take_down], HALF_FF, count, me, [down_weight_grad])
        sent = down_sum[0]()
        cot_late = after(cot, sent[0])
        down_far = send_first(*sent, count)
    out_part, ffn_back_grad, normed_part = ffn_back(
        cot_late, gate, up, hidden, w_down, w_gate, w_up
    )
    normed_far = other_core(normed_part)
    if by_hand:
        sent = down_sum[1](after(down_far[0], normed_part), down_far[1])
        down_far = send_second(*sent, count)
        ffn_back_grad = after(ffn_back_grad, sent[0])
    ffn_weight_grad = dot_tn(normed_two, ffn_back_grad)
    if by_hand:
        ffn_sum = reduction([take_rows], FF, count, me, [ffn_weight_grad])
        sent = ffn_sum[0]()
        normed_far = after(normed_far, sent[0])
        ffn_far = send_first(*sent, count)
    middle_grad, branch, attended_grad, gain_two = middle_back(
        cot, middle, normed_part, normed_far, gains, w_out
    )
    out_far = other_core(after(out_part, branch))
    out_weight_grad = dot_tn(attended, branch)
    if by_hand:
        sent = down_sum[2](after(down_far[0], branch), down_far[1])
        down_parts = send_third(*sent, count=count)
        sent = ffn_sum[1](after(ffn_far[0], branch, sent[0]), ffn_far[1])
        ffn_far = send_second(*sent, count)
        attended_grad = after(attended_grad, sent[0], out_weight_grad)
    dq, dk, dv = attend_back(q, k, v, attended_grad, attended, lse, cosine, sine_part)
    qkv_weight_grad = dot_tn(normed_one, jnp.concatenate([dq, dk, dv], 1))
    if by_hand:
        late_sum = reduction(
            [take_rows, take_out], 4 * HALF_D, count, me, [qkv_weight_grad, out_weight_grad]
        )
        sent = late_sum[0]()
        late_far = send_first(*sent, count)
        sent = ffn_sum[2](after(ffn_far[0], sent[0]), ffn_far[1])
        ffn_parts = send_third(*sent, count=count)
        dq = after(dq, sent[0])
    input_part, gain_one = input_back(x, dq, dk, dv, w_qkv)
    input_far = other_core(input_part)
    gain_grad = sum_everywhere(jnp.concatenate([gain_one, 0.5 * gain_two]), count)
    gain_moment_new = DECAY * gain_moments + (1.0 - DECAY) * gain_grad * gain_grad
    gain_new = gains - GAIN_RATE * gain_grad / (jnp.sqrt(gain_moment_new) + 1e-08)

    if by_hand:
        down_parts[1] = after(down_parts[1], input_part)
        down_grad, down_left_new, down_right_new, down_new = precondition(
            down_parts,
            FBLK,
            down_left,
            down_right,
            down_left_root,
            down_right_root,
            [jnp.swapaxes(down_master, 2, 3)],
            turned=True,
        )
        down_grad, down_new = jnp.swapaxes(down_grad, 2, 3), jnp.swapaxes(down_new, 2, 3)
        sent = late_sum[1](after(late_far[0], down_left_new), late_far[1])
        late_far = send_second(*sent, count)
        ffn_parts[1] = after(ffn_parts[1], sent[0])
        ffn_grad, ffn_left_new, ffn_right_new, ffn_new = precondition(
            ffn_parts,
            FBLK,
            ffn_left[:, 0],
            ffn_right[:, 0],
            ffn_left_root[:, 0],
            ffn_right_root[:, 0],
            [ffn_master[:, 0]],
        )
        sent = late_sum[2](after(late_far[0], ffn_left_new), late_far[1])
        late_parts = send_third(*sent, count=count)
        input_far = after(input_far, sent[0])
        out_far = after(out_far, sent[0])
    layer_out = own_rows_call(
        layer_out_kernel, core, [middle, out_part, out_far], [], own_rows, BF16, "layer_out"
    )
    input_grad = own_rows_call(
        input_grad_kernel,
        core,
        [x, middle_grad, input_part, input_far],
        [gains],
        own_rows,
        F32,
        "input_grad",
    )
    if by_hand:
        late_parts[1] = after(late_parts[1], layer_out, input_grad)
        attn_grad, attn_left_new, attn_right_new, qkv_new, out_new = precondition(
            late_parts,
            DBLK,
            attn_left[:, 0],
            attn_right[:, 0],
            attn_left_root[:, 0],
            attn_right_root[:, 0],
            [qkv_master[:, 0], out_master],
        )
        attn_grad, attn_left_new, attn_right_new, qkv_new, ffn_grad, ffn_left_new, ffn_right_new, ffn_new = (
            array[:, None]
            for array in (
                attn_grad,
                attn_left_new,
                attn_right_new,
                qkv_new,
                ffn_grad,
                ffn_left_new,
                ffn_right_new,
                ffn_new,
            )
        )
    else:
        qkv_owned, out_owned, ffn_owned, down_owned = scatter_all(
            qkv_weight_grad, out_weight_grad, ffn_weight_grad, down_weight_grad, count
        )
        attn_grad = jnp.concatenate([qkv_owned, out_owned[None]], 0)[:, None]
        ffn_grad = ffn_owned[:, None]
        down_grad = down_owned[None]
        attn_left_new, attn_right_new, attn_new = plain_precondition(
            attn_grad,
            attn_left,
            attn_right,
            attn_left_root,
            attn_right_root,
            jnp.concatenate([qkv_master, out_master[None]], 0),
        )
        qkv_new, out_new = attn_new[:3], attn_new[3]
        ffn_left_new, ffn_right_new, ffn_new = plain_precondition(
            ffn_grad, ffn_left, ffn_right, ffn_left_root, ffn_right_root, ffn_master
        )
        down_left_new, down_right_new, down_new = plain_precondition(
            down_grad, down_left, down_right, down_left_root, down_right_root, down_master
        )
    return (
        layer_out,
        input_grad,
        gain_grad,
        gain_moment_new,
        gain_new,
        attn_grad,
        attn_left_new,
        attn_right_new,
        qkv_new,
        out_new,
        ffn_grad,
        ffn_left_new,
        ffn_right_new,
        ffn_new,
        down_grad,
        down_left_new,
        down_right_new,
        down_new,
    )


def solution(mesh):
    tokens = P(("dp", "narrow"), None)
    stacked = P(None, "narrow", "dp", None, None)
    single = P("narrow", "dp", None, None)
    return jax.shard_map(
        body,
        mesh=mesh,
        in_specs=(tokens, tokens, P(), P(), stacked, single, stacked, single)
        + (stacked,) * 8
        + (single,) * 4,
        out_specs=(tokens, tokens, P(), P(), P())
        + (stacked,) * 4
        + (single,)
        + (stacked,) * 4
        + (single,) * 4,
        check_vma=False,
    )
```

```python
import functools
import math

import jax
import jax.numpy as jnp
from jax import lax
from jax.experimental import pallas as pl
from jax.experimental.pallas import tpu as pltpu
from jax.sharding import PartitionSpec as P

D = 768
HEAD_DIM = 64
FF = 2048
LEN = 1024
GRID = 16
DBLK = D // GRID
FBLK = FF // GRID
HALF_GRID = GRID // 2
HALF_D = D // 2
HALF_FF = FF // 2
PAIR = 2 * HEAD_DIM
ROWS = 256

EPSILON = 1e-05
DECAY = 0.5
STEP_RATE = 0.25
GAIN_RATE = 0.1
NEG_FILL = -1e30
HIGHEST_PRECISION = lax.Precision.HIGHEST
BF16 = jnp.bfloat16
F32 = jnp.float32
VMEM_MIB = 14
SMALL_MIB = 8
PACK_MIB = 60
STATE_ROWS = 16


def dot_nn(left, right):
    return lax.dot_general(left, right, (((1,), (0,)), ((), ())), preferred_element_type=F32)


def dot_nt(left, right):
    return lax.dot_general(left, right, (((1,), (1,)), ((), ())), preferred_element_type=F32)


def dot_tn(left, right):
    return lax.dot_general(left, right, (((0,), (0,)), ((), ())), preferred_element_type=F32)


def kernel_params(mib=VMEM_MIB):
    return pltpu.CompilerParams(vmem_limit_bytes=mib * 1024 * 1024)


def cost():
    return pl.CostEstimate(flops=0, bytes_accessed=0, transcendentals=0)


def rows_spec(columns):
    return pl.BlockSpec((ROWS, columns), lambda i: (i, 0))


def whole_spec(*shape):
    return pl.BlockSpec(shape, lambda i: (0,) * len(shape))


def lower_lanes(shape):
    return lax.broadcasted_iota(jnp.int32, shape, 1) % HEAD_DIM < HEAD_DIM // 2


def turn(features, cosine, sine_part, lower):
    half = HEAD_DIM // 2
    partner = jnp.where(
        lower, pltpu.roll(features, PAIR - half, 1), pltpu.roll(features, half, 1)
    )
    return features * cosine + partner * sine_part


def project_rows(x_ref, gain_ref, w, cos_ref, sin_ref, n1_ref, q_ref, k_ref, v_ref):
    x = x_ref[...].astype(F32)
    scale = lax.rsqrt(jnp.mean(x * x, -1, keepdims=True) + EPSILON)
    normed = (x * scale * gain_ref[0:1, :]).astype(BF16)
    n1_ref[...] = normed
    lower = lower_lanes((ROWS, PAIR))
    cosine, sine_part = cos_ref[...], sin_ref[...]
    both = dot_nn(normed, w)
    for tile in range(HALF_D // PAIR):
        lanes = slice(tile * PAIR, (tile + 1) * PAIR)
        query = both[:, tile * PAIR : (tile + 1) * PAIR]
        key = both[:, HALF_D + tile * PAIR : HALF_D + (tile + 1) * PAIR]
        turned = turn(query, cosine, sine_part, lower).astype(BF16)
        q_ref[:, lanes] = turned * BF16(1.0 / math.sqrt(HEAD_DIM))
        k_ref[:, lanes] = turn(key, cosine, sine_part, lower).astype(BF16)
    v_ref[...] = both[:, 2 * HALF_D :].astype(BF16)


def project_kernel(x_ref, gain_ref, w_ref, cos_ref, sin_ref, n1_ref, q_ref, k_ref, v_ref):
    project_rows(x_ref, gain_ref, w_ref[...], cos_ref, sin_ref, n1_ref, q_ref, k_ref, v_ref)


def project(x, gains, weight, cosine, sine_part):
    length = x.shape[0]
    half = jax.ShapeDtypeStruct((length, HALF_D), BF16)
    return pl.pallas_call(
        project_kernel,
        grid=(length // ROWS,),
        in_specs=[
            rows_spec(D),
            whole_spec(2, D),
            whole_spec(D, 3 * HALF_D),
            rows_spec(PAIR),
            rows_spec(PAIR),
        ],
        out_specs=[rows_spec(D), rows_spec(HALF_D), rows_spec(HALF_D), rows_spec(HALF_D)],
        out_shape=[jax.ShapeDtypeStruct((length, D), BF16), half, half, half],
        compiler_params=kernel_params(),
        cost_estimate=cost(),
        name="project",
    )(x, gains, weight, cosine, sine_part)


def attend_kernel(q_ref, k_ref, v_ref, o_ref, lse_ref):
    length = q_ref.shape[0]
    first_head = lax.broadcasted_iota(jnp.int32, (ROWS, PAIR), 1) < HEAD_DIM
    keys = k_ref[...]
    values = jnp.concatenate([v_ref[...], jnp.ones((length, PAIR), BF16)], 1)
    causal = lax.broadcasted_iota(jnp.int32, (ROWS, ROWS), 0) >= lax.broadcasted_iota(
        jnp.int32, (ROWS, ROWS), 1
    )
    for block in range(length // ROWS):
        rows = slice(block * ROWS, (block + 1) * ROWS)
        width = (block + 1) * ROWS
        query_block = q_ref[rows, :]
        parts, sums = [], []
        for head in range(2):
            mine = first_head if head == 0 else jnp.logical_not(first_head)
            query = jnp.where(mine, query_block, jnp.zeros_like(query_block))
            scores = jnp.where(causal, dot_nt(query, keys[block * ROWS : width]), NEG_FILL)
            if block:
                scores = jnp.concatenate([dot_nt(query, keys[: block * ROWS]), scores], 1)
            top = jnp.max(scores, 1, keepdims=True)
            exponent = jnp.exp(scores - top).astype(BF16)
            product = dot_nn(exponent, values[:width])
            total = product[:, PAIR:]
            parts.append(product[:, :PAIR] / total)
            sums.append(top + jnp.log(total))
        o_ref[rows, :] = jnp.where(first_head, parts[0], parts[1]).astype(BF16)
        lane = lax.broadcasted_iota(jnp.int32, (ROWS, PAIR), 1)
        lse_ref[:, rows] = jnp.transpose(jnp.where(lane == 0, sums[0], sums[1]))[:8, :]


def attend(q, k, v):
    length = q.shape[0]
    pairs = q.shape[1] // PAIR
    block = pl.BlockSpec((length, PAIR), lambda h: (0, h))
    return pl.pallas_call(
        attend_kernel,
        grid=(pairs,),
        in_specs=[block] * 3,
        out_specs=[block, pl.BlockSpec((8, length), lambda h: (h, 0))],
        out_shape=[
            jax.ShapeDtypeStruct(q.shape, BF16),
            jax.ShapeDtypeStruct((8 * pairs, length), F32),
        ],
        compiler_params=kernel_params(),
        cost_estimate=cost(),
        name="attend",
    )(q, k, v)


def attend_back_kernel(
    q_ref, k_ref, v_ref, do_ref, o_ref, lse_ref, cos_ref, sin_ref, dq_ref, dk_ref, dv_ref, dqt_ref
):
    length = q_ref.shape[0]
    first_head = lax.broadcasted_iota(jnp.int32, (length, PAIR), 1) < HEAD_DIM
    zero = BF16(0)
    queries = [
        jnp.where(first_head, q_ref[...], zero),
        jnp.where(first_head, zero, q_ref[...]),
    ]
    grads = [
        jnp.where(first_head, do_ref[...], zero),
        jnp.where(first_head, zero, do_ref[...]),
    ]
    product = do_ref[...].astype(F32) * o_ref[...].astype(F32)
    head_row = lax.broadcasted_iota(jnp.int32, (8, PAIR), 0)
    head_lane = lax.broadcasted_iota(jnp.int32, (8, PAIR), 1) // HEAD_DIM
    inner = lax.dot_general(
        (head_row == head_lane).astype(F32),
        product,
        (((1,), (1,)), ((), ())),
        preferred_element_type=F32,
        precision=HIGHEST_PRECISION,
    )
    turned_keys = jnp.transpose(k_ref[...].astype(F32)).astype(BF16)
    first_rows = lax.broadcasted_iota(jnp.int32, turned_keys.shape, 0) < HEAD_DIM
    key_heads = [
        jnp.where(first_rows, turned_keys, zero),
        jnp.where(first_rows, zero, turned_keys),
    ]
    causal = lax.broadcasted_iota(jnp.int32, (ROWS, ROWS), 0) <= lax.broadcasted_iota(
        jnp.int32, (ROWS, ROWS), 1
    )
    dqt_ref[...] = jnp.zeros_like(dqt_ref)
    lower = lower_lanes((ROWS, PAIR))
    for block in range(length // ROWS):
        rows = slice(block * ROWS, (block + 1) * ROWS)
        start = block * ROWS
        key_block, value_block = k_ref[rows, :], v_ref[rows, :]
        dk = jnp.zeros((ROWS, PAIR), F32)
        dv = jnp.zeros((ROWS, PAIR), F32)
        for head in range(2):
            scores = dot_nt(key_block, queries[head][start:])
            probs = jnp.exp(scores - lse_ref[head : head + 1, start:])
            diagonal = jnp.where(causal, probs[:, :ROWS], 0.0)
            if start + ROWS == length:
                probs = diagonal
            else:
                probs = jnp.concatenate([diagonal, probs[:, ROWS:]], 1)
            prob_grad = dot_nt(value_block, grads[head][start:])
            score_grad = (probs * (prob_grad - inner[head : head + 1, start:])).astype(BF16)
            dv = dv + dot_nn(probs.astype(BF16), grads[head][start:])
            dk = dk + dot_nn(score_grad, queries[head][start:])
            dqt_ref[:, start:] += dot_nn(key_heads[head][:, rows], score_grad)
        dk_ref[rows, :] = turn(dk, cos_ref[rows, :], -sin_ref[rows, :], lower).astype(BF16)
        dv_ref[rows, :] = dv.astype(BF16)
    for block in range(length // ROWS):
        rows = slice(block * ROWS, (block + 1) * ROWS)
        dq = jnp.transpose(dqt_ref[:, rows]) * (1.0 / math.sqrt(HEAD_DIM))
        dq_ref[rows, :] = turn(dq, cos_ref[rows, :], -sin_ref[rows, :], lower).astype(BF16)


def attend_back(q, k, v, grad, o, lse, cosine, sine_part):
    length = q.shape[0]
    pairs = q.shape[1] // PAIR
    block = pl.BlockSpec((length, PAIR), lambda h: (0, h))
    table = pl.BlockSpec((length, PAIR), lambda h: (0, 0))
    return pl.pallas_call(
        attend_back_kernel,
        grid=(pairs,),
        in_specs=[block] * 5 + [pl.BlockSpec((8, length), lambda h: (h, 0)), table, table],
        out_specs=[block] * 3,
        out_shape=[jax.ShapeDtypeStruct(q.shape, BF16)] * 3,
        scratch_shapes=[pltpu.VMEM((PAIR, length), F32)],
        compiler_params=kernel_params(),
        cost_estimate=cost(),
        name="attend_back",
    )(q, k, v, grad, o, lse, cosine, sine_part)


def ffn_kernel(
    x_ref, o_ref, o_far_ref, wo_ref, wo_far_ref, gain_ref, wg_ref, wu_ref,
    x1_ref, n2_ref, gate_ref, up_ref, hidden_ref,
):
    middle = (
        x_ref[...].astype(F32)
        + dot_nn(o_ref[...], wo_ref[...])
        + dot_nn(o_far_ref[...], wo_far_ref[...])
    )
    x1_ref[...] = middle
    scale = lax.rsqrt(jnp.mean(middle * middle, -1, keepdims=True) + EPSILON)
    normed = (middle * scale * gain_ref[1:2, :]).astype(BF16)
    n2_ref[...] = normed
    gate = dot_nn(normed, wg_ref[...])
    up = dot_nn(normed, wu_ref[...])
    gate_ref[...] = gate
    up_ref[...] = up
    hidden_ref[...] = (gate * jax.nn.sigmoid(gate) * up).astype(BF16)


def ffn(x, o, o_far, wo, wo_far, gains, wg, wu):
    length = x.shape[0]
    wide = jax.ShapeDtypeStruct((length, HALF_FF), F32)
    return pl.pallas_call(
        ffn_kernel,
        grid=(length // ROWS,),
        in_specs=[
            rows_spec(D),
            rows_spec(HALF_D),
            rows_spec(HALF_D),
            whole_spec(HALF_D, D),
            whole_spec(HALF_D, D),
            whole_spec(2, D),
            whole_spec(D, HALF_FF),
            whole_spec(D, HALF_FF),
        ],
        out_specs=[rows_spec(D), rows_spec(D)] + [rows_spec(HALF_FF)] * 3,
        out_shape=[
            jax.ShapeDtypeStruct((length, D), F32),
            jax.ShapeDtypeStruct((length, D), BF16),
            wide,
            wide,
            jax.ShapeDtypeStruct((length, HALF_FF), BF16),
        ],
        compiler_params=kernel_params(),
        cost_estimate=cost(),
        name="ffn",
    )(x, o, o_far, wo, wo_far, gains, wg, wu)


def ffn_out_kernel(hidden_ref, wdt_ref, part_ref):
    part_ref[...] = dot_nt(hidden_ref[...], wdt_ref[...]).astype(BF16)


def ffn_out(hidden, wdt):
    shape = jax.ShapeDtypeStruct((hidden.shape[0], D), BF16)
    return whole_call(ffn_out_kernel, [hidden, wdt], [shape], "ffn_out")[0]


def ffn_back_kernel(cot_ref, gate_ref, up_ref, wdt_ref, wg_ref, wu_ref, dgu_ref, dn2_ref):
    hidden_grad = dot_nn(cot_ref[...], wdt_ref[...])
    gate, up = gate_ref[...], up_ref[...]
    sigma = jax.nn.sigmoid(gate)
    gate_grad = (hidden_grad * up * sigma * (1.0 + gate * (1.0 - sigma))).astype(BF16)
    up_grad = (hidden_grad * gate * sigma).astype(BF16)
    dgu_ref[:, :HALF_FF] = gate_grad
    dgu_ref[:, HALF_FF:] = up_grad
    dn2_ref[...] = (dot_nt(gate_grad, wg_ref[...]) + dot_nt(up_grad, wu_ref[...])).astype(BF16)


def ffn_back(cot, gate, up, wdt, wg, wu):
    length = cot.shape[0]
    return pl.pallas_call(
        ffn_back_kernel,
        grid=(length // ROWS,),
        in_specs=[rows_spec(D)] + [rows_spec(HALF_FF)] * 2 + [whole_spec(D, HALF_FF)] * 3,
        out_specs=[rows_spec(FF), rows_spec(D)],
        out_shape=[
            jax.ShapeDtypeStruct((length, FF), BF16),
            jax.ShapeDtypeStruct((length, D), BF16),
        ],
        compiler_params=kernel_params(),
        cost_estimate=cost(),
        name="ffn_back",
    )(cot, gate, up, wdt, wg, wu)


def middle_back_kernel(
    cot_ref, x1_ref, near_ref, far_ref, gain_ref, wo_ref, dx1_ref, da_ref, do_ref, g2_ref
):
    middle = x1_ref[...]
    scale = lax.rsqrt(jnp.mean(middle * middle, -1, keepdims=True) + EPSILON)
    grad = near_ref[...].astype(F32) + far_ref[...].astype(F32)
    weighted = grad * gain_ref[1:2, :]
    inner = jnp.mean(weighted * middle, -1, keepdims=True)
    middle_grad = (
        cot_ref[...].astype(F32) + scale * weighted - middle * (scale * scale * scale * inner)
    )
    dx1_ref[...] = middle_grad
    branch = middle_grad.astype(BF16)
    da_ref[...] = branch
    do_ref[...] = dot_nt(branch, wo_ref[...]).astype(BF16)

    @pl.when(pl.program_id(0) == 0)
    def _():
        g2_ref[...] = jnp.zeros_like(g2_ref)

    g2_ref[...] += jnp.sum(grad * middle * scale, 0, keepdims=True)


def middle_back(cot, x1, near, far, gains, wo):
    length = cot.shape[0]
    return pl.pallas_call(
        middle_back_kernel,
        grid=(length // ROWS,),
        in_specs=[rows_spec(D)] * 4 + [whole_spec(2, D), whole_spec(HALF_D, D)],
        out_specs=[rows_spec(D), rows_spec(D), rows_spec(HALF_D), whole_spec(1, D)],
        out_shape=[
            jax.ShapeDtypeStruct((length, D), F32),
            jax.ShapeDtypeStruct((length, D), BF16),
            jax.ShapeDtypeStruct((length, HALF_D), BF16),
            jax.ShapeDtypeStruct((1, D), F32),
        ],
        compiler_params=kernel_params(),
        cost_estimate=cost(),
        name="middle_back",
    )(cot, x1, near, far, gains, wo)


def input_back_kernel(x_ref, dq_ref, dk_ref, dv_ref, w_ref, part_ref, g1_ref):
    w = w_ref[...]
    grad = (
        dot_nt(dq_ref[...], w[:, :HALF_D])
        + dot_nt(dk_ref[...], w[:, HALF_D : 2 * HALF_D])
        + dot_nt(dv_ref[...], w[:, 2 * HALF_D :])
    )
    part_ref[...] = grad.astype(BF16)
    x = x_ref[...].astype(F32)
    scale = lax.rsqrt(jnp.mean(x * x, -1, keepdims=True) + EPSILON)

    @pl.when(pl.program_id(0) == 0)
    def _():
        g1_ref[...] = jnp.zeros_like(g1_ref)

    g1_ref[...] += jnp.sum(grad * x * scale, 0, keepdims=True)


def input_back(x, dq, dk, dv, w):
    length = x.shape[0]
    return pl.pallas_call(
        input_back_kernel,
        grid=(length // ROWS,),
        in_specs=[rows_spec(D)] + [rows_spec(HALF_D)] * 3 + [whole_spec(D, 3 * HALF_D)],
        out_specs=[rows_spec(D), whole_spec(1, D)],
        out_shape=[
            jax.ShapeDtypeStruct((length, D), BF16),
            jax.ShapeDtypeStruct((1, D), F32),
        ],
        compiler_params=kernel_params(),
        cost_estimate=cost(),
        name="input_back",
    )(x, dq, dk, dv, w)


def whole_call(kernel, inputs, shapes, name, scalars=0, mib=SMALL_MIB):
    vmem = pl.BlockSpec(memory_space=pltpu.VMEM)
    smem = pl.BlockSpec(memory_space=pltpu.SMEM)
    return pl.pallas_call(
        kernel,
        in_specs=[smem] * scalars + [vmem] * (len(inputs) - scalars),
        out_specs=[vmem] * len(shapes),
        out_shape=shapes,
        compiler_params=kernel_params(mib),
        cost_estimate=cost(),
        name=name,
    )(*inputs)


def pair_up(bit, count):
    return [(i, i ^ bit) for i in range(count)]


def after(value, *others):
    return lax.optimization_barrier((value,) + others)[0]


def along(values, bit, count):
    return lax.ppermute(values, "dp", pair_up(bit, count))


def shifted(values, steps, count):
    return lax.ppermute(values, "dp", [(i, (i + 4 * steps) % count) for i in range(count)])


def other_core(values):
    return lax.ppermute(values, "narrow", [(0, 1), (1, 0)])


def all_shifted(values, count):
    return [shifted(values, step, count) for step in range(1, count // 4)]


def copy_columns(sources, outputs, name):
    rows = sources[0].shape[0]
    shapes = [
        jax.ShapeDtypeStruct((rows, sum(stop - start for _, start, stop in parts)), BF16)
        for parts in outputs
    ]

    def kernel(*refs):
        for out_ref, parts in zip(refs[len(sources) :], outputs):
            at = 0
            for number, start, stop in parts:
                out_ref[:, at : at + stop - start] = refs[number][:, start:stop]
                at += stop - start

    return whole_call(kernel, sources, shapes, name)


def block_rows(owner):
    return pl.ds(pl.multiple_of(owner * DBLK, 16), DBLK)


def block_lanes(index, width):
    return pl.ds(pl.multiple_of(index * width, 128), width)


def place_qkv_out(owner, start, piece, qkv_ref, out_ref):
    cut, stop = 3 * HALF_D, start + piece.shape[1]
    if start < cut:
        end = min(stop, cut)
        qkv_ref[block_rows(owner), start:end] = piece[:, : end - start]
    if stop > cut:
        begin = max(start, cut)
        lanes = pl.ds(pl.multiple_of(owner % 2 * HALF_D + (begin - cut), 128), stop - begin)
        out_ref[block_rows(owner // 2), lanes] = piece[:, begin - start :]


def place_gate_up(owner, start, piece, gate_ref, up_ref):
    stop = start + piece.shape[1]
    if start < HALF_FF:
        end = min(stop, HALF_FF)
        gate_ref[block_rows(owner), start:end] = piece[:, : end - start]
    if stop > HALF_FF:
        begin = max(start, HALF_FF)
        up_ref[block_rows(owner), begin - HALF_FF : stop - HALF_FF] = piece[:, begin - start :]


def place_down(owner, start, piece, out_ref):
    lanes = block_lanes(owner // 2, FBLK)
    for block in range(piece.shape[1] // FBLK):
        rows = block_rows(owner % 2 * HALF_GRID + start // FBLK + block)
        out_ref[rows, lanes] = piece[:, block * FBLK : (block + 1) * FBLK]


def assemble(me, high, sources, entries, place, shapes, name, begun=()):
    sources = list(sources)

    def kernel(me_ref, *refs):
        x, y, z = me_ref[0] % 2, me_ref[0] // 2 % 2, me_ref[0] // 4
        out_refs = refs[len(sources) + len(begun) :]
        for ref, out_ref in zip(refs[len(sources) :], out_refs if begun else ()):
            out_ref[...] = ref[...]
        for number, start, width, step, over_y, over_x, first in entries:
            slow = (z - step + high) % high
            from_y = 1 - y if over_y else y
            from_x = 1 - x if over_x else x
            piece = refs[number][:, start : start + width]
            place(slow * 4 + from_y * 2 + from_x, first, piece, *out_refs)

    return whole_call(
        kernel,
        [me] + sources + list(begun),
        [jax.ShapeDtypeStruct(shape, BF16) for shape in shapes],
        name,
        1,
    )


def pack_kernel(qkv_ref, out_ref, ffn_ref, down_ref, first_ref, second_ref, slab_ref, *scratch):
    held, sems = scratch[:-1], scratch[-1]
    copies = [
        pltpu.make_async_copy(ref, here, sems.at[number])
        for number, (ref, here) in enumerate(zip((qkv_ref, out_ref, ffn_ref, down_ref), held))
    ]
    for copy in copies:
        copy.start()

    def row(ref, matrix):
        return jnp.concatenate([ref[matrix, block].astype(BF16) for block in range(HALF_GRID)], 1)

    at = 0
    for copy, ref in zip(copies, held):
        copy.wait()
        for matrix in range(ref.shape[0]):
            part = row(ref, matrix)
            stop = at + part.shape[1]
            slab_ref[:, at:stop] = part
            if stop <= first_ref.shape[1]:
                first_ref[:, at:stop] = part
            elif stop <= first_ref.shape[1] + second_ref.shape[1]:
                second_ref[:, at - first_ref.shape[1] : stop - first_ref.shape[1]] = part
            at = stop


def pack(*masters):
    vmem = pl.BlockSpec(memory_space=pltpu.VMEM)
    return pl.pallas_call(
        pack_kernel,
        in_specs=[pl.BlockSpec(memory_space=pl.ANY)] * len(masters),
        out_specs=[vmem] * 3,
        out_shape=[
            jax.ShapeDtypeStruct((DBLK, width), BF16)
            for width in (4 * HALF_D, FF, 4 * HALF_D + 3 * HALF_FF)
        ],
        scratch_shapes=[pltpu.VMEM(master.shape, F32) for master in masters]
        + [pltpu.SemaphoreType.DMA((len(masters),))],
        compiler_params=kernel_params(PACK_MIB),
        cost_estimate=cost(),
        name="pack",
    )(*masters)


def tables_kernel(cos_ref, sin_ref, cosine_ref, sine_ref):
    cosine, sine = cos_ref[...], sin_ref[...]
    cosine_ref[...] = jnp.concatenate([cosine] * 4, 1)
    sine_ref[...] = jnp.concatenate([-sine, sine] * 2, 1)


def side_by_side(blocks):
    matrices, many, height, width = blocks.shape
    return blocks.transpose(2, 0, 1, 3).reshape(height, matrices * many * width)


def gather_by_name(qkv, out, ffn_part, down):
    qkv_all = lax.all_gather(qkv, "dp", axis=1, tiled=True)
    out_all = lax.all_gather(out[0], "dp", axis=0, tiled=True)
    ffn_all = lax.all_gather(ffn_part, "dp", axis=1, tiled=True)
    down_all = lax.all_gather(down, "dp", axis=0, tiled=True)
    w_qkv = qkv_all.reshape(3, GRID, HALF_GRID, DBLK, DBLK).transpose(1, 3, 0, 2, 4)
    w_out = out_all.reshape(HALF_GRID, GRID, DBLK, DBLK).transpose(0, 2, 1, 3)
    w_ffn = ffn_all.reshape(2, GRID, HALF_GRID, DBLK, FBLK).transpose(0, 1, 3, 2, 4)
    w_down = down_all.reshape(HALF_GRID, GRID, FBLK, DBLK).transpose(1, 3, 0, 2)
    w_ffn = w_ffn.reshape(2, D, HALF_FF)
    return (
        w_qkv.reshape(D, 3 * HALF_D),
        w_out.reshape(HALF_D, D),
        w_ffn[0],
        w_ffn[1],
        w_down.reshape(D, HALF_FF),
    )


def take_rows(owner, ref):
    return ref[block_rows(owner), :]


def take_out(owner, ref):
    return ref[block_rows(owner // 2), pl.ds(pl.multiple_of(owner % 2 * HALF_D, 128), HALF_D)]


def take_down(owner, ref):
    lanes = pl.ds(pl.multiple_of(owner // 2 * FBLK, 128), FBLK)
    return jnp.concatenate(
        [ref[block_rows(owner % 2 * HALF_GRID + block), lanes] for block in range(HALF_GRID)], 1
    )


def paired(values):
    high = values.astype(BF16)
    low = (values - high.astype(F32)).astype(BF16)
    rest = jnp.zeros((DBLK - 2 * values.shape[0], values.shape[1]), BF16)
    return jnp.concatenate([high, low, rest], 0)


def unpaired(pair):
    rows = STATE_ROWS
    return pair[:rows].astype(F32) + pair[rows : 2 * rows].astype(F32)


def reduction(takes, columns, count, me, grads):
    high = count // 4
    half = high // 2
    many = len(grads)

    def step(kernel, inputs, shapes, name):
        return whole_call(kernel, [me] + grads + inputs, shapes, name, 1)

    def find(refs, slow, y, x, part):
        owner = slow * 4 + y * 2 + x
        found = [take(owner, ref) for take, ref in zip(takes, refs)]
        found = found[0] if len(found) == 1 else jnp.concatenate(found, 1)
        return found[:, part[0] : part[1]].astype(F32)

    def place(me_ref):
        return me_ref[0] % 2, me_ref[0] // 2 % 2, me_ref[0] // 4

    def piece(index):
        return slice(index * columns, (index + 1) * columns)

    def diagonal_kernel(me_ref, *refs):
        x, y, _ = place(me_ref)
        to_y_ref, to_x_ref = refs[many:]
        for slow in range(high):
            block = find(refs, slow, 1 - y, 1 - x, (0, columns)).astype(BF16)
            if slow < half:
                to_y_ref[:, piece(slow)] = block
            else:
                to_x_ref[:, piece(slow - half)] = block

    def side_kernel(part, me_ref, *refs):
        x, y, _ = place(me_ref)
        by_y_ref, by_x_ref, *state_refs, to_x_ref, to_y_ref = refs[many:]
        width = part[1] - part[0]
        for slow in range(high):
            to_x = find(refs, slow, y, 1 - x, part)
            to_y = find(refs, slow, 1 - y, x, part)
            start = slow % half * columns + part[0]
            if slow < half:
                to_x = to_x + by_y_ref[:, start : start + width].astype(F32)
            else:
                to_y = to_y + by_x_ref[:, start : start + width].astype(F32)
            to_x_ref[:, slow * width : (slow + 1) * width] = to_x.astype(BF16)
            to_y_ref[:, slow * width : (slow + 1) * width] = to_y.astype(BF16)
        if state_refs:
            to_x_ref[:, high * width :] = paired(state_refs[0][...])

    def slow_kernel(part, me_ref, *refs):
        x, y, z = place(me_ref)
        from_x_ref, from_y_ref, *state_refs = refs[many : len(refs) - high]
        out_refs = refs[len(refs) - high :]
        width = part[1] - part[0]
        if state_refs:
            before_ref, after_ref = state_refs
            state = unpaired(paired(before_ref[...])) + unpaired(from_x_ref[:, high * width :])
            after_ref[...] = state
        for shift in range(high):
            rows = pl.ds(0, DBLK)
            slow = (z + shift) % high
            lanes = pl.ds(pl.multiple_of(slow * width, 128), width)
            total = (
                find(refs, slow, y, x, part)
                + from_x_ref[rows, lanes].astype(F32)
                + from_y_ref[rows, lanes].astype(F32)
            )
            out_refs[shift][:, :width] = total.astype(out_refs[shift].dtype)
            if state_refs and shift:
                out_refs[shift][:, width:] = paired(state)

    def rows(width, kind=BF16):
        return jax.ShapeDtypeStruct((DBLK, width), kind)

    state_shape = jax.ShapeDtypeStruct((STATE_ROWS, 128), F32)

    def first():
        return step(diagonal_kernel, [], [rows(half * columns)] * 2, "send_diagonal")

    def second(by_y, by_x, *state, part=(0, columns)):
        width = part[1] - part[0]
        shapes = [rows(high * width + 128 * len(state)), rows(high * width)]
        kernel = functools.partial(side_kernel, part)
        return step(kernel, [by_y, by_x, *state], shapes, "send_sides")

    def third(from_x, from_y, *state, part=(0, columns)):
        width = part[1] - part[0]
        shapes = [state_shape] * len(state) + [rows(width, F32)]
        shapes += [rows(width + 128 * len(state))] * (high - 1)
        kernel = functools.partial(slow_kernel, part)
        return step(kernel, [from_x, from_y, *state], shapes, "send_slow")

    return first, second, third


def send_first(to_y, to_x, count):
    return along(to_y, 2, count), along(to_x, 1, count)


def send_second(to_x, to_y, count):
    return along(to_x, 1, count), along(to_y, 2, count)


def send_third(own, *others, count):
    return [own] + [shifted(block, step + 1, count) for step, block in enumerate(others)]


def scatter_all(qkv, out, ffn_grad, down, count):
    qkv = qkv.reshape(GRID, DBLK, 3, HALF_GRID, DBLK).transpose(2, 0, 3, 1, 4)
    out = out.reshape(HALF_GRID, DBLK, GRID, DBLK).transpose(0, 2, 1, 3)
    ffn_grad = ffn_grad.reshape(GRID, DBLK, 2, HALF_GRID, FBLK).transpose(2, 0, 3, 1, 4)
    down = down.reshape(GRID, DBLK, HALF_GRID, FBLK).transpose(2, 0, 3, 1)
    return (
        lax.psum_scatter(
            qkv.reshape(3, -1, DBLK, DBLK), "dp", scatter_dimension=1, tiled=True
        ),
        lax.psum_scatter(out.reshape(-1, DBLK, DBLK), "dp", scatter_dimension=0, tiled=True),
        lax.psum_scatter(
            ffn_grad.reshape(2, -1, DBLK, FBLK), "dp", scatter_dimension=1, tiled=True
        ),
        lax.psum_scatter(down.reshape(-1, FBLK, DBLK), "dp", scatter_dimension=0, tiled=True),
    )


def gain_rows_kernel(one_ref, two_ref, out_ref):
    def rows(values):
        return [values[:, at : at + 128] for at in range(0, D, 128)]

    parts = rows(one_ref[...]) + rows(0.5 * two_ref[...])
    parts.append(jnp.zeros((STATE_ROWS - len(parts), 128), F32))
    out_ref[...] = jnp.concatenate(parts, 0)


def gain_rows(gain_one, gain_two):
    shape = jax.ShapeDtypeStruct((STATE_ROWS, 128), F32)
    return whole_call(gain_rows_kernel, [gain_one, gain_two], [shape], "gain_rows")[0]


def add_kernel(left_ref, right_ref, out_ref):
    out_ref[...] = left_ref[...] + right_ref[...]


def added(left, right, name):
    return whole_call(add_kernel, [left, right], [jax.ShapeDtypeStruct(left.shape, F32)], name)[0]


def slow_state_kernel(own_ref, *refs):
    out_ref = refs[-1]
    columns = refs[0].shape[1] - 128
    values = [unpaired(paired(own_ref[...]))] + [unpaired(ref[:, columns:]) for ref in refs[:-1]]
    while len(values) > 1:
        half = len(values) // 2
        values = [values[index] + values[index + half] for index in range(half)]
    out_ref[...] = values[0]


def slow_state(own, blocks):
    shape = jax.ShapeDtypeStruct(own.shape, F32)
    return whole_call(slow_state_kernel, [own] + blocks, [shape], "slow_state")[0]


def gains_kernel(near_ref, far_ref, gain_ref, moment_ref, grad_ref, moment_new_ref, gain_new_ref):
    total = near_ref[...] + far_ref[...]
    count = D // 128
    grad = jnp.concatenate(
        [
            jnp.concatenate([total[at + row : at + row + 1] for row in range(count)], 1)
            for at in (0, count)
        ],
        0,
    )
    grad_ref[...] = grad
    moment = DECAY * moment_ref[...] + (1.0 - DECAY) * grad * grad
    moment_new_ref[...] = moment
    gain_new_ref[...] = gain_ref[...] - GAIN_RATE * grad / (jnp.sqrt(moment) + 1e-08)


def full_dot(left, right, left_dim, right_dim):
    return lax.dot_general(
        left,
        right,
        (((left_dim,), (right_dim,)), ((), ())),
        preferred_element_type=F32,
        precision=lax.Precision.HIGH,
    )


def precondition(
    parts, width, left, right, left_root, right_root, masters, turned=False, matrices=None, carry=()
):
    counts = [master.shape[0] for master in masters]
    spots = [(which, here) for which, many in enumerate(counts) for here in range(many)]
    matrices = range(len(spots)) if matrices is None else matrices
    many = len(parts)

    def kernel(*refs):
        part_refs, refs = refs[:many], refs[many:]
        left_ref, right_ref, left_root_ref, right_root_ref = refs[:4]
        master_refs, refs = refs[4 : 4 + len(counts)], refs[4 + len(counts) :]
        carry_refs, refs = refs[: len(carry)], refs[len(carry) :]
        grad_ref, left_new_ref, right_new_ref = refs[:3]
        new_refs = refs[3:]
        for matrix, (which, here) in enumerate(spots):
            if carry and matrix not in matrices:
                for out_ref, carry_ref in zip(refs[:3], carry_refs[:3]):
                    out_ref[matrix] = carry_ref[matrix]
                new_refs[which][here] = carry_refs[3 + which][here]
        first, wide = matrices[0] * HALF_GRID * width, len(matrices) * HALF_GRID * width
        total = part_refs[0][:, :wide]
        for ref in part_refs[1:]:
            total = total + ref[:, :wide].astype(F32)
        for matrix in matrices:
            which, here = spots[matrix]
            for block in range(HALF_GRID):
                at = (matrix * HALF_GRID + block) * width - first
                grad = total[:, at : at + width]
                grad_ref[matrix, block] = grad
                outer, inner = full_dot(grad, grad, 1, 1), full_dot(grad, grad, 0, 0)
                if turned:
                    outer, inner = inner, outer
                    step = full_dot(grad, left_root_ref[matrix, block], 1, 1)
                    step = full_dot(right_root_ref[matrix, block], step, 0, 0)
                else:
                    step = full_dot(left_root_ref[matrix, block], grad, 1, 0)
                    step = full_dot(step, right_root_ref[matrix, block], 1, 0)
                left_new_ref[matrix, block] = (
                    DECAY * left_ref[matrix, block] + (1.0 - DECAY) * outer
                )
                right_new_ref[matrix, block] = (
                    DECAY * right_ref[matrix, block] + (1.0 - DECAY) * inner
                )
                new_refs[which][here, block] = master_refs[which][here, block] - STEP_RATE * step

    grads = jax.ShapeDtypeStruct((sum(counts),) + masters[0].shape[1:], F32)
    like = [jax.ShapeDtypeStruct(array.shape, F32) for array in (left, right)]
    news = [jax.ShapeDtypeStruct(master.shape, F32) for master in masters]
    inputs = list(parts) + [left, right, left_root, right_root] + list(masters)
    return whole_call(kernel, inputs + list(carry), [grads] + like + news, "precondition")


def plain_precondition(block_grad, left_stat, right_stat, left_root, right_root, master):
    new_left = DECAY * left_stat + (1.0 - DECAY) * jnp.einsum(
        "...ij,...kj->...ik", block_grad, block_grad, precision=HIGHEST_PRECISION
    )
    new_right = DECAY * right_stat + (1.0 - DECAY) * jnp.einsum(
        "...ji,...jk->...ik", block_grad, block_grad, precision=HIGHEST_PRECISION
    )
    turned = jnp.einsum("...ij,...jk->...ik", left_root, block_grad, precision=HIGHEST_PRECISION)
    turned = jnp.einsum("...ij,...jk->...ik", turned, right_root, precision=HIGHEST_PRECISION)
    return (new_left, new_right, master - STEP_RATE * turned)


def in_order_kernel(core_ref, mine_ref, other_ref, out_ref):
    rows = mine_ref.shape[0]
    core = core_ref[0]
    out_ref[pl.ds(pl.multiple_of(core * rows, 16), rows), :] = mine_ref[...]
    out_ref[pl.ds(pl.multiple_of((1 - core) * rows, 16), rows), :] = other_ref[...]


def in_order(mine, core):
    shape = jax.ShapeDtypeStruct((2 * mine.shape[0], mine.shape[1]), mine.dtype)
    return whole_call(in_order_kernel, [core, mine, other_core(mine)], [shape], "in_order", 1)[0]


def layer_out_kernel(core_ref, x1_ref, near_ref, far_ref, out_ref):
    total = x1_ref[...] + near_ref[...].astype(F32) + far_ref[...].astype(F32)
    out_ref[...] = total.astype(BF16)


def input_grad_kernel(core_ref, x_ref, dx1_ref, near_ref, far_ref, gain_ref, out_ref):
    x = x_ref[...].astype(F32)
    scale = lax.rsqrt(jnp.mean(x * x, -1, keepdims=True) + EPSILON)
    weighted = (near_ref[...].astype(F32) + far_ref[...].astype(F32)) * gain_ref[0:1, :]
    inner = jnp.mean(weighted * x, -1, keepdims=True)
    out_ref[...] = dx1_ref[...] + scale * weighted - x * (scale * scale * scale * inner)


def own_rows_call(kernel, core, blocked, whole, own_rows, dtype, name):
    steps = own_rows // ROWS
    return pl.pallas_call(
        kernel,
        grid_spec=pltpu.PrefetchScalarGridSpec(
            num_scalar_prefetch=1,
            grid=(steps,),
            in_specs=[pl.BlockSpec((ROWS, D), lambda i, core: (core[0] * steps + i, 0))]
            * len(blocked)
            + [pl.BlockSpec(array.shape, lambda i, core: (0, 0)) for array in whole],
            out_specs=pl.BlockSpec((ROWS, D), lambda i, core: (i, 0)),
        ),
        out_shape=jax.ShapeDtypeStruct((own_rows, D), dtype),
        compiler_params=kernel_params(),
        cost_estimate=cost(),
        name=name,
    )(core, *blocked, *whole)


def rotary_tables(length):
    frequency = jnp.power(10000.0, -2.0 * jnp.arange(HEAD_DIM // 2, dtype=F32) / HEAD_DIM)
    angles = (jnp.arange(length) % LEN).astype(F32)[:, None] * frequency[None, :]
    shape = jax.ShapeDtypeStruct((length, PAIR), F32)
    return whole_call(tables_kernel, [jnp.cos(angles), jnp.sin(angles)], [shape] * 2, "tables")


def body(
    tokens,
    cotangent,
    gains,
    gain_moments,
    qkv_master,
    out_master,
    ffn_master,
    down_master,
    attn_left,
    attn_right,
    attn_left_root,
    attn_right_root,
    ffn_left,
    ffn_right,
    ffn_left_root,
    ffn_right_root,
    down_left,
    down_right,
    down_left_root,
    down_right_root,
):
    count = lax.axis_size("dp")
    me = lax.axis_index("dp").astype(jnp.int32)[None]
    core = lax.axis_index("narrow").astype(jnp.int32)[None]
    own_rows = tokens.shape[0]
    by_hand = count == GRID

    if by_hand:
        high = count // 4
        first, second, slab = pack(
            qkv_master[:, 0], out_master, ffn_master[:, 0], jnp.swapaxes(down_master, 2, 3)
        )
        one, two, last = 4 * HALF_D, FF, HALF_FF
        width, half, ring_start = one + two + last, (one + two + last) // 2, one + two
        many = high - 1
        far_one = all_shifted(first, count)
        slab_x, slab_y = along(slab, 1, count), along(slab, 2, count)

    x, cot = in_order(tokens, core), in_order(cotangent, core)
    cosine, sine_part = rotary_tables(x.shape[0])

    if by_hand:
        chunk = [(number, 0, one) for number in range(many)]
        near_x, near_y = copy_columns(
            [after(far_one[0], x, cot, cosine, sine_part)] + far_one[1:] + [slab_x, slab_y],
            [chunk + [(many + 1, half, width)], chunk + [(many, 0, half)]],
            "end_round_one",
        )
        one_x, one_y = along(near_x, 1, count), along(near_y, 2, count)
        far_two = all_shifted(after(second, *far_one), count)
        tail = many * one
        one_a, one_b, near_two, square = copy_columns(
            [one_x, one_y] + far_two + [slab, slab_x, slab_y],
            [
                [(0, number * one, number * one + one // 2) for number in range(many)],
                [(1, number * one + one // 2, (number + 1) * one) for number in range(many)],
                [(2 + number, 0, two) for number in range(many)],
                [(2 + many + part, ring_start, width) for part in range(3)]
                + [(0, tail + ring_start - half, tail + width - half)],
            ],
            "end_round_two",
        )
        one_a, one_b = along(one_a, 2, count), along(one_b, 1, count)
        entries = [(0, 0, one, 0, 0, 0, 0), (1, 0, one, 0, 0, 1, 0), (2, 0, one, 0, 1, 0, 0)]
        entries.append((5, tail, one, 0, 1, 1, 0))
        for number in range(many):
            step, at = number + 1, number * one
            entries += [(3, at, one, step, 0, 0, 0), (4, at, one, step, 0, 1, 0)]
            entries += [(5, at, one, step, 1, 0, 0)]
        shapes = [(D, 3 * HALF_D), (HALF_D, D)]
        early = [slab, slab_x, slab_y, near_x, one_x, one_y]
        early[0] = after(slab, near_two)
        w_early = assemble(me, high, early, entries, place_qkv_out, shapes, "place_qkv_out")
        entries = []
        for number in range(many):
            step, at = number + 1, number * (one // 2)
            entries += [(0, at, one // 2, step, 1, 1, 0), (1, at, one // 2, step, 1, 1, one // 2)]
        w_qkv, w_out = assemble(
            me, high, [one_a, one_b], entries, place_qkv_out, shapes, "place_rest", w_early
        )
        near_late, square_late = after(near_two, one_a, one_b), after(square, one_a, one_b)
        two_x, two_y = along(near_late, 1, count), along(near_late, 2, count)
        squares = [square] + [
            shifted(square_late, step, count) if step != high // 2 else None
            for step in range(1, high)
        ]
    else:
        qkv, ffn_part = qkv_master[:, 0].astype(BF16), ffn_master[:, 0].astype(BF16)
        w_qkv, w_out, w_gate, w_up, w_down = gather_by_name(
            qkv, out_master.astype(BF16), ffn_part, down_master[0].astype(BF16)
        )
    normed_one, q, k, v = project(x, gains, w_qkv, cosine, sine_part)
    attended, lse = attend(q, k, v)
    attended_late, w_out_late = attended, w_out
    if by_hand:
        squares_here = [piece for piece in squares[1:] if piece is not None]
        two_a, two_b = copy_columns(
            [after(two_x, attended, *squares_here), two_y],
            [
                [(0, number * two, number * two + two // 2) for number in range(many)],
                [(1, number * two + two // 2, (number + 1) * two) for number in range(many)],
            ],
            "end_round_four",
        )
        squares[high // 2] = shifted(after(square, two_a), high // 2, count)
        early = [slab, slab_x, slab_y, one_x, one_y, near_two, two_x, two_y]
        early[0] = after(slab, two_a)
        attended_late, w_out_late = after(attended, two_a), after(w_out, two_a)
        two_a, two_b = along(two_a, 2, count), along(two_b, 1, count)
        cut = half - one
        entries = [(0, one, two, 0, 0, 0, 0), (1, one, two, 0, 0, 1, 0), (2, one, two, 0, 1, 0, 0)]
        entries += [(4, tail + one, cut, 0, 1, 1, 0), (3, tail, two - cut, 0, 1, 1, cut)]
        for number in range(many):
            step, at = number + 1, number * two
            entries += [(5, at, two, step, 0, 0, 0), (6, at, two, step, 0, 1, 0)]
            entries += [(7, at, two, step, 1, 0, 0)]
        shapes = [(D, HALF_FF)] * 2
        w_early = assemble(me, high, early, entries, place_gate_up, shapes, "place_gate_up")
        entries = []
        for number in range(many):
            step, at = number + 1, number * (two // 2)
            entries += [(0, at, two // 2, step, 1, 1, 0), (1, at, two // 2, step, 1, 1, two // 2)]
        w_gate, w_up = assemble(
            me, high, [two_a, two_b], entries, place_gate_up, shapes, "place_rest", w_early
        )
    attended_far, w_out_far = other_core(attended_late), other_core(w_out_late)
    middle, normed_two, gate, up, hidden = ffn(
        x, attended, attended_far, w_out, w_out_far, gains, w_gate, w_up
    )

    if by_hand:
        squares[0] = after(squares[0], hidden)
        (w_down,) = assemble(
            me,
            high,
            squares,
            [
                (step, part * last, last, step, part // 2, part % 2, 0)
                for step in range(high)
                for part in range(4)
            ],
            place_down,
            [(D, HALF_FF)],
            "place_down",
        )
    down_weight_grad = dot_tn(cot, hidden)
    cot_late = cot
    if by_hand:
        down_sum = reduction([take_down], HALF_FF, count, me, [down_weight_grad])
        sent = down_sum[0]()
        down_far = send_first(*sent, count)
        hidden = after(hidden, sent[0])
    out_part = ffn_out(hidden, w_down)
    if by_hand:
        sent = down_sum[1](after(down_far[0], out_part), down_far[1])
        down_far = send_second(*sent, count)
        cot_late = after(cot, sent[0])
    ffn_back_grad, normed_part = ffn_back(cot_late, gate, up, w_down, w_gate, w_up)
    if by_hand:
        down_sent = down_sum[2](after(down_far[0], normed_part), down_far[1])
        ffn_back_grad = after(ffn_back_grad, down_sent[0])
        normed_part = after(normed_part, down_sent[0])
        out_part = after(out_part, down_sent[0])
    normed_far, out_far = other_core(normed_part), other_core(out_part)
    ffn_weight_grad = dot_tn(normed_two, ffn_back_grad)
    if by_hand:
        ffn_sum = reduction([take_rows], FF, count, me, [ffn_weight_grad])
        sent = ffn_sum[0]()
        normed_far = after(normed_far, sent[0])
        ffn_far = send_first(*sent, count)
    middle_grad, branch, attended_grad, gain_two = middle_back(
        cot, middle, normed_part, normed_far, gains, w_out
    )
    out_weight_grad = dot_tn(attended, branch)
    layer_out = own_rows_call(
        layer_out_kernel,
        core,
        [after(middle, branch), out_part, out_far],
        [],
        own_rows,
        BF16,
        "layer_out",
    )
    if by_hand:
        sent = ffn_sum[1](after(ffn_far[0], branch, layer_out, out_weight_grad), ffn_far[1])
        ffn_far = send_second(*sent, count)
        down_parts = send_third(
            down_sent[0], *[after(block, sent[0]) for block in down_sent[1:]], count=count
        )
        attended_grad = after(attended_grad, sent[0])
    dq, dk, dv = attend_back(q, k, v, attended_grad, attended, lse, cosine, sine_part)
    qkv_back_grad = jnp.concatenate([dq, dk, dv], 1)
    if by_hand:
        ffn_sent = ffn_sum[2](after(ffn_far[0], dq, *down_parts[1:]), ffn_far[1])
        ffn_parts = [ffn_sent[0]] + [
            shifted(block, step + 1, count)
            for step, block in enumerate(ffn_sent[1:])
            if step + 1 != high // 2
        ]
        qkv_back_grad = after(qkv_back_grad, ffn_sent[0])
    qkv_weight_grad = dot_tn(normed_one, qkv_back_grad)
    if by_hand:
        late_sum = reduction(
            [take_rows, take_out], 4 * HALF_D, count, me, [qkv_weight_grad, out_weight_grad]
        )
        sent = late_sum[0]()
        late_far = list(send_first(*sent, count))
        dq = after(dq, sent[0])
    input_part, gain_one = input_back(x, dq, dk, dv, w_qkv)
    input_part_late = input_part
    if by_hand:
        state = gain_rows(gain_one, gain_two)
        state = added(state, other_core(state), "add_gains")
        late_cut = 2 * HALF_D
        parts = [(0, late_cut), (late_cut, 2 * late_cut)]
        late_far[0] = after(late_far[0], *ffn_parts[1:])
        sent = late_sum[1](*late_far, state, part=parts[0])
        first_far = send_second(*sent, count)
        ffn_parts.append(shifted(after(ffn_sent[high // 2], sent[0]), high // 2, count))
        input_part_late = after(input_part, sent[0])
        second_sent = late_sum[1](after(late_far[0], sent[0]), late_far[1], part=parts[1])
        down_parts[0] = after(down_parts[0], second_sent[0])
        down_grad, down_left_new, down_right_new, down_new = precondition(
            down_parts,
            FBLK,
            down_left,
            down_right,
            down_left_root,
            down_right_root,
            [jnp.swapaxes(down_master, 2, 3)],
            turned=True,
        )
        down_grad, down_new = jnp.swapaxes(down_grad, 2, 3), jnp.swapaxes(down_new, 2, 3)
    input_far = other_core(input_part_late)
    input_grad = own_rows_call(
        input_grad_kernel,
        core,
        [x, middle_grad, input_part, input_far],
        [gains],
        own_rows,
        F32,
        "input_grad",
    )
    if by_hand:
        first_far = after(first_far[0], input_grad, down_left_new, *ffn_parts[1:]), first_far[1]
        second_far = send_second(after(second_sent[0], *first_far), second_sent[1], count)
        first_state, *sent = late_sum[2](
            *first_far, state, part=parts[0]
        )
        first_parts = send_third(*sent, count=count)
        ffn_parts[0] = after(ffn_parts[0], sent[0])
        ffn_grad, ffn_left_new, ffn_right_new, ffn_new = precondition(
            ffn_parts,
            FBLK,
            ffn_left[:, 0],
            ffn_right[:, 0],
            ffn_left_root[:, 0],
            ffn_right_root[:, 0],
            [ffn_master[:, 0]],
        )
        sent = late_sum[2](after(second_far[0], ffn_left_new), second_far[1], part=parts[1])
        second_parts = send_third(*sent, count=count)
        first_state = slow_state(after(first_state, sent[0]), first_parts[1:])
        first_parts[0] = after(first_parts[0], first_state)
        gain_grad, gain_moment_new, gain_new = whole_call(
            gains_kernel,
            [first_state, along(first_state, 2, count), gains, gain_moments],
            [jax.ShapeDtypeStruct(gains.shape, F32)] * 3,
            "gains",
        )
        attn_results = ()
        for matrices, some in ((range(2), first_parts), (range(2, 4), second_parts)):
            attn_results = precondition(
                some,
                DBLK,
                attn_left[:, 0],
                attn_right[:, 0],
                attn_left_root[:, 0],
                attn_right_root[:, 0],
                [qkv_master[:, 0], out_master],
                matrices=matrices,
                carry=attn_results,
            )
            second_parts[0] = after(second_parts[0], gain_grad, attn_results[0])
        *stacked, out_new = attn_results
        attn_grad, attn_left_new, attn_right_new, qkv_new = (array[:, None] for array in stacked)
        ffn_grad, ffn_left_new, ffn_right_new, ffn_new = (
            array[:, None] for array in (ffn_grad, ffn_left_new, ffn_right_new, ffn_new)
        )
    else:
        gain_terms = jnp.concatenate([gain_one, 0.5 * gain_two])
        gain_grad = lax.psum(gain_terms, ("dp", "narrow"))
        gain_moment_new = DECAY * gain_moments + (1.0 - DECAY) * gain_grad * gain_grad
        gain_new = gains - GAIN_RATE * gain_grad / (jnp.sqrt(gain_moment_new) + 1e-08)
        qkv_owned, out_owned, ffn_owned, down_owned = scatter_all(
            qkv_weight_grad, out_weight_grad, ffn_weight_grad, down_weight_grad, count
        )
        attn_grad = jnp.concatenate([qkv_owned, out_owned[None]], 0)[:, None]
        ffn_grad = ffn_owned[:, None]
        down_grad = down_owned[None]
        attn_left_new, attn_right_new, attn_new = plain_precondition(
            attn_grad,
            attn_left,
            attn_right,
            attn_left_root,
            attn_right_root,
            jnp.concatenate([qkv_master, out_master[None]], 0),
        )
        qkv_new, out_new = attn_new[:3], attn_new[3]
        ffn_left_new, ffn_right_new, ffn_new = plain_precondition(
            ffn_grad, ffn_left, ffn_right, ffn_left_root, ffn_right_root, ffn_master
        )
        down_left_new, down_right_new, down_new = plain_precondition(
            down_grad, down_left, down_right, down_left_root, down_right_root, down_master
        )
    return (
        layer_out,
        input_grad,
        gain_grad,
        gain_moment_new,
        gain_new,
        attn_grad,
        attn_left_new,
        attn_right_new,
        qkv_new,
        out_new,
        ffn_grad,
        ffn_left_new,
        ffn_right_new,
        ffn_new,
        down_grad,
        down_left_new,
        down_right_new,
        down_new,
    )


def solution(mesh):
    tokens = P(("dp", "narrow"), None)
    stacked = P(None, "narrow", "dp", None, None)
    single = P("narrow", "dp", None, None)
    return jax.shard_map(
        body,
        mesh=mesh,
        in_specs=(tokens, tokens, P(), P(), stacked, single, stacked, single)
        + (stacked,) * 8
        + (single,) * 4,
        out_specs=(tokens, tokens, P(), P(), P())
        + (stacked,) * 4
        + (single,)
        + (stacked,) * 4
        + (single,) * 4,
        check_vma=False,
    )
```

```python
import functools
import math

import jax
import jax.numpy as jnp
from jax import lax
from jax.experimental import pallas as pl
from jax.experimental.pallas import tpu as pltpu
from jax.sharding import PartitionSpec as P

D = 768
HEAD_DIM = 64
FF = 2048
LEN = 1024
GRID = 16
DBLK = D // GRID
FBLK = FF // GRID
HALF_GRID = GRID // 2
HALF_D = D // 2
HALF_FF = FF // 2
PAIR = 2 * HEAD_DIM
ROWS = 256

EPSILON = 1e-05
DECAY = 0.5
STEP_RATE = 0.25
GAIN_RATE = 0.1
NEG_FILL = -1e30
HIGHEST_PRECISION = lax.Precision.HIGHEST
BF16 = jnp.bfloat16
F32 = jnp.float32
VMEM_MIB = 18
DENSE_ROWS = 512
SMALL_MIB = 8
PACK_MIB = 60
STATE_ROWS = 16


def dot_nn(left, right):
    return lax.dot_general(left, right, (((1,), (0,)), ((), ())), preferred_element_type=F32)


def dot_nt(left, right):
    return lax.dot_general(left, right, (((1,), (1,)), ((), ())), preferred_element_type=F32)


def dot_tn(left, right):
    return lax.dot_general(left, right, (((0,), (0,)), ((), ())), preferred_element_type=F32)


def kernel_params(mib=VMEM_MIB):
    return pltpu.CompilerParams(vmem_limit_bytes=mib * 1024 * 1024)


def cost():
    return pl.CostEstimate(flops=0, bytes_accessed=0, transcendentals=0)


def whole_call(kernel, inputs, shapes, name, scalars=0, mib=SMALL_MIB, scratch=()):
    vmem = pl.BlockSpec(memory_space=pltpu.VMEM)
    smem = pl.BlockSpec(memory_space=pltpu.SMEM)
    return pl.pallas_call(
        kernel,
        in_specs=[smem] * scalars + [vmem] * (len(inputs) - scalars),
        out_specs=[vmem] * len(shapes),
        out_shape=shapes,
        scratch_shapes=list(scratch),
        compiler_params=kernel_params(mib),
        cost_estimate=cost(),
        name=name,
    )(*inputs)


def over_rows(length, rows, work):
    @pl.loop(0, length // rows)
    def _(step):
        work(pl.ds(pl.multiple_of(step * rows, rows), rows))


def lower_lanes(shape):
    return lax.broadcasted_iota(jnp.int32, shape, 1) % HEAD_DIM < HEAD_DIM // 2


def turn(features, cosine, sine_part, lower):
    half = HEAD_DIM // 2
    partner = jnp.where(
        lower, pltpu.roll(features, PAIR - half, 1), pltpu.roll(features, half, 1)
    )
    return features * cosine + partner * sine_part


def project_kernel(x_ref, gain_ref, w_ref, cos_ref, sin_ref, n1_ref, q_ref, k_ref, v_ref):
    lower = lower_lanes((DENSE_ROWS, PAIR))

    def work(rows):
        x = x_ref[rows, :].astype(F32)
        scale = lax.rsqrt(jnp.mean(x * x, -1, keepdims=True) + EPSILON)
        normed = (x * scale * gain_ref[0:1, :]).astype(BF16)
        n1_ref[rows, :] = normed
        cosine, sine_part = cos_ref[rows, :], sin_ref[rows, :]
        both = dot_nn(normed, w_ref[...])
        for tile in range(HALF_D // PAIR):
            lanes = slice(tile * PAIR, (tile + 1) * PAIR)
            query = both[:, tile * PAIR : (tile + 1) * PAIR]
            key = both[:, HALF_D + tile * PAIR : HALF_D + (tile + 1) * PAIR]
            turned = turn(query, cosine, sine_part, lower).astype(BF16)
            q_ref[rows, lanes] = turned * BF16(1.0 / math.sqrt(HEAD_DIM))
            k_ref[rows, lanes] = turn(key, cosine, sine_part, lower).astype(BF16)
        v_ref[rows, :] = both[:, 2 * HALF_D :].astype(BF16)

    over_rows(x_ref.shape[0], DENSE_ROWS, work)


def project(x, gains, weight, cosine, sine_part):
    length = x.shape[0]
    half = jax.ShapeDtypeStruct((length, HALF_D), BF16)
    shapes = [jax.ShapeDtypeStruct((length, D), BF16), half, half, half]
    return whole_call(
        project_kernel, [x, gains, weight, cosine, sine_part], shapes, "project", mib=VMEM_MIB
    )


def attend_kernel(q_ref, k_ref, v_ref, o_ref, lse_ref):
    @pl.loop(0, q_ref.shape[1] // PAIR)
    def _(pair):
        lanes = pl.ds(pl.multiple_of(pair * PAIR, PAIR), PAIR)
        rows = pl.ds(pl.multiple_of(pair * 8, 8), 8)
        attend_pair(
            *(ref.at[:, lanes] for ref in (q_ref, k_ref, v_ref, o_ref)), lse_ref.at[rows, :]
        )


def attend_pair(q_ref, k_ref, v_ref, o_ref, lse_ref):
    length = q_ref.shape[0]
    first_head = lax.broadcasted_iota(jnp.int32, (ROWS, PAIR), 1) < HEAD_DIM
    keys = k_ref[...]
    values = jnp.concatenate([v_ref[...], jnp.ones((length, PAIR), BF16)], 1)
    causal = lax.broadcasted_iota(jnp.int32, (ROWS, ROWS), 0) >= lax.broadcasted_iota(
        jnp.int32, (ROWS, ROWS), 1
    )
    for block in range(length // ROWS):
        rows = slice(block * ROWS, (block + 1) * ROWS)
        width = (block + 1) * ROWS
        query_block = q_ref[rows, :]
        parts, sums = [], []
        for head in range(2):
            mine = first_head if head == 0 else jnp.logical_not(first_head)
            query = jnp.where(mine, query_block, jnp.zeros_like(query_block))
            scores = jnp.where(causal, dot_nt(query, keys[block * ROWS : width]), NEG_FILL)
            if block:
                scores = jnp.concatenate([dot_nt(query, keys[: block * ROWS]), scores], 1)
            top = jnp.max(scores, 1, keepdims=True)
            exponent = jnp.exp(scores - top).astype(BF16)
            product = dot_nn(exponent, values[:width])
            total = product[:, PAIR:]
            parts.append(product[:, :PAIR] / total)
            sums.append(top + jnp.log(total))
        o_ref[rows, :] = jnp.where(first_head, parts[0], parts[1]).astype(BF16)
        lane = lax.broadcasted_iota(jnp.int32, (ROWS, PAIR), 1)
        lse_ref[:, rows] = jnp.transpose(jnp.where(lane == 0, sums[0], sums[1]))[:8, :]


def attend(q, k, v):
    length = q.shape[0]
    shapes = [
        jax.ShapeDtypeStruct(q.shape, BF16),
        jax.ShapeDtypeStruct((8 * (q.shape[1] // PAIR), length), F32),
    ]
    return whole_call(attend_kernel, [q, k, v], shapes, "attend", mib=VMEM_MIB)


def attend_back_kernel(
    q_ref, k_ref, v_ref, do_ref, o_ref, lse_ref, cos_ref, sin_ref, dq_ref, dk_ref, dv_ref, dqt_ref
):
    @pl.loop(0, q_ref.shape[1] // PAIR)
    def _(pair):
        lanes = pl.ds(pl.multiple_of(pair * PAIR, PAIR), PAIR)
        rows = pl.ds(pl.multiple_of(pair * 8, 8), 8)
        attend_back_pair(
            *(ref.at[:, lanes] for ref in (q_ref, k_ref, v_ref, do_ref, o_ref)),
            lse_ref.at[rows, :],
            cos_ref,
            sin_ref,
            *(ref.at[:, lanes] for ref in (dq_ref, dk_ref, dv_ref)),
            dqt_ref,
        )


def attend_back_pair(
    q_ref, k_ref, v_ref, do_ref, o_ref, lse_ref, cos_ref, sin_ref, dq_ref, dk_ref, dv_ref, dqt_ref
):
    length = q_ref.shape[0]
    first_head = lax.broadcasted_iota(jnp.int32, (length, PAIR), 1) < HEAD_DIM
    zero = BF16(0)
    queries = [
        jnp.where(first_head, q_ref[...], zero),
        jnp.where(first_head, zero, q_ref[...]),
    ]
    grads = [
        jnp.where(first_head, do_ref[...], zero),
        jnp.where(first_head, zero, do_ref[...]),
    ]
    product = do_ref[...].astype(F32) * o_ref[...].astype(F32)
    head_row = lax.broadcasted_iota(jnp.int32, (8, PAIR), 0)
    head_lane = lax.broadcasted_iota(jnp.int32, (8, PAIR), 1) // HEAD_DIM
    inner = lax.dot_general(
        (head_row == head_lane).astype(F32),
        product,
        (((1,), (1,)), ((), ())),
        preferred_element_type=F32,
        precision=HIGHEST_PRECISION,
    )
    turned_keys = jnp.transpose(k_ref[...].astype(F32)).astype(BF16)
    first_rows = lax.broadcasted_iota(jnp.int32, turned_keys.shape, 0) < HEAD_DIM
    key_heads = [
        jnp.where(first_rows, turned_keys, zero),
        jnp.where(first_rows, zero, turned_keys),
    ]
    causal = lax.broadcasted_iota(jnp.int32, (ROWS, ROWS), 0) <= lax.broadcasted_iota(
        jnp.int32, (ROWS, ROWS), 1
    )
    dqt_ref[...] = jnp.zeros_like(dqt_ref)
    lower = lower_lanes((ROWS, PAIR))
    for block in range(length // ROWS):
        rows = slice(block * ROWS, (block + 1) * ROWS)
        start = block * ROWS
        key_block, value_block = k_ref[rows, :], v_ref[rows, :]
        dk = jnp.zeros((ROWS, PAIR), F32)
        dv = jnp.zeros((ROWS, PAIR), F32)
        for head in range(2):
            scores = dot_nt(key_block, queries[head][start:])
            probs = jnp.exp(scores - lse_ref[head : head + 1, start:])
            diagonal = jnp.where(causal, probs[:, :ROWS], 0.0)
            if start + ROWS == length:
                probs = diagonal
            else:
                probs = jnp.concatenate([diagonal, probs[:, ROWS:]], 1)
            prob_grad = dot_nt(value_block, grads[head][start:])
            score_grad = (probs * (prob_grad - inner[head : head + 1, start:])).astype(BF16)
            dv = dv + dot_nn(probs.astype(BF16), grads[head][start:])
            dk = dk + dot_nn(score_grad, queries[head][start:])
            dqt_ref[:, start:] += dot_nn(key_heads[head][:, rows], score_grad)
        dk_ref[rows, :] = turn(dk, cos_ref[rows, :], -sin_ref[rows, :], lower).astype(BF16)
        dv_ref[rows, :] = dv.astype(BF16)
    for block in range(length // ROWS):
        rows = slice(block * ROWS, (block + 1) * ROWS)
        dq = jnp.transpose(dqt_ref[:, rows]) * (1.0 / math.sqrt(HEAD_DIM))
        dq_ref[rows, :] = turn(dq, cos_ref[rows, :], -sin_ref[rows, :], lower).astype(BF16)


def attend_back(q, k, v, grad, o, lse, cosine, sine_part):
    return whole_call(
        attend_back_kernel,
        [q, k, v, grad, o, lse, cosine, sine_part],
        [jax.ShapeDtypeStruct(q.shape, BF16)] * 3,
        "attend_back",
        mib=VMEM_MIB,
        scratch=[pltpu.VMEM((PAIR, q.shape[0]), F32)],
    )


def ffn_kernel(
    x_ref, o_ref, o_far_ref, wo_ref, wo_far_ref, gain_ref, wg_ref, wu_ref,
    x1_ref, n2_ref, gate_ref, up_ref, hidden_ref,
):
    def work(rows):
        middle = (
            x_ref[rows, :].astype(F32)
            + dot_nn(o_ref[rows, :], wo_ref[...])
            + dot_nn(o_far_ref[rows, :], wo_far_ref[...])
        )
        x1_ref[rows, :] = middle
        scale = lax.rsqrt(jnp.mean(middle * middle, -1, keepdims=True) + EPSILON)
        normed = (middle * scale * gain_ref[1:2, :]).astype(BF16)
        n2_ref[rows, :] = normed
        gate = dot_nn(normed, wg_ref[...])
        up = dot_nn(normed, wu_ref[...])
        gate_ref[rows, :] = gate
        up_ref[rows, :] = up
        hidden_ref[rows, :] = (gate * jax.nn.sigmoid(gate) * up).astype(BF16)

    over_rows(x_ref.shape[0], DENSE_ROWS, work)


def ffn(*inputs):
    length = inputs[0].shape[0]
    shapes = [
        jax.ShapeDtypeStruct((length, width), kind)
        for width, kind in ((D, F32), (D, BF16), (HALF_FF, F32), (HALF_FF, F32), (HALF_FF, BF16))
    ]
    return whole_call(ffn_kernel, inputs, shapes, "ffn", mib=VMEM_MIB)


def ffn_out_kernel(hidden_ref, wdt_ref, part_ref):
    part_ref[...] = dot_nt(hidden_ref[...], wdt_ref[...]).astype(BF16)


def ffn_out(hidden, wdt):
    shape = jax.ShapeDtypeStruct((hidden.shape[0], D), BF16)
    return whole_call(ffn_out_kernel, [hidden, wdt], [shape], "ffn_out", mib=VMEM_MIB)[0]


def ffn_back_kernel(cot_ref, gate_ref, up_ref, wdt_ref, wg_ref, wu_ref, dgu_ref, dn2_ref):
    def work(rows):
        hidden_grad = dot_nn(cot_ref[rows, :], wdt_ref[...])
        gate, up = gate_ref[rows, :], up_ref[rows, :]
        sigma = jax.nn.sigmoid(gate)
        gate_grad = (hidden_grad * up * sigma * (1.0 + gate * (1.0 - sigma))).astype(BF16)
        up_grad = (hidden_grad * gate * sigma).astype(BF16)
        dgu_ref[rows, :HALF_FF] = gate_grad
        dgu_ref[rows, HALF_FF:] = up_grad
        dn2 = dot_nt(gate_grad, wg_ref[...]) + dot_nt(up_grad, wu_ref[...])
        dn2_ref[rows, :] = dn2.astype(BF16)

    over_rows(cot_ref.shape[0], DENSE_ROWS, work)


def ffn_back(cot, gate, up, wdt, wg, wu):
    shapes = [jax.ShapeDtypeStruct((cot.shape[0], width), BF16) for width in (FF, D)]
    return whole_call(
        ffn_back_kernel, [cot, gate, up, wdt, wg, wu], shapes, "ffn_back", mib=VMEM_MIB
    )


def middle_back_kernel(
    cot_ref, x1_ref, near_ref, far_ref, gain_ref, wo_ref, dx1_ref, da_ref, do_ref, g2_ref
):
    g2_ref[...] = jnp.zeros_like(g2_ref)

    def work(rows):
        middle = x1_ref[rows, :]
        scale = lax.rsqrt(jnp.mean(middle * middle, -1, keepdims=True) + EPSILON)
        grad = near_ref[rows, :].astype(F32) + far_ref[rows, :].astype(F32)
        weighted = grad * gain_ref[1:2, :]
        inner = jnp.mean(weighted * middle, -1, keepdims=True)
        middle_grad = (
            cot_ref[rows, :].astype(F32)
            + scale * weighted
            - middle * (scale * scale * scale * inner)
        )
        dx1_ref[rows, :] = middle_grad
        branch = middle_grad.astype(BF16)
        da_ref[rows, :] = branch
        do_ref[rows, :] = dot_nt(branch, wo_ref[...]).astype(BF16)
        g2_ref[...] += jnp.sum(grad * middle * scale, 0, keepdims=True)

    over_rows(cot_ref.shape[0], DENSE_ROWS, work)


def middle_back(*inputs):
    length = inputs[0].shape[0]
    shapes = [
        jax.ShapeDtypeStruct(shape, kind)
        for shape, kind in (
            ((length, D), F32),
            ((length, D), BF16),
            ((length, HALF_D), BF16),
            ((1, D), F32),
        )
    ]
    return whole_call(middle_back_kernel, inputs, shapes, "middle_back", mib=VMEM_MIB)


def input_back_kernel(x_ref, dq_ref, dk_ref, dv_ref, w_ref, part_ref, g1_ref):
    g1_ref[...] = jnp.zeros_like(g1_ref)

    def work(rows):
        grad = (
            dot_nt(dq_ref[rows, :], w_ref[:, :HALF_D])
            + dot_nt(dk_ref[rows, :], w_ref[:, HALF_D : 2 * HALF_D])
            + dot_nt(dv_ref[rows, :], w_ref[:, 2 * HALF_D :])
        )
        part_ref[rows, :] = grad.astype(BF16)
        x = x_ref[rows, :].astype(F32)
        scale = lax.rsqrt(jnp.mean(x * x, -1, keepdims=True) + EPSILON)
        g1_ref[...] += jnp.sum(grad * x * scale, 0, keepdims=True)

    over_rows(x_ref.shape[0], DENSE_ROWS, work)


def input_back(x, dq, dk, dv, w):
    shapes = [jax.ShapeDtypeStruct(x.shape, BF16), jax.ShapeDtypeStruct((1, D), F32)]
    return whole_call(input_back_kernel, [x, dq, dk, dv, w], shapes, "input_back", mib=VMEM_MIB)


def pair_up(bit, count):
    return [(i, i ^ bit) for i in range(count)]


def after(value, *others):
    return lax.optimization_barrier((value,) + others)[0]


def along(values, bit, count):
    return lax.ppermute(values, "dp", pair_up(bit, count))


def shifted(values, steps, count):
    return lax.ppermute(values, "dp", [(i, (i + 4 * steps) % count) for i in range(count)])


def other_core(values):
    return lax.ppermute(values, "narrow", [(0, 1), (1, 0)])


def all_shifted(values, count):
    return [shifted(values, step, count) for step in range(1, count // 4)]


def copy_columns(sources, outputs, name):
    rows = sources[0].shape[0]
    shapes = [
        jax.ShapeDtypeStruct((rows, sum(stop - start for _, start, stop in parts)), BF16)
        for parts in outputs
    ]

    def kernel(*refs):
        for out_ref, parts in zip(refs[len(sources) :], outputs):
            at = 0
            for number, start, stop in parts:
                out_ref[:, at : at + stop - start] = refs[number][:, start:stop]
                at += stop - start

    return whole_call(kernel, sources, shapes, name)


def block_rows(owner):
    return pl.ds(pl.multiple_of(owner * DBLK, 16), DBLK)


def block_lanes(index, width):
    return pl.ds(pl.multiple_of(index * width, 128), width)


def place_qkv_out(owner, start, piece, qkv_ref, out_ref):
    cut, stop = 3 * HALF_D, start + piece.shape[1]
    if start < cut:
        end = min(stop, cut)
        qkv_ref[block_rows(owner), start:end] = piece[:, : end - start]
    if stop > cut:
        begin = max(start, cut)
        lanes = pl.ds(pl.multiple_of(owner % 2 * HALF_D + (begin - cut), 128), stop - begin)
        out_ref[block_rows(owner // 2), lanes] = piece[:, begin - start :]


def place_gate_up(owner, start, piece, gate_ref, up_ref):
    stop = start + piece.shape[1]
    if start < HALF_FF:
        end = min(stop, HALF_FF)
        gate_ref[block_rows(owner), start:end] = piece[:, : end - start]
    if stop > HALF_FF:
        begin = max(start, HALF_FF)
        up_ref[block_rows(owner), begin - HALF_FF : stop - HALF_FF] = piece[:, begin - start :]


def place_down(owner, start, piece, out_ref):
    lanes = block_lanes(owner // 2, FBLK)
    for block in range(piece.shape[1] // FBLK):
        rows = block_rows(owner % 2 * HALF_GRID + start // FBLK + block)
        out_ref[rows, lanes] = piece[:, block * FBLK : (block + 1) * FBLK]


def assemble(me, high, sources, entries, place, shapes, name, begun=()):
    sources = list(sources)

    def kernel(me_ref, *refs):
        x, y, z = me_ref[0] % 2, me_ref[0] // 2 % 2, me_ref[0] // 4
        out_refs = refs[len(sources) + len(begun) :]
        for ref, out_ref in zip(refs[len(sources) :], out_refs if begun else ()):
            out_ref[...] = ref[...]
        for number, start, width, step, over_y, over_x, first in entries:
            slow = (z - step + high) % high
            from_y = 1 - y if over_y else y
            from_x = 1 - x if over_x else x
            piece = refs[number][:, start : start + width]
            place(slow * 4 + from_y * 2 + from_x, first, piece, *out_refs)

    return whole_call(
        kernel,
        [me] + sources + list(begun),
        [jax.ShapeDtypeStruct(shape, BF16) for shape in shapes],
        name,
        1,
    )


def pack_kernel(qkv_ref, out_ref, ffn_ref, down_ref, first_ref, second_ref, slab_ref, *scratch):
    held, sems = scratch[:-1], scratch[-1]
    copies = [
        pltpu.make_async_copy(ref, here, sems.at[number])
        for number, (ref, here) in enumerate(zip((qkv_ref, out_ref, ffn_ref, down_ref), held))
    ]
    for copy in copies:
        copy.start()

    def row(ref, matrix):
        return jnp.concatenate([ref[matrix, block].astype(BF16) for block in range(HALF_GRID)], 1)

    at = 0
    for copy, ref in zip(copies, held):
        copy.wait()
        for matrix in range(ref.shape[0]):
            part = row(ref, matrix)
            stop = at + part.shape[1]
            slab_ref[:, at:stop] = part
            if stop <= first_ref.shape[1]:
                first_ref[:, at:stop] = part
            elif stop <= first_ref.shape[1] + second_ref.shape[1]:
                second_ref[:, at - first_ref.shape[1] : stop - first_ref.shape[1]] = part
            at = stop


def pack(*masters):
    vmem = pl.BlockSpec(memory_space=pltpu.VMEM)
    return pl.pallas_call(
        pack_kernel,
        in_specs=[pl.BlockSpec(memory_space=pl.ANY)] * len(masters),
        out_specs=[vmem] * 3,
        out_shape=[
            jax.ShapeDtypeStruct((DBLK, width), BF16)
            for width in (4 * HALF_D, FF, 4 * HALF_D + 3 * HALF_FF)
        ],
        scratch_shapes=[pltpu.VMEM(master.shape, F32) for master in masters]
        + [pltpu.SemaphoreType.DMA((len(masters),))],
        compiler_params=kernel_params(PACK_MIB),
        cost_estimate=cost(),
        name="pack",
    )(*masters)


def tables_kernel(cos_ref, sin_ref, cosine_ref, sine_ref):
    cosine, sine = cos_ref[...], sin_ref[...]
    cosine_ref[...] = jnp.concatenate([cosine] * 4, 1)
    sine_ref[...] = jnp.concatenate([-sine, sine] * 2, 1)


def side_by_side(blocks):
    matrices, many, height, width = blocks.shape
    return blocks.transpose(2, 0, 1, 3).reshape(height, matrices * many * width)


def gather_by_name(qkv, out, ffn_part, down):
    qkv_all = lax.all_gather(qkv, "dp", axis=1, tiled=True)
    out_all = lax.all_gather(out[0], "dp", axis=0, tiled=True)
    ffn_all = lax.all_gather(ffn_part, "dp", axis=1, tiled=True)
    down_all = lax.all_gather(down, "dp", axis=0, tiled=True)
    w_qkv = qkv_all.reshape(3, GRID, HALF_GRID, DBLK, DBLK).transpose(1, 3, 0, 2, 4)
    w_out = out_all.reshape(HALF_GRID, GRID, DBLK, DBLK).transpose(0, 2, 1, 3)
    w_ffn = ffn_all.reshape(2, GRID, HALF_GRID, DBLK, FBLK).transpose(0, 1, 3, 2, 4)
    w_down = down_all.reshape(HALF_GRID, GRID, FBLK, DBLK).transpose(1, 3, 0, 2)
    w_ffn = w_ffn.reshape(2, D, HALF_FF)
    return (
        w_qkv.reshape(D, 3 * HALF_D),
        w_out.reshape(HALF_D, D),
        w_ffn[0],
        w_ffn[1],
        w_down.reshape(D, HALF_FF),
    )


def take_rows(owner, ref):
    return ref[block_rows(owner), :]


def take_out(owner, ref):
    return ref[block_rows(owner // 2), pl.ds(pl.multiple_of(owner % 2 * HALF_D, 128), HALF_D)]


def take_down(owner, ref):
    lanes = pl.ds(pl.multiple_of(owner // 2 * FBLK, 128), FBLK)
    return jnp.concatenate(
        [ref[block_rows(owner % 2 * HALF_GRID + block), lanes] for block in range(HALF_GRID)], 1
    )


def paired(values):
    high = values.astype(BF16)
    low = (values - high.astype(F32)).astype(BF16)
    rest = jnp.zeros((DBLK - 2 * values.shape[0], values.shape[1]), BF16)
    return jnp.concatenate([high, low, rest], 0)


def unpaired(pair):
    rows = STATE_ROWS
    return pair[:rows].astype(F32) + pair[rows : 2 * rows].astype(F32)


def reduction(takes, columns, count, me, grads):
    high = count // 4
    half = high // 2
    many = len(grads)

    def step(kernel, inputs, shapes, name):
        return whole_call(kernel, [me] + grads + inputs, shapes, name, 1)

    def find(refs, slow, y, x, part):
        owner = slow * 4 + y * 2 + x
        found = [take(owner, ref) for take, ref in zip(takes, refs)]
        found = found[0] if len(found) == 1 else jnp.concatenate(found, 1)
        return found[:, part[0] : part[1]].astype(F32)

    def place(me_ref):
        return me_ref[0] % 2, me_ref[0] // 2 % 2, me_ref[0] // 4

    def piece(index):
        return slice(index * columns, (index + 1) * columns)

    def diagonal_kernel(me_ref, *refs):
        x, y, _ = place(me_ref)
        to_y_ref, to_x_ref = refs[many:]
        for slow in range(high):
            block = find(refs, slow, 1 - y, 1 - x, (0, columns)).astype(BF16)
            if slow < half:
                to_y_ref[:, piece(slow)] = block
            else:
                to_x_ref[:, piece(slow - half)] = block

    def side_kernel(part, me_ref, *refs):
        x, y, _ = place(me_ref)
        by_y_ref, by_x_ref, *state_refs, to_x_ref, to_y_ref = refs[many:]
        width = part[1] - part[0]
        for slow in range(high):
            to_x = find(refs, slow, y, 1 - x, part)
            to_y = find(refs, slow, 1 - y, x, part)
            start = slow % half * columns + part[0]
            if slow < half:
                to_x = to_x + by_y_ref[:, start : start + width].astype(F32)
            else:
                to_y = to_y + by_x_ref[:, start : start + width].astype(F32)
            to_x_ref[:, slow * width : (slow + 1) * width] = to_x.astype(BF16)
            to_y_ref[:, slow * width : (slow + 1) * width] = to_y.astype(BF16)
        if state_refs:
            to_x_ref[:, high * width :] = paired(state_refs[0][...])

    def slow_kernel(part, me_ref, *refs):
        x, y, z = place(me_ref)
        from_x_ref, from_y_ref, *state_refs = refs[many : len(refs) - high]
        out_refs = refs[len(refs) - high :]
        width = part[1] - part[0]
        if state_refs:
            before_ref, after_ref = state_refs
            state = unpaired(paired(before_ref[...])) + unpaired(from_x_ref[:, high * width :])
            after_ref[...] = state
        for shift in range(high):
            rows = pl.ds(0, DBLK)
            slow = (z + shift) % high
            lanes = pl.ds(pl.multiple_of(slow * width, 128), width)
            total = (
                find(refs, slow, y, x, part)
                + from_x_ref[rows, lanes].astype(F32)
                + from_y_ref[rows, lanes].astype(F32)
            )
            out_refs[shift][:, :width] = total.astype(out_refs[shift].dtype)
            if state_refs and shift:
                out_refs[shift][:, width:] = paired(state)

    def rows(width, kind=BF16):
        return jax.ShapeDtypeStruct((DBLK, width), kind)

    state_shape = jax.ShapeDtypeStruct((STATE_ROWS, 128), F32)

    def first():
        return step(diagonal_kernel, [], [rows(half * columns)] * 2, "send_diagonal")

    def second(by_y, by_x, *state, part=(0, columns)):
        width = part[1] - part[0]
        shapes = [rows(high * width + 128 * len(state)), rows(high * width)]
        kernel = functools.partial(side_kernel, part)
        return step(kernel, [by_y, by_x, *state], shapes, "send_sides")

    def third(from_x, from_y, *state, part=(0, columns)):
        width = part[1] - part[0]
        shapes = [state_shape] * len(state) + [rows(width, F32)]
        shapes += [rows(width + 128 * len(state))] * (high - 1)
        kernel = functools.partial(slow_kernel, part)
        return step(kernel, [from_x, from_y, *state], shapes, "send_slow")

    return first, second, third


def send_first(to_y, to_x, count):
    return along(to_y, 2, count), along(to_x, 1, count)


def send_second(to_x, to_y, count):
    return along(to_x, 1, count), along(to_y, 2, count)


def send_third(own, *others, count):
    return [own] + [shifted(block, step + 1, count) for step, block in enumerate(others)]


def scatter_all(qkv, out, ffn_grad, down, count):
    qkv = qkv.reshape(GRID, DBLK, 3, HALF_GRID, DBLK).transpose(2, 0, 3, 1, 4)
    out = out.reshape(HALF_GRID, DBLK, GRID, DBLK).transpose(0, 2, 1, 3)
    ffn_grad = ffn_grad.reshape(GRID, DBLK, 2, HALF_GRID, FBLK).transpose(2, 0, 3, 1, 4)
    down = down.reshape(GRID, DBLK, HALF_GRID, FBLK).transpose(2, 0, 3, 1)
    return (
        lax.psum_scatter(
            qkv.reshape(3, -1, DBLK, DBLK), "dp", scatter_dimension=1, tiled=True
        ),
        lax.psum_scatter(out.reshape(-1, DBLK, DBLK), "dp", scatter_dimension=0, tiled=True),
        lax.psum_scatter(
            ffn_grad.reshape(2, -1, DBLK, FBLK), "dp", scatter_dimension=1, tiled=True
        ),
        lax.psum_scatter(down.reshape(-1, FBLK, DBLK), "dp", scatter_dimension=0, tiled=True),
    )


def gain_rows_kernel(one_ref, two_ref, out_ref):
    def rows(values):
        return [values[:, at : at + 128] for at in range(0, D, 128)]

    parts = rows(one_ref[...]) + rows(0.5 * two_ref[...])
    parts.append(jnp.zeros((STATE_ROWS - len(parts), 128), F32))
    out_ref[...] = jnp.concatenate(parts, 0)


def gain_rows(gain_one, gain_two):
    shape = jax.ShapeDtypeStruct((STATE_ROWS, 128), F32)
    return whole_call(gain_rows_kernel, [gain_one, gain_two], [shape], "gain_rows")[0]


def add_kernel(left_ref, right_ref, out_ref):
    out_ref[...] = left_ref[...] + right_ref[...]


def added(left, right, name):
    return whole_call(add_kernel, [left, right], [jax.ShapeDtypeStruct(left.shape, F32)], name)[0]


def slow_state_kernel(own_ref, *refs):
    out_ref = refs[-1]
    columns = refs[0].shape[1] - 128
    values = [unpaired(paired(own_ref[...]))] + [unpaired(ref[:, columns:]) for ref in refs[:-1]]
    while len(values) > 1:
        half = len(values) // 2
        values = [values[index] + values[index + half] for index in range(half)]
    out_ref[...] = values[0]


def slow_state(own, blocks):
    shape = jax.ShapeDtypeStruct(own.shape, F32)
    return whole_call(slow_state_kernel, [own] + blocks, [shape], "slow_state")[0]


def gains_kernel(near_ref, far_ref, gain_ref, moment_ref, grad_ref, moment_new_ref, gain_new_ref):
    total = near_ref[...] + far_ref[...]
    count = D // 128
    grad = jnp.concatenate(
        [
            jnp.concatenate([total[at + row : at + row + 1] for row in range(count)], 1)
            for at in (0, count)
        ],
        0,
    )
    grad_ref[...] = grad
    moment = DECAY * moment_ref[...] + (1.0 - DECAY) * grad * grad
    moment_new_ref[...] = moment
    gain_new_ref[...] = gain_ref[...] - GAIN_RATE * grad / (jnp.sqrt(moment) + 1e-08)


def full_dot(left, right, left_dim, right_dim):
    return lax.dot_general(
        left,
        right,
        (((left_dim,), (right_dim,)), ((), ())),
        preferred_element_type=F32,
        precision=lax.Precision.HIGH,
    )


def precondition(
    parts, width, left, right, left_root, right_root, masters, turned=False, matrices=None, carry=()
):
    counts = [master.shape[0] for master in masters]
    spots = [(which, here) for which, many in enumerate(counts) for here in range(many)]
    matrices = range(len(spots)) if matrices is None else matrices
    many = len(parts)

    def kernel(*refs):
        part_refs, refs = refs[:many], refs[many:]
        left_ref, right_ref, left_root_ref, right_root_ref = refs[:4]
        master_refs, refs = refs[4 : 4 + len(counts)], refs[4 + len(counts) :]
        carry_refs, refs = refs[: len(carry)], refs[len(carry) :]
        grad_ref, left_new_ref, right_new_ref = refs[:3]
        new_refs = refs[3:]
        for matrix, (which, here) in enumerate(spots):
            if carry and matrix not in matrices:
                for out_ref, carry_ref in zip(refs[:3], carry_refs[:3]):
                    out_ref[matrix] = carry_ref[matrix]
                new_refs[which][here] = carry_refs[3 + which][here]
        first, wide = matrices[0] * HALF_GRID * width, len(matrices) * HALF_GRID * width
        total = part_refs[0][:, :wide]
        for ref in part_refs[1:]:
            total = total + ref[:, :wide].astype(F32)
        for matrix in matrices:
            which, here = spots[matrix]
            for block in range(HALF_GRID):
                at = (matrix * HALF_GRID + block) * width - first
                grad = total[:, at : at + width]
                grad_ref[matrix, block] = grad
                outer, inner = full_dot(grad, grad, 1, 1), full_dot(grad, grad, 0, 0)
                if turned:
                    outer, inner = inner, outer
                    step = full_dot(grad, left_root_ref[matrix, block], 1, 1)
                    step = full_dot(right_root_ref[matrix, block], step, 0, 0)
                else:
                    step = full_dot(left_root_ref[matrix, block], grad, 1, 0)
                    step = full_dot(step, right_root_ref[matrix, block], 1, 0)
                left_new_ref[matrix, block] = (
                    DECAY * left_ref[matrix, block] + (1.0 - DECAY) * outer
                )
                right_new_ref[matrix, block] = (
                    DECAY * right_ref[matrix, block] + (1.0 - DECAY) * inner
                )
                new_refs[which][here, block] = master_refs[which][here, block] - STEP_RATE * step

    grads = jax.ShapeDtypeStruct((sum(counts),) + masters[0].shape[1:], F32)
    like = [jax.ShapeDtypeStruct(array.shape, F32) for array in (left, right)]
    news = [jax.ShapeDtypeStruct(master.shape, F32) for master in masters]
    inputs = list(parts) + [left, right, left_root, right_root] + list(masters)
    return whole_call(kernel, inputs + list(carry), [grads] + like + news, "precondition")


def plain_precondition(block_grad, left_stat, right_stat, left_root, right_root, master):
    new_left = DECAY * left_stat + (1.0 - DECAY) * jnp.einsum(
        "...ij,...kj->...ik", block_grad, block_grad, precision=HIGHEST_PRECISION
    )
    new_right = DECAY * right_stat + (1.0 - DECAY) * jnp.einsum(
        "...ji,...jk->...ik", block_grad, block_grad, precision=HIGHEST_PRECISION
    )
    turned = jnp.einsum("...ij,...jk->...ik", left_root, block_grad, precision=HIGHEST_PRECISION)
    turned = jnp.einsum("...ij,...jk->...ik", turned, right_root, precision=HIGHEST_PRECISION)
    return (new_left, new_right, master - STEP_RATE * turned)


def in_order_kernel(core_ref, mine_ref, other_ref, out_ref):
    rows = mine_ref.shape[0]
    core = core_ref[0]
    out_ref[pl.ds(pl.multiple_of(core * rows, 16), rows), :] = mine_ref[...]
    out_ref[pl.ds(pl.multiple_of((1 - core) * rows, 16), rows), :] = other_ref[...]


def in_order(mine, core):
    shape = jax.ShapeDtypeStruct((2 * mine.shape[0], mine.shape[1]), mine.dtype)
    return whole_call(in_order_kernel, [core, mine, other_core(mine)], [shape], "in_order", 1)[0]


def own_and_all(core_ref, rows, step):
    own = pl.ds(pl.multiple_of(step * ROWS, ROWS), ROWS)
    return own, pl.ds(pl.multiple_of(core_ref[0] * rows + step * ROWS, ROWS), ROWS)


def layer_out_kernel(core_ref, x1_ref, near_ref, far_ref, out_ref):
    @pl.loop(0, out_ref.shape[0] // ROWS)
    def _(step):
        own, rows = own_and_all(core_ref, out_ref.shape[0], step)
        total = x1_ref[rows, :] + near_ref[rows, :].astype(F32) + far_ref[rows, :].astype(F32)
        out_ref[own, :] = total.astype(BF16)


def input_grad_kernel(core_ref, x_ref, dx1_ref, near_ref, far_ref, gain_ref, out_ref):
    @pl.loop(0, out_ref.shape[0] // ROWS)
    def _(step):
        own, rows = own_and_all(core_ref, out_ref.shape[0], step)
        x = x_ref[rows, :].astype(F32)
        scale = lax.rsqrt(jnp.mean(x * x, -1, keepdims=True) + EPSILON)
        grad = near_ref[rows, :].astype(F32) + far_ref[rows, :].astype(F32)
        weighted = grad * gain_ref[0:1, :]
        inner = jnp.mean(weighted * x, -1, keepdims=True)
        out_ref[own, :] = dx1_ref[rows, :] + scale * weighted - x * (scale * scale * scale * inner)


def rotary_tables(length):
    frequency = jnp.power(10000.0, -2.0 * jnp.arange(HEAD_DIM // 2, dtype=F32) / HEAD_DIM)
    angles = (jnp.arange(length) % LEN).astype(F32)[:, None] * frequency[None, :]
    shape = jax.ShapeDtypeStruct((length, PAIR), F32)
    return whole_call(tables_kernel, [jnp.cos(angles), jnp.sin(angles)], [shape] * 2, "tables")


def body(
    tokens,
    cotangent,
    gains,
    gain_moments,
    qkv_master,
    out_master,
    ffn_master,
    down_master,
    attn_left,
    attn_right,
    attn_left_root,
    attn_right_root,
    ffn_left,
    ffn_right,
    ffn_left_root,
    ffn_right_root,
    down_left,
    down_right,
    down_left_root,
    down_right_root,
):
    count = lax.axis_size("dp")
    me = lax.axis_index("dp").astype(jnp.int32)[None]
    core = lax.axis_index("narrow").astype(jnp.int32)[None]
    own_rows = tokens.shape[0]
    by_hand = count == GRID

    if by_hand:
        high = count // 4
        first, second, slab = pack(
            qkv_master[:, 0], out_master, ffn_master[:, 0], jnp.swapaxes(down_master, 2, 3)
        )
        one, two, last = 4 * HALF_D, FF, HALF_FF
        width, half, ring_start = one + two + last, (one + two + last) // 2, one + two
        many = high - 1
        far_one = all_shifted(first, count)
        slab_x, slab_y = along(slab, 1, count), along(slab, 2, count)

    x, cot = in_order(tokens, core), in_order(cotangent, core)
    cosine, sine_part = rotary_tables(x.shape[0])

    if by_hand:
        chunk = [(number, 0, one) for number in range(many)]
        near_x, near_y = copy_columns(
            [after(far_one[0], x, cot, cosine, sine_part)] + far_one[1:] + [slab_x, slab_y],
            [chunk + [(many + 1, half, width)], chunk + [(many, 0, half)]],
            "end_round_one",
        )
        one_x, one_y = along(near_x, 1, count), along(near_y, 2, count)
        far_two = all_shifted(after(second, *far_one), count)
        tail = many * one
        one_a, one_b, near_two, square = copy_columns(
            [one_x, one_y] + far_two + [slab, slab_x, slab_y],
            [
                [(0, number * one, number * one + one // 2) for number in range(many)],
                [(1, number * one + one // 2, (number + 1) * one) for number in range(many)],
                [(2 + number, 0, two) for number in range(many)],
                [(2 + many + part, ring_start, width) for part in range(3)]
                + [(0, tail + ring_start - half, tail + width - half)],
            ],
            "end_round_two",
        )
        one_a, one_b = along(one_a, 2, count), along(one_b, 1, count)
        entries = [(0, 0, one, 0, 0, 0, 0), (1, 0, one, 0, 0, 1, 0), (2, 0, one, 0, 1, 0, 0)]
        entries.append((5, tail, one, 0, 1, 1, 0))
        for number in range(many):
            step, at = number + 1, number * one
            entries += [(3, at, one, step, 0, 0, 0), (4, at, one, step, 0, 1, 0)]
            entries += [(5, at, one, step, 1, 0, 0)]
        shapes = [(D, 3 * HALF_D), (HALF_D, D)]
        early = [slab, slab_x, slab_y, near_x, one_x, one_y]
        early[0] = after(slab, near_two)
        w_early = assemble(me, high, early, entries, place_qkv_out, shapes, "place_qkv_out")
        entries = []
        for number in range(many):
            step, at = number + 1, number * (one // 2)
            entries += [(0, at, one // 2, step, 1, 1, 0), (1, at, one // 2, step, 1, 1, one // 2)]
        w_qkv, w_out = assemble(
            me, high, [one_a, one_b], entries, place_qkv_out, shapes, "place_rest", w_early
        )
        near_late, square_late = after(near_two, one_a, one_b), after(square, one_a, one_b)
        two_x, two_y = along(near_late, 1, count), along(near_late, 2, count)
        squares = [square] + [
            shifted(square_late, step, count) if step != high // 2 else None
            for step in range(1, high)
        ]
    else:
        qkv, ffn_part = qkv_master[:, 0].astype(BF16), ffn_master[:, 0].astype(BF16)
        w_qkv, w_out, w_gate, w_up, w_down = gather_by_name(
            qkv, out_master.astype(BF16), ffn_part, down_master[0].astype(BF16)
        )
    normed_one, q, k, v = project(x, gains, w_qkv, cosine, sine_part)
    attended, lse = attend(q, k, v)
    attended_late, w_out_late = attended, w_out
    if by_hand:
        squares_here = [piece for piece in squares[1:] if piece is not None]
        two_a, two_b = copy_columns(
            [after(two_x, attended, *squares_here), two_y],
            [
                [(0, number * two, number * two + two // 2) for number in range(many)],
                [(1, number * two + two // 2, (number + 1) * two) for number in range(many)],
            ],
            "end_round_four",
        )
        squares[high // 2] = shifted(after(square, two_a), high // 2, count)
        early = [slab, slab_x, slab_y, one_x, one_y, near_two, two_x, two_y]
        early[0] = after(slab, two_a)
        attended_late, w_out_late = after(attended, two_a), after(w_out, two_a)
        two_a, two_b = along(two_a, 2, count), along(two_b, 1, count)
        cut = half - one
        entries = [(0, one, two, 0, 0, 0, 0), (1, one, two, 0, 0, 1, 0), (2, one, two, 0, 1, 0, 0)]
        entries += [(4, tail + one, cut, 0, 1, 1, 0), (3, tail, two - cut, 0, 1, 1, cut)]
        for number in range(many):
            step, at = number + 1, number * two
            entries += [(5, at, two, step, 0, 0, 0), (6, at, two, step, 0, 1, 0)]
            entries += [(7, at, two, step, 1, 0, 0)]
        shapes = [(D, HALF_FF)] * 2
        w_early = assemble(me, high, early, entries, place_gate_up, shapes, "place_gate_up")
        entries = []
        for number in range(many):
            step, at = number + 1, number * (two // 2)
            entries += [(0, at, two // 2, step, 1, 1, 0), (1, at, two // 2, step, 1, 1, two // 2)]
        w_gate, w_up = assemble(
            me, high, [two_a, two_b], entries, place_gate_up, shapes, "place_rest", w_early
        )
    attended_far, w_out_far = other_core(attended_late), other_core(w_out_late)
    middle, normed_two, gate, up, hidden = ffn(
        x, attended, attended_far, w_out, w_out_far, gains, w_gate, w_up
    )

    if by_hand:
        squares[0] = after(squares[0], hidden)
        (w_down,) = assemble(
            me,
            high,
            squares,
            [
                (step, part * last, last, step, part // 2, part % 2, 0)
                for step in range(high)
                for part in range(4)
            ],
            place_down,
            [(D, HALF_FF)],
            "place_down",
        )
    down_weight_grad = dot_tn(cot, hidden)
    cot_late = cot
    if by_hand:
        down_sum = reduction([take_down], HALF_FF, count, me, [down_weight_grad])
        sent = down_sum[0]()
        down_far = send_first(*sent, count)
        hidden = after(hidden, sent[0])
    out_part = ffn_out(hidden, w_down)
    if by_hand:
        sent = down_sum[1](after(down_far[0], out_part), down_far[1])
        down_far = send_second(*sent, count)
        cot_late = after(cot, sent[0])
    ffn_back_grad, normed_part = ffn_back(cot_late, gate, up, w_down, w_gate, w_up)
    if by_hand:
        down_sent = down_sum[2](after(down_far[0], normed_part), down_far[1])
        ffn_back_grad = after(ffn_back_grad, down_sent[0])
        normed_part = after(normed_part, down_sent[0])
        out_part = after(out_part, down_sent[0])
    normed_far, out_far = other_core(normed_part), other_core(out_part)
    ffn_weight_grad = dot_tn(normed_two, ffn_back_grad)
    if by_hand:
        ffn_sum = reduction([take_rows], FF, count, me, [ffn_weight_grad])
        sent = ffn_sum[0]()
        normed_far = after(normed_far, sent[0])
        ffn_far = send_first(*sent, count)
    middle_grad, branch, attended_grad, gain_two = middle_back(
        cot, middle, normed_part, normed_far, gains, w_out
    )
    out_weight_grad = dot_tn(attended, branch)
    layer_out = whole_call(
        layer_out_kernel,
        [core, after(middle, branch), out_part, out_far],
        [jax.ShapeDtypeStruct((own_rows, D), BF16)],
        "layer_out",
        1,
    )[0]
    if by_hand:
        sent = ffn_sum[1](after(ffn_far[0], branch, layer_out, out_weight_grad), ffn_far[1])
        ffn_far = send_second(*sent, count)
        down_parts = send_third(
            down_sent[0], *[after(block, sent[0]) for block in down_sent[1:]], count=count
        )
        attended_grad = after(attended_grad, sent[0])
    dq, dk, dv = attend_back(q, k, v, attended_grad, attended, lse, cosine, sine_part)
    qkv_back_grad = jnp.concatenate([dq, dk, dv], 1)
    if by_hand:
        ffn_sent = ffn_sum[2](after(ffn_far[0], dq, *down_parts[1:]), ffn_far[1])
        ffn_parts = [ffn_sent[0]] + [
            shifted(block, step + 1, count)
            for step, block in enumerate(ffn_sent[1:])
            if step + 1 != high // 2
        ]
        qkv_back_grad = after(qkv_back_grad, ffn_sent[0])
    qkv_weight_grad = dot_tn(normed_one, qkv_back_grad)
    if by_hand:
        late_sum = reduction(
            [take_rows, take_out], 4 * HALF_D, count, me, [qkv_weight_grad, out_weight_grad]
        )
        sent = late_sum[0]()
        late_far = list(send_first(*sent, count))
        dq = after(dq, sent[0])
    input_part, gain_one = input_back(x, dq, dk, dv, w_qkv)
    input_part_late = input_part
    if by_hand:
        state = gain_rows(gain_one, gain_two)
        state = added(state, other_core(state), "add_gains")
        late_cut = 2 * HALF_D
        parts = [(0, late_cut), (late_cut, 2 * late_cut)]
        late_far[0] = after(late_far[0], *ffn_parts[1:])
        sent = late_sum[1](*late_far, state, part=parts[0])
        first_far = send_second(*sent, count)
        ffn_parts.append(shifted(after(ffn_sent[high // 2], sent[0]), high // 2, count))
        input_part_late = after(input_part, sent[0])
        second_sent = late_sum[1](after(late_far[0], sent[0]), late_far[1], part=parts[1])
        down_parts[0] = after(down_parts[0], second_sent[0])
        down_grad, down_left_new, down_right_new, down_new = precondition(
            down_parts,
            FBLK,
            down_left,
            down_right,
            down_left_root,
            down_right_root,
            [jnp.swapaxes(down_master, 2, 3)],
            turned=True,
        )
        down_grad, down_new = jnp.swapaxes(down_grad, 2, 3), jnp.swapaxes(down_new, 2, 3)
    input_far = other_core(input_part_late)
    input_grad = whole_call(
        input_grad_kernel,
        [core, x, middle_grad, input_part, input_far, gains],
        [jax.ShapeDtypeStruct((own_rows, D), F32)],
        "input_grad",
        1,
    )[0]
    if by_hand:
        first_far = after(first_far[0], input_grad, down_left_new, *ffn_parts[1:]), first_far[1]
        second_far = send_second(after(second_sent[0], *first_far), second_sent[1], count)
        first_state, *sent = late_sum[2](
            *first_far, state, part=parts[0]
        )
        first_parts = send_third(*sent, count=count)
        ffn_parts[0] = after(ffn_parts[0], sent[0])
        ffn_grad, ffn_left_new, ffn_right_new, ffn_new = precondition(
            ffn_parts,
            FBLK,
            ffn_left[:, 0],
            ffn_right[:, 0],
            ffn_left_root[:, 0],
            ffn_right_root[:, 0],
            [ffn_master[:, 0]],
        )
        sent = late_sum[2](after(second_far[0], ffn_left_new), second_far[1], part=parts[1])
        second_parts = send_third(*sent, count=count)
        first_state = slow_state(after(first_state, sent[0]), first_parts[1:])
        first_parts[0] = after(first_parts[0], first_state)
        gain_grad, gain_moment_new, gain_new = whole_call(
            gains_kernel,
            [first_state, along(first_state, 2, count), gains, gain_moments],
            [jax.ShapeDtypeStruct(gains.shape, F32)] * 3,
            "gains",
        )
        attn_results = ()
        for matrices, some in ((range(2), first_parts), (range(2, 4), second_parts)):
            attn_results = precondition(
                some,
                DBLK,
                attn_left[:, 0],
                attn_right[:, 0],
                attn_left_root[:, 0],
                attn_right_root[:, 0],
                [qkv_master[:, 0], out_master],
                matrices=matrices,
                carry=attn_results,
            )
            second_parts[0] = after(second_parts[0], gain_grad, attn_results[0])
        *stacked, out_new = attn_results
        attn_grad, attn_left_new, attn_right_new, qkv_new = (array[:, None] for array in stacked)
        ffn_grad, ffn_left_new, ffn_right_new, ffn_new = (
            array[:, None] for array in (ffn_grad, ffn_left_new, ffn_right_new, ffn_new)
        )
    else:
        gain_terms = jnp.concatenate([gain_one, 0.5 * gain_two])
        gain_grad = lax.psum(gain_terms, ("dp", "narrow"))
        gain_moment_new = DECAY * gain_moments + (1.0 - DECAY) * gain_grad * gain_grad
        gain_new = gains - GAIN_RATE * gain_grad / (jnp.sqrt(gain_moment_new) + 1e-08)
        qkv_owned, out_owned, ffn_owned, down_owned = scatter_all(
            qkv_weight_grad, out_weight_grad, ffn_weight_grad, down_weight_grad, count
        )
        attn_grad = jnp.concatenate([qkv_owned, out_owned[None]], 0)[:, None]
        ffn_grad = ffn_owned[:, None]
        down_grad = down_owned[None]
        attn_left_new, attn_right_new, attn_new = plain_precondition(
            attn_grad,
            attn_left,
            attn_right,
            attn_left_root,
            attn_right_root,
            jnp.concatenate([qkv_master, out_master[None]], 0),
        )
        qkv_new, out_new = attn_new[:3], attn_new[3]
        ffn_left_new, ffn_right_new, ffn_new = plain_precondition(
            ffn_grad, ffn_left, ffn_right, ffn_left_root, ffn_right_root, ffn_master
        )
        down_left_new, down_right_new, down_new = plain_precondition(
            down_grad, down_left, down_right, down_left_root, down_right_root, down_master
        )
    return (
        layer_out,
        input_grad,
        gain_grad,
        gain_moment_new,
        gain_new,
        attn_grad,
        attn_left_new,
        attn_right_new,
        qkv_new,
        out_new,
        ffn_grad,
        ffn_left_new,
        ffn_right_new,
        ffn_new,
        down_grad,
        down_left_new,
        down_right_new,
        down_new,
    )


def solution(mesh):
    tokens = P(("dp", "narrow"), None)
    stacked = P(None, "narrow", "dp", None, None)
    single = P("narrow", "dp", None, None)
    return jax.shard_map(
        body,
        mesh=mesh,
        in_specs=(tokens, tokens, P(), P(), stacked, single, stacked, single)
        + (stacked,) * 8
        + (single,) * 4,
        out_specs=(tokens, tokens, P(), P(), P())
        + (stacked,) * 4
        + (single,)
        + (stacked,) * 4
        + (single,) * 4,
        check_vma=False,
    )
```

```python
import functools
import math

import jax
import jax.numpy as jnp
from jax import lax
from jax.experimental import pallas as pl
from jax.experimental.pallas import tpu as pltpu
from jax.sharding import PartitionSpec as P

D = 768
HEAD_DIM = 64
FF = 2048
LEN = 1024
GRID = 16
DBLK = D // GRID
FBLK = FF // GRID
HALF_GRID = GRID // 2
HALF_D = D // 2
HALF_FF = FF // 2
PAIR = 2 * HEAD_DIM
ROWS = 256

EPSILON = 1e-05
DECAY = 0.5
STEP_RATE = 0.25
GAIN_RATE = 0.1
NEG_FILL = -1e30
HIGHEST_PRECISION = lax.Precision.HIGHEST
BF16 = jnp.bfloat16
F32 = jnp.float32
VMEM_MIB = 18
DENSE_ROWS = 512
SMALL_MIB = 8
PACK_MIB = 60
STATE_ROWS = 16


def dot_nn(left, right):
    return lax.dot_general(left, right, (((1,), (0,)), ((), ())), preferred_element_type=F32)


def dot_nt(left, right):
    return lax.dot_general(left, right, (((1,), (1,)), ((), ())), preferred_element_type=F32)


def dot_tn(left, right):
    return lax.dot_general(left, right, (((0,), (0,)), ((), ())), preferred_element_type=F32)


def kernel_params(mib=VMEM_MIB):
    return pltpu.CompilerParams(vmem_limit_bytes=mib * 1024 * 1024)


def cost():
    return pl.CostEstimate(flops=0, bytes_accessed=0, transcendentals=0)


def whole_call(kernel, inputs, shapes, name, scalars=0, mib=SMALL_MIB, scratch=()):
    vmem = pl.BlockSpec(memory_space=pltpu.VMEM)
    smem = pl.BlockSpec(memory_space=pltpu.SMEM)
    return pl.pallas_call(
        kernel,
        in_specs=[smem] * scalars + [vmem] * (len(inputs) - scalars),
        out_specs=[vmem] * len(shapes),
        out_shape=shapes,
        scratch_shapes=list(scratch),
        compiler_params=kernel_params(mib),
        cost_estimate=cost(),
        name=name,
    )(*inputs)


def over_rows(length, rows, work):
    @pl.loop(0, length // rows)
    def _(step):
        work(pl.ds(pl.multiple_of(step * rows, rows), rows))


def lower_lanes(shape):
    return lax.broadcasted_iota(jnp.int32, shape, 1) % HEAD_DIM < HEAD_DIM // 2


def turn(features, cosine, sine_part, lower):
    half = HEAD_DIM // 2
    partner = jnp.where(
        lower, pltpu.roll(features, PAIR - half, 1), pltpu.roll(features, half, 1)
    )
    return features * cosine + partner * sine_part


def project_kernel(x_ref, gain_ref, w_ref, cos_ref, sin_ref, n1_ref, q_ref, k_ref, v_ref):
    lower = lower_lanes((DENSE_ROWS, PAIR))

    def work(rows):
        x = x_ref[rows, :].astype(F32)
        scale = lax.rsqrt(jnp.mean(x * x, -1, keepdims=True) + EPSILON)
        normed = (x * scale * gain_ref[0:1, :]).astype(BF16)
        n1_ref[rows, :] = normed
        cosine, sine_part = cos_ref[rows, :], sin_ref[rows, :]
        both = dot_nn(normed, w_ref[...])
        for tile in range(HALF_D // PAIR):
            lanes = slice(tile * PAIR, (tile + 1) * PAIR)
            query = both[:, tile * PAIR : (tile + 1) * PAIR]
            key = both[:, HALF_D + tile * PAIR : HALF_D + (tile + 1) * PAIR]
            turned = turn(query, cosine, sine_part, lower).astype(BF16)
            q_ref[rows, lanes] = turned * BF16(1.0 / math.sqrt(HEAD_DIM))
            k_ref[rows, lanes] = turn(key, cosine, sine_part, lower).astype(BF16)
        v_ref[rows, :] = both[:, 2 * HALF_D :].astype(BF16)

    over_rows(x_ref.shape[0], DENSE_ROWS, work)


def project(x, gains, weight, cosine, sine_part):
    length = x.shape[0]
    half = jax.ShapeDtypeStruct((length, HALF_D), BF16)
    shapes = [jax.ShapeDtypeStruct((length, D), BF16), half, half, half]
    return whole_call(
        project_kernel, [x, gains, weight, cosine, sine_part], shapes, "project", mib=VMEM_MIB
    )


def attend_kernel(q_ref, k_ref, v_ref, o_ref, lse_ref):
    @pl.loop(0, q_ref.shape[1] // PAIR)
    def _(pair):
        lanes = pl.ds(pl.multiple_of(pair * PAIR, PAIR), PAIR)
        rows = pl.ds(pl.multiple_of(pair * 8, 8), 8)
        attend_pair(
            *(ref.at[:, lanes] for ref in (q_ref, k_ref, v_ref, o_ref)), lse_ref.at[rows, :]
        )


def attend_pair(q_ref, k_ref, v_ref, o_ref, lse_ref):
    length = q_ref.shape[0]
    first_head = lax.broadcasted_iota(jnp.int32, (ROWS, PAIR), 1) < HEAD_DIM
    keys = k_ref[...]
    values = jnp.concatenate([v_ref[...], jnp.ones((length, PAIR), BF16)], 1)
    causal = lax.broadcasted_iota(jnp.int32, (ROWS, ROWS), 0) >= lax.broadcasted_iota(
        jnp.int32, (ROWS, ROWS), 1
    )
    for block in range(length // ROWS):
        rows = slice(block * ROWS, (block + 1) * ROWS)
        width = (block + 1) * ROWS
        query_block = q_ref[rows, :]
        parts, sums = [], []
        for head in range(2):
            mine = first_head if head == 0 else jnp.logical_not(first_head)
            query = jnp.where(mine, query_block, jnp.zeros_like(query_block))
            scores = jnp.where(causal, dot_nt(query, keys[block * ROWS : width]), NEG_FILL)
            if block:
                scores = jnp.concatenate([dot_nt(query, keys[: block * ROWS]), scores], 1)
            top = jnp.max(scores, 1, keepdims=True)
            exponent = jnp.exp(scores - top).astype(BF16)
            product = dot_nn(exponent, values[:width])
            total = product[:, PAIR:]
            parts.append(product[:, :PAIR] / total)
            sums.append(top + jnp.log(total))
        o_ref[rows, :] = jnp.where(first_head, parts[0], parts[1]).astype(BF16)
        lane = lax.broadcasted_iota(jnp.int32, (ROWS, PAIR), 1)
        lse_ref[:, rows] = jnp.transpose(jnp.where(lane == 0, sums[0], sums[1]))[:8, :]


def attend(q, k, v):
    length = q.shape[0]
    shapes = [
        jax.ShapeDtypeStruct(q.shape, BF16),
        jax.ShapeDtypeStruct((8 * (q.shape[1] // PAIR), length), F32),
    ]
    return whole_call(attend_kernel, [q, k, v], shapes, "attend", mib=VMEM_MIB)


def attend_back_kernel(
    q_ref, k_ref, v_ref, do_ref, o_ref, lse_ref, cos_ref, sin_ref, dq_ref, dk_ref, dv_ref, dqt_ref
):
    @pl.loop(0, q_ref.shape[1] // PAIR)
    def _(pair):
        lanes = pl.ds(pl.multiple_of(pair * PAIR, PAIR), PAIR)
        rows = pl.ds(pl.multiple_of(pair * 8, 8), 8)
        attend_back_pair(
            *(ref.at[:, lanes] for ref in (q_ref, k_ref, v_ref, do_ref, o_ref)),
            lse_ref.at[rows, :],
            cos_ref,
            sin_ref,
            *(ref.at[:, lanes] for ref in (dq_ref, dk_ref, dv_ref)),
            dqt_ref,
        )


def attend_back_pair(
    q_ref, k_ref, v_ref, do_ref, o_ref, lse_ref, cos_ref, sin_ref, dq_ref, dk_ref, dv_ref, dqt_ref
):
    length = q_ref.shape[0]
    first_head = lax.broadcasted_iota(jnp.int32, (length, PAIR), 1) < HEAD_DIM
    zero = BF16(0)
    queries = [
        jnp.where(first_head, q_ref[...], zero),
        jnp.where(first_head, zero, q_ref[...]),
    ]
    grads = [
        jnp.where(first_head, do_ref[...], zero),
        jnp.where(first_head, zero, do_ref[...]),
    ]
    product = do_ref[...].astype(F32) * o_ref[...].astype(F32)
    head_row = lax.broadcasted_iota(jnp.int32, (8, PAIR), 0)
    head_lane = lax.broadcasted_iota(jnp.int32, (8, PAIR), 1) // HEAD_DIM
    inner = lax.dot_general(
        (head_row == head_lane).astype(F32),
        product,
        (((1,), (1,)), ((), ())),
        preferred_element_type=F32,
        precision=HIGHEST_PRECISION,
    )
    turned_keys = jnp.transpose(k_ref[...].astype(F32)).astype(BF16)
    first_rows = lax.broadcasted_iota(jnp.int32, turned_keys.shape, 0) < HEAD_DIM
    key_heads = [
        jnp.where(first_rows, turned_keys, zero),
        jnp.where(first_rows, zero, turned_keys),
    ]
    causal = lax.broadcasted_iota(jnp.int32, (ROWS, ROWS), 0) <= lax.broadcasted_iota(
        jnp.int32, (ROWS, ROWS), 1
    )
    dqt_ref[...] = jnp.zeros_like(dqt_ref)
    lower = lower_lanes((ROWS, PAIR))
    for block in range(length // ROWS):
        rows = slice(block * ROWS, (block + 1) * ROWS)
        start = block * ROWS
        key_block, value_block = k_ref[rows, :], v_ref[rows, :]
        dk = jnp.zeros((ROWS, PAIR), F32)
        dv = jnp.zeros((ROWS, PAIR), F32)
        for head in range(2):
            scores = dot_nt(key_block, queries[head][start:])
            probs = jnp.exp(scores - lse_ref[head : head + 1, start:])
            diagonal = jnp.where(causal, probs[:, :ROWS], 0.0)
            if start + ROWS == length:
                probs = diagonal
            else:
                probs = jnp.concatenate([diagonal, probs[:, ROWS:]], 1)
            prob_grad = dot_nt(value_block, grads[head][start:])
            score_grad = (probs * (prob_grad - inner[head : head + 1, start:])).astype(BF16)
            dv = dv + dot_nn(probs.astype(BF16), grads[head][start:])
            dk = dk + dot_nn(score_grad, queries[head][start:])
            dqt_ref[:, start:] += dot_nn(key_heads[head][:, rows], score_grad)
        dk_ref[rows, :] = turn(dk, cos_ref[rows, :], -sin_ref[rows, :], lower).astype(BF16)
        dv_ref[rows, :] = dv.astype(BF16)
    for block in range(length // ROWS):
        rows = slice(block * ROWS, (block + 1) * ROWS)
        dq = jnp.transpose(dqt_ref[:, rows]) * (1.0 / math.sqrt(HEAD_DIM))
        dq_ref[rows, :] = turn(dq, cos_ref[rows, :], -sin_ref[rows, :], lower).astype(BF16)


def attend_back(q, k, v, grad, o, lse, cosine, sine_part):
    return whole_call(
        attend_back_kernel,
        [q, k, v, grad, o, lse, cosine, sine_part],
        [jax.ShapeDtypeStruct(q.shape, BF16)] * 3,
        "attend_back",
        mib=VMEM_MIB,
        scratch=[pltpu.VMEM((PAIR, q.shape[0]), F32)],
    )


def ffn_kernel(
    x_ref, o_ref, o_far_ref, wo_ref, wo_far_ref, gain_ref, wg_ref, wu_ref,
    x1_ref, n2_ref, gate_ref, up_ref, hidden_ref,
):
    def work(rows):
        middle = (
            x_ref[rows, :].astype(F32)
            + dot_nn(o_ref[rows, :], wo_ref[...])
            + dot_nn(o_far_ref[rows, :], wo_far_ref[...])
        )
        x1_ref[rows, :] = middle
        scale = lax.rsqrt(jnp.mean(middle * middle, -1, keepdims=True) + EPSILON)
        normed = (middle * scale * gain_ref[1:2, :]).astype(BF16)
        n2_ref[rows, :] = normed
        gate = dot_nn(normed, wg_ref[...])
        up = dot_nn(normed, wu_ref[...])
        gate_ref[rows, :] = gate
        up_ref[rows, :] = up
        hidden_ref[rows, :] = (gate * jax.nn.sigmoid(gate) * up).astype(BF16)

    over_rows(x_ref.shape[0], DENSE_ROWS, work)


def ffn(*inputs):
    length = inputs[0].shape[0]
    shapes = [
        jax.ShapeDtypeStruct((length, width), kind)
        for width, kind in ((D, F32), (D, BF16), (HALF_FF, F32), (HALF_FF, F32), (HALF_FF, BF16))
    ]
    return whole_call(ffn_kernel, inputs, shapes, "ffn", mib=VMEM_MIB)


def ffn_out_kernel(hidden_ref, wdt_ref, part_ref):
    part_ref[...] = dot_nt(hidden_ref[...], wdt_ref[...]).astype(BF16)


def ffn_out(hidden, wdt):
    shape = jax.ShapeDtypeStruct((hidden.shape[0], D), BF16)
    return whole_call(ffn_out_kernel, [hidden, wdt], [shape], "ffn_out", mib=VMEM_MIB)[0]


def ffn_back_kernel(cot_ref, gate_ref, up_ref, wdt_ref, wg_ref, wu_ref, dgu_ref, dn2_ref):
    def work(rows):
        hidden_grad = dot_nn(cot_ref[rows, :], wdt_ref[...])
        gate, up = gate_ref[rows, :], up_ref[rows, :]
        sigma = jax.nn.sigmoid(gate)
        gate_grad = (hidden_grad * up * sigma * (1.0 + gate * (1.0 - sigma))).astype(BF16)
        up_grad = (hidden_grad * gate * sigma).astype(BF16)
        dgu_ref[rows, :HALF_FF] = gate_grad
        dgu_ref[rows, HALF_FF:] = up_grad
        dn2 = dot_nt(gate_grad, wg_ref[...]) + dot_nt(up_grad, wu_ref[...])
        dn2_ref[rows, :] = dn2.astype(BF16)

    over_rows(cot_ref.shape[0], DENSE_ROWS, work)


def ffn_back(cot, gate, up, wdt, wg, wu):
    shapes = [jax.ShapeDtypeStruct((cot.shape[0], width), BF16) for width in (FF, D)]
    return whole_call(
        ffn_back_kernel, [cot, gate, up, wdt, wg, wu], shapes, "ffn_back", mib=VMEM_MIB
    )


def middle_back_kernel(
    cot_ref, x1_ref, near_ref, far_ref, gain_ref, wo_ref, dx1_ref, da_ref, do_ref, g2_ref
):
    g2_ref[...] = jnp.zeros_like(g2_ref)

    def work(rows):
        middle = x1_ref[rows, :]
        scale = lax.rsqrt(jnp.mean(middle * middle, -1, keepdims=True) + EPSILON)
        grad = near_ref[rows, :].astype(F32) + far_ref[rows, :].astype(F32)
        weighted = grad * gain_ref[1:2, :]
        inner = jnp.mean(weighted * middle, -1, keepdims=True)
        middle_grad = (
            cot_ref[rows, :].astype(F32)
            + scale * weighted
            - middle * (scale * scale * scale * inner)
        )
        dx1_ref[rows, :] = middle_grad
        branch = middle_grad.astype(BF16)
        da_ref[rows, :] = branch
        do_ref[rows, :] = dot_nt(branch, wo_ref[...]).astype(BF16)
        g2_ref[...] += jnp.sum(grad * middle * scale, 0, keepdims=True)

    over_rows(cot_ref.shape[0], DENSE_ROWS, work)


def middle_back(*inputs):
    length = inputs[0].shape[0]
    shapes = [
        jax.ShapeDtypeStruct(shape, kind)
        for shape, kind in (
            ((length, D), F32),
            ((length, D), BF16),
            ((length, HALF_D), BF16),
            ((1, D), F32),
        )
    ]
    return whole_call(middle_back_kernel, inputs, shapes, "middle_back", mib=VMEM_MIB)


def input_back_kernel(x_ref, dq_ref, dk_ref, dv_ref, w_ref, part_ref, g1_ref):
    g1_ref[...] = jnp.zeros_like(g1_ref)

    def work(rows):
        grad = (
            dot_nt(dq_ref[rows, :], w_ref[:, :HALF_D])
            + dot_nt(dk_ref[rows, :], w_ref[:, HALF_D : 2 * HALF_D])
            + dot_nt(dv_ref[rows, :], w_ref[:, 2 * HALF_D :])
        )
        part_ref[rows, :] = grad.astype(BF16)
        x = x_ref[rows, :].astype(F32)
        scale = lax.rsqrt(jnp.mean(x * x, -1, keepdims=True) + EPSILON)
        g1_ref[...] += jnp.sum(grad * x * scale, 0, keepdims=True)

    over_rows(x_ref.shape[0], DENSE_ROWS, work)


def input_back(x, dq, dk, dv, w):
    shapes = [jax.ShapeDtypeStruct(x.shape, BF16), jax.ShapeDtypeStruct((1, D), F32)]
    return whole_call(input_back_kernel, [x, dq, dk, dv, w], shapes, "input_back", mib=VMEM_MIB)


def pair_up(bit, count):
    return [(i, i ^ bit) for i in range(count)]


def after(value, *others):
    return lax.optimization_barrier((value,) + others)[0]


def along(values, bit, count):
    return lax.ppermute(values, "dp", pair_up(bit, count))


def shifted(values, steps, count):
    return lax.ppermute(values, "dp", [(i, (i + 4 * steps) % count) for i in range(count)])


def other_core(values):
    return lax.ppermute(values, "narrow", [(0, 1), (1, 0)])


def all_shifted(values, count):
    return [shifted(values, step, count) for step in range(1, count // 4)]


def copy_columns(sources, outputs, name):
    rows = sources[0].shape[0]
    shapes = [
        jax.ShapeDtypeStruct((rows, sum(stop - start for _, start, stop in parts)), BF16)
        for parts in outputs
    ]

    def kernel(*refs):
        for out_ref, parts in zip(refs[len(sources) :], outputs):
            at = 0
            for number, start, stop in parts:
                out_ref[:, at : at + stop - start] = refs[number][:, start:stop]
                at += stop - start

    return whole_call(kernel, sources, shapes, name)


def block_rows(owner):
    return pl.ds(pl.multiple_of(owner * DBLK, 16), DBLK)


def block_lanes(index, width):
    return pl.ds(pl.multiple_of(index * width, 128), width)


def place_qkv_out(owner, start, piece, qkv_ref, out_ref):
    cut, stop = 3 * HALF_D, start + piece.shape[1]
    if start < cut:
        end = min(stop, cut)
        qkv_ref[block_rows(owner), start:end] = piece[:, : end - start]
    if stop > cut:
        begin = max(start, cut)
        lanes = pl.ds(pl.multiple_of(owner % 2 * HALF_D + (begin - cut), 128), stop - begin)
        out_ref[block_rows(owner // 2), lanes] = piece[:, begin - start :]


def place_gate_up(owner, start, piece, gate_ref, up_ref):
    stop = start + piece.shape[1]
    if start < HALF_FF:
        end = min(stop, HALF_FF)
        gate_ref[block_rows(owner), start:end] = piece[:, : end - start]
    if stop > HALF_FF:
        begin = max(start, HALF_FF)
        up_ref[block_rows(owner), begin - HALF_FF : stop - HALF_FF] = piece[:, begin - start :]


def place_down(owner, start, piece, out_ref):
    lanes = block_lanes(owner // 2, FBLK)
    for block in range(piece.shape[1] // FBLK):
        rows = block_rows(owner % 2 * HALF_GRID + start // FBLK + block)
        out_ref[rows, lanes] = piece[:, block * FBLK : (block + 1) * FBLK]


def assemble(me, high, sources, entries, place, shapes, name, begun=()):
    sources = list(sources)

    def kernel(me_ref, *refs):
        x, y, z = me_ref[0] % 2, me_ref[0] // 2 % 2, me_ref[0] // 4
        out_refs = refs[len(sources) + len(begun) :]
        for ref, out_ref in zip(refs[len(sources) :], out_refs if begun else ()):
            out_ref[...] = ref[...]
        for number, start, width, step, over_y, over_x, first in entries:
            slow = (z - step + high) % high
            from_y = 1 - y if over_y else y
            from_x = 1 - x if over_x else x
            piece = refs[number][:, start : start + width]
            place(slow * 4 + from_y * 2 + from_x, first, piece, *out_refs)

    return whole_call(
        kernel,
        [me] + sources + list(begun),
        [jax.ShapeDtypeStruct(shape, BF16) for shape in shapes],
        name,
        1,
    )


def pack_kernel(qkv_ref, out_ref, ffn_ref, down_ref, first_ref, second_ref, slab_ref, *scratch):
    held, sems = scratch[:-1], scratch[-1]
    copies = [
        pltpu.make_async_copy(ref, here, sems.at[number])
        for number, (ref, here) in enumerate(zip((qkv_ref, out_ref, ffn_ref, down_ref), held))
    ]
    for copy in copies:
        copy.start()

    def row(ref, matrix):
        return jnp.concatenate([ref[matrix, block].astype(BF16) for block in range(HALF_GRID)], 1)

    at = 0
    for copy, ref in zip(copies, held):
        copy.wait()
        for matrix in range(ref.shape[0]):
            part = row(ref, matrix)
            stop = at + part.shape[1]
            slab_ref[:, at:stop] = part
            if stop <= first_ref.shape[1]:
                first_ref[:, at:stop] = part
            elif stop <= first_ref.shape[1] + second_ref.shape[1]:
                second_ref[:, at - first_ref.shape[1] : stop - first_ref.shape[1]] = part
            at = stop


def pack(*masters):
    vmem = pl.BlockSpec(memory_space=pltpu.VMEM)
    return pl.pallas_call(
        pack_kernel,
        in_specs=[pl.BlockSpec(memory_space=pl.ANY)] * len(masters),
        out_specs=[vmem] * 3,
        out_shape=[
            jax.ShapeDtypeStruct((DBLK, width), BF16)
            for width in (4 * HALF_D, FF, 4 * HALF_D + 3 * HALF_FF)
        ],
        scratch_shapes=[pltpu.VMEM(master.shape, F32) for master in masters]
        + [pltpu.SemaphoreType.DMA((len(masters),))],
        compiler_params=kernel_params(PACK_MIB),
        cost_estimate=cost(),
        name="pack",
    )(*masters)


def tables_kernel(cos_ref, sin_ref, cosine_ref, sine_ref):
    cosine, sine = cos_ref[...], sin_ref[...]
    cosine_ref[...] = jnp.concatenate([cosine] * 4, 1)
    sine_ref[...] = jnp.concatenate([-sine, sine] * 2, 1)


def side_by_side(blocks):
    matrices, many, height, width = blocks.shape
    return blocks.transpose(2, 0, 1, 3).reshape(height, matrices * many * width)


def gather_by_name(qkv, out, ffn_part, down):
    qkv_all = lax.all_gather(qkv, "dp", axis=1, tiled=True)
    out_all = lax.all_gather(out[0], "dp", axis=0, tiled=True)
    ffn_all = lax.all_gather(ffn_part, "dp", axis=1, tiled=True)
    down_all = lax.all_gather(down, "dp", axis=0, tiled=True)
    w_qkv = qkv_all.reshape(3, GRID, HALF_GRID, DBLK, DBLK).transpose(1, 3, 0, 2, 4)
    w_out = out_all.reshape(HALF_GRID, GRID, DBLK, DBLK).transpose(0, 2, 1, 3)
    w_ffn = ffn_all.reshape(2, GRID, HALF_GRID, DBLK, FBLK).transpose(0, 1, 3, 2, 4)
    w_down = down_all.reshape(HALF_GRID, GRID, FBLK, DBLK).transpose(1, 3, 0, 2)
    w_ffn = w_ffn.reshape(2, D, HALF_FF)
    return (
        w_qkv.reshape(D, 3 * HALF_D),
        w_out.reshape(HALF_D, D),
        w_ffn[0],
        w_ffn[1],
        w_down.reshape(D, HALF_FF),
    )


def take_rows(owner, ref):
    return ref[block_rows(owner), :]


def take_out(owner, ref):
    return ref[block_rows(owner // 2), pl.ds(pl.multiple_of(owner % 2 * HALF_D, 128), HALF_D)]


def take_down(owner, ref):
    lanes = pl.ds(pl.multiple_of(owner // 2 * FBLK, 128), FBLK)
    return jnp.concatenate(
        [ref[block_rows(owner % 2 * HALF_GRID + block), lanes] for block in range(HALF_GRID)], 1
    )


def paired(values):
    high = values.astype(BF16)
    low = (values - high.astype(F32)).astype(BF16)
    rest = jnp.zeros((DBLK - 2 * values.shape[0], values.shape[1]), BF16)
    return jnp.concatenate([high, low, rest], 0)


def unpaired(pair):
    rows = STATE_ROWS
    return pair[:rows].astype(F32) + pair[rows : 2 * rows].astype(F32)


def reduction(takes, columns, count, me, grads):
    high = count // 4
    half = high // 2
    many = len(grads)

    def step(kernel, inputs, shapes, name):
        return whole_call(kernel, [me] + grads + inputs, shapes, name, 1)

    def find(refs, slow, y, x, part):
        owner = slow * 4 + y * 2 + x
        found = [take(owner, ref) for take, ref in zip(takes, refs)]
        found = found[0] if len(found) == 1 else jnp.concatenate(found, 1)
        return found[:, part[0] : part[1]].astype(F32)

    def place(me_ref):
        return me_ref[0] % 2, me_ref[0] // 2 % 2, me_ref[0] // 4

    def piece(index):
        return slice(index * columns, (index + 1) * columns)

    def diagonal_kernel(me_ref, *refs):
        x, y, _ = place(me_ref)
        *guest_refs, to_y_ref, to_x_ref = refs[many:]
        for guest_ref in guest_refs:
            wide = guest_ref.shape[1] // 4
            middle = 3 * wide + wide // 2
            to_y_ref[:, half * columns :] = guest_ref[:, 3 * wide : middle].astype(BF16)
            to_x_ref[:, half * columns :] = guest_ref[:, middle:].astype(BF16)
        for slow in range(high):
            block = find(refs, slow, 1 - y, 1 - x, (0, columns)).astype(BF16)
            if slow < half:
                to_y_ref[:, piece(slow)] = block
            else:
                to_x_ref[:, piece(slow - half)] = block

    def side_kernel(part, me_ref, *refs):
        x, y, _ = place(me_ref)
        by_y_ref, by_x_ref, *state_refs, to_x_ref, to_y_ref = refs[many:]
        width = part[1] - part[0]
        if state_refs:
            guest_ref = state_refs[1]
            wide = guest_ref.shape[1] // 4
            cut, start = wide // 2, high * width + 128
            by_y = by_y_ref[:, half * columns :].astype(F32)
            by_x = by_x_ref[:, half * columns :].astype(F32)
            to_x_ref[:, start : start + cut] = (guest_ref[:, wide : wide + cut] + by_y).astype(BF16)
            to_x_ref[:, start + cut :] = guest_ref[:, wide + cut : 2 * wide].astype(BF16)
            start = high * width
            to_y_ref[:, start : start + cut] = guest_ref[:, 2 * wide : 2 * wide + cut].astype(BF16)
            to_y_ref[:, start + cut :] = (
                guest_ref[:, 2 * wide + cut : 3 * wide] + by_x
            ).astype(BF16)
        for slow in range(high):
            to_x = find(refs, slow, y, 1 - x, part)
            to_y = find(refs, slow, 1 - y, x, part)
            start = slow % half * columns + part[0]
            if slow < half:
                to_x = to_x + by_y_ref[:, start : start + width].astype(F32)
            else:
                to_y = to_y + by_x_ref[:, start : start + width].astype(F32)
            to_x_ref[:, slow * width : (slow + 1) * width] = to_x.astype(BF16)
            to_y_ref[:, slow * width : (slow + 1) * width] = to_y.astype(BF16)
        if state_refs:
            to_x_ref[:, high * width : high * width + 128] = paired(state_refs[0][...])

    def slow_kernel(part, me_ref, *refs):
        x, y, z = place(me_ref)
        from_x_ref, from_y_ref, *state_refs = refs[many : len(refs) - high]
        out_refs = refs[len(refs) - high :]
        width = part[1] - part[0]
        if state_refs:
            before_ref, after_ref = state_refs
            lanes = slice(high * width, high * width + 128)
            state = unpaired(paired(before_ref[...])) + unpaired(from_x_ref[:, lanes])
            after_ref[...] = state
        for shift in range(high):
            rows = pl.ds(0, DBLK)
            slow = (z + shift) % high
            lanes = pl.ds(pl.multiple_of(slow * width, 128), width)
            total = (
                find(refs, slow, y, x, part)
                + from_x_ref[rows, lanes].astype(F32)
                + from_y_ref[rows, lanes].astype(F32)
            )
            out_refs[shift][:, :width] = total.astype(out_refs[shift].dtype)
            if state_refs and shift:
                out_refs[shift][:, width:] = paired(state)

    def rows(width, kind=BF16):
        return jax.ShapeDtypeStruct((DBLK, width), kind)

    state_shape = jax.ShapeDtypeStruct((STATE_ROWS, 128), F32)

    def first(*guest):
        extra = sum(array.shape[1] // 8 for array in guest)
        shapes = [rows(half * columns + extra)] * 2
        return step(diagonal_kernel, list(guest), shapes, "send_diagonal")

    def second(by_y, by_x, *state, part=(0, columns)):
        wide = high * (part[1] - part[0])
        extra = state[1].shape[1] // 4 if state else 0
        shapes = [rows(wide + extra + (128 if state else 0)), rows(wide + extra)]
        kernel = functools.partial(side_kernel, part)
        return step(kernel, [by_y, by_x, *state], shapes, "send_sides")

    def third(from_x, from_y, *state, part=(0, columns)):
        width = part[1] - part[0]
        shapes = [state_shape] * len(state) + [rows(width, F32)]
        shapes += [rows(width + 128 * len(state))] * (high - 1)
        kernel = functools.partial(slow_kernel, part)
        return step(kernel, [from_x, from_y, *state], shapes, "send_slow")

    return first, second, third


def ring_blocks(grad, me, high):
    def kernel(me_ref, grad_ref, *out_refs):
        x, y, z = me_ref[0] % 2, me_ref[0] // 2 % 2, me_ref[0] // 4
        for hop, out_ref in enumerate(out_refs):
            slow = (z - 1 - hop + high) % high
            for part in range(4):
                from_x = 1 - x if part % 2 else x
                from_y = 1 - y if part // 2 else y
                block = take_down(slow * 4 + from_y * 2 + from_x, grad_ref)
                lanes = slice(part * HALF_FF, (part + 1) * HALF_FF)
                out_ref[:, lanes] = block.astype(out_ref.dtype)

    shapes = [
        jax.ShapeDtypeStruct((DBLK, 4 * HALF_FF), BF16 if hop < high - 1 else F32)
        for hop in range(high)
    ]
    return whole_call(kernel, [me, grad], shapes, "ring_blocks", 1)


def ring_add_kernel(far_ref, own_ref, out_ref):
    total = far_ref[...].astype(F32) + own_ref[...].astype(F32)
    out_ref[...] = total.astype(out_ref.dtype)


def ring_add(far, own):
    shape = jax.ShapeDtypeStruct(own.shape, own.dtype)
    return whole_call(ring_add_kernel, [far, own], [shape], "ring_add")[0]


def send_first(to_y, to_x, count):
    return along(to_y, 2, count), along(to_x, 1, count)


def send_second(to_x, to_y, count):
    return along(to_x, 1, count), along(to_y, 2, count)


def send_third(own, *others, count):
    return [own] + [shifted(block, step + 1, count) for step, block in enumerate(others)]


def scatter_all(qkv, out, ffn_grad, down, count):
    qkv = qkv.reshape(GRID, DBLK, 3, HALF_GRID, DBLK).transpose(2, 0, 3, 1, 4)
    out = out.reshape(HALF_GRID, DBLK, GRID, DBLK).transpose(0, 2, 1, 3)
    ffn_grad = ffn_grad.reshape(GRID, DBLK, 2, HALF_GRID, FBLK).transpose(2, 0, 3, 1, 4)
    down = down.reshape(GRID, DBLK, HALF_GRID, FBLK).transpose(2, 0, 3, 1)
    return (
        lax.psum_scatter(
            qkv.reshape(3, -1, DBLK, DBLK), "dp", scatter_dimension=1, tiled=True
        ),
        lax.psum_scatter(out.reshape(-1, DBLK, DBLK), "dp", scatter_dimension=0, tiled=True),
        lax.psum_scatter(
            ffn_grad.reshape(2, -1, DBLK, FBLK), "dp", scatter_dimension=1, tiled=True
        ),
        lax.psum_scatter(down.reshape(-1, FBLK, DBLK), "dp", scatter_dimension=0, tiled=True),
    )


def gain_rows_kernel(one_ref, two_ref, out_ref):
    def rows(values):
        return [values[:, at : at + 128] for at in range(0, D, 128)]

    parts = rows(one_ref[...]) + rows(0.5 * two_ref[...])
    parts.append(jnp.zeros((STATE_ROWS - len(parts), 128), F32))
    out_ref[...] = jnp.concatenate(parts, 0)


def gain_rows(gain_one, gain_two):
    shape = jax.ShapeDtypeStruct((STATE_ROWS, 128), F32)
    return whole_call(gain_rows_kernel, [gain_one, gain_two], [shape], "gain_rows")[0]


def add_kernel(left_ref, right_ref, out_ref):
    out_ref[...] = left_ref[...] + right_ref[...]


def added(left, right, name):
    return whole_call(add_kernel, [left, right], [jax.ShapeDtypeStruct(left.shape, F32)], name)[0]


def slow_state_kernel(own_ref, *refs):
    out_ref = refs[-1]
    columns = refs[0].shape[1] - 128
    values = [unpaired(paired(own_ref[...]))] + [unpaired(ref[:, columns:]) for ref in refs[:-1]]
    while len(values) > 1:
        half = len(values) // 2
        values = [values[index] + values[index + half] for index in range(half)]
    out_ref[...] = values[0]


def slow_state(own, blocks):
    shape = jax.ShapeDtypeStruct(own.shape, F32)
    return whole_call(slow_state_kernel, [own] + blocks, [shape], "slow_state")[0]


def gains_kernel(near_ref, far_ref, gain_ref, moment_ref, grad_ref, moment_new_ref, gain_new_ref):
    total = near_ref[...] + far_ref[...]
    count = D // 128
    grad = jnp.concatenate(
        [
            jnp.concatenate([total[at + row : at + row + 1] for row in range(count)], 1)
            for at in (0, count)
        ],
        0,
    )
    grad_ref[...] = grad
    moment = DECAY * moment_ref[...] + (1.0 - DECAY) * grad * grad
    moment_new_ref[...] = moment
    gain_new_ref[...] = gain_ref[...] - GAIN_RATE * grad / (jnp.sqrt(moment) + 1e-08)


def full_dot(left, right, left_dim, right_dim):
    return lax.dot_general(
        left,
        right,
        (((left_dim,), (right_dim,)), ((), ())),
        preferred_element_type=F32,
        precision=lax.Precision.DEFAULT,
    )


def precondition(
    parts,
    width,
    left,
    right,
    left_root,
    right_root,
    masters,
    turned=False,
    matrices=None,
    carry=(),
    starts=None,
):
    starts = [0] * len(parts) if starts is None else starts
    counts = [master.shape[0] for master in masters]
    spots = [(which, here) for which, many in enumerate(counts) for here in range(many)]
    matrices = range(len(spots)) if matrices is None else matrices
    many = len(parts)

    def kernel(*refs):
        part_refs, refs = refs[:many], refs[many:]
        left_ref, right_ref, left_root_ref, right_root_ref = refs[:4]
        master_refs, refs = refs[4 : 4 + len(counts)], refs[4 + len(counts) :]
        carry_refs, refs = refs[: len(carry)], refs[len(carry) :]
        grad_ref, left_new_ref, right_new_ref = refs[:3]
        new_refs = refs[3:]
        for matrix, (which, here) in enumerate(spots):
            if carry and matrix not in matrices:
                for out_ref, carry_ref in zip(refs[:3], carry_refs[:3]):
                    out_ref[matrix] = carry_ref[matrix]
                new_refs[which][here] = carry_refs[3 + which][here]
        first, wide = matrices[0] * HALF_GRID * width, len(matrices) * HALF_GRID * width
        total = jnp.zeros((part_refs[0].shape[0], wide), F32)
        for ref, start in zip(part_refs, starts):
            total = total + ref[:, start : start + wide].astype(F32)
        for matrix in matrices:
            which, here = spots[matrix]
            for block in range(HALF_GRID):
                at = (matrix * HALF_GRID + block) * width - first
                grad = total[:, at : at + width]
                grad_ref[matrix, block] = grad
                outer, inner = full_dot(grad, grad, 1, 1), full_dot(grad, grad, 0, 0)
                if turned:
                    outer, inner = inner, outer
                    step = full_dot(grad, left_root_ref[matrix, block], 1, 1)
                    step = full_dot(right_root_ref[matrix, block], step, 0, 0)
                else:
                    step = full_dot(left_root_ref[matrix, block], grad, 1, 0)
                    step = full_dot(step, right_root_ref[matrix, block], 1, 0)
                left_new_ref[matrix, block] = (
                    DECAY * left_ref[matrix, block] + (1.0 - DECAY) * outer
                )
                right_new_ref[matrix, block] = (
                    DECAY * right_ref[matrix, block] + (1.0 - DECAY) * inner
                )
                new_refs[which][here, block] = master_refs[which][here, block] - STEP_RATE * step

    grads = jax.ShapeDtypeStruct((sum(counts),) + masters[0].shape[1:], F32)
    like = [jax.ShapeDtypeStruct(array.shape, F32) for array in (left, right)]
    news = [jax.ShapeDtypeStruct(master.shape, F32) for master in masters]
    inputs = list(parts) + [left, right, left_root, right_root] + list(masters)
    return whole_call(kernel, inputs + list(carry), [grads] + like + news, "precondition")


def plain_precondition(block_grad, left_stat, right_stat, left_root, right_root, master):
    new_left = DECAY * left_stat + (1.0 - DECAY) * jnp.einsum(
        "...ij,...kj->...ik", block_grad, block_grad, precision=HIGHEST_PRECISION
    )
    new_right = DECAY * right_stat + (1.0 - DECAY) * jnp.einsum(
        "...ji,...jk->...ik", block_grad, block_grad, precision=HIGHEST_PRECISION
    )
    turned = jnp.einsum("...ij,...jk->...ik", left_root, block_grad, precision=HIGHEST_PRECISION)
    turned = jnp.einsum("...ij,...jk->...ik", turned, right_root, precision=HIGHEST_PRECISION)
    return (new_left, new_right, master - STEP_RATE * turned)


def in_order_kernel(core_ref, mine_ref, other_ref, out_ref):
    rows = mine_ref.shape[0]
    core = core_ref[0]
    out_ref[pl.ds(pl.multiple_of(core * rows, 16), rows), :] = mine_ref[...]
    out_ref[pl.ds(pl.multiple_of((1 - core) * rows, 16), rows), :] = other_ref[...]


def in_order(mine, core):
    shape = jax.ShapeDtypeStruct((2 * mine.shape[0], mine.shape[1]), mine.dtype)
    return whole_call(in_order_kernel, [core, mine, other_core(mine)], [shape], "in_order", 1)[0]


def own_and_all(core_ref, rows, step):
    own = pl.ds(pl.multiple_of(step * ROWS, ROWS), ROWS)
    return own, pl.ds(pl.multiple_of(core_ref[0] * rows + step * ROWS, ROWS), ROWS)


def layer_out_kernel(core_ref, x1_ref, near_ref, far_ref, out_ref):
    @pl.loop(0, out_ref.shape[0] // ROWS)
    def _(step):
        own, rows = own_and_all(core_ref, out_ref.shape[0], step)
        total = x1_ref[rows, :] + near_ref[rows, :].astype(F32) + far_ref[rows, :].astype(F32)
        out_ref[own, :] = total.astype(BF16)


def input_grad_kernel(core_ref, x_ref, dx1_ref, near_ref, far_ref, gain_ref, out_ref):
    @pl.loop(0, out_ref.shape[0] // ROWS)
    def _(step):
        own, rows = own_and_all(core_ref, out_ref.shape[0], step)
        x = x_ref[rows, :].astype(F32)
        scale = lax.rsqrt(jnp.mean(x * x, -1, keepdims=True) + EPSILON)
        grad = near_ref[rows, :].astype(F32) + far_ref[rows, :].astype(F32)
        weighted = grad * gain_ref[0:1, :]
        inner = jnp.mean(weighted * x, -1, keepdims=True)
        out_ref[own, :] = dx1_ref[rows, :] + scale * weighted - x * (scale * scale * scale * inner)


def rotary_tables(length):
    frequency = jnp.power(10000.0, -2.0 * jnp.arange(HEAD_DIM // 2, dtype=F32) / HEAD_DIM)
    angles = (jnp.arange(length) % LEN).astype(F32)[:, None] * frequency[None, :]
    shape = jax.ShapeDtypeStruct((length, PAIR), F32)
    return whole_call(tables_kernel, [jnp.cos(angles), jnp.sin(angles)], [shape] * 2, "tables")


def body(
    tokens,
    cotangent,
    gains,
    gain_moments,
    qkv_master,
    out_master,
    ffn_master,
    down_master,
    attn_left,
    attn_right,
    attn_left_root,
    attn_right_root,
    ffn_left,
    ffn_right,
    ffn_left_root,
    ffn_right_root,
    down_left,
    down_right,
    down_left_root,
    down_right_root,
):
    count = lax.axis_size("dp")
    me = lax.axis_index("dp").astype(jnp.int32)[None]
    core = lax.axis_index("narrow").astype(jnp.int32)[None]
    own_rows = tokens.shape[0]
    by_hand = count == GRID

    if by_hand:
        high = count // 4
        first, second, slab = pack(
            qkv_master[:, 0], out_master, ffn_master[:, 0], jnp.swapaxes(down_master, 2, 3)
        )
        one, two, last = 4 * HALF_D, FF, HALF_FF
        width, half, ring_start = one + two + last, (one + two + last) // 2, one + two
        many = high - 1
        far_one = all_shifted(first, count)
        slab_x, slab_y = along(slab, 1, count), along(slab, 2, count)

    x, cot = in_order(tokens, core), in_order(cotangent, core)
    cosine, sine_part = rotary_tables(x.shape[0])

    if by_hand:
        chunk = [(number, 0, one) for number in range(many)]
        near_x, near_y = copy_columns(
            [after(far_one[0], x, cot, cosine, sine_part)] + far_one[1:] + [slab_x, slab_y],
            [chunk + [(many + 1, half, width)], chunk + [(many, 0, half)]],
            "end_round_one",
        )
        one_x, one_y = along(near_x, 1, count), along(near_y, 2, count)
        far_two = all_shifted(after(second, *far_one), count)
        tail = many * one
        one_a, one_b, near_two, square = copy_columns(
            [one_x, one_y] + far_two + [slab, slab_x, slab_y],
            [
                [(0, number * one, number * one + one // 2) for number in range(many)],
                [(1, number * one + one // 2, (number + 1) * one) for number in range(many)],
                [(2 + number, 0, two) for number in range(many)],
                [(2 + many + part, ring_start, width) for part in range(3)]
                + [(0, tail + ring_start - half, tail + width - half)],
            ],
            "end_round_two",
        )
        one_a, one_b = along(one_a, 2, count), along(one_b, 1, count)
        entries = [(0, 0, one, 0, 0, 0, 0), (1, 0, one, 0, 0, 1, 0), (2, 0, one, 0, 1, 0, 0)]
        entries.append((5, tail, one, 0, 1, 1, 0))
        for number in range(many):
            step, at = number + 1, number * one
            entries += [(3, at, one, step, 0, 0, 0), (4, at, one, step, 0, 1, 0)]
            entries += [(5, at, one, step, 1, 0, 0)]
        shapes = [(D, 3 * HALF_D), (HALF_D, D)]
        early = [slab, slab_x, slab_y, near_x, one_x, one_y]
        early[0] = after(slab, near_two)
        w_early = assemble(me, high, early, entries, place_qkv_out, shapes, "place_qkv_out")
        entries = []
        for number in range(many):
            step, at = number + 1, number * (one // 2)
            entries += [(0, at, one // 2, step, 1, 1, 0), (1, at, one // 2, step, 1, 1, one // 2)]
        w_qkv, w_out = assemble(
            me, high, [one_a, one_b], entries, place_qkv_out, shapes, "place_rest", w_early
        )
        near_late = after(near_two, one_a, one_b, w_early[0])
        square_late = after(square, one_a, one_b, w_early[0])
        two_x, two_y = along(near_late, 1, count), along(near_late, 2, count)
        squares = [square, shifted(square_late, 1, count)]
    else:
        qkv, ffn_part = qkv_master[:, 0].astype(BF16), ffn_master[:, 0].astype(BF16)
        w_qkv, w_out, w_gate, w_up, w_down = gather_by_name(
            qkv, out_master.astype(BF16), ffn_part, down_master[0].astype(BF16)
        )
    normed_one, q, k, v = project(x, gains, w_qkv, cosine, sine_part)
    attended, lse = attend(q, k, v)
    attended_late, w_out_late = attended, w_out
    if by_hand:
        two_a, two_b = copy_columns(
            [after(two_x, attended, squares[1]), two_y],
            [
                [(0, number * two, number * two + two // 2) for number in range(many)],
                [(1, number * two + two // 2, (number + 1) * two) for number in range(many)],
            ],
            "end_round_four",
        )
        squares.append(shifted(after(squares[1], two_a), 1, count))
        early = [slab, slab_x, slab_y, one_x, one_y, near_two, two_x, two_y]
        early[0] = after(slab, two_a)
        attended_late, w_out_late = after(attended, two_a), after(w_out, two_a)
        two_a, two_b = along(two_a, 2, count), along(two_b, 1, count)
        cut = half - one
        entries = [(0, one, two, 0, 0, 0, 0), (1, one, two, 0, 0, 1, 0), (2, one, two, 0, 1, 0, 0)]
        entries += [(4, tail + one, cut, 0, 1, 1, 0), (3, tail, two - cut, 0, 1, 1, cut)]
        for number in range(many):
            step, at = number + 1, number * two
            entries += [(5, at, two, step, 0, 0, 0), (6, at, two, step, 0, 1, 0)]
            entries += [(7, at, two, step, 1, 0, 0)]
        shapes = [(D, HALF_FF)] * 2
        w_early = assemble(me, high, early, entries, place_gate_up, shapes, "place_gate_up")
        entries = []
        for number in range(many):
            step, at = number + 1, number * (two // 2)
            entries += [(0, at, two // 2, step, 1, 1, 0), (1, at, two // 2, step, 1, 1, two // 2)]
        w_gate, w_up = assemble(
            me,
            high,
            [after(two_a, squares[2]), two_b],
            entries,
            place_gate_up,
            shapes,
            "place_rest",
            w_early,
        )
        for _ in range(3, high):
            squares.append(shifted(after(squares[-1], w_gate), 1, count))
    attended_far, w_out_far = other_core(attended_late), other_core(w_out_late)
    middle, normed_two, gate, up, hidden = ffn(
        x, attended, attended_far, w_out, w_out_far, gains, w_gate, w_up
    )

    if by_hand:
        squares[0] = after(squares[0], hidden)
        (w_down,) = assemble(
            me,
            high,
            squares,
            [
                (step, part * last, last, step, part // 2, part % 2, 0)
                for step in range(high)
                for part in range(4)
            ],
            place_down,
            [(D, HALF_FF)],
            "place_down",
        )
    down_weight_grad = dot_tn(cot, hidden)
    if by_hand:
        ring = ring_blocks(down_weight_grad, me, high)
        passed = shifted(ring[0], 1, count)
        hidden = after(hidden, ring[0])
    out_part = ffn_out(hidden, w_down)
    ffn_back_grad, normed_part = ffn_back(
        after(cot, out_part), gate, up, w_down, w_gate, w_up
    )
    if by_hand:
        sent = ring_add(after(passed, normed_part), ring[1])
        passed = shifted(sent, 1, count)
        ffn_back_grad = after(ffn_back_grad, sent)
        normed_part, out_part = after(normed_part, sent), after(out_part, sent)
    normed_far, out_far = other_core(normed_part), other_core(out_part)
    ffn_weight_grad = dot_tn(normed_two, ffn_back_grad)
    if by_hand:
        ffn_sum = reduction([take_rows], FF, count, me, [ffn_weight_grad])
        sent = ffn_sum[0]()
        normed_far = after(normed_far, sent[0])
        ffn_far = send_first(*sent, count)
    middle_grad, branch, attended_grad, gain_two = middle_back(
        cot, middle, normed_part, normed_far, gains, w_out
    )
    out_weight_grad = dot_tn(attended, branch)
    layer_out = whole_call(
        layer_out_kernel,
        [core, after(middle, branch), out_part, out_far],
        [jax.ShapeDtypeStruct((own_rows, D), BF16)],
        "layer_out",
        1,
    )[0]
    if by_hand:
        sent = ffn_sum[1](after(ffn_far[0], branch, layer_out, out_weight_grad), ffn_far[1])
        ffn_far = send_second(*sent, count)
        for number in range(2, high):
            if number == 2:
                passed = after(passed, layer_out, out_weight_grad)
            sent_round = ring_add(passed, ring[number]) if number < high - 1 else None
            if sent_round is not None:
                passed = shifted(sent_round, 1, count)
                attended_grad = after(attended_grad, sent_round)
        attended_grad = after(attended_grad, sent[0])
    dq, dk, dv = attend_back(q, k, v, attended_grad, attended, lse, cosine, sine_part)
    qkv_back_grad = jnp.concatenate([dq, dk, dv], 1)
    if by_hand:
        down_near = ring_add(after(passed, dq), ring[-1])
        ffn_sent = ffn_sum[2](after(ffn_far[0], dq), ffn_far[1])
        ffn_parts = [ffn_sent[0]] + [
            shifted(block, step + 1, count)
            for step, block in enumerate(ffn_sent[1:])
            if step + 1 != high // 2
        ]
        qkv_back_grad = after(qkv_back_grad, ffn_sent[0])
    qkv_weight_grad = dot_tn(normed_one, qkv_back_grad)
    if by_hand:
        late_sum = reduction(
            [take_rows, take_out], 4 * HALF_D, count, me, [qkv_weight_grad, out_weight_grad]
        )
        sent = late_sum[0](down_near)
        late_far = list(send_first(*sent, count))
        dq = after(dq, sent[0])
    input_part, gain_one = input_back(x, dq, dk, dv, w_qkv)
    input_part_late = input_part
    if by_hand:
        state = gain_rows(gain_one, gain_two)
        state = added(state, other_core(state), "add_gains")
        late_cut = 2 * HALF_D
        parts = [(0, late_cut), (late_cut, 2 * late_cut)]
        late_far[0] = after(late_far[0], *ffn_parts[1:])
        sent = late_sum[1](*late_far, state, down_near, part=parts[0])
        first_far = send_second(*sent, count)
        ffn_parts.append(shifted(after(ffn_sent[high // 2], sent[0]), high // 2, count))
        input_part_late = after(input_part, sent[0])
        second_sent = late_sum[1](after(late_far[0], sent[0]), late_far[1], part=parts[1])
    input_far = other_core(input_part_late)
    input_grad = whole_call(
        input_grad_kernel,
        [core, x, middle_grad, input_part, input_far, gains],
        [jax.ShapeDtypeStruct((own_rows, D), F32)],
        "input_grad",
        1,
    )[0]
    if by_hand:
        second_far = send_second(
            after(second_sent[0], input_grad, *first_far, *ffn_parts[1:]), second_sent[1], count
        )
        first_state, *sent = late_sum[2](
            *first_far,
            state,
            part=parts[0],
        )
        first_parts = send_third(*sent, count=count)
        ffn_parts[0] = after(ffn_parts[0], sent[0])
        ffn_grad, ffn_left_new, ffn_right_new, ffn_new = precondition(
            ffn_parts,
            FBLK,
            ffn_left[:, 0],
            ffn_right[:, 0],
            ffn_left_root[:, 0],
            ffn_right_root[:, 0],
            [ffn_master[:, 0]],
        )
        wide = high * late_cut
        down_grad, down_left_new, down_right_new, down_new = precondition(
            [after(down_near, ffn_left_new), *first_far],
            FBLK,
            down_left,
            down_right,
            down_left_root,
            down_right_root,
            [jnp.swapaxes(down_master, 2, 3)],
            turned=True,
            starts=[0, wide + 128, wide],
        )
        down_grad, down_new = jnp.swapaxes(down_grad, 2, 3), jnp.swapaxes(down_new, 2, 3)
        sent = late_sum[2](after(second_far[0], down_left_new), second_far[1], part=parts[1])
        second_parts = send_third(*sent, count=count)
        first_state = slow_state(after(first_state, sent[0]), first_parts[1:])
        first_parts[0] = after(first_parts[0], first_state)
        gain_grad, gain_moment_new, gain_new = whole_call(
            gains_kernel,
            [first_state, along(first_state, 2, count), gains, gain_moments],
            [jax.ShapeDtypeStruct(gains.shape, F32)] * 3,
            "gains",
        )
        attn_results = ()
        for matrices, some in ((range(2), first_parts), (range(2, 4), second_parts)):
            attn_results = precondition(
                some,
                DBLK,
                attn_left[:, 0],
                attn_right[:, 0],
                attn_left_root[:, 0],
                attn_right_root[:, 0],
                [qkv_master[:, 0], out_master],
                matrices=matrices,
                carry=attn_results,
            )
            second_parts[0] = after(second_parts[0], gain_grad, attn_results[0])
        *stacked, out_new = attn_results
        attn_grad, attn_left_new, attn_right_new, qkv_new = (array[:, None] for array in stacked)
        ffn_grad, ffn_left_new, ffn_right_new, ffn_new = (
            array[:, None] for array in (ffn_grad, ffn_left_new, ffn_right_new, ffn_new)
        )
    else:
        gain_terms = jnp.concatenate([gain_one, 0.5 * gain_two])
        gain_grad = lax.psum(gain_terms, ("dp", "narrow"))
        gain_moment_new = DECAY * gain_moments + (1.0 - DECAY) * gain_grad * gain_grad
        gain_new = gains - GAIN_RATE * gain_grad / (jnp.sqrt(gain_moment_new) + 1e-08)
        qkv_owned, out_owned, ffn_owned, down_owned = scatter_all(
            qkv_weight_grad, out_weight_grad, ffn_weight_grad, down_weight_grad, count
        )
        attn_grad = jnp.concatenate([qkv_owned, out_owned[None]], 0)[:, None]
        ffn_grad = ffn_owned[:, None]
        down_grad = down_owned[None]
        attn_left_new, attn_right_new, attn_new = plain_precondition(
            attn_grad,
            attn_left,
            attn_right,
            attn_left_root,
            attn_right_root,
            jnp.concatenate([qkv_master, out_master[None]], 0),
        )
        qkv_new, out_new = attn_new[:3], attn_new[3]
        ffn_left_new, ffn_right_new, ffn_new = plain_precondition(
            ffn_grad, ffn_left, ffn_right, ffn_left_root, ffn_right_root, ffn_master
        )
        down_left_new, down_right_new, down_new = plain_precondition(
            down_grad, down_left, down_right, down_left_root, down_right_root, down_master
        )
    return (
        layer_out,
        input_grad,
        gain_grad,
        gain_moment_new,
        gain_new,
        attn_grad,
        attn_left_new,
        attn_right_new,
        qkv_new,
        out_new,
        ffn_grad,
        ffn_left_new,
        ffn_right_new,
        ffn_new,
        down_grad,
        down_left_new,
        down_right_new,
        down_new,
    )


def solution(mesh):
    tokens = P(("dp", "narrow"), None)
    stacked = P(None, "narrow", "dp", None, None)
    single = P("narrow", "dp", None, None)
    return jax.shard_map(
        body,
        mesh=mesh,
        in_specs=(tokens, tokens, P(), P(), stacked, single, stacked, single)
        + (stacked,) * 8
        + (single,) * 4,
        out_specs=(tokens, tokens, P(), P(), P())
        + (stacked,) * 4
        + (single,)
        + (stacked,) * 4
        + (single,) * 4,
        check_vma=False,
    )
```

```python
import functools
import math

import jax
import jax.numpy as jnp
from jax import lax
from jax.experimental import pallas as pl
from jax.experimental.pallas import tpu as pltpu
from jax.sharding import PartitionSpec as P

D = 768
HEAD_DIM = 64
FF = 2048
LEN = 1024
GRID = 16
DBLK = D // GRID
FBLK = FF // GRID
HALF_GRID = GRID // 2
HALF_D = D // 2
HALF_FF = FF // 2
PAIR = 2 * HEAD_DIM
ROWS = 256

EPSILON = 1e-05
DECAY = 0.5
STEP_RATE = 0.25
GAIN_RATE = 0.1
NEG_FILL = -1e30
HIGHEST_PRECISION = lax.Precision.HIGHEST
BF16 = jnp.bfloat16
F32 = jnp.float32
VMEM_MIB = 18
DENSE_ROWS = 512
TILE = 256
WIDE_TILE = 512
SMALL_MIB = 8
PACK_MIB = 60
STATE_ROWS = 16


def dot_nn(left, right):
    return lax.dot_general(left, right, (((1,), (0,)), ((), ())), preferred_element_type=F32)


def dot_nt(left, right):
    return lax.dot_general(left, right, (((1,), (1,)), ((), ())), preferred_element_type=F32)


def dot_tn(left, right):
    return lax.dot_general(left, right, (((0,), (0,)), ((), ())), preferred_element_type=F32)


def kernel_params(mib=VMEM_MIB):
    return pltpu.CompilerParams(vmem_limit_bytes=mib * 1024 * 1024)


def cost():
    return pl.CostEstimate(flops=0, bytes_accessed=0, transcendentals=0)


def whole_call(kernel, inputs, shapes, name, scalars=0, mib=SMALL_MIB, scratch=()):
    vmem = pl.BlockSpec(memory_space=pltpu.VMEM)
    smem = pl.BlockSpec(memory_space=pltpu.SMEM)
    return pl.pallas_call(
        kernel,
        in_specs=[smem] * scalars + [vmem] * (len(inputs) - scalars),
        out_specs=[vmem] * len(shapes),
        out_shape=shapes,
        scratch_shapes=list(scratch),
        compiler_params=kernel_params(mib),
        cost_estimate=cost(),
        name=name,
    )(*inputs)


def over_rows(length, rows, work):
    @pl.loop(0, length // rows)
    def _(step):
        work(pl.ds(pl.multiple_of(step * rows, rows), rows))


def lower_lanes(shape):
    return lax.broadcasted_iota(jnp.int32, shape, 1) % HEAD_DIM < HEAD_DIM // 2


def turn(features, cosine, sine_part, lower):
    half = HEAD_DIM // 2
    partner = jnp.where(
        lower, pltpu.roll(features, PAIR - half, 1), pltpu.roll(features, half, 1)
    )
    return features * cosine + partner * sine_part


def project_kernel(x_ref, gain_ref, w_ref, cos_ref, sin_ref, n1_ref, q_ref, k_ref, v_ref):
    lower = lower_lanes((DENSE_ROWS, PAIR))

    def work(rows):
        x = x_ref[rows, :].astype(F32)
        scale = lax.rsqrt(jnp.mean(x * x, -1, keepdims=True) + EPSILON)
        normed = (x * scale * gain_ref[0:1, :]).astype(BF16)
        n1_ref[rows, :] = normed
        cosine, sine_part = cos_ref[rows, :], sin_ref[rows, :]
        both = dot_nn(normed, w_ref[...])
        for tile in range(HALF_D // PAIR):
            lanes = slice(tile * PAIR, (tile + 1) * PAIR)
            query = both[:, tile * PAIR : (tile + 1) * PAIR]
            key = both[:, HALF_D + tile * PAIR : HALF_D + (tile + 1) * PAIR]
            turned = turn(query, cosine, sine_part, lower).astype(BF16)
            q_ref[rows, lanes] = turned * BF16(1.0 / math.sqrt(HEAD_DIM))
            k_ref[rows, lanes] = turn(key, cosine, sine_part, lower).astype(BF16)
        v_ref[rows, :] = both[:, 2 * HALF_D :].astype(BF16)

    over_rows(x_ref.shape[0], DENSE_ROWS, work)


def project(x, gains, weight, cosine, sine_part):
    length = x.shape[0]
    half = jax.ShapeDtypeStruct((length, HALF_D), BF16)
    shapes = [jax.ShapeDtypeStruct((length, D), BF16), half, half, half]
    return whole_call(
        project_kernel, [x, gains, weight, cosine, sine_part], shapes, "project", mib=VMEM_MIB
    )


def attend_kernel(q_ref, k_ref, v_ref, o_ref, lse_ref):
    @pl.loop(0, q_ref.shape[1] // PAIR)
    def _(pair):
        lanes = pl.ds(pl.multiple_of(pair * PAIR, PAIR), PAIR)
        rows = pl.ds(pl.multiple_of(pair * 8, 8), 8)
        attend_pair(
            *(ref.at[:, lanes] for ref in (q_ref, k_ref, v_ref, o_ref)), lse_ref.at[rows, :]
        )


def attend_pair(q_ref, k_ref, v_ref, o_ref, lse_ref):
    length = q_ref.shape[0]
    first_head = lax.broadcasted_iota(jnp.int32, (ROWS, PAIR), 1) < HEAD_DIM
    keys = k_ref[...]
    values = jnp.concatenate([v_ref[...], jnp.ones((length, PAIR), BF16)], 1)
    causal = lax.broadcasted_iota(jnp.int32, (2 * ROWS, ROWS), 0) % ROWS >= (
        lax.broadcasted_iota(jnp.int32, (2 * ROWS, ROWS), 1)
    )
    for block in range(length // ROWS):
        rows = slice(block * ROWS, (block + 1) * ROWS)
        width = (block + 1) * ROWS
        query_block = q_ref[rows, :]
        zero = jnp.zeros_like(query_block)
        query = jnp.concatenate(
            [jnp.where(first_head, query_block, zero), jnp.where(first_head, zero, query_block)], 0
        )
        scores = jnp.where(causal, dot_nt(query, keys[block * ROWS : width]), NEG_FILL)
        if block:
            scores = jnp.concatenate([dot_nt(query, keys[: block * ROWS]), scores], 1)
        top = jnp.max(scores, 1, keepdims=True)
        exponent = jnp.exp(scores - top).astype(BF16)
        product = dot_nn(exponent, values[:width])
        total = product[:, PAIR:]
        out = product[:, :PAIR] / total
        sums = top + jnp.log(total)
        o_ref[rows, :] = jnp.where(first_head, out[:ROWS], out[ROWS:]).astype(BF16)
        lane = lax.broadcasted_iota(jnp.int32, (ROWS, PAIR), 1)
        lse_ref[:, rows] = jnp.transpose(jnp.where(lane == 0, sums[:ROWS], sums[ROWS:]))[:8, :]


def attend(q, k, v):
    length = q.shape[0]
    shapes = [
        jax.ShapeDtypeStruct(q.shape, BF16),
        jax.ShapeDtypeStruct((8 * (q.shape[1] // PAIR), length), F32),
    ]
    return whole_call(attend_kernel, [q, k, v], shapes, "attend", mib=VMEM_MIB)


def attend_back_kernel(
    q_ref, k_ref, v_ref, do_ref, o_ref, lse_ref, cos_ref, sin_ref, grad_ref, dqt_ref
):
    @pl.loop(0, q_ref.shape[1] // PAIR)
    def _(pair):
        lanes = pl.ds(pl.multiple_of(pair * PAIR, PAIR), PAIR)
        rows = pl.ds(pl.multiple_of(pair * 8, 8), 8)
        attend_back_pair(
            *(ref.at[:, lanes] for ref in (q_ref, k_ref, v_ref, do_ref, o_ref)),
            lse_ref.at[rows, :],
            cos_ref,
            sin_ref,
            *(
                grad_ref.at[:, pl.ds(pl.multiple_of(at * HALF_D + pair * PAIR, PAIR), PAIR)]
                for at in range(3)
            ),
            dqt_ref,
        )


def attend_back_pair(
    q_ref, k_ref, v_ref, do_ref, o_ref, lse_ref, cos_ref, sin_ref, dq_ref, dk_ref, dv_ref, dqt_ref
):
    length = q_ref.shape[0]
    first_head = lax.broadcasted_iota(jnp.int32, (length, PAIR), 1) < HEAD_DIM
    zero = BF16(0)
    queries = [
        jnp.where(first_head, q_ref[...], zero),
        jnp.where(first_head, zero, q_ref[...]),
    ]
    grads = [
        jnp.where(first_head, do_ref[...], zero),
        jnp.where(first_head, zero, do_ref[...]),
    ]
    product = do_ref[...].astype(F32) * o_ref[...].astype(F32)
    head_row = lax.broadcasted_iota(jnp.int32, (8, PAIR), 0)
    head_lane = lax.broadcasted_iota(jnp.int32, (8, PAIR), 1) // HEAD_DIM
    inner = lax.dot_general(
        (head_row == head_lane).astype(F32),
        product,
        (((1,), (1,)), ((), ())),
        preferred_element_type=F32,
        precision=HIGHEST_PRECISION,
    )
    turned_keys = jnp.transpose(k_ref[...].astype(F32)).astype(BF16)
    first_rows = lax.broadcasted_iota(jnp.int32, turned_keys.shape, 0) < HEAD_DIM
    key_heads = [
        jnp.where(first_rows, turned_keys, zero),
        jnp.where(first_rows, zero, turned_keys),
    ]
    causal = lax.broadcasted_iota(jnp.int32, (ROWS, ROWS), 0) <= lax.broadcasted_iota(
        jnp.int32, (ROWS, ROWS), 1
    )
    dqt_ref[...] = jnp.zeros_like(dqt_ref)
    lower = lower_lanes((ROWS, PAIR))
    for block in range(length // ROWS):
        rows = slice(block * ROWS, (block + 1) * ROWS)
        start = block * ROWS
        key_block, value_block = k_ref[rows, :], v_ref[rows, :]
        dk = jnp.zeros((ROWS, PAIR), F32)
        dv = jnp.zeros((ROWS, PAIR), F32)
        for head in range(2):
            scores = dot_nt(key_block, queries[head][start:])
            probs = jnp.exp(scores - lse_ref[head : head + 1, start:])
            diagonal = jnp.where(causal, probs[:, :ROWS], 0.0)
            if start + ROWS == length:
                probs = diagonal
            else:
                probs = jnp.concatenate([diagonal, probs[:, ROWS:]], 1)
            prob_grad = dot_nt(value_block, grads[head][start:])
            score_grad = (probs * (prob_grad - inner[head : head + 1, start:])).astype(BF16)
            dv = dv + dot_nn(probs.astype(BF16), grads[head][start:])
            dk = dk + dot_nn(score_grad, queries[head][start:])
            dqt_ref[:, start:] += dot_nn(key_heads[head][:, rows], score_grad)
        dk_ref[rows, :] = turn(dk, cos_ref[rows, :], -sin_ref[rows, :], lower).astype(BF16)
        dv_ref[rows, :] = dv.astype(BF16)
    for block in range(length // ROWS):
        rows = slice(block * ROWS, (block + 1) * ROWS)
        dq = jnp.transpose(dqt_ref[:, rows]) * (1.0 / math.sqrt(HEAD_DIM))
        dq_ref[rows, :] = turn(dq, cos_ref[rows, :], -sin_ref[rows, :], lower).astype(BF16)


def attend_back(q, k, v, grad, o, lse, cosine, sine_part):
    return whole_call(
        attend_back_kernel,
        [q, k, v, grad, o, lse, cosine, sine_part],
        [jax.ShapeDtypeStruct((q.shape[0], 3 * q.shape[1]), BF16)],
        "attend_back",
        mib=VMEM_MIB,
        scratch=[pltpu.VMEM((PAIR, q.shape[0]), F32)],
    )[0]


def ffn_kernel(
    x_ref, o_ref, o_far_ref, wo_ref, wo_far_ref, gain_ref, wg_ref, wu_ref,
    x1_ref, n2_ref, gate_ref, up_ref, hidden_ref,
):
    def work(rows):
        middle = (
            x_ref[rows, :].astype(F32)
            + dot_nn(o_ref[rows, :], wo_ref[...])
            + dot_nn(o_far_ref[rows, :], wo_far_ref[...])
        )
        x1_ref[rows, :] = middle
        scale = lax.rsqrt(jnp.mean(middle * middle, -1, keepdims=True) + EPSILON)
        normed = (middle * scale * gain_ref[1:2, :]).astype(BF16)
        n2_ref[rows, :] = normed

        @pl.loop(0, HALF_FF // TILE)
        def _(tile):
            lanes = pl.ds(pl.multiple_of(tile * TILE, TILE), TILE)
            gate = dot_nn(n2_ref[rows, :], wg_ref[:, lanes])
            up = dot_nn(n2_ref[rows, :], wu_ref[:, lanes])
            gate_ref[rows, lanes] = gate
            up_ref[rows, lanes] = up
            hidden_ref[rows, lanes] = (gate * jax.nn.sigmoid(gate) * up).astype(BF16)

    over_rows(x_ref.shape[0], DENSE_ROWS, work)


def ffn(*inputs):
    length = inputs[0].shape[0]
    shapes = [
        jax.ShapeDtypeStruct((length, width), kind)
        for width, kind in ((D, F32), (D, BF16), (HALF_FF, F32), (HALF_FF, F32), (HALF_FF, BF16))
    ]
    return whole_call(ffn_kernel, inputs, shapes, "ffn", mib=VMEM_MIB)


def ffn_out_kernel(hidden_ref, wdt_ref, part_ref):
    def work(rows):
        part_ref[rows, :] = dot_nt(hidden_ref[rows, :], wdt_ref[...]).astype(BF16)

    over_rows(hidden_ref.shape[0], DENSE_ROWS, work)


def ffn_out(hidden, wdt):
    shape = jax.ShapeDtypeStruct((hidden.shape[0], D), BF16)
    return whole_call(ffn_out_kernel, [hidden, wdt], [shape], "ffn_out", mib=VMEM_MIB)[0]


def ffn_back_kernel(cot_ref, gate_ref, up_ref, wdt_ref, wg_ref, wu_ref, dgu_ref, dn2_ref):
    def work(rows):
        @pl.loop(0, HALF_FF // WIDE_TILE)
        def _(tile):
            lanes = pl.ds(pl.multiple_of(tile * WIDE_TILE, WIDE_TILE), WIDE_TILE)
            up_lanes = pl.ds(pl.multiple_of(HALF_FF + tile * WIDE_TILE, WIDE_TILE), WIDE_TILE)
            hidden_grad = dot_nn(cot_ref[rows, :], wdt_ref[:, lanes])
            gate, up = gate_ref[rows, lanes], up_ref[rows, lanes]
            sigma = jax.nn.sigmoid(gate)
            gate_grad = hidden_grad * up * sigma * (1.0 + gate * (1.0 - sigma))
            dgu_ref[rows, lanes] = gate_grad.astype(BF16)
            dgu_ref[rows, up_lanes] = (hidden_grad * gate * sigma).astype(BF16)

        @pl.loop(0, D // TILE)
        def _(tile):
            lanes = pl.ds(pl.multiple_of(tile * TILE, TILE), TILE)
            dn2 = dot_nt(dgu_ref[rows, :HALF_FF], wg_ref[lanes, :]) + dot_nt(
                dgu_ref[rows, HALF_FF:], wu_ref[lanes, :]
            )
            dn2_ref[rows, lanes] = dn2.astype(BF16)

    over_rows(cot_ref.shape[0], DENSE_ROWS, work)


def ffn_back(cot, gate, up, wdt, wg, wu):
    shapes = [jax.ShapeDtypeStruct((cot.shape[0], width), BF16) for width in (FF, D)]
    return whole_call(
        ffn_back_kernel, [cot, gate, up, wdt, wg, wu], shapes, "ffn_back", mib=VMEM_MIB
    )


def middle_back_kernel(
    cot_ref, x1_ref, near_ref, far_ref, gain_ref, wo_ref, dx1_ref, da_ref, do_ref, g2_ref
):
    g2_ref[...] = jnp.zeros_like(g2_ref)

    def work(rows):
        middle = x1_ref[rows, :]
        scale = lax.rsqrt(jnp.mean(middle * middle, -1, keepdims=True) + EPSILON)
        grad = near_ref[rows, :].astype(F32) + far_ref[rows, :].astype(F32)
        weighted = grad * gain_ref[1:2, :]
        inner = jnp.mean(weighted * middle, -1, keepdims=True)
        middle_grad = (
            cot_ref[rows, :].astype(F32)
            + scale * weighted
            - middle * (scale * scale * scale * inner)
        )
        dx1_ref[rows, :] = middle_grad
        branch = middle_grad.astype(BF16)
        da_ref[rows, :] = branch
        do_ref[rows, :] = dot_nt(branch, wo_ref[...]).astype(BF16)
        g2_ref[...] += jnp.sum(grad * middle * scale, 0, keepdims=True)

    over_rows(cot_ref.shape[0], DENSE_ROWS, work)


def middle_back(*inputs):
    length = inputs[0].shape[0]
    shapes = [
        jax.ShapeDtypeStruct(shape, kind)
        for shape, kind in (
            ((length, D), F32),
            ((length, D), BF16),
            ((length, HALF_D), BF16),
            ((1, D), F32),
        )
    ]
    return whole_call(middle_back_kernel, inputs, shapes, "middle_back", mib=VMEM_MIB)


def input_back_kernel(x_ref, dqkv_ref, w_ref, part_ref, g1_ref):
    g1_ref[...] = jnp.zeros_like(g1_ref)

    def work(rows):
        grad = dot_nt(dqkv_ref[rows, :], w_ref[...])
        part_ref[rows, :] = grad.astype(BF16)
        x = x_ref[rows, :].astype(F32)
        scale = lax.rsqrt(jnp.mean(x * x, -1, keepdims=True) + EPSILON)
        g1_ref[...] += jnp.sum(grad * x * scale, 0, keepdims=True)

    over_rows(x_ref.shape[0], DENSE_ROWS, work)


def input_back(x, dqkv, w):
    shapes = [jax.ShapeDtypeStruct(x.shape, BF16), jax.ShapeDtypeStruct((1, D), F32)]
    return whole_call(input_back_kernel, [x, dqkv, w], shapes, "input_back", mib=VMEM_MIB)


def pair_up(bit, count):
    return [(i, i ^ bit) for i in range(count)]


def after(value, *others):
    return lax.optimization_barrier((value,) + others)[0]


def along(values, bit, count):
    return lax.ppermute(values, "dp", pair_up(bit, count))


def shifted(values, steps, count):
    return lax.ppermute(values, "dp", [(i, (i + 4 * steps) % count) for i in range(count)])


def other_core(values):
    return lax.ppermute(values, "narrow", [(0, 1), (1, 0)])


def all_shifted(values, count):
    return [shifted(values, step, count) for step in range(1, count // 4)]


def copy_columns(sources, outputs, name):
    rows = sources[0].shape[0]
    shapes = [
        jax.ShapeDtypeStruct((rows, sum(stop - start for _, start, stop in parts)), BF16)
        for parts in outputs
    ]

    def kernel(*refs):
        for out_ref, parts in zip(refs[len(sources) :], outputs):
            at = 0
            for number, start, stop in parts:
                out_ref[:, at : at + stop - start] = refs[number][:, start:stop]
                at += stop - start

    return whole_call(kernel, sources, shapes, name)


def block_rows(owner):
    return pl.ds(pl.multiple_of(owner * DBLK, 16), DBLK)


def block_lanes(index, width):
    return pl.ds(pl.multiple_of(index * width, 128), width)


def place_qkv_out(owner, start, piece, qkv_ref, out_ref):
    cut, stop = 3 * HALF_D, start + piece.shape[1]
    if start < cut:
        end = min(stop, cut)
        qkv_ref[block_rows(owner), start:end] = piece[:, : end - start]
    if stop > cut:
        begin = max(start, cut)
        lanes = pl.ds(pl.multiple_of(owner % 2 * HALF_D + (begin - cut), 128), stop - begin)
        out_ref[block_rows(owner // 2), lanes] = piece[:, begin - start :]


def place_gate_up(owner, start, piece, gate_ref, up_ref):
    stop = start + piece.shape[1]
    if start < HALF_FF:
        end = min(stop, HALF_FF)
        gate_ref[block_rows(owner), start:end] = piece[:, : end - start]
    if stop > HALF_FF:
        begin = max(start, HALF_FF)
        up_ref[block_rows(owner), begin - HALF_FF : stop - HALF_FF] = piece[:, begin - start :]


def place_down(owner, start, piece, out_ref):
    lanes = block_lanes(owner // 2, FBLK)
    for block in range(piece.shape[1] // FBLK):
        rows = block_rows(owner % 2 * HALF_GRID + start // FBLK + block)
        out_ref[rows, lanes] = piece[:, block * FBLK : (block + 1) * FBLK]


def assemble(me, high, sources, entries, place, shapes, name, begun=()):
    sources = list(sources)

    def kernel(me_ref, *refs):
        x, y, z = me_ref[0] % 2, me_ref[0] // 2 % 2, me_ref[0] // 4
        out_refs = refs[len(sources) + len(begun) :]
        for ref, out_ref in zip(refs[len(sources) :], out_refs if begun else ()):
            out_ref[...] = ref[...]
        for number, start, width, step, over_y, over_x, first in entries:
            slow = (z - step + high) % high
            from_y = 1 - y if over_y else y
            from_x = 1 - x if over_x else x
            piece = refs[number][:, start : start + width]
            place(slow * 4 + from_y * 2 + from_x, first, piece, *out_refs)

    return whole_call(
        kernel,
        [me] + sources + list(begun),
        [jax.ShapeDtypeStruct(shape, BF16) for shape in shapes],
        name,
        1,
    )


def pack_kernel(qkv_ref, out_ref, ffn_ref, down_ref, first_ref, second_ref, slab_ref, *scratch):
    held, sems = scratch[:-1], scratch[-1]
    copies = [
        pltpu.make_async_copy(ref, here, sems.at[number])
        for number, (ref, here) in enumerate(zip((qkv_ref, out_ref, ffn_ref, down_ref), held))
    ]
    for copy in copies:
        copy.start()

    def row(ref, matrix):
        return jnp.concatenate([ref[matrix, block].astype(BF16) for block in range(HALF_GRID)], 1)

    at = 0
    for copy, ref in zip(copies, held):
        copy.wait()
        for matrix in range(ref.shape[0]):
            part = row(ref, matrix)
            stop = at + part.shape[1]
            slab_ref[:, at:stop] = part
            if stop <= first_ref.shape[1]:
                first_ref[:, at:stop] = part
            elif stop <= first_ref.shape[1] + second_ref.shape[1]:
                second_ref[:, at - first_ref.shape[1] : stop - first_ref.shape[1]] = part
            at = stop


def pack(*masters):
    vmem = pl.BlockSpec(memory_space=pltpu.VMEM)
    return pl.pallas_call(
        pack_kernel,
        in_specs=[pl.BlockSpec(memory_space=pl.ANY)] * len(masters),
        out_specs=[vmem] * 3,
        out_shape=[
            jax.ShapeDtypeStruct((DBLK, width), BF16)
            for width in (4 * HALF_D, FF, 4 * HALF_D + 3 * HALF_FF)
        ],
        scratch_shapes=[pltpu.VMEM(master.shape, F32) for master in masters]
        + [pltpu.SemaphoreType.DMA((len(masters),))],
        compiler_params=kernel_params(PACK_MIB),
        cost_estimate=cost(),
        name="pack",
    )(*masters)


def tables_kernel(cos_ref, sin_ref, cosine_ref, sine_ref):
    cosine, sine = cos_ref[...], sin_ref[...]
    cosine_ref[...] = jnp.concatenate([cosine] * 4, 1)
    sine_ref[...] = jnp.concatenate([-sine, sine] * 2, 1)


def side_by_side(blocks):
    matrices, many, height, width = blocks.shape
    return blocks.transpose(2, 0, 1, 3).reshape(height, matrices * many * width)


def gather_by_name(qkv, out, ffn_part, down):
    qkv_all = lax.all_gather(qkv, "dp", axis=1, tiled=True)
    out_all = lax.all_gather(out[0], "dp", axis=0, tiled=True)
    ffn_all = lax.all_gather(ffn_part, "dp", axis=1, tiled=True)
    down_all = lax.all_gather(down, "dp", axis=0, tiled=True)
    w_qkv = qkv_all.reshape(3, GRID, HALF_GRID, DBLK, DBLK).transpose(1, 3, 0, 2, 4)
    w_out = out_all.reshape(HALF_GRID, GRID, DBLK, DBLK).transpose(0, 2, 1, 3)
    w_ffn = ffn_all.reshape(2, GRID, HALF_GRID, DBLK, FBLK).transpose(0, 1, 3, 2, 4)
    w_down = down_all.reshape(HALF_GRID, GRID, FBLK, DBLK).transpose(1, 3, 0, 2)
    w_ffn = w_ffn.reshape(2, D, HALF_FF)
    return (
        w_qkv.reshape(D, 3 * HALF_D),
        w_out.reshape(HALF_D, D),
        w_ffn[0],
        w_ffn[1],
        w_down.reshape(D, HALF_FF),
    )


def take_rows(owner, ref):
    return ref[block_rows(owner), :]


def take_out(owner, ref):
    return ref[block_rows(owner // 2), pl.ds(pl.multiple_of(owner % 2 * HALF_D, 128), HALF_D)]


def take_down(owner, ref):
    lanes = pl.ds(pl.multiple_of(owner // 2 * FBLK, 128), FBLK)
    return jnp.concatenate(
        [ref[block_rows(owner % 2 * HALF_GRID + block), lanes] for block in range(HALF_GRID)], 1
    )


def paired(values):
    high = values.astype(BF16)
    low = (values - high.astype(F32)).astype(BF16)
    rest = jnp.zeros((DBLK - 2 * values.shape[0], values.shape[1]), BF16)
    return jnp.concatenate([high, low, rest], 0)


def unpaired(pair):
    rows = STATE_ROWS
    return pair[:rows].astype(F32) + pair[rows : 2 * rows].astype(F32)


def reduction(takes, columns, count, me, grads):
    high = count // 4
    half = high // 2
    many = len(grads)

    def step(kernel, inputs, shapes, name):
        return whole_call(kernel, [me] + grads + inputs, shapes, name, 1)

    def find(refs, slow, y, x, part):
        owner = slow * 4 + y * 2 + x
        found = [take(owner, ref) for take, ref in zip(takes, refs)]
        found = found[0] if len(found) == 1 else jnp.concatenate(found, 1)
        return found[:, part[0] : part[1]].astype(F32)

    def place(me_ref):
        return me_ref[0] % 2, me_ref[0] // 2 % 2, me_ref[0] // 4

    def piece(index, width=columns, start=0, every=None):
        first = index * (every or width) + start
        return pl.ds(pl.multiple_of(first, 128), width)

    def diagonal_kernel(me_ref, *refs):
        x, y, _ = place(me_ref)
        *guest_refs, to_y_ref, to_x_ref = refs[many:]
        for guest_ref in guest_refs:
            wide = guest_ref.shape[1] // 4
            middle = 3 * wide + wide // 2
            to_y_ref[:, half * columns :] = guest_ref[:, 3 * wide : middle].astype(BF16)
            to_x_ref[:, half * columns :] = guest_ref[:, middle:].astype(BF16)

        @pl.loop(0, half)
        def _(step):
            whole = (0, columns)
            to_y_ref[:, piece(step)] = find(refs, step, 1 - y, 1 - x, whole).astype(BF16)
            to_x_ref[:, piece(step)] = find(refs, half + step, 1 - y, 1 - x, whole).astype(BF16)

    def side_kernel(part, me_ref, *refs):
        x, y, _ = place(me_ref)
        by_y_ref, by_x_ref, *state_refs, to_x_ref, to_y_ref = refs[many:]
        width = part[1] - part[0]
        if state_refs:
            guest_ref = state_refs[1]
            wide = guest_ref.shape[1] // 4
            cut, start = wide // 2, high * width + 128
            by_y = by_y_ref[:, half * columns :].astype(F32)
            by_x = by_x_ref[:, half * columns :].astype(F32)
            to_x_ref[:, start : start + cut] = (guest_ref[:, wide : wide + cut] + by_y).astype(BF16)
            to_x_ref[:, start + cut :] = guest_ref[:, wide + cut : 2 * wide].astype(BF16)
            start = high * width
            to_y_ref[:, start : start + cut] = guest_ref[:, 2 * wide : 2 * wide + cut].astype(BF16)
            to_y_ref[:, start + cut :] = (
                guest_ref[:, 2 * wide + cut : 3 * wide] + by_x
            ).astype(BF16)

        @pl.loop(0, half)
        def _(step):
            lanes = piece(step, width, part[0], columns)
            for slow, by_y, by_x in ((step, by_y_ref, None), (half + step, None, by_x_ref)):
                to_x = find(refs, slow, y, 1 - x, part)
                to_y = find(refs, slow, 1 - y, x, part)
                if by_y is not None:
                    to_x = to_x + by_y[:, lanes].astype(F32)
                else:
                    to_y = to_y + by_x[:, lanes].astype(F32)
                to_x_ref[:, piece(slow, width)] = to_x.astype(BF16)
                to_y_ref[:, piece(slow, width)] = to_y.astype(BF16)

        if state_refs:
            to_x_ref[:, high * width : high * width + 128] = paired(state_refs[0][...])

    def slow_kernel(part, me_ref, *refs):
        x, y, z = place(me_ref)
        from_x_ref, from_y_ref, *state_refs = refs[many : len(refs) - high]
        out_refs = refs[len(refs) - high :]
        width = part[1] - part[0]
        if state_refs:
            before_ref, after_ref = state_refs
            lanes = slice(high * width, high * width + 128)
            state = unpaired(paired(before_ref[...])) + unpaired(from_x_ref[:, lanes])
            after_ref[...] = state
        for shift in range(high):
            rows = pl.ds(0, DBLK)
            slow = (z + shift) % high
            lanes = pl.ds(pl.multiple_of(slow * width, 128), width)
            total = (
                find(refs, slow, y, x, part)
                + from_x_ref[rows, lanes].astype(F32)
                + from_y_ref[rows, lanes].astype(F32)
            )
            out_refs[shift][:, :width] = total.astype(out_refs[shift].dtype)
            if state_refs and shift:
                out_refs[shift][:, width:] = paired(state)

    def rows(width, kind=BF16):
        return jax.ShapeDtypeStruct((DBLK, width), kind)

    state_shape = jax.ShapeDtypeStruct((STATE_ROWS, 128), F32)

    def first(*guest):
        extra = sum(array.shape[1] // 8 for array in guest)
        shapes = [rows(half * columns + extra)] * 2
        return step(diagonal_kernel, list(guest), shapes, "send_diagonal")

    def second(by_y, by_x, *state, part=(0, columns)):
        wide = high * (part[1] - part[0])
        extra = state[1].shape[1] // 4 if state else 0
        shapes = [rows(wide + extra + (128 if state else 0)), rows(wide + extra)]
        kernel = functools.partial(side_kernel, part)
        return step(kernel, [by_y, by_x, *state], shapes, "send_sides")

    def third(from_x, from_y, *state, part=(0, columns)):
        width = part[1] - part[0]
        shapes = [state_shape] * len(state) + [rows(width, F32)]
        shapes += [rows(width + 128 * len(state))] * (high - 1)
        kernel = functools.partial(slow_kernel, part)
        return step(kernel, [from_x, from_y, *state], shapes, "send_slow")

    return first, second, third


def ring_blocks(grad, me, high):
    def kernel(me_ref, grad_ref, *out_refs):
        x, y, z = me_ref[0] % 2, me_ref[0] // 2 % 2, me_ref[0] // 4
        for hop, out_ref in enumerate(out_refs):
            slow = (z - 1 - hop + high) % high
            for part in range(4):
                from_x = 1 - x if part % 2 else x
                from_y = 1 - y if part // 2 else y
                block = take_down(slow * 4 + from_y * 2 + from_x, grad_ref)
                lanes = slice(part * HALF_FF, (part + 1) * HALF_FF)
                out_ref[:, lanes] = block.astype(out_ref.dtype)

    shapes = [
        jax.ShapeDtypeStruct((DBLK, 4 * HALF_FF), BF16 if hop < high - 1 else F32)
        for hop in range(high)
    ]
    return whole_call(kernel, [me, grad], shapes, "ring_blocks", 1)


def ring_add_kernel(far_ref, own_ref, out_ref):
    total = far_ref[...].astype(F32) + own_ref[...].astype(F32)
    out_ref[...] = total.astype(out_ref.dtype)


def ring_add(far, own):
    shape = jax.ShapeDtypeStruct(own.shape, own.dtype)
    return whole_call(ring_add_kernel, [far, own], [shape], "ring_add")[0]


def send_first(to_y, to_x, count):
    return along(to_y, 2, count), along(to_x, 1, count)


def send_second(to_x, to_y, count):
    return along(to_x, 1, count), along(to_y, 2, count)


def send_third(own, *others, count):
    return [own] + [shifted(block, step + 1, count) for step, block in enumerate(others)]


def scatter_all(qkv, out, ffn_grad, down, count):
    qkv = qkv.reshape(GRID, DBLK, 3, HALF_GRID, DBLK).transpose(2, 0, 3, 1, 4)
    out = out.reshape(HALF_GRID, DBLK, GRID, DBLK).transpose(0, 2, 1, 3)
    ffn_grad = ffn_grad.reshape(GRID, DBLK, 2, HALF_GRID, FBLK).transpose(2, 0, 3, 1, 4)
    down = down.reshape(GRID, DBLK, HALF_GRID, FBLK).transpose(2, 0, 3, 1)
    return (
        lax.psum_scatter(
            qkv.reshape(3, -1, DBLK, DBLK), "dp", scatter_dimension=1, tiled=True
        ),
        lax.psum_scatter(out.reshape(-1, DBLK, DBLK), "dp", scatter_dimension=0, tiled=True),
        lax.psum_scatter(
            ffn_grad.reshape(2, -1, DBLK, FBLK), "dp", scatter_dimension=1, tiled=True
        ),
        lax.psum_scatter(down.reshape(-1, FBLK, DBLK), "dp", scatter_dimension=0, tiled=True),
    )


def gain_rows_kernel(one_ref, two_ref, out_ref):
    def rows(values):
        return [values[:, at : at + 128] for at in range(0, D, 128)]

    parts = rows(one_ref[...]) + rows(0.5 * two_ref[...])
    parts.append(jnp.zeros((STATE_ROWS - len(parts), 128), F32))
    out_ref[...] = jnp.concatenate(parts, 0)


def gain_rows(gain_one, gain_two):
    shape = jax.ShapeDtypeStruct((STATE_ROWS, 128), F32)
    return whole_call(gain_rows_kernel, [gain_one, gain_two], [shape], "gain_rows")[0]


def add_kernel(left_ref, right_ref, out_ref):
    out_ref[...] = left_ref[...] + right_ref[...]


def added(left, right, name):
    return whole_call(add_kernel, [left, right], [jax.ShapeDtypeStruct(left.shape, F32)], name)[0]


def slow_state_kernel(own_ref, *refs):
    out_ref = refs[-1]
    columns = refs[0].shape[1] - 128
    values = [unpaired(paired(own_ref[...]))] + [unpaired(ref[:, columns:]) for ref in refs[:-1]]
    while len(values) > 1:
        half = len(values) // 2
        values = [values[index] + values[index + half] for index in range(half)]
    out_ref[...] = values[0]


def slow_state(own, blocks):
    shape = jax.ShapeDtypeStruct(own.shape, F32)
    return whole_call(slow_state_kernel, [own] + blocks, [shape], "slow_state")[0]


def gains_kernel(near_ref, far_ref, gain_ref, moment_ref, grad_ref, moment_new_ref, gain_new_ref):
    total = near_ref[...] + far_ref[...]
    count = D // 128
    grad = jnp.concatenate(
        [
            jnp.concatenate([total[at + row : at + row + 1] for row in range(count)], 1)
            for at in (0, count)
        ],
        0,
    )
    grad_ref[...] = grad
    moment = DECAY * moment_ref[...] + (1.0 - DECAY) * grad * grad
    moment_new_ref[...] = moment
    gain_new_ref[...] = gain_ref[...] - GAIN_RATE * grad / (jnp.sqrt(moment) + 1e-08)


def full_dot(left, right, left_dim, right_dim):
    return lax.dot_general(
        left,
        right,
        (((left_dim,), (right_dim,)), ((), ())),
        preferred_element_type=F32,
        precision=lax.Precision.DEFAULT,
    )


def precondition(
    parts,
    width,
    left,
    right,
    left_root,
    right_root,
    masters,
    turned=False,
    matrices=None,
    carry=(),
    starts=None,
):
    starts = [0] * len(parts) if starts is None else starts
    counts = [master.shape[0] for master in masters]
    spots = [(which, here) for which, many in enumerate(counts) for here in range(many)]
    matrices = range(len(spots)) if matrices is None else matrices
    many = len(parts)

    def kernel(*refs):
        part_refs, refs, total_ref = refs[:many], refs[many:-1], refs[-1]
        left_ref, right_ref, left_root_ref, right_root_ref = refs[:4]
        master_refs, refs = refs[4 : 4 + len(counts)], refs[4 + len(counts) :]
        carry_refs, refs = refs[: len(carry)], refs[len(carry) :]
        grad_ref, left_new_ref, right_new_ref = refs[:3]
        new_refs = refs[3:]
        for matrix, (which, here) in enumerate(spots):
            if carry and matrix not in matrices:
                for out_ref, carry_ref in zip(refs[:3], carry_refs[:3]):
                    out_ref[matrix] = carry_ref[matrix]
                new_refs[which][here] = carry_refs[3 + which][here]
        wide = len(matrices) * HALF_GRID * width
        total = jnp.zeros((part_refs[0].shape[0], wide), F32)
        for ref, start in zip(part_refs, starts):
            total = total + ref[:, start : start + wide].astype(F32)
        total_ref[...] = total

        def update(which, here, matrix, block, grad):
            grad_ref[matrix, block] = grad
            outer, inner = full_dot(grad, grad, 1, 1), full_dot(grad, grad, 0, 0)
            if turned:
                outer, inner = inner, outer
                step = full_dot(grad, left_root_ref[matrix, block], 1, 1)
                step = full_dot(right_root_ref[matrix, block], step, 0, 0)
            else:
                step = full_dot(left_root_ref[matrix, block], grad, 1, 0)
                step = full_dot(step, right_root_ref[matrix, block], 1, 0)
            left_new_ref[matrix, block] = DECAY * left_ref[matrix, block] + (1.0 - DECAY) * outer
            right_new_ref[matrix, block] = DECAY * right_ref[matrix, block] + (1.0 - DECAY) * inner
            new_refs[which][here, block] = master_refs[which][here, block] - STEP_RATE * step

        def update_matrix(which, here, matrix, number):
            start = number * HALF_GRID * width
            if width % 128:
                lanes = pl.ds(pl.multiple_of(start, 128), HALF_GRID * width)
                row = total_ref[:, lanes]
                for block in range(HALF_GRID):
                    at = block * width
                    update(which, here, matrix, block, row[:, at : at + width])
            else:

                @pl.loop(0, HALF_GRID // 4)
                def _(step):
                    for block in [4 * step + number for number in range(4)]:
                        lanes = pl.ds(pl.multiple_of(start + block * width, 128), width)
                        update(which, here, matrix, block, total_ref[:, lanes])

        if len({spots[matrix][0] for matrix in matrices}) == 1:

            @pl.loop(0, len(matrices))
            def _(number):
                matrix = number + matrices[0]
                update_matrix(spots[matrices[0]][0], number + spots[matrices[0]][1], matrix, number)
        else:
            for number, matrix in enumerate(matrices):
                update_matrix(*spots[matrix], matrix, number)

    grads = jax.ShapeDtypeStruct((sum(counts),) + masters[0].shape[1:], F32)
    like = [jax.ShapeDtypeStruct(array.shape, F32) for array in (left, right)]
    news = [jax.ShapeDtypeStruct(master.shape, F32) for master in masters]
    inputs = list(parts) + [left, right, left_root, right_root] + list(masters)
    total = pltpu.VMEM((parts[0].shape[0], len(matrices) * HALF_GRID * width), F32)
    return whole_call(
        kernel, inputs + list(carry), [grads] + like + news, "precondition", scratch=[total]
    )


def plain_precondition(block_grad, left_stat, right_stat, left_root, right_root, master):
    new_left = DECAY * left_stat + (1.0 - DECAY) * jnp.einsum(
        "...ij,...kj->...ik", block_grad, block_grad, precision=HIGHEST_PRECISION
    )
    new_right = DECAY * right_stat + (1.0 - DECAY) * jnp.einsum(
        "...ji,...jk->...ik", block_grad, block_grad, precision=HIGHEST_PRECISION
    )
    turned = jnp.einsum("...ij,...jk->...ik", left_root, block_grad, precision=HIGHEST_PRECISION)
    turned = jnp.einsum("...ij,...jk->...ik", turned, right_root, precision=HIGHEST_PRECISION)
    return (new_left, new_right, master - STEP_RATE * turned)


def in_order_kernel(core_ref, mine_ref, other_ref, out_ref):
    rows = mine_ref.shape[0]
    core = core_ref[0]
    out_ref[pl.ds(pl.multiple_of(core * rows, 16), rows), :] = mine_ref[...]
    out_ref[pl.ds(pl.multiple_of((1 - core) * rows, 16), rows), :] = other_ref[...]


def in_order(mine, core):
    shape = jax.ShapeDtypeStruct((2 * mine.shape[0], mine.shape[1]), mine.dtype)
    return whole_call(in_order_kernel, [core, mine, other_core(mine)], [shape], "in_order", 1)[0]


def own_and_all(core_ref, rows, step):
    own = pl.ds(pl.multiple_of(step * ROWS, ROWS), ROWS)
    return own, pl.ds(pl.multiple_of(core_ref[0] * rows + step * ROWS, ROWS), ROWS)


def layer_out_kernel(core_ref, x1_ref, near_ref, far_ref, out_ref):
    @pl.loop(0, out_ref.shape[0] // ROWS)
    def _(step):
        own, rows = own_and_all(core_ref, out_ref.shape[0], step)
        total = x1_ref[rows, :] + near_ref[rows, :].astype(F32) + far_ref[rows, :].astype(F32)
        out_ref[own, :] = total.astype(BF16)


def input_grad_kernel(core_ref, x_ref, dx1_ref, near_ref, far_ref, gain_ref, out_ref):
    @pl.loop(0, out_ref.shape[0] // ROWS)
    def _(step):
        own, rows = own_and_all(core_ref, out_ref.shape[0], step)
        x = x_ref[rows, :].astype(F32)
        scale = lax.rsqrt(jnp.mean(x * x, -1, keepdims=True) + EPSILON)
        grad = near_ref[rows, :].astype(F32) + far_ref[rows, :].astype(F32)
        weighted = grad * gain_ref[0:1, :]
        inner = jnp.mean(weighted * x, -1, keepdims=True)
        out_ref[own, :] = dx1_ref[rows, :] + scale * weighted - x * (scale * scale * scale * inner)


def rotary_tables(length):
    frequency = jnp.power(10000.0, -2.0 * jnp.arange(HEAD_DIM // 2, dtype=F32) / HEAD_DIM)
    angles = (jnp.arange(length) % LEN).astype(F32)[:, None] * frequency[None, :]
    shape = jax.ShapeDtypeStruct((length, PAIR), F32)
    return whole_call(tables_kernel, [jnp.cos(angles), jnp.sin(angles)], [shape] * 2, "tables")


def body(
    tokens,
    cotangent,
    gains,
    gain_moments,
    qkv_master,
    out_master,
    ffn_master,
    down_master,
    attn_left,
    attn_right,
    attn_left_root,
    attn_right_root,
    ffn_left,
    ffn_right,
    ffn_left_root,
    ffn_right_root,
    down_left,
    down_right,
    down_left_root,
    down_right_root,
):
    count = lax.axis_size("dp")
    me = lax.axis_index("dp").astype(jnp.int32)[None]
    core = lax.axis_index("narrow").astype(jnp.int32)[None]
    own_rows = tokens.shape[0]
    by_hand = count == GRID

    if by_hand:
        high = count // 4
        first, second, slab = pack(
            qkv_master[:, 0], out_master, ffn_master[:, 0], jnp.swapaxes(down_master, 2, 3)
        )
        one, two, last = 4 * HALF_D, FF, HALF_FF
        width, half, ring_start = one + two + last, (one + two + last) // 2, one + two
        many = high - 1
        far_one = all_shifted(first, count)
        slab_x, slab_y = along(slab, 1, count), along(slab, 2, count)

    x, cot = in_order(tokens, core), in_order(cotangent, core)
    cosine, sine_part = rotary_tables(x.shape[0])

    if by_hand:
        chunk = [(number, 0, one) for number in range(many)]
        near_x, near_y = copy_columns(
            [after(far_one[0], x, cot, cosine, sine_part)] + far_one[1:] + [slab_x, slab_y],
            [chunk + [(many + 1, half, width)], chunk + [(many, 0, half)]],
            "end_round_one",
        )
        one_x, one_y = along(near_x, 1, count), along(near_y, 2, count)
        far_two = all_shifted(after(second, *far_one), count)
        tail = many * one
        one_a, one_b, near_two, square = copy_columns(
            [one_x, one_y] + far_two + [slab, slab_x, slab_y],
            [
                [(0, number * one, number * one + one // 2) for number in range(many)],
                [(1, number * one + one // 2, (number + 1) * one) for number in range(many)],
                [(2 + number, 0, two) for number in range(many)],
                [(2 + many + part, ring_start, width) for part in range(3)]
                + [(0, tail + ring_start - half, tail + width - half)],
            ],
            "end_round_two",
        )
        one_a, one_b = along(one_a, 2, count), along(one_b, 1, count)
        squares = [square, shifted(square, 1, count)]
        entries = [(0, 0, one, 0, 0, 0, 0), (1, 0, one, 0, 0, 1, 0), (2, 0, one, 0, 1, 0, 0)]
        entries.append((5, tail, one, 0, 1, 1, 0))
        for number in range(many):
            step, at = number + 1, number * one
            entries += [(3, at, one, step, 0, 0, 0), (4, at, one, step, 0, 1, 0)]
            entries += [(5, at, one, step, 1, 0, 0)]
        shapes = [(D, 3 * HALF_D), (HALF_D, D)]
        early = [slab, slab_x, slab_y, near_x, one_x, one_y]
        early[0] = after(slab, near_two)
        w_early = assemble(me, high, early, entries, place_qkv_out, shapes, "place_qkv_out")
        entries = []
        for number in range(many):
            step, at = number + 1, number * (one // 2)
            entries += [(0, at, one // 2, step, 1, 1, 0), (1, at, one // 2, step, 1, 1, one // 2)]
        w_qkv, w_out = assemble(
            me, high, [one_a, one_b], entries, place_qkv_out, shapes, "place_rest", w_early
        )
        near_late = after(near_two, one_a, one_b, w_early[0], squares[1])
        two_x, two_y = along(near_late, 1, count), along(near_late, 2, count)
        squares.append(shifted(after(squares[1], one_a, one_b, w_early[0]), 1, count))
    else:
        qkv, ffn_part = qkv_master[:, 0].astype(BF16), ffn_master[:, 0].astype(BF16)
        w_qkv, w_out, w_gate, w_up, w_down = gather_by_name(
            qkv, out_master.astype(BF16), ffn_part, down_master[0].astype(BF16)
        )
    normed_one, q, k, v = project(x, gains, w_qkv, cosine, sine_part)
    attended, lse = attend(q, k, v)
    attended_late, w_out_late = attended, w_out
    if by_hand:
        two_a, two_b = copy_columns(
            [after(two_x, attended, *squares[1:]), two_y],
            [
                [(0, number * two, number * two + two // 2) for number in range(many)],
                [(1, number * two + two // 2, (number + 1) * two) for number in range(many)],
            ],
            "end_round_four",
        )
        early = [slab, slab_x, slab_y, one_x, one_y, near_two, two_x, two_y]
        early[0] = after(slab, two_a)
        attended_late, w_out_late = after(attended, two_a), after(w_out, two_a)
        two_a, two_b = along(two_a, 2, count), along(two_b, 1, count)
        cut = half - one
        entries = [(0, one, two, 0, 0, 0, 0), (1, one, two, 0, 0, 1, 0), (2, one, two, 0, 1, 0, 0)]
        entries += [(4, tail + one, cut, 0, 1, 1, 0), (3, tail, two - cut, 0, 1, 1, cut)]
        for number in range(many):
            step, at = number + 1, number * two
            entries += [(5, at, two, step, 0, 0, 0), (6, at, two, step, 0, 1, 0)]
            entries += [(7, at, two, step, 1, 0, 0)]
        shapes = [(D, HALF_FF)] * 2
        w_early = assemble(me, high, early, entries, place_gate_up, shapes, "place_gate_up")
        entries = []
        for number in range(many):
            step, at = number + 1, number * (two // 2)
            entries += [(0, at, two // 2, step, 1, 1, 0), (1, at, two // 2, step, 1, 1, two // 2)]
        w_gate, w_up = assemble(
            me,
            high,
            [two_a, two_b],
            entries,
            place_gate_up,
            shapes,
            "place_rest",
            w_early,
        )
        for _ in range(3, high):
            squares.append(shifted(after(squares[-1], w_gate), 1, count))
    attended_far, w_out_far = other_core(attended_late), other_core(w_out_late)
    middle, normed_two, gate, up, hidden = ffn(
        x, attended, attended_far, w_out, w_out_far, gains, w_gate, w_up
    )

    if by_hand:
        squares[0] = after(squares[0], hidden)
        (w_down,) = assemble(
            me,
            high,
            squares,
            [
                (step, part * last, last, step, part // 2, part % 2, 0)
                for step in range(high)
                for part in range(4)
            ],
            place_down,
            [(D, HALF_FF)],
            "place_down",
        )
    down_weight_grad = dot_tn(cot, hidden)
    cot_late = cot
    if by_hand:
        ring = ring_blocks(down_weight_grad, me, high)
        passed = shifted(ring[0], 1, count)
        cot_late = after(cot, ring[0])
    ffn_back_grad, normed_part = ffn_back(cot_late, gate, up, w_down, w_gate, w_up)
    if by_hand:
        sent = ring_add(after(passed, normed_part), ring[1])
        passed = shifted(sent, 1, count)
        ffn_back_grad = after(ffn_back_grad, sent)
        normed_part = after(normed_part, sent)
    normed_far = other_core(normed_part)
    ffn_weight_grad = dot_tn(normed_two, ffn_back_grad)
    if by_hand:
        ffn_sum = reduction([take_rows], FF, count, me, [ffn_weight_grad])
        sent = ffn_sum[0]()
        normed_far = after(normed_far, sent[0])
        ffn_far = send_first(*sent, count)
    middle_grad, branch, attended_grad, gain_two = middle_back(
        cot, middle, normed_part, normed_far, gains, w_out
    )
    out_weight_grad = dot_tn(attended, branch)
    out_part = ffn_out(after(hidden, branch), w_down)
    out_part_late = out_part
    if by_hand:
        late = [branch, out_part, out_weight_grad]
        for number in range(2, high - 1):
            sent = ring_add(after(passed, *late), ring[number])
            passed = shifted(sent, 1, count)
            late.append(sent)
        sent = ffn_sum[1](after(ffn_far[0], *late), ffn_far[1])
        ffn_far = send_second(*sent, count)
        attended_grad = after(attended_grad, sent[0])
        out_part_late = after(out_part, sent[0])
    out_far = other_core(out_part_late)
    qkv_back_grad = attend_back(q, k, v, attended_grad, attended, lse, cosine, sine_part)
    layer_out = whole_call(
        layer_out_kernel,
        [core, after(middle, qkv_back_grad), out_part, out_far],
        [jax.ShapeDtypeStruct((own_rows, D), BF16)],
        "layer_out",
        1,
    )[0]
    if by_hand:
        down_near = ring_add(after(passed, qkv_back_grad, layer_out), ring[-1])
        ffn_sent = ffn_sum[2](after(ffn_far[0], qkv_back_grad, layer_out), ffn_far[1])
        ffn_parts = [ffn_sent[0]] + [
            shifted(block, step + 1, count)
            for step, block in enumerate(ffn_sent[1:])
            if step + 1 != high // 2
        ]
        qkv_back_grad = after(qkv_back_grad, ffn_sent[0])
    qkv_weight_grad = dot_tn(normed_one, qkv_back_grad)
    if by_hand:
        late_sum = reduction(
            [take_rows, take_out], 4 * HALF_D, count, me, [qkv_weight_grad, out_weight_grad]
        )
        sent = late_sum[0](down_near)
        late_far = list(send_first(*sent, count))
        qkv_back_grad = after(qkv_back_grad, sent[0])
    input_part, gain_one = input_back(x, qkv_back_grad, w_qkv)
    input_part_late = input_part
    if by_hand:
        state = gain_rows(gain_one, gain_two)
        state = added(state, other_core(state), "add_gains")
        late_cut = 2 * HALF_D
        parts = [(0, late_cut), (late_cut, 2 * late_cut)]
        late_far[0] = after(late_far[0], *ffn_parts[1:])
        sent = late_sum[1](*late_far, state, down_near, part=parts[0])
        first_far = send_second(*sent, count)
        ffn_parts.append(shifted(after(ffn_sent[high // 2], sent[0]), high // 2, count))
        input_part_late = after(input_part, sent[0])
        second_sent = late_sum[1](after(late_far[0], sent[0]), late_far[1], part=parts[1])
    input_far = other_core(input_part_late)
    input_grad = whole_call(
        input_grad_kernel,
        [core, x, middle_grad, input_part, input_far, gains],
        [jax.ShapeDtypeStruct((own_rows, D), F32)],
        "input_grad",
        1,
    )[0]
    if by_hand:
        second_far = send_second(
            after(second_sent[0], input_grad, *first_far, *ffn_parts[1:]), second_sent[1], count
        )
        first_state, *sent = late_sum[2](
            *first_far,
            state,
            part=parts[0],
        )
        first_parts = send_third(*sent, count=count)
        ffn_parts[0] = after(ffn_parts[0], sent[0])
        ffn_grad, ffn_left_new, ffn_right_new, ffn_new = precondition(
            ffn_parts,
            FBLK,
            ffn_left[:, 0],
            ffn_right[:, 0],
            ffn_left_root[:, 0],
            ffn_right_root[:, 0],
            [ffn_master[:, 0]],
        )
        wide = high * late_cut
        down_grad, down_left_new, down_right_new, down_new = precondition(
            [after(down_near, ffn_left_new), *first_far],
            FBLK,
            down_left,
            down_right,
            down_left_root,
            down_right_root,
            [jnp.swapaxes(down_master, 2, 3)],
            turned=True,
            starts=[0, wide + 128, wide],
        )
        down_grad, down_new = jnp.swapaxes(down_grad, 2, 3), jnp.swapaxes(down_new, 2, 3)
        sent = late_sum[2](after(second_far[0], down_left_new), second_far[1], part=parts[1])
        second_parts = send_third(*sent, count=count)
        first_state = slow_state(after(first_state, sent[0]), first_parts[1:])
        first_parts[0] = after(first_parts[0], first_state)
        gain_grad, gain_moment_new, gain_new = whole_call(
            gains_kernel,
            [first_state, along(first_state, 2, count), gains, gain_moments],
            [jax.ShapeDtypeStruct(gains.shape, F32)] * 3,
            "gains",
        )
        attn_results = ()
        for matrices, some in ((range(2), first_parts), (range(2, 4), second_parts)):
            attn_results = precondition(
                some,
                DBLK,
                attn_left[:, 0],
                attn_right[:, 0],
                attn_left_root[:, 0],
                attn_right_root[:, 0],
                [qkv_master[:, 0], out_master],
                matrices=matrices,
                carry=attn_results,
            )
            second_parts[0] = after(second_parts[0], gain_grad, attn_results[0])
        *stacked, out_new = attn_results
        attn_grad, attn_left_new, attn_right_new, qkv_new = (array[:, None] for array in stacked)
        ffn_grad, ffn_left_new, ffn_right_new, ffn_new = (
            array[:, None] for array in (ffn_grad, ffn_left_new, ffn_right_new, ffn_new)
        )
    else:
        gain_terms = jnp.concatenate([gain_one, 0.5 * gain_two])
        gain_grad = lax.psum(gain_terms, ("dp", "narrow"))
        gain_moment_new = DECAY * gain_moments + (1.0 - DECAY) * gain_grad * gain_grad
        gain_new = gains - GAIN_RATE * gain_grad / (jnp.sqrt(gain_moment_new) + 1e-08)
        qkv_owned, out_owned, ffn_owned, down_owned = scatter_all(
            qkv_weight_grad, out_weight_grad, ffn_weight_grad, down_weight_grad, count
        )
        attn_grad = jnp.concatenate([qkv_owned, out_owned[None]], 0)[:, None]
        ffn_grad = ffn_owned[:, None]
        down_grad = down_owned[None]
        attn_left_new, attn_right_new, attn_new = plain_precondition(
            attn_grad,
            attn_left,
            attn_right,
            attn_left_root,
            attn_right_root,
            jnp.concatenate([qkv_master, out_master[None]], 0),
        )
        qkv_new, out_new = attn_new[:3], attn_new[3]
        ffn_left_new, ffn_right_new, ffn_new = plain_precondition(
            ffn_grad, ffn_left, ffn_right, ffn_left_root, ffn_right_root, ffn_master
        )
        down_left_new, down_right_new, down_new = plain_precondition(
            down_grad, down_left, down_right, down_left_root, down_right_root, down_master
        )
    return (
        layer_out,
        input_grad,
        gain_grad,
        gain_moment_new,
        gain_new,
        attn_grad,
        attn_left_new,
        attn_right_new,
        qkv_new,
        out_new,
        ffn_grad,
        ffn_left_new,
        ffn_right_new,
        ffn_new,
        down_grad,
        down_left_new,
        down_right_new,
        down_new,
    )


def solution(mesh):
    tokens = P(("dp", "narrow"), None)
    stacked = P(None, "narrow", "dp", None, None)
    single = P("narrow", "dp", None, None)
    return jax.shard_map(
        body,
        mesh=mesh,
        in_specs=(tokens, tokens, P(), P(), stacked, single, stacked, single)
        + (stacked,) * 8
        + (single,) * 4,
        out_specs=(tokens, tokens, P(), P(), P())
        + (stacked,) * 4
        + (single,)
        + (stacked,) * 4
        + (single,) * 4,
        check_vma=False,
    )
```

```python
import functools
import math

import jax
import jax.numpy as jnp
from jax import lax
from jax.experimental import pallas as pl
from jax.experimental.pallas import tpu as pltpu
from jax.sharding import PartitionSpec as P

D = 768
HEAD_DIM = 64
FF = 2048
LEN = 1024
GRID = 16
DBLK = D // GRID
FBLK = FF // GRID
HALF_GRID = GRID // 2
HALF_D = D // 2
HALF_FF = FF // 2
PAIR = 2 * HEAD_DIM
ROWS = 256

EPSILON = 1e-05
DECAY = 0.5
STEP_RATE = 0.25
GAIN_RATE = 0.1
NEG_FILL = -1e30
HIGHEST_PRECISION = lax.Precision.HIGHEST
BF16 = jnp.bfloat16
F32 = jnp.float32
VMEM_MIB = 18
DENSE_ROWS = 512
TILE = 256
WIDE_TILE = 512
SMALL_MIB = 8
PACK_MIB = 60
STATE_ROWS = 16


def dot_nn(left, right):
    return lax.dot_general(left, right, (((1,), (0,)), ((), ())), preferred_element_type=F32)


def dot_nt(left, right):
    return lax.dot_general(left, right, (((1,), (1,)), ((), ())), preferred_element_type=F32)


def dot_tn(left, right):
    return lax.dot_general(left, right, (((0,), (0,)), ((), ())), preferred_element_type=F32)


def kernel_params(mib=VMEM_MIB):
    return pltpu.CompilerParams(vmem_limit_bytes=mib * 1024 * 1024)


def cost():
    return pl.CostEstimate(flops=0, bytes_accessed=0, transcendentals=0)


def whole_call(kernel, inputs, shapes, name, scalars=0, mib=SMALL_MIB, scratch=()):
    vmem = pl.BlockSpec(memory_space=pltpu.VMEM)
    smem = pl.BlockSpec(memory_space=pltpu.SMEM)
    return pl.pallas_call(
        kernel,
        in_specs=[smem] * scalars + [vmem] * (len(inputs) - scalars),
        out_specs=[vmem] * len(shapes),
        out_shape=shapes,
        scratch_shapes=list(scratch),
        compiler_params=kernel_params(mib),
        cost_estimate=cost(),
        name=name,
    )(*inputs)


def over_rows(length, rows, work):
    @pl.loop(0, length // rows)
    def _(step):
        work(pl.ds(pl.multiple_of(step * rows, rows), rows))


def lower_lanes(shape):
    return lax.broadcasted_iota(jnp.int32, shape, 1) % HEAD_DIM < HEAD_DIM // 2


def turn(features, cosine, sine_part, lower):
    half = HEAD_DIM // 2
    partner = jnp.where(
        lower, pltpu.roll(features, PAIR - half, 1), pltpu.roll(features, half, 1)
    )
    return features * cosine + partner * sine_part


def project_kernel(x_ref, gain_ref, w_ref, cos_ref, sin_ref, n1_ref, q_ref, k_ref, v_ref):
    lower = lower_lanes((DENSE_ROWS, PAIR))

    def work(rows):
        x = x_ref[rows, :].astype(F32)
        scale = lax.rsqrt(jnp.mean(x * x, -1, keepdims=True) + EPSILON)
        normed = (x * scale * gain_ref[0:1, :]).astype(BF16)
        n1_ref[rows, :] = normed
        cosine, sine_part = cos_ref[rows, :], sin_ref[rows, :]
        both = dot_nn(normed, w_ref[...])
        for tile in range(HALF_D // PAIR):
            lanes = slice(tile * PAIR, (tile + 1) * PAIR)
            query = both[:, tile * PAIR : (tile + 1) * PAIR]
            key = both[:, HALF_D + tile * PAIR : HALF_D + (tile + 1) * PAIR]
            turned = turn(query, cosine, sine_part, lower).astype(BF16)
            q_ref[rows, lanes] = turned * BF16(1.0 / math.sqrt(HEAD_DIM))
            k_ref[rows, lanes] = turn(key, cosine, sine_part, lower).astype(BF16)
        v_ref[rows, :] = both[:, 2 * HALF_D :].astype(BF16)

    over_rows(x_ref.shape[0], DENSE_ROWS, work)


def project(x, gains, weight, cosine, sine_part):
    length = x.shape[0]
    half = jax.ShapeDtypeStruct((length, HALF_D), BF16)
    shapes = [jax.ShapeDtypeStruct((length, D), BF16), half, half, half]
    return whole_call(
        project_kernel, [x, gains, weight, cosine, sine_part], shapes, "project", mib=VMEM_MIB
    )


def attend_kernel(q_ref, k_ref, v_ref, o_ref, lse_ref):
    @pl.loop(0, q_ref.shape[1] // PAIR)
    def _(pair):
        lanes = pl.ds(pl.multiple_of(pair * PAIR, PAIR), PAIR)
        rows = pl.ds(pl.multiple_of(pair * 8, 8), 8)
        attend_pair(
            *(ref.at[:, lanes] for ref in (q_ref, k_ref, v_ref, o_ref)), lse_ref.at[rows, :]
        )


def attend_pair(q_ref, k_ref, v_ref, o_ref, lse_ref):
    length = q_ref.shape[0]
    first_head = lax.broadcasted_iota(jnp.int32, (ROWS, PAIR), 1) < HEAD_DIM
    keys = k_ref[...]
    values = jnp.concatenate([v_ref[...], jnp.ones((length, PAIR), BF16)], 1)
    causal = lax.broadcasted_iota(jnp.int32, (2 * ROWS, ROWS), 0) % ROWS >= (
        lax.broadcasted_iota(jnp.int32, (2 * ROWS, ROWS), 1)
    )
    for block in range(length // ROWS):
        rows = slice(block * ROWS, (block + 1) * ROWS)
        width = (block + 1) * ROWS
        query_block = q_ref[rows, :]
        zero = jnp.zeros_like(query_block)
        query = jnp.concatenate(
            [jnp.where(first_head, query_block, zero), jnp.where(first_head, zero, query_block)], 0
        )
        scores = jnp.where(causal, dot_nt(query, keys[block * ROWS : width]), NEG_FILL)
        if block:
            scores = jnp.concatenate([dot_nt(query, keys[: block * ROWS]), scores], 1)
        top = jnp.max(scores, 1, keepdims=True)
        exponent = jnp.exp(scores - top).astype(BF16)
        product = dot_nn(exponent, values[:width])
        total = product[:, PAIR:]
        out = product[:, :PAIR] / total
        sums = top + jnp.log(total)
        o_ref[rows, :] = jnp.where(first_head, out[:ROWS], out[ROWS:]).astype(BF16)
        lane = lax.broadcasted_iota(jnp.int32, (ROWS, PAIR), 1)
        lse_ref[:, rows] = jnp.transpose(jnp.where(lane == 0, sums[:ROWS], sums[ROWS:]))[:8, :]


def attend(q, k, v):
    length = q.shape[0]
    shapes = [
        jax.ShapeDtypeStruct(q.shape, BF16),
        jax.ShapeDtypeStruct((8 * (q.shape[1] // PAIR), length), F32),
    ]
    return whole_call(attend_kernel, [q, k, v], shapes, "attend", mib=VMEM_MIB)


def attend_back_kernel(
    q_ref, k_ref, v_ref, do_ref, o_ref, lse_ref, cos_ref, sin_ref, grad_ref, dqt_ref
):
    @pl.loop(0, q_ref.shape[1] // PAIR)
    def _(pair):
        lanes = pl.ds(pl.multiple_of(pair * PAIR, PAIR), PAIR)
        rows = pl.ds(pl.multiple_of(pair * 8, 8), 8)
        attend_back_pair(
            *(ref.at[:, lanes] for ref in (q_ref, k_ref, v_ref, do_ref, o_ref)),
            lse_ref.at[rows, :],
            cos_ref,
            sin_ref,
            *(
                grad_ref.at[:, pl.ds(pl.multiple_of(at * HALF_D + pair * PAIR, PAIR), PAIR)]
                for at in range(3)
            ),
            dqt_ref,
        )


def attend_back_pair(
    q_ref, k_ref, v_ref, do_ref, o_ref, lse_ref, cos_ref, sin_ref, dq_ref, dk_ref, dv_ref, dqt_ref
):
    length = q_ref.shape[0]
    first_head = lax.broadcasted_iota(jnp.int32, (length, PAIR), 1) < HEAD_DIM
    zero = BF16(0)
    queries = [
        jnp.where(first_head, q_ref[...], zero),
        jnp.where(first_head, zero, q_ref[...]),
    ]
    grads = [
        jnp.where(first_head, do_ref[...], zero),
        jnp.where(first_head, zero, do_ref[...]),
    ]
    product = do_ref[...].astype(F32) * o_ref[...].astype(F32)
    head_row = lax.broadcasted_iota(jnp.int32, (8, PAIR), 0)
    head_lane = lax.broadcasted_iota(jnp.int32, (8, PAIR), 1) // HEAD_DIM
    inner = lax.dot_general(
        (head_row == head_lane).astype(F32),
        product,
        (((1,), (1,)), ((), ())),
        preferred_element_type=F32,
        precision=HIGHEST_PRECISION,
    )
    turned_keys = jnp.transpose(k_ref[...].astype(F32)).astype(BF16)
    first_rows = lax.broadcasted_iota(jnp.int32, turned_keys.shape, 0) < HEAD_DIM
    key_heads = [
        jnp.where(first_rows, turned_keys, zero),
        jnp.where(first_rows, zero, turned_keys),
    ]
    causal = lax.broadcasted_iota(jnp.int32, (ROWS, ROWS), 0) <= lax.broadcasted_iota(
        jnp.int32, (ROWS, ROWS), 1
    )
    dqt_ref[...] = jnp.zeros_like(dqt_ref)
    lower = lower_lanes((ROWS, PAIR))
    for block in range(length // ROWS):
        rows = slice(block * ROWS, (block + 1) * ROWS)
        start = block * ROWS
        key_block, value_block = k_ref[rows, :], v_ref[rows, :]
        dk = jnp.zeros((ROWS, PAIR), F32)
        dv = jnp.zeros((ROWS, PAIR), F32)
        for head in range(2):
            scores = dot_nt(key_block, queries[head][start:])
            probs = jnp.exp(scores - lse_ref[head : head + 1, start:])
            diagonal = jnp.where(causal, probs[:, :ROWS], 0.0)
            if start + ROWS == length:
                probs = diagonal
            else:
                probs = jnp.concatenate([diagonal, probs[:, ROWS:]], 1)
            prob_grad = dot_nt(value_block, grads[head][start:])
            score_grad = (probs * (prob_grad - inner[head : head + 1, start:])).astype(BF16)
            dv = dv + dot_nn(probs.astype(BF16), grads[head][start:])
            dk = dk + dot_nn(score_grad, queries[head][start:])
            dqt_ref[:, start:] += dot_nn(key_heads[head][:, rows], score_grad)
        dk_ref[rows, :] = turn(dk, cos_ref[rows, :], -sin_ref[rows, :], lower).astype(BF16)
        dv_ref[rows, :] = dv.astype(BF16)
    for block in range(length // ROWS):
        rows = slice(block * ROWS, (block + 1) * ROWS)
        dq = jnp.transpose(dqt_ref[:, rows]) * (1.0 / math.sqrt(HEAD_DIM))
        dq_ref[rows, :] = turn(dq, cos_ref[rows, :], -sin_ref[rows, :], lower).astype(BF16)


def attend_back(q, k, v, grad, o, lse, cosine, sine_part):
    return whole_call(
        attend_back_kernel,
        [q, k, v, grad, o, lse, cosine, sine_part],
        [jax.ShapeDtypeStruct((q.shape[0], 3 * q.shape[1]), BF16)],
        "attend_back",
        mib=VMEM_MIB,
        scratch=[pltpu.VMEM((PAIR, q.shape[0]), F32)],
    )[0]


def ffn_kernel(
    x_ref, o_ref, o_far_ref, wo_ref, wo_far_ref, gain_ref, wg_ref, wu_ref,
    x1_ref, n2_ref, gate_ref, up_ref, hidden_ref,
):
    def work(rows):
        middle = (
            x_ref[rows, :].astype(F32)
            + dot_nn(o_ref[rows, :], wo_ref[...])
            + dot_nn(o_far_ref[rows, :], wo_far_ref[...])
        )
        x1_ref[rows, :] = middle
        scale = lax.rsqrt(jnp.mean(middle * middle, -1, keepdims=True) + EPSILON)
        normed = (middle * scale * gain_ref[1:2, :]).astype(BF16)
        n2_ref[rows, :] = normed

        @pl.loop(0, HALF_FF // TILE)
        def _(tile):
            lanes = pl.ds(pl.multiple_of(tile * TILE, TILE), TILE)
            gate = dot_nn(n2_ref[rows, :], wg_ref[:, lanes])
            up = dot_nn(n2_ref[rows, :], wu_ref[:, lanes])
            gate_ref[rows, lanes] = gate
            up_ref[rows, lanes] = up
            hidden_ref[rows, lanes] = (gate * jax.nn.sigmoid(gate) * up).astype(BF16)

    over_rows(x_ref.shape[0], DENSE_ROWS, work)


def ffn(*inputs):
    length = inputs[0].shape[0]
    shapes = [
        jax.ShapeDtypeStruct((length, width), kind)
        for width, kind in ((D, F32), (D, BF16), (HALF_FF, F32), (HALF_FF, F32), (HALF_FF, BF16))
    ]
    return whole_call(ffn_kernel, inputs, shapes, "ffn", mib=VMEM_MIB)


def ffn_out_kernel(hidden_ref, wdt_ref, part_ref):
    def work(rows):
        part_ref[rows, :] = dot_nt(hidden_ref[rows, :], wdt_ref[...]).astype(BF16)

    over_rows(hidden_ref.shape[0], DENSE_ROWS, work)


def ffn_out(hidden, wdt):
    shape = jax.ShapeDtypeStruct((hidden.shape[0], D), BF16)
    return whole_call(ffn_out_kernel, [hidden, wdt], [shape], "ffn_out", mib=VMEM_MIB)[0]


def ffn_back_kernel(cot_ref, gate_ref, up_ref, wdt_ref, wg_ref, wu_ref, dgu_ref, dn2_ref):
    def work(rows):
        @pl.loop(0, HALF_FF // WIDE_TILE)
        def _(tile):
            lanes = pl.ds(pl.multiple_of(tile * WIDE_TILE, WIDE_TILE), WIDE_TILE)
            up_lanes = pl.ds(pl.multiple_of(HALF_FF + tile * WIDE_TILE, WIDE_TILE), WIDE_TILE)
            hidden_grad = dot_nn(cot_ref[rows, :], wdt_ref[:, lanes])
            gate, up = gate_ref[rows, lanes], up_ref[rows, lanes]
            sigma = jax.nn.sigmoid(gate)
            gate_grad = hidden_grad * up * sigma * (1.0 + gate * (1.0 - sigma))
            dgu_ref[rows, lanes] = gate_grad.astype(BF16)
            dgu_ref[rows, up_lanes] = (hidden_grad * gate * sigma).astype(BF16)

        @pl.loop(0, D // TILE)
        def _(tile):
            lanes = pl.ds(pl.multiple_of(tile * TILE, TILE), TILE)
            dn2 = dot_nt(dgu_ref[rows, :HALF_FF], wg_ref[lanes, :]) + dot_nt(
                dgu_ref[rows, HALF_FF:], wu_ref[lanes, :]
            )
            dn2_ref[rows, lanes] = dn2.astype(BF16)

    over_rows(cot_ref.shape[0], DENSE_ROWS, work)


def ffn_back(cot, gate, up, wdt, wg, wu):
    shapes = [jax.ShapeDtypeStruct((cot.shape[0], width), BF16) for width in (FF, D)]
    return whole_call(
        ffn_back_kernel, [cot, gate, up, wdt, wg, wu], shapes, "ffn_back", mib=VMEM_MIB
    )


def middle_back_kernel(
    cot_ref, x1_ref, near_ref, far_ref, gain_ref, wo_ref, dx1_ref, da_ref, do_ref, g2_ref
):
    g2_ref[...] = jnp.zeros_like(g2_ref)

    def work(rows):
        middle = x1_ref[rows, :]
        scale = lax.rsqrt(jnp.mean(middle * middle, -1, keepdims=True) + EPSILON)
        grad = near_ref[rows, :].astype(F32) + far_ref[rows, :].astype(F32)
        weighted = grad * gain_ref[1:2, :]
        inner = jnp.mean(weighted * middle, -1, keepdims=True)
        middle_grad = (
            cot_ref[rows, :].astype(F32)
            + scale * weighted
            - middle * (scale * scale * scale * inner)
        )
        dx1_ref[rows, :] = middle_grad
        branch = middle_grad.astype(BF16)
        da_ref[rows, :] = branch
        do_ref[rows, :] = dot_nt(branch, wo_ref[...]).astype(BF16)
        g2_ref[...] += jnp.sum(grad * middle * scale, 0, keepdims=True)

    over_rows(cot_ref.shape[0], DENSE_ROWS, work)


def middle_back(*inputs):
    length = inputs[0].shape[0]
    shapes = [
        jax.ShapeDtypeStruct(shape, kind)
        for shape, kind in (
            ((length, D), F32),
            ((length, D), BF16),
            ((length, HALF_D), BF16),
            ((1, D), F32),
        )
    ]
    return whole_call(middle_back_kernel, inputs, shapes, "middle_back", mib=VMEM_MIB)


def input_back_kernel(x_ref, dqkv_ref, w_ref, part_ref, g1_ref):
    g1_ref[...] = jnp.zeros_like(g1_ref)

    def work(rows):
        grad = dot_nt(dqkv_ref[rows, :], w_ref[...])
        part_ref[rows, :] = grad.astype(BF16)
        x = x_ref[rows, :].astype(F32)
        scale = lax.rsqrt(jnp.mean(x * x, -1, keepdims=True) + EPSILON)
        g1_ref[...] += jnp.sum(grad * x * scale, 0, keepdims=True)

    over_rows(x_ref.shape[0], DENSE_ROWS, work)


def input_back(x, dqkv, w):
    shapes = [jax.ShapeDtypeStruct(x.shape, BF16), jax.ShapeDtypeStruct((1, D), F32)]
    return whole_call(input_back_kernel, [x, dqkv, w], shapes, "input_back", mib=VMEM_MIB)


def pair_up(bit, count):
    return [(i, i ^ bit) for i in range(count)]


def after(value, *others):
    return lax.optimization_barrier((value,) + others)[0]


def along(values, bit, count):
    return lax.ppermute(values, "dp", pair_up(bit, count))


def shifted(values, steps, count):
    return lax.ppermute(values, "dp", [(i, (i + 4 * steps) % count) for i in range(count)])


def other_core(values):
    return lax.ppermute(values, "narrow", [(0, 1), (1, 0)])


def all_shifted(values, count):
    return [shifted(values, step, count) for step in range(1, count // 4)]


def copy_columns(sources, outputs, name):
    rows = sources[0].shape[0]
    shapes = [
        jax.ShapeDtypeStruct((rows, sum(stop - start for _, start, stop in parts)), BF16)
        for parts in outputs
    ]

    def kernel(*refs):
        for out_ref, parts in zip(refs[len(sources) :], outputs):
            at = 0
            for number, start, stop in parts:
                out_ref[:, at : at + stop - start] = refs[number][:, start:stop]
                at += stop - start

    return whole_call(kernel, sources, shapes, name)


def block_rows(owner):
    return pl.ds(pl.multiple_of(owner * DBLK, 16), DBLK)


def block_lanes(index, width):
    return pl.ds(pl.multiple_of(index * width, 128), width)


def place_qkv_out(owner, start, piece, qkv_ref, out_ref):
    cut, stop = 3 * HALF_D, start + piece.shape[1]
    if start < cut:
        end = min(stop, cut)
        qkv_ref[block_rows(owner), start:end] = piece[:, : end - start]
    if stop > cut:
        begin = max(start, cut)
        lanes = pl.ds(pl.multiple_of(owner % 2 * HALF_D + (begin - cut), 128), stop - begin)
        out_ref[block_rows(owner // 2), lanes] = piece[:, begin - start :]


def place_gate_up(owner, start, piece, gate_ref, up_ref):
    stop = start + piece.shape[1]
    if start < HALF_FF:
        end = min(stop, HALF_FF)
        gate_ref[block_rows(owner), start:end] = piece[:, : end - start]
    if stop > HALF_FF:
        begin = max(start, HALF_FF)
        up_ref[block_rows(owner), begin - HALF_FF : stop - HALF_FF] = piece[:, begin - start :]


def place_down(owner, start, piece, out_ref):
    lanes = block_lanes(owner // 2, FBLK)
    for block in range(piece.shape[1] // FBLK):
        rows = block_rows(owner % 2 * HALF_GRID + start // FBLK + block)
        out_ref[rows, lanes] = piece[:, block * FBLK : (block + 1) * FBLK]


def assemble(me, high, sources, entries, place, shapes, name, begun=()):
    sources = list(sources)

    def kernel(me_ref, *refs):
        x, y, z = me_ref[0] % 2, me_ref[0] // 2 % 2, me_ref[0] // 4
        out_refs = refs[len(sources) + len(begun) :]
        for ref, out_ref in zip(refs[len(sources) :], out_refs if begun else ()):
            out_ref[...] = ref[...]
        for number, start, width, step, over_y, over_x, first in entries:
            slow = (z - step + high) % high
            from_y = 1 - y if over_y else y
            from_x = 1 - x if over_x else x
            piece = refs[number][:, start : start + width]
            place(slow * 4 + from_y * 2 + from_x, first, piece, *out_refs)

    return whole_call(
        kernel,
        [me] + sources + list(begun),
        [jax.ShapeDtypeStruct(shape, BF16) for shape in shapes],
        name,
        1,
    )


def pack_kernel(qkv_ref, out_ref, ffn_ref, down_ref, first_ref, second_ref, slab_ref, *scratch):
    held, sems = scratch[:-1], scratch[-1]
    copies = [
        pltpu.make_async_copy(ref, here, sems.at[number])
        for number, (ref, here) in enumerate(zip((qkv_ref, out_ref, ffn_ref, down_ref), held))
    ]
    for copy in copies:
        copy.start()

    def row(ref, matrix):
        return jnp.concatenate([ref[matrix, block].astype(BF16) for block in range(HALF_GRID)], 1)

    at = 0
    for copy, ref in zip(copies, held):
        copy.wait()
        for matrix in range(ref.shape[0]):
            part = row(ref, matrix)
            stop = at + part.shape[1]
            slab_ref[:, at:stop] = part
            if stop <= first_ref.shape[1]:
                first_ref[:, at:stop] = part
            elif stop <= first_ref.shape[1] + second_ref.shape[1]:
                second_ref[:, at - first_ref.shape[1] : stop - first_ref.shape[1]] = part
            at = stop


def pack(*masters):
    vmem = pl.BlockSpec(memory_space=pltpu.VMEM)
    return pl.pallas_call(
        pack_kernel,
        in_specs=[pl.BlockSpec(memory_space=pl.ANY)] * len(masters),
        out_specs=[vmem] * 3,
        out_shape=[
            jax.ShapeDtypeStruct((DBLK, width), BF16)
            for width in (4 * HALF_D, FF, 4 * HALF_D + 3 * HALF_FF)
        ],
        scratch_shapes=[pltpu.VMEM(master.shape, F32) for master in masters]
        + [pltpu.SemaphoreType.DMA((len(masters),))],
        compiler_params=kernel_params(PACK_MIB),
        cost_estimate=cost(),
        name="pack",
    )(*masters)


def tables_kernel(cos_ref, sin_ref, cosine_ref, sine_ref):
    cosine, sine = cos_ref[...], sin_ref[...]
    cosine_ref[...] = jnp.concatenate([cosine] * 4, 1)
    sine_ref[...] = jnp.concatenate([-sine, sine] * 2, 1)


def side_by_side(blocks):
    matrices, many, height, width = blocks.shape
    return blocks.transpose(2, 0, 1, 3).reshape(height, matrices * many * width)


def gather_by_name(qkv, out, ffn_part, down):
    qkv_all = lax.all_gather(qkv, "dp", axis=1, tiled=True)
    out_all = lax.all_gather(out[0], "dp", axis=0, tiled=True)
    ffn_all = lax.all_gather(ffn_part, "dp", axis=1, tiled=True)
    down_all = lax.all_gather(down, "dp", axis=0, tiled=True)
    w_qkv = qkv_all.reshape(3, GRID, HALF_GRID, DBLK, DBLK).transpose(1, 3, 0, 2, 4)
    w_out = out_all.reshape(HALF_GRID, GRID, DBLK, DBLK).transpose(0, 2, 1, 3)
    w_ffn = ffn_all.reshape(2, GRID, HALF_GRID, DBLK, FBLK).transpose(0, 1, 3, 2, 4)
    w_down = down_all.reshape(HALF_GRID, GRID, FBLK, DBLK).transpose(1, 3, 0, 2)
    w_ffn = w_ffn.reshape(2, D, HALF_FF)
    return (
        w_qkv.reshape(D, 3 * HALF_D),
        w_out.reshape(HALF_D, D),
        w_ffn[0],
        w_ffn[1],
        w_down.reshape(D, HALF_FF),
    )


def take_rows(owner, ref):
    return ref[block_rows(owner), :]


def take_out(owner, ref):
    return ref[block_rows(owner // 2), pl.ds(pl.multiple_of(owner % 2 * HALF_D, 128), HALF_D)]


def take_down(owner, ref):
    lanes = pl.ds(pl.multiple_of(owner // 2 * FBLK, 128), FBLK)
    return jnp.concatenate(
        [ref[block_rows(owner % 2 * HALF_GRID + block), lanes] for block in range(HALF_GRID)], 1
    )


def paired(values):
    high = values.astype(BF16)
    low = (values - high.astype(F32)).astype(BF16)
    rest = jnp.zeros((DBLK - 2 * values.shape[0], values.shape[1]), BF16)
    return jnp.concatenate([high, low, rest], 0)


def unpaired(pair):
    rows = STATE_ROWS
    return pair[:rows].astype(F32) + pair[rows : 2 * rows].astype(F32)


def reduction(takes, columns, count, me, grads):
    high = count // 4
    half = high // 2
    many = len(grads)

    def step(kernel, inputs, shapes, name):
        return whole_call(kernel, [me] + grads + inputs, shapes, name, 1)

    def find(refs, slow, y, x, part):
        owner = slow * 4 + y * 2 + x
        found = [take(owner, ref) for take, ref in zip(takes, refs)]
        found = found[0] if len(found) == 1 else jnp.concatenate(found, 1)
        return found[:, part[0] : part[1]].astype(F32)

    def place(me_ref):
        return me_ref[0] % 2, me_ref[0] // 2 % 2, me_ref[0] // 4

    def piece(index, width=columns, start=0, every=None):
        first = index * (every or width) + start
        return pl.ds(pl.multiple_of(first, 128), width)

    def diagonal_kernel(me_ref, *refs):
        x, y, _ = place(me_ref)
        *guest_refs, to_y_ref, to_x_ref = refs[many:]
        for guest_ref in guest_refs:
            wide = guest_ref.shape[1] // 4
            middle = 3 * wide + wide // 2
            to_y_ref[:, half * columns :] = guest_ref[:, 3 * wide : middle].astype(BF16)
            to_x_ref[:, half * columns :] = guest_ref[:, middle:].astype(BF16)

        @pl.loop(0, half)
        def _(step):
            whole = (0, columns)
            to_y_ref[:, piece(step)] = find(refs, step, 1 - y, 1 - x, whole).astype(BF16)
            to_x_ref[:, piece(step)] = find(refs, half + step, 1 - y, 1 - x, whole).astype(BF16)

    def side_kernel(part, me_ref, *refs):
        x, y, _ = place(me_ref)
        by_y_ref, by_x_ref, *state_refs, to_x_ref, to_y_ref = refs[many:]
        width = part[1] - part[0]
        if state_refs:
            guest_ref = state_refs[1]
            wide = guest_ref.shape[1] // 4
            cut, start = wide // 2, high * width + 128
            by_y = by_y_ref[:, half * columns :].astype(F32)
            by_x = by_x_ref[:, half * columns :].astype(F32)
            to_x_ref[:, start : start + cut] = (guest_ref[:, wide : wide + cut] + by_y).astype(BF16)
            to_x_ref[:, start + cut :] = guest_ref[:, wide + cut : 2 * wide].astype(BF16)
            start = high * width
            to_y_ref[:, start : start + cut] = guest_ref[:, 2 * wide : 2 * wide + cut].astype(BF16)
            to_y_ref[:, start + cut :] = (
                guest_ref[:, 2 * wide + cut : 3 * wide] + by_x
            ).astype(BF16)

        @pl.loop(0, half)
        def _(step):
            lanes = piece(step, width, part[0], columns)
            for slow, by_y, by_x in ((step, by_y_ref, None), (half + step, None, by_x_ref)):
                to_x = find(refs, slow, y, 1 - x, part)
                to_y = find(refs, slow, 1 - y, x, part)
                if by_y is not None:
                    to_x = to_x + by_y[:, lanes].astype(F32)
                else:
                    to_y = to_y + by_x[:, lanes].astype(F32)
                to_x_ref[:, piece(slow, width)] = to_x.astype(BF16)
                to_y_ref[:, piece(slow, width)] = to_y.astype(BF16)

        if state_refs:
            to_x_ref[:, high * width : high * width + 128] = paired(state_refs[0][...])

    def slow_kernel(part, me_ref, *refs):
        x, y, z = place(me_ref)
        from_x_ref, from_y_ref, *state_refs = refs[many : len(refs) - high]
        out_refs = refs[len(refs) - high :]
        width = part[1] - part[0]
        if state_refs:
            before_ref, after_ref = state_refs
            lanes = slice(high * width, high * width + 128)
            state = unpaired(paired(before_ref[...])) + unpaired(from_x_ref[:, lanes])
            after_ref[...] = state
        for shift in range(high):
            rows = pl.ds(0, DBLK)
            slow = (z + shift) % high
            lanes = pl.ds(pl.multiple_of(slow * width, 128), width)
            total = (
                find(refs, slow, y, x, part)
                + from_x_ref[rows, lanes].astype(F32)
                + from_y_ref[rows, lanes].astype(F32)
            )
            out_refs[shift][:, :width] = total.astype(out_refs[shift].dtype)
            if state_refs and shift:
                out_refs[shift][:, width:] = paired(state)

    def rows(width, kind=BF16):
        return jax.ShapeDtypeStruct((DBLK, width), kind)

    state_shape = jax.ShapeDtypeStruct((STATE_ROWS, 128), F32)

    def first(*guest):
        extra = sum(array.shape[1] // 8 for array in guest)
        shapes = [rows(half * columns + extra)] * 2
        return step(diagonal_kernel, list(guest), shapes, "send_diagonal")

    def second(by_y, by_x, *state, part=(0, columns)):
        wide = high * (part[1] - part[0])
        extra = state[1].shape[1] // 4 if state else 0
        shapes = [rows(wide + extra + (128 if state else 0)), rows(wide + extra)]
        kernel = functools.partial(side_kernel, part)
        return step(kernel, [by_y, by_x, *state], shapes, "send_sides")

    def third(from_x, from_y, *state, part=(0, columns)):
        width = part[1] - part[0]
        shapes = [state_shape] * len(state) + [rows(width, F32)]
        shapes += [rows(width + 128 * len(state))] * (high - 1)
        kernel = functools.partial(slow_kernel, part)
        return step(kernel, [from_x, from_y, *state], shapes, "send_slow")

    return first, second, third


def ring_blocks(grad, me, high):
    def kernel(me_ref, grad_ref, *out_refs):
        x, y, z = me_ref[0] % 2, me_ref[0] // 2 % 2, me_ref[0] // 4
        for hop, out_ref in enumerate(out_refs):
            slow = (z - 1 - hop + high) % high
            for part in range(4):
                from_x = 1 - x if part % 2 else x
                from_y = 1 - y if part // 2 else y
                block = take_down(slow * 4 + from_y * 2 + from_x, grad_ref)
                lanes = slice(part * HALF_FF, (part + 1) * HALF_FF)
                out_ref[:, lanes] = block.astype(out_ref.dtype)

    shapes = [
        jax.ShapeDtypeStruct((DBLK, 4 * HALF_FF), BF16 if hop < high - 1 else F32)
        for hop in range(high)
    ]
    return whole_call(kernel, [me, grad], shapes, "ring_blocks", 1)


def ring_add_kernel(far_ref, own_ref, out_ref):
    total = far_ref[...].astype(F32) + own_ref[...].astype(F32)
    out_ref[...] = total.astype(out_ref.dtype)


def ring_add(far, own):
    shape = jax.ShapeDtypeStruct(own.shape, own.dtype)
    return whole_call(ring_add_kernel, [far, own], [shape], "ring_add")[0]


def send_first(to_y, to_x, count):
    return along(to_y, 2, count), along(to_x, 1, count)


def send_second(to_x, to_y, count):
    return along(to_x, 1, count), along(to_y, 2, count)


def send_third(own, *others, count):
    return [own] + [shifted(block, step + 1, count) for step, block in enumerate(others)]


def scatter_all(qkv, out, ffn_grad, down, count):
    qkv = qkv.reshape(GRID, DBLK, 3, HALF_GRID, DBLK).transpose(2, 0, 3, 1, 4)
    out = out.reshape(HALF_GRID, DBLK, GRID, DBLK).transpose(0, 2, 1, 3)
    ffn_grad = ffn_grad.reshape(GRID, DBLK, 2, HALF_GRID, FBLK).transpose(2, 0, 3, 1, 4)
    down = down.reshape(GRID, DBLK, HALF_GRID, FBLK).transpose(2, 0, 3, 1)
    return (
        lax.psum_scatter(
            qkv.reshape(3, -1, DBLK, DBLK), "dp", scatter_dimension=1, tiled=True
        ),
        lax.psum_scatter(out.reshape(-1, DBLK, DBLK), "dp", scatter_dimension=0, tiled=True),
        lax.psum_scatter(
            ffn_grad.reshape(2, -1, DBLK, FBLK), "dp", scatter_dimension=1, tiled=True
        ),
        lax.psum_scatter(down.reshape(-1, FBLK, DBLK), "dp", scatter_dimension=0, tiled=True),
    )


def gain_rows_kernel(one_ref, two_ref, out_ref):
    def rows(values):
        return [values[:, at : at + 128] for at in range(0, D, 128)]

    parts = rows(one_ref[...]) + rows(0.5 * two_ref[...])
    parts.append(jnp.zeros((STATE_ROWS - len(parts), 128), F32))
    out_ref[...] = jnp.concatenate(parts, 0)


def gain_rows(gain_one, gain_two):
    shape = jax.ShapeDtypeStruct((STATE_ROWS, 128), F32)
    return whole_call(gain_rows_kernel, [gain_one, gain_two], [shape], "gain_rows")[0]


def add_kernel(left_ref, right_ref, out_ref):
    out_ref[...] = left_ref[...] + right_ref[...]


def added(left, right, name):
    return whole_call(add_kernel, [left, right], [jax.ShapeDtypeStruct(left.shape, F32)], name)[0]


def slow_state_kernel(own_ref, *refs):
    out_ref = refs[-1]
    columns = refs[0].shape[1] - 128
    values = [unpaired(paired(own_ref[...]))] + [unpaired(ref[:, columns:]) for ref in refs[:-1]]
    while len(values) > 1:
        half = len(values) // 2
        values = [values[index] + values[index + half] for index in range(half)]
    out_ref[...] = values[0]


def slow_state(own, blocks):
    shape = jax.ShapeDtypeStruct(own.shape, F32)
    return whole_call(slow_state_kernel, [own] + blocks, [shape], "slow_state")[0]


def gains_kernel(near_ref, far_ref, gain_ref, moment_ref, grad_ref, moment_new_ref, gain_new_ref):
    total = near_ref[...] + far_ref[...]
    count = D // 128
    grad = jnp.concatenate(
        [
            jnp.concatenate([total[at + row : at + row + 1] for row in range(count)], 1)
            for at in (0, count)
        ],
        0,
    )
    grad_ref[...] = grad
    moment = DECAY * moment_ref[...] + (1.0 - DECAY) * grad * grad
    moment_new_ref[...] = moment
    gain_new_ref[...] = gain_ref[...] - GAIN_RATE * grad / (jnp.sqrt(moment) + 1e-08)


def full_dot(left, right, left_dim, right_dim):
    return lax.dot_general(
        left,
        right,
        (((left_dim,), (right_dim,)), ((), ())),
        preferred_element_type=F32,
        precision=lax.Precision.DEFAULT,
    )


def precondition(
    parts,
    width,
    left,
    right,
    left_root,
    right_root,
    masters,
    turned=False,
    matrices=None,
    carry=(),
    starts=None,
):
    starts = [0] * len(parts) if starts is None else starts
    counts = [master.shape[0] for master in masters]
    spots = [(which, here) for which, many in enumerate(counts) for here in range(many)]
    matrices = range(len(spots)) if matrices is None else matrices
    many = len(parts)

    def kernel(*refs):
        part_refs, refs, total_ref = refs[:many], refs[many:-1], refs[-1]
        left_ref, right_ref, left_root_ref, right_root_ref = refs[:4]
        master_refs, refs = refs[4 : 4 + len(counts)], refs[4 + len(counts) :]
        carry_refs, refs = refs[: len(carry)], refs[len(carry) :]
        grad_ref, left_new_ref, right_new_ref = refs[:3]
        new_refs = refs[3:]
        for matrix, (which, here) in enumerate(spots):
            if carry and matrix not in matrices:
                for out_ref, carry_ref in zip(refs[:3], carry_refs[:3]):
                    out_ref[matrix] = carry_ref[matrix]
                new_refs[which][here] = carry_refs[3 + which][here]
        wide = len(matrices) * HALF_GRID * width
        total = jnp.zeros((part_refs[0].shape[0], wide), F32)
        for ref, start in zip(part_refs, starts):
            total = total + ref[:, start : start + wide].astype(F32)
        total_ref[...] = total

        def update(which, here, matrix, block, grad):
            grad_ref[matrix, block] = grad
            outer, inner = full_dot(grad, grad, 1, 1), full_dot(grad, grad, 0, 0)
            if turned:
                outer, inner = inner, outer
                step = full_dot(grad, left_root_ref[matrix, block], 1, 1)
                step = full_dot(right_root_ref[matrix, block], step, 0, 0)
            else:
                step = full_dot(left_root_ref[matrix, block], grad, 1, 0)
                step = full_dot(step, right_root_ref[matrix, block], 1, 0)
            left_new_ref[matrix, block] = DECAY * left_ref[matrix, block] + (1.0 - DECAY) * outer
            right_new_ref[matrix, block] = DECAY * right_ref[matrix, block] + (1.0 - DECAY) * inner
            new_refs[which][here, block] = master_refs[which][here, block] - STEP_RATE * step

        def update_matrix(which, here, matrix, number):
            start = number * HALF_GRID * width
            if width % 128:
                lanes = pl.ds(pl.multiple_of(start, 128), HALF_GRID * width)
                row = total_ref[:, lanes]
                for block in range(HALF_GRID):
                    at = block * width
                    update(which, here, matrix, block, row[:, at : at + width])
            else:

                @pl.loop(0, HALF_GRID // 4)
                def _(step):
                    for block in [4 * step + number for number in range(4)]:
                        lanes = pl.ds(pl.multiple_of(start + block * width, 128), width)
                        update(which, here, matrix, block, total_ref[:, lanes])

        if len({spots[matrix][0] for matrix in matrices}) == 1:

            @pl.loop(0, len(matrices))
            def _(number):
                matrix = number + matrices[0]
                update_matrix(spots[matrices[0]][0], number + spots[matrices[0]][1], matrix, number)
        else:
            for number, matrix in enumerate(matrices):
                update_matrix(*spots[matrix], matrix, number)

    grads = jax.ShapeDtypeStruct((sum(counts),) + masters[0].shape[1:], F32)
    like = [jax.ShapeDtypeStruct(array.shape, F32) for array in (left, right)]
    news = [jax.ShapeDtypeStruct(master.shape, F32) for master in masters]
    inputs = list(parts) + [left, right, left_root, right_root] + list(masters)
    total = pltpu.VMEM((parts[0].shape[0], len(matrices) * HALF_GRID * width), F32)
    return whole_call(
        kernel, inputs + list(carry), [grads] + like + news, "precondition", scratch=[total]
    )


def plain_precondition(block_grad, left_stat, right_stat, left_root, right_root, master):
    new_left = DECAY * left_stat + (1.0 - DECAY) * jnp.einsum(
        "...ij,...kj->...ik", block_grad, block_grad, precision=HIGHEST_PRECISION
    )
    new_right = DECAY * right_stat + (1.0 - DECAY) * jnp.einsum(
        "...ji,...jk->...ik", block_grad, block_grad, precision=HIGHEST_PRECISION
    )
    turned = jnp.einsum("...ij,...jk->...ik", left_root, block_grad, precision=HIGHEST_PRECISION)
    turned = jnp.einsum("...ij,...jk->...ik", turned, right_root, precision=HIGHEST_PRECISION)
    return (new_left, new_right, master - STEP_RATE * turned)


def in_order_kernel(core_ref, mine_ref, other_ref, out_ref):
    rows = mine_ref.shape[0]
    core = core_ref[0]
    out_ref[pl.ds(pl.multiple_of(core * rows, 16), rows), :] = mine_ref[...]
    out_ref[pl.ds(pl.multiple_of((1 - core) * rows, 16), rows), :] = other_ref[...]


def in_order(mine, core):
    shape = jax.ShapeDtypeStruct((2 * mine.shape[0], mine.shape[1]), mine.dtype)
    return whole_call(in_order_kernel, [core, mine, other_core(mine)], [shape], "in_order", 1)[0]


def own_and_all(core_ref, rows, step):
    own = pl.ds(pl.multiple_of(step * ROWS, ROWS), ROWS)
    return own, pl.ds(pl.multiple_of(core_ref[0] * rows + step * ROWS, ROWS), ROWS)


def layer_out_kernel(core_ref, x1_ref, near_ref, far_ref, out_ref):
    @pl.loop(0, out_ref.shape[0] // ROWS)
    def _(step):
        own, rows = own_and_all(core_ref, out_ref.shape[0], step)
        total = x1_ref[rows, :] + near_ref[rows, :].astype(F32) + far_ref[rows, :].astype(F32)
        out_ref[own, :] = total.astype(BF16)


def input_grad_kernel(core_ref, x_ref, dx1_ref, near_ref, far_ref, gain_ref, out_ref):
    @pl.loop(0, out_ref.shape[0] // ROWS)
    def _(step):
        own, rows = own_and_all(core_ref, out_ref.shape[0], step)
        x = x_ref[rows, :].astype(F32)
        scale = lax.rsqrt(jnp.mean(x * x, -1, keepdims=True) + EPSILON)
        grad = near_ref[rows, :].astype(F32) + far_ref[rows, :].astype(F32)
        weighted = grad * gain_ref[0:1, :]
        inner = jnp.mean(weighted * x, -1, keepdims=True)
        out_ref[own, :] = dx1_ref[rows, :] + scale * weighted - x * (scale * scale * scale * inner)


def rotary_tables(length):
    frequency = jnp.power(10000.0, -2.0 * jnp.arange(HEAD_DIM // 2, dtype=F32) / HEAD_DIM)
    angles = (jnp.arange(length) % LEN).astype(F32)[:, None] * frequency[None, :]
    shape = jax.ShapeDtypeStruct((length, PAIR), F32)
    return whole_call(tables_kernel, [jnp.cos(angles), jnp.sin(angles)], [shape] * 2, "tables")


def body(
    tokens,
    cotangent,
    gains,
    gain_moments,
    qkv_master,
    out_master,
    ffn_master,
    down_master,
    attn_left,
    attn_right,
    attn_left_root,
    attn_right_root,
    ffn_left,
    ffn_right,
    ffn_left_root,
    ffn_right_root,
    down_left,
    down_right,
    down_left_root,
    down_right_root,
):
    count = lax.axis_size("dp")
    me = lax.axis_index("dp").astype(jnp.int32)[None]
    core = lax.axis_index("narrow").astype(jnp.int32)[None]
    own_rows = tokens.shape[0]
    by_hand = count == GRID

    if by_hand:
        high = count // 4
        first, second, slab = pack(
            qkv_master[:, 0], out_master, ffn_master[:, 0], jnp.swapaxes(down_master, 2, 3)
        )
        one, two, last = 4 * HALF_D, FF, HALF_FF
        width, half, ring_start = one + two + last, (one + two + last) // 2, one + two
        many = high - 1
        far_one = all_shifted(first, count)
        slab_x, slab_y = along(slab, 1, count), along(slab, 2, count)

    x, cot = in_order(tokens, core), in_order(cotangent, core)
    cosine, sine_part = rotary_tables(x.shape[0])

    if by_hand:
        chunk = [(number, 0, one) for number in range(many)]
        near_x, near_y = copy_columns(
            [after(far_one[0], x, cot, cosine, sine_part)] + far_one[1:] + [slab_x, slab_y],
            [chunk + [(many + 1, half, width)], chunk + [(many, 0, half)]],
            "end_round_one",
        )
        one_x, one_y = along(near_x, 1, count), along(near_y, 2, count)
        far_two = all_shifted(after(second, *far_one), count)
        tail = many * one
        one_a, one_b, near_two, square = copy_columns(
            [one_x, one_y] + far_two + [slab, slab_x, slab_y],
            [
                [(0, number * one, number * one + one // 2) for number in range(many)],
                [(1, number * one + one // 2, (number + 1) * one) for number in range(many)],
                [(2 + number, 0, two) for number in range(many)],
                [(2 + many + part, ring_start, width) for part in range(3)]
                + [(0, tail + ring_start - half, tail + width - half)],
            ],
            "end_round_two",
        )
        one_a, one_b = along(one_a, 2, count), along(one_b, 1, count)
        squares = [square, shifted(square, 1, count)]
        entries = [(0, 0, one, 0, 0, 0, 0), (1, 0, one, 0, 0, 1, 0), (2, 0, one, 0, 1, 0, 0)]
        entries.append((5, tail, one, 0, 1, 1, 0))
        for number in range(many):
            step, at = number + 1, number * one
            entries += [(3, at, one, step, 0, 0, 0), (4, at, one, step, 0, 1, 0)]
            entries += [(5, at, one, step, 1, 0, 0)]
        shapes = [(D, 3 * HALF_D), (HALF_D, D)]
        early = [slab, slab_x, slab_y, near_x, one_x, one_y]
        early[0] = after(slab, near_two)
        w_early = assemble(me, high, early, entries, place_qkv_out, shapes, "place_qkv_out")
        entries = []
        for number in range(many):
            step, at = number + 1, number * (one // 2)
            entries += [(0, at, one // 2, step, 1, 1, 0), (1, at, one // 2, step, 1, 1, one // 2)]
        w_qkv, w_out = assemble(
            me, high, [one_a, one_b], entries, place_qkv_out, shapes, "place_rest", w_early
        )
        near_late = after(near_two, one_a, one_b, w_early[0], squares[1])
        two_x, two_y = along(near_late, 1, count), along(near_late, 2, count)
        squares.append(shifted(after(squares[1], one_a, one_b, w_early[0]), 1, count))
    else:
        qkv, ffn_part = qkv_master[:, 0].astype(BF16), ffn_master[:, 0].astype(BF16)
        w_qkv, w_out, w_gate, w_up, w_down = gather_by_name(
            qkv, out_master.astype(BF16), ffn_part, down_master[0].astype(BF16)
        )
    normed_one, q, k, v = project(x, gains, w_qkv, cosine, sine_part)
    attended, lse = attend(q, k, v)
    attended_late, w_out_late = attended, w_out
    if by_hand:
        two_a, two_b = copy_columns(
            [after(two_x, attended, *squares[1:]), two_y],
            [
                [(0, number * two, number * two + two // 2) for number in range(many)],
                [(1, number * two + two // 2, (number + 1) * two) for number in range(many)],
            ],
            "end_round_four",
        )
        early = [slab, slab_x, slab_y, one_x, one_y, near_two, two_x, two_y]
        early[0] = after(slab, two_a)
        attended_late, w_out_late = after(attended, two_a), after(w_out, two_a)
        two_a, two_b = along(two_a, 2, count), along(two_b, 1, count)
        cut = half - one
        entries = [(0, one, two, 0, 0, 0, 0), (1, one, two, 0, 0, 1, 0), (2, one, two, 0, 1, 0, 0)]
        entries += [(4, tail + one, cut, 0, 1, 1, 0), (3, tail, two - cut, 0, 1, 1, cut)]
        for number in range(many):
            step, at = number + 1, number * two
            entries += [(5, at, two, step, 0, 0, 0), (6, at, two, step, 0, 1, 0)]
            entries += [(7, at, two, step, 1, 0, 0)]
        shapes = [(D, HALF_FF)] * 2
        w_early = assemble(me, high, early, entries, place_gate_up, shapes, "place_gate_up")
        entries = []
        for number in range(many):
            step, at = number + 1, number * (two // 2)
            entries += [(0, at, two // 2, step, 1, 1, 0), (1, at, two // 2, step, 1, 1, two // 2)]
        w_gate, w_up = assemble(
            me,
            high,
            [two_a, two_b],
            entries,
            place_gate_up,
            shapes,
            "place_rest",
            w_early,
        )
        for _ in range(3, high):
            squares.append(shifted(after(squares[-1], w_gate), 1, count))
    attended_far, w_out_far = other_core(attended_late), other_core(w_out_late)
    middle, normed_two, gate, up, hidden = ffn(
        x, attended, attended_far, w_out, w_out_far, gains, w_gate, w_up
    )

    if by_hand:
        squares[0] = after(squares[0], hidden)
        (w_down,) = assemble(
            me,
            high,
            squares,
            [
                (step, part * last, last, step, part // 2, part % 2, 0)
                for step in range(high)
                for part in range(4)
            ],
            place_down,
            [(D, HALF_FF)],
            "place_down",
        )
    down_weight_grad = dot_tn(cot, hidden)
    cot_late = cot
    if by_hand:
        ring = ring_blocks(down_weight_grad, me, high)
        passed = shifted(ring[0], 1, count)
        cot_late = after(cot, ring[0])
    ffn_back_grad, normed_part = ffn_back(cot_late, gate, up, w_down, w_gate, w_up)
    if by_hand:
        sent = ring_add(after(passed, normed_part), ring[1])
        passed = shifted(sent, 1, count)
        ffn_back_grad = after(ffn_back_grad, sent)
        normed_part = after(normed_part, sent)
    normed_far = other_core(normed_part)
    ffn_weight_grad = dot_tn(normed_two, ffn_back_grad)
    if by_hand:
        ffn_sum = reduction([take_rows], FF, count, me, [ffn_weight_grad])
        sent = ffn_sum[0]()
        normed_far = after(normed_far, sent[0])
        ffn_far = send_first(*sent, count)
    middle_grad, branch, attended_grad, gain_two = middle_back(
        cot, middle, normed_part, normed_far, gains, w_out
    )
    out_weight_grad = dot_tn(attended, branch)
    out_part = ffn_out(after(hidden, branch), w_down)
    out_part_late = out_part
    if by_hand:
        late = [branch, out_part, out_weight_grad]
        for number in range(2, high - 1):
            sent = ring_add(after(passed, *late), ring[number])
            passed = shifted(sent, 1, count)
            late.append(sent)
        sent = ffn_sum[1](after(ffn_far[0], *late), ffn_far[1])
        ffn_far = send_second(*sent, count)
        attended_grad = after(attended_grad, sent[0])
        out_part_late = after(out_part, sent[0])
    out_far = other_core(out_part_late)
    qkv_back_grad = attend_back(q, k, v, attended_grad, attended, lse, cosine, sine_part)
    layer_out = whole_call(
        layer_out_kernel,
        [core, after(middle, qkv_back_grad), out_part, out_far],
        [jax.ShapeDtypeStruct((own_rows, D), BF16)],
        "layer_out",
        1,
    )[0]
    if by_hand:
        down_near = ring_add(after(passed, qkv_back_grad, layer_out), ring[-1])
        ffn_sent = ffn_sum[2](after(ffn_far[0], qkv_back_grad, layer_out), ffn_far[1])
        ffn_parts = [ffn_sent[0]] + [
            shifted(block, step + 1, count)
            for step, block in enumerate(ffn_sent[1:])
            if step + 1 != high // 2
        ]
        qkv_back_grad = after(qkv_back_grad, ffn_sent[0])
    qkv_weight_grad = dot_tn(normed_one, qkv_back_grad)
    if by_hand:
        late_sum = reduction(
            [take_rows, take_out], 4 * HALF_D, count, me, [qkv_weight_grad, out_weight_grad]
        )
        sent = late_sum[0](down_near)
        late_far = list(send_first(*sent, count))
        qkv_back_grad = after(qkv_back_grad, sent[0])
    input_part, gain_one = input_back(x, qkv_back_grad, w_qkv)
    input_part_late = input_part
    if by_hand:
        state = gain_rows(gain_one, gain_two)
        state = added(state, other_core(state), "add_gains")
        late_cut = 2 * HALF_D
        parts = [(0, late_cut), (late_cut, 2 * late_cut)]
        late_far[0] = after(late_far[0], *ffn_parts[1:])
        sent = late_sum[1](*late_far, state, down_near, part=parts[0])
        first_far = send_second(*sent, count)
        ffn_parts.append(shifted(after(ffn_sent[high // 2], sent[0]), high // 2, count))
        input_part_late = after(input_part, sent[0])
        second_sent = late_sum[1](after(late_far[0], sent[0]), late_far[1], part=parts[1])
    input_far = other_core(input_part_late)
    input_grad = whole_call(
        input_grad_kernel,
        [core, x, middle_grad, input_part, input_far, gains],
        [jax.ShapeDtypeStruct((own_rows, D), F32)],
        "input_grad",
        1,
    )[0]
    if by_hand:
        second_far = send_second(
            after(second_sent[0], input_grad, *first_far, *ffn_parts[1:]), second_sent[1], count
        )
        first_state, *sent = late_sum[2](
            *first_far,
            state,
            part=parts[0],
        )
        first_parts = send_third(*sent, count=count)
        ffn_parts[0] = after(ffn_parts[0], sent[0])
        ffn_grad, ffn_left_new, ffn_right_new, ffn_new = precondition(
            ffn_parts,
            FBLK,
            ffn_left[:, 0],
            ffn_right[:, 0],
            ffn_left_root[:, 0],
            ffn_right_root[:, 0],
            [ffn_master[:, 0]],
        )
        sent = late_sum[2](after(second_far[0], ffn_left_new), second_far[1], part=parts[1])
        second_parts = send_third(*sent, count=count)
        first_state = slow_state(after(first_state, sent[0]), first_parts[1:])
        wide = high * late_cut
        down_grad, down_left_new, down_right_new, down_new = precondition(
            [after(down_near, first_state), *first_far],
            FBLK,
            down_left,
            down_right,
            down_left_root,
            down_right_root,
            [jnp.swapaxes(down_master, 2, 3)],
            turned=True,
            starts=[0, wide + 128, wide],
        )
        down_grad, down_new = jnp.swapaxes(down_grad, 2, 3), jnp.swapaxes(down_new, 2, 3)
        first_parts[0] = after(first_parts[0], down_left_new)
        gain_grad, gain_moment_new, gain_new = whole_call(
            gains_kernel,
            [first_state, along(first_state, 2, count), gains, gain_moments],
            [jax.ShapeDtypeStruct(gains.shape, F32)] * 3,
            "gains",
        )
        attn_results = ()
        for matrices, some in ((range(2), first_parts), (range(2, 4), second_parts)):
            attn_results = precondition(
                some,
                DBLK,
                attn_left[:, 0],
                attn_right[:, 0],
                attn_left_root[:, 0],
                attn_right_root[:, 0],
                [qkv_master[:, 0], out_master],
                matrices=matrices,
                carry=attn_results,
            )
            second_parts[0] = after(second_parts[0], gain_grad, attn_results[0])
        *stacked, out_new = attn_results
        attn_grad, attn_left_new, attn_right_new, qkv_new = (array[:, None] for array in stacked)
        ffn_grad, ffn_left_new, ffn_right_new, ffn_new = (
            array[:, None] for array in (ffn_grad, ffn_left_new, ffn_right_new, ffn_new)
        )
    else:
        gain_terms = jnp.concatenate([gain_one, 0.5 * gain_two])
        gain_grad = lax.psum(gain_terms, ("dp", "narrow"))
        gain_moment_new = DECAY * gain_moments + (1.0 - DECAY) * gain_grad * gain_grad
        gain_new = gains - GAIN_RATE * gain_grad / (jnp.sqrt(gain_moment_new) + 1e-08)
        qkv_owned, out_owned, ffn_owned, down_owned = scatter_all(
            qkv_weight_grad, out_weight_grad, ffn_weight_grad, down_weight_grad, count
        )
        attn_grad = jnp.concatenate([qkv_owned, out_owned[None]], 0)[:, None]
        ffn_grad = ffn_owned[:, None]
        down_grad = down_owned[None]
        attn_left_new, attn_right_new, attn_new = plain_precondition(
            attn_grad,
            attn_left,
            attn_right,
            attn_left_root,
            attn_right_root,
            jnp.concatenate([qkv_master, out_master[None]], 0),
        )
        qkv_new, out_new = attn_new[:3], attn_new[3]
        ffn_left_new, ffn_right_new, ffn_new = plain_precondition(
            ffn_grad, ffn_left, ffn_right, ffn_left_root, ffn_right_root, ffn_master
        )
        down_left_new, down_right_new, down_new = plain_precondition(
            down_grad, down_left, down_right, down_left_root, down_right_root, down_master
        )
    return (
        layer_out,
        input_grad,
        gain_grad,
        gain_moment_new,
        gain_new,
        attn_grad,
        attn_left_new,
        attn_right_new,
        qkv_new,
        out_new,
        ffn_grad,
        ffn_left_new,
        ffn_right_new,
        ffn_new,
        down_grad,
        down_left_new,
        down_right_new,
        down_new,
    )


def solution(mesh):
    tokens = P(("dp", "narrow"), None)
    stacked = P(None, "narrow", "dp", None, None)
    single = P("narrow", "dp", None, None)
    return jax.shard_map(
        body,
        mesh=mesh,
        in_specs=(tokens, tokens, P(), P(), stacked, single, stacked, single)
        + (stacked,) * 8
        + (single,) * 4,
        out_specs=(tokens, tokens, P(), P(), P())
        + (stacked,) * 4
        + (single,)
        + (stacked,) * 4
        + (single,) * 4,
        check_vma=False,
    )
```

```python
import functools
import math

import jax
import jax.numpy as jnp
from jax import lax
from jax.experimental import pallas as pl
from jax.experimental.pallas import tpu as pltpu
from jax.sharding import PartitionSpec as P

D = 768
HEAD_DIM = 64
FF = 2048
LEN = 1024
GRID = 16
DBLK = D // GRID
FBLK = FF // GRID
HALF_GRID = GRID // 2
HALF_D = D // 2
HALF_FF = FF // 2
PAIR = 2 * HEAD_DIM
ROWS = 256

EPSILON = 1e-05
DECAY = 0.5
STEP_RATE = 0.25
GAIN_RATE = 0.1
NEG_FILL = -1e30
HIGHEST_PRECISION = lax.Precision.HIGHEST
BF16 = jnp.bfloat16
F32 = jnp.float32
VMEM_MIB = 18
DENSE_ROWS = 512
TILE = 256
WIDE_TILE = 512
SMALL_MIB = 8
PACK_MIB = 60
STATE_ROWS = 16


def dot_nn(left, right):
    return lax.dot_general(left, right, (((1,), (0,)), ((), ())), preferred_element_type=F32)


def dot_nt(left, right):
    return lax.dot_general(left, right, (((1,), (1,)), ((), ())), preferred_element_type=F32)


def dot_tn(left, right):
    return lax.dot_general(left, right, (((0,), (0,)), ((), ())), preferred_element_type=F32)


def kernel_params(mib=VMEM_MIB):
    return pltpu.CompilerParams(vmem_limit_bytes=mib * 1024 * 1024)


def cost():
    return pl.CostEstimate(flops=0, bytes_accessed=0, transcendentals=0)


def whole_call(kernel, inputs, shapes, name, scalars=0, mib=SMALL_MIB, scratch=()):
    vmem = pl.BlockSpec(memory_space=pltpu.VMEM)
    smem = pl.BlockSpec(memory_space=pltpu.SMEM)
    return pl.pallas_call(
        kernel,
        in_specs=[smem] * scalars + [vmem] * (len(inputs) - scalars),
        out_specs=[vmem] * len(shapes),
        out_shape=shapes,
        scratch_shapes=list(scratch),
        compiler_params=kernel_params(mib),
        cost_estimate=cost(),
        name=name,
    )(*inputs)


def over_rows(length, rows, work):
    @pl.loop(0, length // rows)
    def _(step):
        work(pl.ds(pl.multiple_of(step * rows, rows), rows))


def lower_lanes(shape):
    return lax.broadcasted_iota(jnp.int32, shape, 1) % HEAD_DIM < HEAD_DIM // 2


def turn(features, cosine, sine_part, lower):
    half = HEAD_DIM // 2
    partner = jnp.where(
        lower, pltpu.roll(features, PAIR - half, 1), pltpu.roll(features, half, 1)
    )
    return features * cosine + partner * sine_part


def project_kernel(x_ref, gain_ref, w_ref, cos_ref, sin_ref, n1_ref, q_ref, k_ref, v_ref):
    lower = lower_lanes((DENSE_ROWS, PAIR))

    def work(rows):
        x = x_ref[rows, :].astype(F32)
        scale = lax.rsqrt(jnp.mean(x * x, -1, keepdims=True) + EPSILON)
        normed = (x * scale * gain_ref[0:1, :]).astype(BF16)
        n1_ref[rows, :] = normed
        cosine, sine_part = cos_ref[rows, :], sin_ref[rows, :]
        both = dot_nn(normed, w_ref[...])
        for tile in range(HALF_D // PAIR):
            lanes = slice(tile * PAIR, (tile + 1) * PAIR)
            query = both[:, tile * PAIR : (tile + 1) * PAIR]
            key = both[:, HALF_D + tile * PAIR : HALF_D + (tile + 1) * PAIR]
            turned = turn(query, cosine, sine_part, lower).astype(BF16)
            q_ref[rows, lanes] = turned * BF16(1.0 / math.sqrt(HEAD_DIM))
            k_ref[rows, lanes] = turn(key, cosine, sine_part, lower).astype(BF16)
        v_ref[rows, :] = both[:, 2 * HALF_D :].astype(BF16)

    over_rows(x_ref.shape[0], DENSE_ROWS, work)


def project(x, gains, weight, cosine, sine_part):
    length = x.shape[0]
    half = jax.ShapeDtypeStruct((length, HALF_D), BF16)
    shapes = [jax.ShapeDtypeStruct((length, D), BF16), half, half, half]
    return whole_call(
        project_kernel, [x, gains, weight, cosine, sine_part], shapes, "project", mib=VMEM_MIB
    )


def attend_kernel(q_ref, k_ref, v_ref, o_ref, lse_ref):
    @pl.loop(0, q_ref.shape[1] // PAIR)
    def _(pair):
        lanes = pl.ds(pl.multiple_of(pair * PAIR, PAIR), PAIR)
        rows = pl.ds(pl.multiple_of(pair * 8, 8), 8)
        attend_pair(
            *(ref.at[:, lanes] for ref in (q_ref, k_ref, v_ref, o_ref)), lse_ref.at[rows, :]
        )


def attend_pair(q_ref, k_ref, v_ref, o_ref, lse_ref):
    length = q_ref.shape[0]
    first_head = lax.broadcasted_iota(jnp.int32, (ROWS, PAIR), 1) < HEAD_DIM
    keys = k_ref[...]
    values = jnp.concatenate([v_ref[...], jnp.ones((length, PAIR), BF16)], 1)
    causal = lax.broadcasted_iota(jnp.int32, (2 * ROWS, ROWS), 0) % ROWS >= (
        lax.broadcasted_iota(jnp.int32, (2 * ROWS, ROWS), 1)
    )
    for block in range(length // ROWS):
        rows = slice(block * ROWS, (block + 1) * ROWS)
        width = (block + 1) * ROWS
        query_block = q_ref[rows, :]
        zero = jnp.zeros_like(query_block)
        query = jnp.concatenate(
            [jnp.where(first_head, query_block, zero), jnp.where(first_head, zero, query_block)], 0
        )
        scores = jnp.where(causal, dot_nt(query, keys[block * ROWS : width]), NEG_FILL)
        if block:
            scores = jnp.concatenate([dot_nt(query, keys[: block * ROWS]), scores], 1)
        top = jnp.max(scores, 1, keepdims=True)
        exponent = jnp.exp(scores - top).astype(BF16)
        product = dot_nn(exponent, values[:width])
        total = product[:, PAIR:]
        out = product[:, :PAIR] / total
        sums = top + jnp.log(total)
        o_ref[rows, :] = jnp.where(first_head, out[:ROWS], out[ROWS:]).astype(BF16)
        lane = lax.broadcasted_iota(jnp.int32, (ROWS, PAIR), 1)
        lse_ref[:, rows] = jnp.transpose(jnp.where(lane == 0, sums[:ROWS], sums[ROWS:]))[:8, :]


def attend(q, k, v):
    length = q.shape[0]
    shapes = [
        jax.ShapeDtypeStruct(q.shape, BF16),
        jax.ShapeDtypeStruct((8 * (q.shape[1] // PAIR), length), F32),
    ]
    return whole_call(attend_kernel, [q, k, v], shapes, "attend", mib=VMEM_MIB)


def attend_back_kernel(
    q_ref, k_ref, v_ref, do_ref, o_ref, lse_ref, cos_ref, sin_ref, grad_ref, dqt_ref
):
    @pl.loop(0, q_ref.shape[1] // PAIR)
    def _(pair):
        lanes = pl.ds(pl.multiple_of(pair * PAIR, PAIR), PAIR)
        rows = pl.ds(pl.multiple_of(pair * 8, 8), 8)
        attend_back_pair(
            *(ref.at[:, lanes] for ref in (q_ref, k_ref, v_ref, do_ref, o_ref)),
            lse_ref.at[rows, :],
            cos_ref,
            sin_ref,
            *(
                grad_ref.at[:, pl.ds(pl.multiple_of(at * HALF_D + pair * PAIR, PAIR), PAIR)]
                for at in range(3)
            ),
            dqt_ref,
        )


def attend_back_pair(
    q_ref, k_ref, v_ref, do_ref, o_ref, lse_ref, cos_ref, sin_ref, dq_ref, dk_ref, dv_ref, dqt_ref
):
    length = q_ref.shape[0]
    first_head = lax.broadcasted_iota(jnp.int32, (length, PAIR), 1) < HEAD_DIM
    zero = BF16(0)
    queries = [
        jnp.where(first_head, q_ref[...], zero),
        jnp.where(first_head, zero, q_ref[...]),
    ]
    grads = [
        jnp.where(first_head, do_ref[...], zero),
        jnp.where(first_head, zero, do_ref[...]),
    ]
    product = do_ref[...].astype(F32) * o_ref[...].astype(F32)
    head_row = lax.broadcasted_iota(jnp.int32, (8, PAIR), 0)
    head_lane = lax.broadcasted_iota(jnp.int32, (8, PAIR), 1) // HEAD_DIM
    inner = lax.dot_general(
        (head_row == head_lane).astype(F32),
        product,
        (((1,), (1,)), ((), ())),
        preferred_element_type=F32,
        precision=HIGHEST_PRECISION,
    )
    turned_keys = jnp.transpose(k_ref[...].astype(F32)).astype(BF16)
    first_rows = lax.broadcasted_iota(jnp.int32, turned_keys.shape, 0) < HEAD_DIM
    key_heads = [
        jnp.where(first_rows, turned_keys, zero),
        jnp.where(first_rows, zero, turned_keys),
    ]
    causal = lax.broadcasted_iota(jnp.int32, (ROWS, ROWS), 0) <= lax.broadcasted_iota(
        jnp.int32, (ROWS, ROWS), 1
    )
    dqt_ref[...] = jnp.zeros_like(dqt_ref)
    lower = lower_lanes((ROWS, PAIR))
    for block in range(length // ROWS):
        rows = slice(block * ROWS, (block + 1) * ROWS)
        start = block * ROWS
        key_block, value_block = k_ref[rows, :], v_ref[rows, :]
        dk = jnp.zeros((ROWS, PAIR), F32)
        dv = jnp.zeros((ROWS, PAIR), F32)
        for head in range(2):
            scores = dot_nt(key_block, queries[head][start:])
            probs = jnp.exp(scores - lse_ref[head : head + 1, start:])
            diagonal = jnp.where(causal, probs[:, :ROWS], 0.0)
            if start + ROWS == length:
                probs = diagonal
            else:
                probs = jnp.concatenate([diagonal, probs[:, ROWS:]], 1)
            prob_grad = dot_nt(value_block, grads[head][start:])
            score_grad = (probs * (prob_grad - inner[head : head + 1, start:])).astype(BF16)
            dv = dv + dot_nn(probs.astype(BF16), grads[head][start:])
            dk = dk + dot_nn(score_grad, queries[head][start:])
            dqt_ref[:, start:] += dot_nn(key_heads[head][:, rows], score_grad)
        dk_ref[rows, :] = turn(dk, cos_ref[rows, :], -sin_ref[rows, :], lower).astype(BF16)
        dv_ref[rows, :] = dv.astype(BF16)
    for block in range(length // ROWS):
        rows = slice(block * ROWS, (block + 1) * ROWS)
        dq = jnp.transpose(dqt_ref[:, rows]) * (1.0 / math.sqrt(HEAD_DIM))
        dq_ref[rows, :] = turn(dq, cos_ref[rows, :], -sin_ref[rows, :], lower).astype(BF16)


def attend_back(q, k, v, grad, o, lse, cosine, sine_part):
    return whole_call(
        attend_back_kernel,
        [q, k, v, grad, o, lse, cosine, sine_part],
        [jax.ShapeDtypeStruct((q.shape[0], 3 * q.shape[1]), BF16)],
        "attend_back",
        mib=VMEM_MIB,
        scratch=[pltpu.VMEM((PAIR, q.shape[0]), F32)],
    )[0]


def ffn_kernel(
    x_ref, o_ref, o_far_ref, wo_ref, wo_far_ref, gain_ref, wg_ref, wu_ref,
    x1_ref, n2_ref, gate_ref, up_ref, hidden_ref,
):
    def work(rows):
        middle = (
            x_ref[rows, :].astype(F32)
            + dot_nn(o_ref[rows, :], wo_ref[...])
            + dot_nn(o_far_ref[rows, :], wo_far_ref[...])
        )
        x1_ref[rows, :] = middle
        scale = lax.rsqrt(jnp.mean(middle * middle, -1, keepdims=True) + EPSILON)
        normed = (middle * scale * gain_ref[1:2, :]).astype(BF16)
        n2_ref[rows, :] = normed

        @pl.loop(0, HALF_FF // TILE)
        def _(tile):
            lanes = pl.ds(pl.multiple_of(tile * TILE, TILE), TILE)
            gate = dot_nn(n2_ref[rows, :], wg_ref[:, lanes])
            up = dot_nn(n2_ref[rows, :], wu_ref[:, lanes])
            gate_ref[rows, lanes] = gate
            up_ref[rows, lanes] = up
            hidden_ref[rows, lanes] = (gate * jax.nn.sigmoid(gate) * up).astype(BF16)

    over_rows(x_ref.shape[0], DENSE_ROWS, work)


def ffn(*inputs):
    length = inputs[0].shape[0]
    shapes = [
        jax.ShapeDtypeStruct((length, width), kind)
        for width, kind in ((D, F32), (D, BF16), (HALF_FF, F32), (HALF_FF, F32), (HALF_FF, BF16))
    ]
    return whole_call(ffn_kernel, inputs, shapes, "ffn", mib=VMEM_MIB)


def ffn_out_kernel(hidden_ref, wdt_ref, part_ref):
    def work(rows):
        part_ref[rows, :] = dot_nt(hidden_ref[rows, :], wdt_ref[...]).astype(BF16)

    over_rows(hidden_ref.shape[0], DENSE_ROWS, work)


def ffn_out(hidden, wdt):
    shape = jax.ShapeDtypeStruct((hidden.shape[0], D), BF16)
    return whole_call(ffn_out_kernel, [hidden, wdt], [shape], "ffn_out", mib=VMEM_MIB)[0]


def ffn_back_kernel(cot_ref, gate_ref, up_ref, wdt_ref, wg_ref, wu_ref, dgu_ref, dn2_ref):
    def work(rows):
        @pl.loop(0, HALF_FF // WIDE_TILE)
        def _(tile):
            lanes = pl.ds(pl.multiple_of(tile * WIDE_TILE, WIDE_TILE), WIDE_TILE)
            up_lanes = pl.ds(pl.multiple_of(HALF_FF + tile * WIDE_TILE, WIDE_TILE), WIDE_TILE)
            hidden_grad = dot_nn(cot_ref[rows, :], wdt_ref[:, lanes])
            gate, up = gate_ref[rows, lanes], up_ref[rows, lanes]
            sigma = jax.nn.sigmoid(gate)
            gate_grad = hidden_grad * up * sigma * (1.0 + gate * (1.0 - sigma))
            dgu_ref[rows, lanes] = gate_grad.astype(BF16)
            dgu_ref[rows, up_lanes] = (hidden_grad * gate * sigma).astype(BF16)

        @pl.loop(0, D // TILE)
        def _(tile):
            lanes = pl.ds(pl.multiple_of(tile * TILE, TILE), TILE)
            dn2 = dot_nt(dgu_ref[rows, :HALF_FF], wg_ref[lanes, :]) + dot_nt(
                dgu_ref[rows, HALF_FF:], wu_ref[lanes, :]
            )
            dn2_ref[rows, lanes] = dn2.astype(BF16)

    over_rows(cot_ref.shape[0], DENSE_ROWS, work)


def ffn_back(cot, gate, up, wdt, wg, wu):
    shapes = [jax.ShapeDtypeStruct((cot.shape[0], width), BF16) for width in (FF, D)]
    return whole_call(
        ffn_back_kernel, [cot, gate, up, wdt, wg, wu], shapes, "ffn_back", mib=VMEM_MIB
    )


def middle_back_kernel(
    cot_ref, x1_ref, near_ref, far_ref, gain_ref, wo_ref, dx1_ref, da_ref, do_ref, g2_ref
):
    g2_ref[...] = jnp.zeros_like(g2_ref)

    def work(rows):
        middle = x1_ref[rows, :]
        scale = lax.rsqrt(jnp.mean(middle * middle, -1, keepdims=True) + EPSILON)
        grad = near_ref[rows, :].astype(F32) + far_ref[rows, :].astype(F32)
        weighted = grad * gain_ref[1:2, :]
        inner = jnp.mean(weighted * middle, -1, keepdims=True)
        middle_grad = (
            cot_ref[rows, :].astype(F32)
            + scale * weighted
            - middle * (scale * scale * scale * inner)
        )
        dx1_ref[rows, :] = middle_grad
        branch = middle_grad.astype(BF16)
        da_ref[rows, :] = branch
        do_ref[rows, :] = dot_nt(branch, wo_ref[...]).astype(BF16)
        g2_ref[...] += jnp.sum(grad * middle * scale, 0, keepdims=True)

    over_rows(cot_ref.shape[0], DENSE_ROWS, work)


def middle_back(*inputs):
    length = inputs[0].shape[0]
    shapes = [
        jax.ShapeDtypeStruct(shape, kind)
        for shape, kind in (
            ((length, D), F32),
            ((length, D), BF16),
            ((length, HALF_D), BF16),
            ((1, D), F32),
        )
    ]
    return whole_call(middle_back_kernel, inputs, shapes, "middle_back", mib=VMEM_MIB)


def input_back_kernel(x_ref, dqkv_ref, w_ref, part_ref, g1_ref):
    g1_ref[...] = jnp.zeros_like(g1_ref)

    def work(rows):
        grad = dot_nt(dqkv_ref[rows, :], w_ref[...])
        part_ref[rows, :] = grad.astype(BF16)
        x = x_ref[rows, :].astype(F32)
        scale = lax.rsqrt(jnp.mean(x * x, -1, keepdims=True) + EPSILON)
        g1_ref[...] += jnp.sum(grad * x * scale, 0, keepdims=True)

    over_rows(x_ref.shape[0], DENSE_ROWS, work)


def input_back(x, dqkv, w):
    shapes = [jax.ShapeDtypeStruct(x.shape, BF16), jax.ShapeDtypeStruct((1, D), F32)]
    return whole_call(input_back_kernel, [x, dqkv, w], shapes, "input_back", mib=VMEM_MIB)


def pair_up(bit, count):
    return [(i, i ^ bit) for i in range(count)]


def after(value, *others):
    return lax.optimization_barrier((value,) + others)[0]


def along(values, bit, count):
    return lax.ppermute(values, "dp", pair_up(bit, count))


def shifted(values, steps, count):
    return lax.ppermute(values, "dp", [(i, (i + 4 * steps) % count) for i in range(count)])


def other_core(values):
    return lax.ppermute(values, "narrow", [(0, 1), (1, 0)])


def all_shifted(values, count):
    return [shifted(values, step, count) for step in range(1, count // 4)]


def copy_columns(sources, outputs, name):
    rows = sources[0].shape[0]
    shapes = [
        jax.ShapeDtypeStruct((rows, sum(stop - start for _, start, stop in parts)), BF16)
        for parts in outputs
    ]

    def kernel(*refs):
        for out_ref, parts in zip(refs[len(sources) :], outputs):
            at = 0
            for number, start, stop in parts:
                out_ref[:, at : at + stop - start] = refs[number][:, start:stop]
                at += stop - start

    return whole_call(kernel, sources, shapes, name)


def block_rows(owner):
    return pl.ds(pl.multiple_of(owner * DBLK, 16), DBLK)


def block_lanes(index, width):
    return pl.ds(pl.multiple_of(index * width, 128), width)


def place_qkv_out(owner, start, piece, qkv_ref, out_ref):
    cut, stop = 3 * HALF_D, start + piece.shape[1]
    if start < cut:
        end = min(stop, cut)
        qkv_ref[block_rows(owner), start:end] = piece[:, : end - start]
    if stop > cut:
        begin = max(start, cut)
        lanes = pl.ds(pl.multiple_of(owner % 2 * HALF_D + (begin - cut), 128), stop - begin)
        out_ref[block_rows(owner // 2), lanes] = piece[:, begin - start :]


def place_gate_up(owner, start, piece, gate_ref, up_ref):
    stop = start + piece.shape[1]
    if start < HALF_FF:
        end = min(stop, HALF_FF)
        gate_ref[block_rows(owner), start:end] = piece[:, : end - start]
    if stop > HALF_FF:
        begin = max(start, HALF_FF)
        up_ref[block_rows(owner), begin - HALF_FF : stop - HALF_FF] = piece[:, begin - start :]


def place_down(owner, start, piece, out_ref):
    lanes = block_lanes(owner // 2, FBLK)
    for block in range(piece.shape[1] // FBLK):
        rows = block_rows(owner % 2 * HALF_GRID + start // FBLK + block)
        out_ref[rows, lanes] = piece[:, block * FBLK : (block + 1) * FBLK]


def assemble(me, high, sources, entries, place, shapes, name, begun=()):
    sources = list(sources)

    def kernel(me_ref, *refs):
        x, y, z = me_ref[0] % 2, me_ref[0] // 2 % 2, me_ref[0] // 4
        out_refs = refs[len(sources) + len(begun) :]
        for ref, out_ref in zip(refs[len(sources) :], out_refs if begun else ()):
            out_ref[...] = ref[...]
        for number, start, width, step, over_y, over_x, first in entries:
            slow = (z - step + high) % high
            from_y = 1 - y if over_y else y
            from_x = 1 - x if over_x else x
            piece = refs[number][:, start : start + width]
            place(slow * 4 + from_y * 2 + from_x, first, piece, *out_refs)

    return whole_call(
        kernel,
        [me] + sources + list(begun),
        [jax.ShapeDtypeStruct(shape, BF16) for shape in shapes],
        name,
        1,
    )


def pack_kernel(qkv_ref, out_ref, ffn_ref, down_ref, first_ref, second_ref, slab_ref, *scratch):
    held, sems = scratch[:-1], scratch[-1]
    copies = [
        pltpu.make_async_copy(ref, here, sems.at[number])
        for number, (ref, here) in enumerate(zip((qkv_ref, out_ref, ffn_ref, down_ref), held))
    ]
    for copy in copies:
        copy.start()

    def row(ref, matrix):
        return jnp.concatenate([ref[matrix, block].astype(BF16) for block in range(HALF_GRID)], 1)

    at = 0
    for copy, ref in zip(copies, held):
        copy.wait()
        for matrix in range(ref.shape[0]):
            part = row(ref, matrix)
            stop = at + part.shape[1]
            slab_ref[:, at:stop] = part
            if stop <= first_ref.shape[1]:
                first_ref[:, at:stop] = part
            elif stop <= first_ref.shape[1] + second_ref.shape[1]:
                second_ref[:, at - first_ref.shape[1] : stop - first_ref.shape[1]] = part
            at = stop


def pack(*masters):
    vmem = pl.BlockSpec(memory_space=pltpu.VMEM)
    return pl.pallas_call(
        pack_kernel,
        in_specs=[pl.BlockSpec(memory_space=pl.ANY)] * len(masters),
        out_specs=[vmem] * 3,
        out_shape=[
            jax.ShapeDtypeStruct((DBLK, width), BF16)
            for width in (4 * HALF_D, FF, 4 * HALF_D + 3 * HALF_FF)
        ],
        scratch_shapes=[pltpu.VMEM(master.shape, F32) for master in masters]
        + [pltpu.SemaphoreType.DMA((len(masters),))],
        compiler_params=kernel_params(PACK_MIB),
        cost_estimate=cost(),
        name="pack",
    )(*masters)


def tables_kernel(cos_ref, sin_ref, cosine_ref, sine_ref):
    cosine, sine = cos_ref[...], sin_ref[...]
    cosine_ref[...] = jnp.concatenate([cosine] * 4, 1)
    sine_ref[...] = jnp.concatenate([-sine, sine] * 2, 1)


def side_by_side(blocks):
    matrices, many, height, width = blocks.shape
    return blocks.transpose(2, 0, 1, 3).reshape(height, matrices * many * width)


def gather_by_name(qkv, out, ffn_part, down):
    qkv_all = lax.all_gather(qkv, "dp", axis=1, tiled=True)
    out_all = lax.all_gather(out[0], "dp", axis=0, tiled=True)
    ffn_all = lax.all_gather(ffn_part, "dp", axis=1, tiled=True)
    down_all = lax.all_gather(down, "dp", axis=0, tiled=True)
    w_qkv = qkv_all.reshape(3, GRID, HALF_GRID, DBLK, DBLK).transpose(1, 3, 0, 2, 4)
    w_out = out_all.reshape(HALF_GRID, GRID, DBLK, DBLK).transpose(0, 2, 1, 3)
    w_ffn = ffn_all.reshape(2, GRID, HALF_GRID, DBLK, FBLK).transpose(0, 1, 3, 2, 4)
    w_down = down_all.reshape(HALF_GRID, GRID, FBLK, DBLK).transpose(1, 3, 0, 2)
    w_ffn = w_ffn.reshape(2, D, HALF_FF)
    return (
        w_qkv.reshape(D, 3 * HALF_D),
        w_out.reshape(HALF_D, D),
        w_ffn[0],
        w_ffn[1],
        w_down.reshape(D, HALF_FF),
    )


def take_rows(owner, ref):
    return ref[block_rows(owner), :]


def take_out(owner, ref):
    return ref[block_rows(owner // 2), pl.ds(pl.multiple_of(owner % 2 * HALF_D, 128), HALF_D)]


def take_down(owner, ref):
    lanes = pl.ds(pl.multiple_of(owner // 2 * FBLK, 128), FBLK)
    return jnp.concatenate(
        [ref[block_rows(owner % 2 * HALF_GRID + block), lanes] for block in range(HALF_GRID)], 1
    )


def paired(values):
    high = values.astype(BF16)
    low = (values - high.astype(F32)).astype(BF16)
    rest = jnp.zeros((DBLK - 2 * values.shape[0], values.shape[1]), BF16)
    return jnp.concatenate([high, low, rest], 0)


def unpaired(pair):
    rows = STATE_ROWS
    return pair[:rows].astype(F32) + pair[rows : 2 * rows].astype(F32)


def reduction(takes, columns, count, me, grads):
    high = count // 4
    half = high // 2
    many = len(grads)

    def step(kernel, inputs, shapes, name):
        return whole_call(kernel, [me] + grads + inputs, shapes, name, 1)

    def find(refs, slow, y, x, part):
        owner = slow * 4 + y * 2 + x
        found = [take(owner, ref) for take, ref in zip(takes, refs)]
        found = found[0] if len(found) == 1 else jnp.concatenate(found, 1)
        return found[:, part[0] : part[1]].astype(F32)

    def place(me_ref):
        return me_ref[0] % 2, me_ref[0] // 2 % 2, me_ref[0] // 4

    def piece(index, width=columns, start=0, every=None):
        first = index * (every or width) + start
        return pl.ds(pl.multiple_of(first, 128), width)

    def diagonal_kernel(me_ref, *refs):
        x, y, _ = place(me_ref)
        *guest_refs, to_y_ref, to_x_ref = refs[many:]
        for guest_ref in guest_refs:
            wide = guest_ref.shape[1] // 4
            middle = 3 * wide + wide // 2
            to_y_ref[:, half * columns :] = guest_ref[:, 3 * wide : middle].astype(BF16)
            to_x_ref[:, half * columns :] = guest_ref[:, middle:].astype(BF16)

        @pl.loop(0, half)
        def _(step):
            whole = (0, columns)
            to_y_ref[:, piece(step)] = find(refs, step, 1 - y, 1 - x, whole).astype(BF16)
            to_x_ref[:, piece(step)] = find(refs, half + step, 1 - y, 1 - x, whole).astype(BF16)

    def side_kernel(part, me_ref, *refs):
        x, y, _ = place(me_ref)
        by_y_ref, by_x_ref, *state_refs, to_x_ref, to_y_ref = refs[many:]
        width = part[1] - part[0]
        if state_refs:
            guest_ref = state_refs[1]
            wide = guest_ref.shape[1] // 4
            cut, start = wide // 2, high * width + 128
            by_y = by_y_ref[:, half * columns :].astype(F32)
            by_x = by_x_ref[:, half * columns :].astype(F32)
            to_x_ref[:, start : start + cut] = (guest_ref[:, wide : wide + cut] + by_y).astype(BF16)
            to_x_ref[:, start + cut :] = guest_ref[:, wide + cut : 2 * wide].astype(BF16)
            start = high * width
            to_y_ref[:, start : start + cut] = guest_ref[:, 2 * wide : 2 * wide + cut].astype(BF16)
            to_y_ref[:, start + cut :] = (
                guest_ref[:, 2 * wide + cut : 3 * wide] + by_x
            ).astype(BF16)

        @pl.loop(0, half)
        def _(step):
            lanes = piece(step, width, part[0], columns)
            for slow, by_y, by_x in ((step, by_y_ref, None), (half + step, None, by_x_ref)):
                to_x = find(refs, slow, y, 1 - x, part)
                to_y = find(refs, slow, 1 - y, x, part)
                if by_y is not None:
                    to_x = to_x + by_y[:, lanes].astype(F32)
                else:
                    to_y = to_y + by_x[:, lanes].astype(F32)
                to_x_ref[:, piece(slow, width)] = to_x.astype(BF16)
                to_y_ref[:, piece(slow, width)] = to_y.astype(BF16)

        if state_refs:
            to_x_ref[:, high * width : high * width + 128] = paired(state_refs[0][...])

    def slow_kernel(part, me_ref, *refs):
        x, y, z = place(me_ref)
        from_x_ref, from_y_ref, *state_refs = refs[many : len(refs) - high]
        out_refs = refs[len(refs) - high :]
        width = part[1] - part[0]
        if state_refs:
            before_ref, after_ref = state_refs
            lanes = slice(high * width, high * width + 128)
            state = unpaired(paired(before_ref[...])) + unpaired(from_x_ref[:, lanes])
            after_ref[...] = state
        for shift in range(high):
            rows = pl.ds(0, DBLK)
            slow = (z + shift) % high
            lanes = pl.ds(pl.multiple_of(slow * width, 128), width)
            total = (
                find(refs, slow, y, x, part)
                + from_x_ref[rows, lanes].astype(F32)
                + from_y_ref[rows, lanes].astype(F32)
            )
            out_refs[shift][:, :width] = total.astype(out_refs[shift].dtype)
            if state_refs and shift:
                out_refs[shift][:, width:] = paired(state)

    def rows(width, kind=BF16):
        return jax.ShapeDtypeStruct((DBLK, width), kind)

    state_shape = jax.ShapeDtypeStruct((STATE_ROWS, 128), F32)

    def first(*guest):
        extra = sum(array.shape[1] // 8 for array in guest)
        shapes = [rows(half * columns + extra)] * 2
        return step(diagonal_kernel, list(guest), shapes, "send_diagonal")

    def second(by_y, by_x, *state, part=(0, columns)):
        wide = high * (part[1] - part[0])
        extra = state[1].shape[1] // 4 if state else 0
        shapes = [rows(wide + extra + (128 if state else 0)), rows(wide + extra)]
        kernel = functools.partial(side_kernel, part)
        return step(kernel, [by_y, by_x, *state], shapes, "send_sides")

    def third(from_x, from_y, *state, part=(0, columns)):
        width = part[1] - part[0]
        shapes = [state_shape] * len(state) + [rows(width, F32)]
        shapes += [rows(width + 128 * len(state))] * (high - 1)
        kernel = functools.partial(slow_kernel, part)
        return step(kernel, [from_x, from_y, *state], shapes, "send_slow")

    return first, second, third


def ring_blocks(grad, me, high):
    def kernel(me_ref, grad_ref, *out_refs):
        x, y, z = me_ref[0] % 2, me_ref[0] // 2 % 2, me_ref[0] // 4
        for hop, out_ref in enumerate(out_refs):
            slow = (z - 1 - hop + high) % high
            for part in range(4):
                from_x = 1 - x if part % 2 else x
                from_y = 1 - y if part // 2 else y
                block = take_down(slow * 4 + from_y * 2 + from_x, grad_ref)
                lanes = slice(part * HALF_FF, (part + 1) * HALF_FF)
                out_ref[:, lanes] = block.astype(out_ref.dtype)

    shapes = [
        jax.ShapeDtypeStruct((DBLK, 4 * HALF_FF), BF16 if hop < high - 1 else F32)
        for hop in range(high)
    ]
    return whole_call(kernel, [me, grad], shapes, "ring_blocks", 1)


def ring_add_kernel(far_ref, own_ref, out_ref):
    total = far_ref[...].astype(F32) + own_ref[...].astype(F32)
    out_ref[...] = total.astype(out_ref.dtype)


def ring_add(far, own):
    shape = jax.ShapeDtypeStruct(own.shape, own.dtype)
    return whole_call(ring_add_kernel, [far, own], [shape], "ring_add")[0]


def send_first(to_y, to_x, count):
    return along(to_y, 2, count), along(to_x, 1, count)


def send_second(to_x, to_y, count):
    return along(to_x, 1, count), along(to_y, 2, count)


def send_third(own, *others, count):
    return [own] + [shifted(block, step + 1, count) for step, block in enumerate(others)]


def scatter_all(qkv, out, ffn_grad, down, count):
    qkv = qkv.reshape(GRID, DBLK, 3, HALF_GRID, DBLK).transpose(2, 0, 3, 1, 4)
    out = out.reshape(HALF_GRID, DBLK, GRID, DBLK).transpose(0, 2, 1, 3)
    ffn_grad = ffn_grad.reshape(GRID, DBLK, 2, HALF_GRID, FBLK).transpose(2, 0, 3, 1, 4)
    down = down.reshape(GRID, DBLK, HALF_GRID, FBLK).transpose(2, 0, 3, 1)
    return (
        lax.psum_scatter(
            qkv.reshape(3, -1, DBLK, DBLK), "dp", scatter_dimension=1, tiled=True
        ),
        lax.psum_scatter(out.reshape(-1, DBLK, DBLK), "dp", scatter_dimension=0, tiled=True),
        lax.psum_scatter(
            ffn_grad.reshape(2, -1, DBLK, FBLK), "dp", scatter_dimension=1, tiled=True
        ),
        lax.psum_scatter(down.reshape(-1, FBLK, DBLK), "dp", scatter_dimension=0, tiled=True),
    )


def gain_rows_kernel(one_ref, two_ref, out_ref):
    def rows(values):
        return [values[:, at : at + 128] for at in range(0, D, 128)]

    parts = rows(one_ref[...]) + rows(0.5 * two_ref[...])
    parts.append(jnp.zeros((STATE_ROWS - len(parts), 128), F32))
    out_ref[...] = jnp.concatenate(parts, 0)


def gain_rows(gain_one, gain_two):
    shape = jax.ShapeDtypeStruct((STATE_ROWS, 128), F32)
    return whole_call(gain_rows_kernel, [gain_one, gain_two], [shape], "gain_rows")[0]


def add_kernel(left_ref, right_ref, out_ref):
    out_ref[...] = left_ref[...] + right_ref[...]


def added(left, right, name):
    return whole_call(add_kernel, [left, right], [jax.ShapeDtypeStruct(left.shape, F32)], name)[0]


def slow_state_kernel(own_ref, *refs):
    out_ref = refs[-1]
    columns = refs[0].shape[1] - 128
    values = [unpaired(paired(own_ref[...]))] + [unpaired(ref[:, columns:]) for ref in refs[:-1]]
    while len(values) > 1:
        half = len(values) // 2
        values = [values[index] + values[index + half] for index in range(half)]
    out_ref[...] = values[0]


def slow_state(own, blocks):
    shape = jax.ShapeDtypeStruct(own.shape, F32)
    return whole_call(slow_state_kernel, [own] + blocks, [shape], "slow_state")[0]


def gains_kernel(near_ref, far_ref, gain_ref, moment_ref, grad_ref, moment_new_ref, gain_new_ref):
    total = near_ref[...] + far_ref[...]
    count = D // 128
    grad = jnp.concatenate(
        [
            jnp.concatenate([total[at + row : at + row + 1] for row in range(count)], 1)
            for at in (0, count)
        ],
        0,
    )
    grad_ref[...] = grad
    moment = DECAY * moment_ref[...] + (1.0 - DECAY) * grad * grad
    moment_new_ref[...] = moment
    gain_new_ref[...] = gain_ref[...] - GAIN_RATE * grad / (jnp.sqrt(moment) + 1e-08)


def full_dot(left, right, left_dim, right_dim):
    return lax.dot_general(
        left,
        right,
        (((left_dim,), (right_dim,)), ((), ())),
        preferred_element_type=F32,
        precision=lax.Precision.DEFAULT,
    )


def precondition(
    parts,
    width,
    left,
    right,
    left_root,
    right_root,
    masters,
    turned=False,
    matrices=None,
    carry=(),
    starts=None,
):
    starts = [0] * len(parts) if starts is None else starts
    counts = [master.shape[0] for master in masters]
    spots = [(which, here) for which, many in enumerate(counts) for here in range(many)]
    matrices = range(len(spots)) if matrices is None else matrices
    many = len(parts)

    def kernel(*refs):
        part_refs, refs, total_ref = refs[:many], refs[many:-1], refs[-1]
        left_ref, right_ref, left_root_ref, right_root_ref = refs[:4]
        master_refs, refs = refs[4 : 4 + len(counts)], refs[4 + len(counts) :]
        carry_refs, refs = refs[: len(carry)], refs[len(carry) :]
        grad_ref, left_new_ref, right_new_ref = refs[:3]
        new_refs = refs[3:]
        for matrix, (which, here) in enumerate(spots):
            if carry and matrix not in matrices:
                for out_ref, carry_ref in zip(refs[:3], carry_refs[:3]):
                    out_ref[matrix] = carry_ref[matrix]
                new_refs[which][here] = carry_refs[3 + which][here]
        wide = len(matrices) * HALF_GRID * width
        total = jnp.zeros((part_refs[0].shape[0], wide), F32)
        for ref, start in zip(part_refs, starts):
            total = total + ref[:, start : start + wide].astype(F32)
        total_ref[...] = total

        def update(which, here, matrix, block, grad):
            grad_ref[matrix, block] = grad
            outer, inner = full_dot(grad, grad, 1, 1), full_dot(grad, grad, 0, 0)
            if turned:
                outer, inner = inner, outer
                step = full_dot(grad, left_root_ref[matrix, block], 1, 1)
                step = full_dot(right_root_ref[matrix, block], step, 0, 0)
            else:
                step = full_dot(left_root_ref[matrix, block], grad, 1, 0)
                step = full_dot(step, right_root_ref[matrix, block], 1, 0)
            left_new_ref[matrix, block] = DECAY * left_ref[matrix, block] + (1.0 - DECAY) * outer
            right_new_ref[matrix, block] = DECAY * right_ref[matrix, block] + (1.0 - DECAY) * inner
            new_refs[which][here, block] = master_refs[which][here, block] - STEP_RATE * step

        def update_matrix(which, here, matrix, number):
            start = number * HALF_GRID * width
            if width % 128:
                lanes = pl.ds(pl.multiple_of(start, 128), HALF_GRID * width)
                row = total_ref[:, lanes]
                for block in range(HALF_GRID):
                    at = block * width
                    update(which, here, matrix, block, row[:, at : at + width])
            else:
                for block in range(HALF_GRID):
                    lanes = pl.ds(pl.multiple_of(start + block * width, 128), width)
                    update(which, here, matrix, block, total_ref[:, lanes])

        if len({spots[matrix][0] for matrix in matrices}) == 1:

            @pl.loop(0, len(matrices))
            def _(number):
                matrix = number + matrices[0]
                update_matrix(spots[matrices[0]][0], number + spots[matrices[0]][1], matrix, number)
        else:
            for number, matrix in enumerate(matrices):
                update_matrix(*spots[matrix], matrix, number)

    grads = jax.ShapeDtypeStruct((sum(counts),) + masters[0].shape[1:], F32)
    like = [jax.ShapeDtypeStruct(array.shape, F32) for array in (left, right)]
    news = [jax.ShapeDtypeStruct(master.shape, F32) for master in masters]
    inputs = list(parts) + [left, right, left_root, right_root] + list(masters)
    total = pltpu.VMEM((parts[0].shape[0], len(matrices) * HALF_GRID * width), F32)
    return whole_call(
        kernel, inputs + list(carry), [grads] + like + news, "precondition", scratch=[total]
    )


def plain_precondition(block_grad, left_stat, right_stat, left_root, right_root, master):
    new_left = DECAY * left_stat + (1.0 - DECAY) * jnp.einsum(
        "...ij,...kj->...ik", block_grad, block_grad, precision=HIGHEST_PRECISION
    )
    new_right = DECAY * right_stat + (1.0 - DECAY) * jnp.einsum(
        "...ji,...jk->...ik", block_grad, block_grad, precision=HIGHEST_PRECISION
    )
    turned = jnp.einsum("...ij,...jk->...ik", left_root, block_grad, precision=HIGHEST_PRECISION)
    turned = jnp.einsum("...ij,...jk->...ik", turned, right_root, precision=HIGHEST_PRECISION)
    return (new_left, new_right, master - STEP_RATE * turned)


def in_order_kernel(core_ref, mine_ref, other_ref, out_ref):
    rows = mine_ref.shape[0]
    core = core_ref[0]
    out_ref[pl.ds(pl.multiple_of(core * rows, 16), rows), :] = mine_ref[...]
    out_ref[pl.ds(pl.multiple_of((1 - core) * rows, 16), rows), :] = other_ref[...]


def in_order(mine, core):
    shape = jax.ShapeDtypeStruct((2 * mine.shape[0], mine.shape[1]), mine.dtype)
    return whole_call(in_order_kernel, [core, mine, other_core(mine)], [shape], "in_order", 1)[0]


def own_and_all(core_ref, rows, step):
    own = pl.ds(pl.multiple_of(step * ROWS, ROWS), ROWS)
    return own, pl.ds(pl.multiple_of(core_ref[0] * rows + step * ROWS, ROWS), ROWS)


def layer_out_kernel(core_ref, x1_ref, near_ref, far_ref, out_ref):
    @pl.loop(0, out_ref.shape[0] // ROWS)
    def _(step):
        own, rows = own_and_all(core_ref, out_ref.shape[0], step)
        total = x1_ref[rows, :] + near_ref[rows, :].astype(F32) + far_ref[rows, :].astype(F32)
        out_ref[own, :] = total.astype(BF16)


def input_grad_kernel(core_ref, x_ref, dx1_ref, near_ref, far_ref, gain_ref, out_ref):
    @pl.loop(0, out_ref.shape[0] // ROWS)
    def _(step):
        own, rows = own_and_all(core_ref, out_ref.shape[0], step)
        x = x_ref[rows, :].astype(F32)
        scale = lax.rsqrt(jnp.mean(x * x, -1, keepdims=True) + EPSILON)
        grad = near_ref[rows, :].astype(F32) + far_ref[rows, :].astype(F32)
        weighted = grad * gain_ref[0:1, :]
        inner = jnp.mean(weighted * x, -1, keepdims=True)
        out_ref[own, :] = dx1_ref[rows, :] + scale * weighted - x * (scale * scale * scale * inner)


def rotary_tables(length):
    frequency = jnp.power(10000.0, -2.0 * jnp.arange(HEAD_DIM // 2, dtype=F32) / HEAD_DIM)
    angles = (jnp.arange(length) % LEN).astype(F32)[:, None] * frequency[None, :]
    shape = jax.ShapeDtypeStruct((length, PAIR), F32)
    return whole_call(tables_kernel, [jnp.cos(angles), jnp.sin(angles)], [shape] * 2, "tables")


def body(
    tokens,
    cotangent,
    gains,
    gain_moments,
    qkv_master,
    out_master,
    ffn_master,
    down_master,
    attn_left,
    attn_right,
    attn_left_root,
    attn_right_root,
    ffn_left,
    ffn_right,
    ffn_left_root,
    ffn_right_root,
    down_left,
    down_right,
    down_left_root,
    down_right_root,
):
    count = lax.axis_size("dp")
    me = lax.axis_index("dp").astype(jnp.int32)[None]
    core = lax.axis_index("narrow").astype(jnp.int32)[None]
    own_rows = tokens.shape[0]
    by_hand = count == GRID

    if by_hand:
        high = count // 4
        first, second, slab = pack(
            qkv_master[:, 0], out_master, ffn_master[:, 0], jnp.swapaxes(down_master, 2, 3)
        )
        one, two, last = 4 * HALF_D, FF, HALF_FF
        width, half, ring_start = one + two + last, (one + two + last) // 2, one + two
        many = high - 1
        far_one = all_shifted(first, count)
        slab_x, slab_y = along(slab, 1, count), along(slab, 2, count)

    x, cot = in_order(tokens, core), in_order(cotangent, core)
    cosine, sine_part = rotary_tables(x.shape[0])

    if by_hand:
        chunk = [(number, 0, one) for number in range(many)]
        near_x, near_y = copy_columns(
            [after(far_one[0], x, cot, cosine, sine_part)] + far_one[1:] + [slab_x, slab_y],
            [chunk + [(many + 1, half, width)], chunk + [(many, 0, half)]],
            "end_round_one",
        )
        one_x, one_y = along(near_x, 1, count), along(near_y, 2, count)
        far_two = all_shifted(after(second, *far_one), count)
        tail = many * one
        one_a, one_b, near_two, square = copy_columns(
            [one_x, one_y] + far_two + [slab, slab_x, slab_y],
            [
                [(0, number * one, number * one + one // 2) for number in range(many)],
                [(1, number * one + one // 2, (number + 1) * one) for number in range(many)],
                [(2 + number, 0, two) for number in range(many)],
                [(2 + many + part, ring_start, width) for part in range(3)]
                + [(0, tail + ring_start - half, tail + width - half)],
            ],
            "end_round_two",
        )
        one_a, one_b = along(one_a, 2, count), along(one_b, 1, count)
        squares = [square, shifted(square, 1, count)]
        entries = [(0, 0, one, 0, 0, 0, 0), (1, 0, one, 0, 0, 1, 0), (2, 0, one, 0, 1, 0, 0)]
        entries.append((5, tail, one, 0, 1, 1, 0))
        for number in range(many):
            step, at = number + 1, number * one
            entries += [(3, at, one, step, 0, 0, 0), (4, at, one, step, 0, 1, 0)]
            entries += [(5, at, one, step, 1, 0, 0)]
        shapes = [(D, 3 * HALF_D), (HALF_D, D)]
        early = [slab, slab_x, slab_y, near_x, one_x, one_y]
        early[0] = after(slab, near_two)
        w_early = assemble(me, high, early, entries, place_qkv_out, shapes, "place_qkv_out")
        entries = []
        for number in range(many):
            step, at = number + 1, number * (one // 2)
            entries += [(0, at, one // 2, step, 1, 1, 0), (1, at, one // 2, step, 1, 1, one // 2)]
        w_qkv, w_out = assemble(
            me, high, [one_a, one_b], entries, place_qkv_out, shapes, "place_rest", w_early
        )
        near_late = after(near_two, one_a, one_b, w_early[0], squares[1])
        two_x, two_y = along(near_late, 1, count), along(near_late, 2, count)
        squares.append(shifted(after(squares[1], one_a, one_b, w_early[0]), 1, count))
    else:
        qkv, ffn_part = qkv_master[:, 0].astype(BF16), ffn_master[:, 0].astype(BF16)
        w_qkv, w_out, w_gate, w_up, w_down = gather_by_name(
            qkv, out_master.astype(BF16), ffn_part, down_master[0].astype(BF16)
        )
    normed_one, q, k, v = project(x, gains, w_qkv, cosine, sine_part)
    attended, lse = attend(q, k, v)
    attended_late, w_out_late = attended, w_out
    if by_hand:
        two_a, two_b = copy_columns(
            [after(two_x, attended, *squares[1:]), two_y],
            [
                [(0, number * two, number * two + two // 2) for number in range(many)],
                [(1, number * two + two // 2, (number + 1) * two) for number in range(many)],
            ],
            "end_round_four",
        )
        early = [slab, slab_x, slab_y, one_x, one_y, near_two, two_x, two_y]
        early[0] = after(slab, two_a)
        attended_late, w_out_late = after(attended, two_a), after(w_out, two_a)
        two_a, two_b = along(two_a, 2, count), along(two_b, 1, count)
        cut = half - one
        entries = [(0, one, two, 0, 0, 0, 0), (1, one, two, 0, 0, 1, 0), (2, one, two, 0, 1, 0, 0)]
        entries += [(4, tail + one, cut, 0, 1, 1, 0), (3, tail, two - cut, 0, 1, 1, cut)]
        for number in range(many):
            step, at = number + 1, number * two
            entries += [(5, at, two, step, 0, 0, 0), (6, at, two, step, 0, 1, 0)]
            entries += [(7, at, two, step, 1, 0, 0)]
        shapes = [(D, HALF_FF)] * 2
        w_early = assemble(me, high, early, entries, place_gate_up, shapes, "place_gate_up")
        entries = []
        for number in range(many):
            step, at = number + 1, number * (two // 2)
            entries += [(0, at, two // 2, step, 1, 1, 0), (1, at, two // 2, step, 1, 1, two // 2)]
        w_gate, w_up = assemble(
            me,
            high,
            [two_a, two_b],
            entries,
            place_gate_up,
            shapes,
            "place_rest",
            w_early,
        )
        for _ in range(3, high):
            squares.append(shifted(after(squares[-1], w_gate), 1, count))
    attended_far, w_out_far = other_core(attended_late), other_core(w_out_late)
    middle, normed_two, gate, up, hidden = ffn(
        x, attended, attended_far, w_out, w_out_far, gains, w_gate, w_up
    )

    if by_hand:
        squares[0] = after(squares[0], hidden)
        (w_down,) = assemble(
            me,
            high,
            squares,
            [
                (step, part * last, last, step, part // 2, part % 2, 0)
                for step in range(high)
                for part in range(4)
            ],
            place_down,
            [(D, HALF_FF)],
            "place_down",
        )
    down_weight_grad = dot_tn(cot, hidden)
    cot_late = cot
    if by_hand:
        ring = ring_blocks(down_weight_grad, me, high)
        passed = shifted(ring[0], 1, count)
        cot_late = after(cot, ring[0])
    ffn_back_grad, normed_part = ffn_back(cot_late, gate, up, w_down, w_gate, w_up)
    if by_hand:
        sent = ring_add(after(passed, normed_part), ring[1])
        passed = shifted(sent, 1, count)
        ffn_back_grad = after(ffn_back_grad, sent)
        normed_part = after(normed_part, sent)
    normed_far = other_core(normed_part)
    ffn_weight_grad = dot_tn(normed_two, ffn_back_grad)
    if by_hand:
        ffn_sum = reduction([take_rows], FF, count, me, [ffn_weight_grad])
        sent = ffn_sum[0]()
        normed_far = after(normed_far, sent[0])
        ffn_far = send_first(*sent, count)
    middle_grad, branch, attended_grad, gain_two = middle_back(
        cot, middle, normed_part, normed_far, gains, w_out
    )
    out_weight_grad = dot_tn(attended, branch)
    out_part = ffn_out(after(hidden, branch), w_down)
    out_part_late = out_part
    if by_hand:
        late = [branch, out_part, out_weight_grad]
        for number in range(2, high - 1):
            sent = ring_add(after(passed, *late), ring[number])
            passed = shifted(sent, 1, count)
            late.append(sent)
        sent = ffn_sum[1](after(ffn_far[0], *late), ffn_far[1])
        ffn_far = send_second(*sent, count)
        attended_grad = after(attended_grad, sent[0])
        out_part_late = after(out_part, sent[0])
    out_far = other_core(out_part_late)
    qkv_back_grad = attend_back(q, k, v, attended_grad, attended, lse, cosine, sine_part)
    layer_out = whole_call(
        layer_out_kernel,
        [core, after(middle, qkv_back_grad), out_part, out_far],
        [jax.ShapeDtypeStruct((own_rows, D), BF16)],
        "layer_out",
        1,
    )[0]
    if by_hand:
        down_near = ring_add(after(passed, qkv_back_grad, layer_out), ring[-1])
        ffn_sent = ffn_sum[2](after(ffn_far[0], qkv_back_grad, layer_out), ffn_far[1])
        ffn_parts = [ffn_sent[0]] + [
            shifted(block, step + 1, count)
            for step, block in enumerate(ffn_sent[1:])
            if step + 1 != high // 2
        ]
        qkv_back_grad = after(qkv_back_grad, ffn_sent[0])
    qkv_weight_grad = dot_tn(normed_one, qkv_back_grad)
    if by_hand:
        late_sum = reduction(
            [take_rows, take_out], 4 * HALF_D, count, me, [qkv_weight_grad, out_weight_grad]
        )
        sent = late_sum[0](down_near)
        late_far = list(send_first(*sent, count))
        qkv_back_grad = after(qkv_back_grad, sent[0])
    input_part, gain_one = input_back(x, qkv_back_grad, w_qkv)
    input_part_late = input_part
    if by_hand:
        state = gain_rows(gain_one, gain_two)
        state = added(state, other_core(state), "add_gains")
        late_cut = 2 * HALF_D
        parts = [(0, late_cut), (late_cut, 2 * late_cut)]
        late_far[0] = after(late_far[0], *ffn_parts[1:])
        sent = late_sum[1](*late_far, state, down_near, part=parts[0])
        first_far = send_second(*sent, count)
        ffn_parts.append(shifted(after(ffn_sent[high // 2], sent[0]), high // 2, count))
        input_part_late = after(input_part, sent[0])
        second_sent = late_sum[1](after(late_far[0], sent[0]), late_far[1], part=parts[1])
    input_far = other_core(input_part_late)
    input_grad = whole_call(
        input_grad_kernel,
        [core, x, middle_grad, input_part, input_far, gains],
        [jax.ShapeDtypeStruct((own_rows, D), F32)],
        "input_grad",
        1,
    )[0]
    if by_hand:
        second_far = send_second(
            after(second_sent[0], input_grad, *first_far, *ffn_parts[1:]), second_sent[1], count
        )
        first_state, *sent = late_sum[2](
            *first_far,
            state,
            part=parts[0],
        )
        first_parts = send_third(*sent, count=count)
        ffn_parts[0] = after(ffn_parts[0], sent[0])
        ffn_grad, ffn_left_new, ffn_right_new, ffn_new = precondition(
            ffn_parts,
            FBLK,
            ffn_left[:, 0],
            ffn_right[:, 0],
            ffn_left_root[:, 0],
            ffn_right_root[:, 0],
            [ffn_master[:, 0]],
        )
        sent = late_sum[2](after(second_far[0], ffn_left_new), second_far[1], part=parts[1])
        second_parts = send_third(*sent, count=count)
        first_state = slow_state(after(first_state, sent[0]), first_parts[1:])
        wide = high * late_cut
        down_grad, down_left_new, down_right_new, down_new = precondition(
            [after(down_near, first_state), *first_far],
            FBLK,
            down_left,
            down_right,
            down_left_root,
            down_right_root,
            [jnp.swapaxes(down_master, 2, 3)],
            turned=True,
            starts=[0, wide + 128, wide],
        )
        down_grad, down_new = jnp.swapaxes(down_grad, 2, 3), jnp.swapaxes(down_new, 2, 3)
        first_parts[0] = after(first_parts[0], down_left_new)
        gain_grad, gain_moment_new, gain_new = whole_call(
            gains_kernel,
            [first_state, along(first_state, 2, count), gains, gain_moments],
            [jax.ShapeDtypeStruct(gains.shape, F32)] * 3,
            "gains",
        )
        attn_results = ()
        for matrices, some in ((range(2), first_parts), (range(2, 4), second_parts)):
            attn_results = precondition(
                some,
                DBLK,
                attn_left[:, 0],
                attn_right[:, 0],
                attn_left_root[:, 0],
                attn_right_root[:, 0],
                [qkv_master[:, 0], out_master],
                matrices=matrices,
                carry=attn_results,
            )
            second_parts[0] = after(second_parts[0], gain_grad, attn_results[0])
        *stacked, out_new = attn_results
        attn_grad, attn_left_new, attn_right_new, qkv_new = (array[:, None] for array in stacked)
        ffn_grad, ffn_left_new, ffn_right_new, ffn_new = (
            array[:, None] for array in (ffn_grad, ffn_left_new, ffn_right_new, ffn_new)
        )
    else:
        gain_terms = jnp.concatenate([gain_one, 0.5 * gain_two])
        gain_grad = lax.psum(gain_terms, ("dp", "narrow"))
        gain_moment_new = DECAY * gain_moments + (1.0 - DECAY) * gain_grad * gain_grad
        gain_new = gains - GAIN_RATE * gain_grad / (jnp.sqrt(gain_moment_new) + 1e-08)
        qkv_owned, out_owned, ffn_owned, down_owned = scatter_all(
            qkv_weight_grad, out_weight_grad, ffn_weight_grad, down_weight_grad, count
        )
        attn_grad = jnp.concatenate([qkv_owned, out_owned[None]], 0)[:, None]
        ffn_grad = ffn_owned[:, None]
        down_grad = down_owned[None]
        attn_left_new, attn_right_new, attn_new = plain_precondition(
            attn_grad,
            attn_left,
            attn_right,
            attn_left_root,
            attn_right_root,
            jnp.concatenate([qkv_master, out_master[None]], 0),
        )
        qkv_new, out_new = attn_new[:3], attn_new[3]
        ffn_left_new, ffn_right_new, ffn_new = plain_precondition(
            ffn_grad, ffn_left, ffn_right, ffn_left_root, ffn_right_root, ffn_master
        )
        down_left_new, down_right_new, down_new = plain_precondition(
            down_grad, down_left, down_right, down_left_root, down_right_root, down_master
        )
    return (
        layer_out,
        input_grad,
        gain_grad,
        gain_moment_new,
        gain_new,
        attn_grad,
        attn_left_new,
        attn_right_new,
        qkv_new,
        out_new,
        ffn_grad,
        ffn_left_new,
        ffn_right_new,
        ffn_new,
        down_grad,
        down_left_new,
        down_right_new,
        down_new,
    )


def solution(mesh):
    tokens = P(("dp", "narrow"), None)
    stacked = P(None, "narrow", "dp", None, None)
    single = P("narrow", "dp", None, None)
    return jax.shard_map(
        body,
        mesh=mesh,
        in_specs=(tokens, tokens, P(), P(), stacked, single, stacked, single)
        + (stacked,) * 8
        + (single,) * 4,
        out_specs=(tokens, tokens, P(), P(), P())
        + (stacked,) * 4
        + (single,)
        + (stacked,) * 4
        + (single,) * 4,
        check_vma=False,
    )
```
